32 devices in a mesh: head: 4 (over z), blk: 8 (over y, x, core).
Axes of the slice: x: 2, y: 2, z: 4, core: 2. Of those that a mesh axis runs over, the one named last changes fastest.
Arguments:
- tokens: bfloat16 [32768, 768], P(('blk', 'head')), may hold values from -6 to 6
- w_query: bfloat16 [768, 768], P(('head', 'blk')), may hold values from -0.21875 to 0.21875
- w_key: bfloat16 [768, 768], P(('head', 'blk')), may hold values from -0.21875 to 0.21875
- w_value: bfloat16 [768, 768], P(('head', 'blk')), may hold values from -0.21875 to 0.21875
- w_attn: bfloat16 [768, 768], P(('head', 'blk')), may hold values from -3.5 to 3.5
- w_inner: bfloat16 [768, 3072], P(('head', 'blk')), may hold values from -0.21875 to 0.21875
- w_outer: bfloat16 [3072, 768], P(('head', 'blk')), may hold values from -0.109375 to 0.109375
- bias_query: bfloat16 [768], P(('head', 'blk')), may hold values from -3 to 3
- bias_value: bfloat16 [768], P(('head', 'blk')), may hold values from -3 to 3
- bias_attn: bfloat16 [768], P(('head', 'blk')), may hold values from -3 to 3
- gain_one: bfloat16 [768], P(('head', 'blk')), may hold values from 0.5 to 1.5
- offset_one: bfloat16 [768], P(('head', 'blk')), may hold values from -3 to 3
- bias_inner: bfloat16 [3072], P(('head', 'blk')), may hold values from -3 to 3
- bias_outer: bfloat16 [768], P(('head', 'blk')), may hold values from -3 to 3
- gain_two: bfloat16 [768], P(('head', 'blk')), may hold values from 0.5 to 1.5
- offset_two: bfloat16 [768], P(('head', 'blk')), may hold values from -3 to 3
- out_grad: bfloat16 [32768, 768], P(('blk', 'head')), may hold values from -6 to 6
- segment_ids: int32 [32768], replicated, may hold values from 0 to 163, as said below
- random_blocks: int32 [12, 512, 3], replicated, may hold values from 0 to 511, as said below
Outputs:
- output_rows: bfloat16 [32768, 768], P(('blk', 'head'))
- grad_tokens: float32 [32768, 768], P(('blk', 'head'))
- grad_w_query: float32 [768, 768], P(('head', 'blk'))
- grad_w_key: float32 [768, 768], P(('head', 'blk'))
- grad_w_value: float32 [768, 768], P(('head', 'blk'))
- grad_w_attn: float32 [768, 768], P(('head', 'blk'))
- grad_w_inner: float32 [768, 3072], P(('head', 'blk'))
- grad_w_outer: float32 [3072, 768], P(('head', 'blk'))
- grad_bias_query: float32 [768], P(('head', 'blk'))
- grad_bias_value: float32 [768], P(('head', 'blk'))
- grad_bias_attn: float32 [768], P(('head', 'blk'))
- grad_gain_one: float32 [768], P(('head', 'blk'))
- grad_offset_one: float32 [768], P(('head', 'blk'))
- grad_bias_inner: float32 [3072], P(('head', 'blk'))
- grad_bias_outer: float32 [768], P(('head', 'blk'))
- grad_gain_two: float32 [768], P(('head', 'blk'))
- grad_offset_two: float32 [768], P(('head', 'blk'))
The draws below stay inside these ranges and needn't reach their ends.
Inputs may be any that keep to these rules, and one draw needn't show every extreme that they name: `segment_ids`: numbers never fall along the tokens; a document holds at most 2000 tokens, the first of every sequence exactly 2000, and every document but the last of its sequence 200 or more; no document crosses a boundary of the sequences of 32768 tokens, and different sequences have different numbers; the last document of all has the largest number. `random_blocks`: entry [h, b, r] is a block from the first to the last block that holds tokens of the document of block b's first token.
All inputs are finite; a program needn't handle non-finite values.
Results may differ from the reference program's by a relative error of at most 0.015.
Values may be sent and summed in bfloat16 or wider, within the bound.
A program may use at most 192 MiB of HBM per device.

```python
from functools import partial
import jax
import jax.numpy as jnp
from jax import lax

D = 768
HEADS = 12
HEAD_DIM = 64
FF = 3072
BLOCK = 64
RANDOM = 3
DOC_MIN = 200
DOC_MAX = 2000
TOKENS = 32768
SEQ = 32768


def document_ids(key):
    seq_count = TOKENS // SEQ
    doc_slots = SEQ // DOC_MIN + 1
    lengths = jax.random.randint(jax.random.fold_in(key, 17), (seq_count, doc_slots), DOC_MIN, DOC_MAX + 1)
    lengths = lengths.at[:, 0].set(DOC_MAX)
    doc_ends = jnp.cumsum(lengths, axis=1)
    places = jnp.arange(SEQ, dtype=jnp.int32)
    inside = jax.vmap(lambda seq_ends: jnp.searchsorted(seq_ends, places, side='right'))(doc_ends)
    numbers = inside.astype(jnp.int32) + doc_slots * jnp.arange(seq_count, dtype=jnp.int32)[:, None]
    numbers = numbers.reshape(TOKENS).astype(jnp.int32)
    last_doc = numbers[TOKENS - 1]
    top_number = jnp.int32(seq_count * doc_slots - 1)
    return jnp.where(numbers == last_doc, top_number, numbers).astype(jnp.int32)


def draw_segment_ids(key, part):
    return document_ids(key)


def draw_random_blocks(key, part):
    numbers = document_ids(key)
    places = jnp.arange(TOKENS, dtype=jnp.int32)
    doc_begins = jnp.concatenate([jnp.ones((1,), jnp.bool_), numbers[1:] != numbers[:-1]])
    doc_finish = jnp.concatenate([numbers[1:] != numbers[:-1], jnp.ones((1,), jnp.bool_)])
    starts = lax.cummax(jnp.where(doc_begins, places, 0))
    doc_ends = lax.cummin(jnp.where(doc_finish, places, TOKENS - 1), reverse=True)
    first_block = starts[::BLOCK] // BLOCK
    last_block = doc_ends[::BLOCK] // BLOCK
    span_blocks = last_block - first_block + 1
    drawn_ints = jax.random.randint(jax.random.fold_in(key, 29), (HEADS, TOKENS // BLOCK, RANDOM), 0, 1 << 20)
    return (first_block[None, :, None] + drawn_ints % span_blocks[None, :, None]).astype(jnp.int32)


def strengthened(array, stream_key, source, target, shards_of, factor):
    def block_of(position):
        return (jnp.arange(array.shape[position]) // (array.shape[position] // shards_of)).reshape((-1,) + (1,) * (array.ndim - 1 - position))

    first = jax.random.permutation(stream_key, shards_of)[block_of(target)]
    other_side = (block_of(target) + shards_of // 2) % shards_of
    return jnp.where((block_of(source) == first) | (block_of(source) == other_side), factor * array, array)


def shard_levels(rng, dims, cuts, low, high):
    def one(dim, parts):
        steps = jax.random.uniform(jax.random.fold_in(jax.random.fold_in(rng, 6), dim), (parts,), jnp.float32, low / len(cuts), high / len(cuts))
        return jnp.repeat(jnp.exp(steps), dims[dim] // parts).reshape((-1,) + (1,) * (len(dims) - dim - 1))

    gain = one(*cuts[0])
    for cut in cuts[1:]:
        gain = gain * one(*cut)
    return gain


def scatter_about(key, shape, width, limit, pieces=(), held_as=jnp.bfloat16):
    drawn = width * jax.random.normal(key, shape, jnp.float32)
    if pieces:
        drawn = drawn * shard_levels(key, shape, pieces, -0.22, 0.18)
    return jnp.clip(drawn, -limit, limit).astype(held_as)


def noise_with(rng, shape, scale, most, shards, heavy, held_as=jnp.bfloat16):
    drawn = scale * jax.random.normal(rng, shape, jnp.float32)
    if shards:
        drawn = drawn * shard_levels(rng, shape, shards, -0.22, 0.18)
    return jnp.clip(strengthened(drawn, jax.random.fold_in(rng, 3), *heavy), -most, most).astype(held_as)


def setup_inputs(seed: int = 0) -> dict:
    key_list = jax.random.split(jax.random.key(seed), 20)
    tokens = scatter_about(key_list[0], (TOKENS, D), 1.0, 6.0, ((0, 32),))
    w_query = scatter_about(key_list[1], (D, D), D ** -0.5, 0.21875, ((0, 32),))
    w_key = scatter_about(key_list[2], (D, D), D ** -0.5, 0.21875, ((0, 32),))
    w_value = scatter_about(key_list[3], (D, D), D ** -0.5, 0.21875, ((0, 32),))
    w_attn = scatter_about(key_list[4], (D, D), (max(1, D // 256)) ** -0.5, 3.5, ((0, 32),))
    w_inner = scatter_about(key_list[5], (D, FF), D ** -0.5, 0.21875, ((0, 32),))
    w_outer = scatter_about(key_list[6], (FF, D), FF ** -0.5, 0.109375, ((0, 32),))
    bias_query = scatter_about(key_list[7], (D,), 0.5, 3.0, ((0, 32),))
    bias_value = scatter_about(key_list[8], (D,), 0.5, 3.0, ((0, 32),))
    bias_attn = scatter_about(key_list[9], (D,), 0.5, 3.0, ((0, 32),))
    gain_one = jnp.clip(1.0 + 0.1 * jax.random.normal(key_list[10], (D,), jnp.float32), 0.5, 1.5).astype(jnp.bfloat16)
    offset_one = scatter_about(key_list[11], (D,), 0.5, 3.0, ((0, 32),))
    bias_inner = scatter_about(key_list[12], (FF,), 0.5, 3.0, ((0, 32),))
    bias_outer = scatter_about(key_list[13], (D,), 0.5, 3.0, ((0, 32),))
    gain_two = jnp.clip(1.0 + 0.1 * jax.random.normal(key_list[14], (D,), jnp.float32), 0.5, 1.5).astype(jnp.bfloat16)
    offset_two = scatter_about(key_list[15], (D,), 0.5, 3.0, ((0, 32),))
    out_grad = noise_with(key_list[16], (TOKENS, D), 1.0, 6.0, ((0, 32),), (0, 1, 32, 2.75))
    segment_ids = draw_segment_ids(jax.random.fold_in(key_list[19], 71), 0)
    random_blocks = draw_random_blocks(jax.random.fold_in(key_list[19], 71), 0)
    return {"tokens": tokens, "w_query": w_query, "w_key": w_key, "w_value": w_value, "w_attn": w_attn, "w_inner": w_inner, "w_outer": w_outer, "bias_query": bias_query, "bias_value": bias_value, "bias_attn": bias_attn, "gain_one": gain_one, "offset_one": offset_one, "bias_inner": bias_inner, "bias_outer": bias_outer, "gain_two": gain_two, "offset_two": offset_two, "out_grad": out_grad, "segment_ids": segment_ids, "random_blocks": random_blocks}


@jax.custom_vjp
def low(v):
    return lax.optimization_barrier(v.astype(jnp.bfloat16)).astype(jnp.float32)

@jax.custom_vjp
def low_back(v):
    return v

def low_keep(v):
    return (low(v), None)

def low_pass(kept, grad):
    return (grad,)

def back_keep(v):
    return (v, None)

def back_low(kept, grad):
    return (low(grad),)
low.defvjp(low_keep, low_pass)
low_back.defvjp(back_keep, back_low)
epsilon = 1e-06
masked_value = -1e+30
row_limit = 512
piece_limit = 4096
query_scale = 0.125
highest_precision = lax.Precision.HIGHEST

def narrow_both(values):
    return low_back(low(values))

def product(left, right):
    return jnp.dot(left, right, precision=highest_precision)

def layer_norm(values, gain_vec, offset):
    centred = values - lax.optimization_barrier(jnp.mean(values, axis=-1, keepdims=True))
    spread = lax.optimization_barrier(jnp.mean(centred * centred, axis=-1, keepdims=True))
    return centred * lax.rsqrt(spread + epsilon) * gain_vec + offset

def choose_tiles(block_ids, first_start, randoms, total_blocks):
    doc_first_block = first_start // BLOCK
    fixed_rows = jnp.stack([block_ids - 1, block_ids, block_ids + 1, doc_first_block, doc_first_block + 1], axis=-1)
    head_count = randoms.shape[1]
    fixed_rows = jnp.broadcast_to(fixed_rows[:, None, :], (fixed_rows.shape[0], head_count, 5))
    tile_rows = jnp.concatenate([fixed_rows, randoms], axis=-1)
    tile_count = tile_rows.shape[-1]
    inside = (tile_rows >= 0) & (tile_rows < total_blocks)
    earlier = jnp.arange(tile_count)[None, :] < jnp.arange(tile_count)[:, None]
    repeat = jnp.any((tile_rows[..., :, None] == tile_rows[..., None, :]) & earlier, axis=-1)
    return (jnp.clip(tile_rows, 0, total_blocks - 1), inside & jnp.logical_not(repeat))

def pick_tiles(tile_table, tile_rows):
    return jax.vmap(lambda one_table, one_rows: one_table[one_rows], in_axes=(0, 1), out_axes=1)(tile_table, tile_rows)

def sequence_plan(seq_segments, random_local):
    seq_blocks = SEQ // BLOCK
    places = jnp.arange(SEQ, dtype=jnp.int32)
    begins = jnp.concatenate([jnp.ones((1,), dtype=jnp.bool_), seq_segments[1:] != seq_segments[:-1]])
    doc_start = lax.cummax(jnp.where(begins, places, 0))
    first_start = doc_start[::BLOCK]
    block_ids = jnp.arange(seq_blocks, dtype=jnp.int32)
    tile_rows, tile_valid = choose_tiles(block_ids, first_start, random_local, seq_blocks)
    key_places = tile_rows[..., None] * BLOCK + jnp.arange(BLOCK, dtype=jnp.int32)
    seg_keys = seq_segments[key_places]
    seg_query = seq_segments.reshape(seq_blocks, BLOCK)
    return (tile_rows, tile_valid, seg_query, seg_keys)

def attend_block(key_table, value_table, step_item):
    query_blocks, tile_rows, tile_valid, seg_query, seg_keys = step_item
    key_tiles = pick_tiles(key_table, tile_rows)
    value_tiles = pick_tiles(value_table, tile_rows)
    scores = jnp.einsum('nqhd,nhjtd->nhqjt', query_blocks, key_tiles, precision=highest_precision)
    scores = low_back(scores)
    allowed = tile_valid[:, :, None, :, None] & (seg_keys[:, :, None, :, :] == seg_query[:, None, :, None, None])
    scores = jnp.where(allowed, scores, masked_value)
    scores = scores.reshape(scores.shape[0], scores.shape[1], scores.shape[2], -1)
    highest = lax.optimization_barrier(jnp.max(scores, axis=-1, keepdims=True))
    raised = jnp.exp(scores - highest)
    prob_rows = low(raised / lax.optimization_barrier(jnp.sum(raised, axis=-1, keepdims=True)))
    values_flat = value_tiles.reshape(prob_rows.shape[0], prob_rows.shape[1], prob_rows.shape[3], -1)
    return jnp.einsum('nhqk,nhkd->nqhd', prob_rows, values_flat, precision=highest_precision)

def post_rows(attended, inputs, params):
    w_query, w_key, w_value, w_attn, w_inner, w_outer, bias_query, bias_value, bias_attn, gain_one, offset_one, bias_inner, bias_outer, gain_two, offset_two = params
    attn_out = low_back(product(attended, w_attn) + bias_attn)
    first_norm = layer_norm(inputs + attn_out, gain_one, offset_one)
    inner_pre = low_back(product(low(first_norm), w_inner) + bias_inner)
    outer_out = low_back(product(low(jax.nn.gelu(inner_pre, approximate=True)), w_outer) + bias_outer)
    return layer_norm(first_norm + outer_out, gain_two, offset_two)

def layer_forward(plan_arrays, inputs, params):
    w_query, w_key, w_value, w_attn, w_inner, w_outer, bias_query, bias_value, bias_attn, gain_one, offset_one, bias_inner, bias_outer, gain_two, offset_two = params
    tile_rows, tile_valid, seg_query, seg_keys = plan_arrays
    queries = narrow_both(query_scale * (product(inputs, w_query) + bias_query))
    key_rows = narrow_both(product(inputs, w_key))
    value_rows = narrow_both(product(inputs, w_value) + bias_value)
    seq_blocks = SEQ // BLOCK
    key_table = jnp.transpose(key_rows.reshape(seq_blocks, BLOCK, HEADS, HEAD_DIM), (2, 0, 1, 3))
    value_table = jnp.transpose(value_rows.reshape(seq_blocks, BLOCK, HEADS, HEAD_DIM), (2, 0, 1, 3))
    step_blocks = min(seq_blocks, row_limit // BLOCK)
    step_count = seq_blocks // step_blocks
    step_items = (queries.reshape(step_count, step_blocks, BLOCK, HEADS, HEAD_DIM), tile_rows.reshape(step_count, step_blocks, HEADS, -1), tile_valid.reshape(step_count, step_blocks, HEADS, -1), seg_query.reshape(step_count, step_blocks, BLOCK), seg_keys.reshape(step_count, step_blocks, HEADS, -1, BLOCK))
    checked_attend = jax.checkpoint(attend_block)
    attended = lax.map(lambda step_item: checked_attend(key_table, value_table, step_item), step_items)
    attended = narrow_both(attended.reshape(SEQ, D))
    piece_rows = min(SEQ, piece_limit)
    checked_rows = jax.checkpoint(post_rows)
    result = lax.map(lambda row_pair: checked_rows(row_pair[0], row_pair[1], params), (attended.reshape(-1, piece_rows, D), inputs.reshape(-1, piece_rows, D)))
    return result.reshape(SEQ, D)

def reference(tokens, w_query, w_key, w_value, w_attn, w_inner, w_outer, bias_query, bias_value, bias_attn, gain_one, offset_one, bias_inner, bias_outer, gain_two, offset_two, out_grad, segment_ids, random_blocks):
    params = tuple((weight_arg.astype(jnp.float32) for weight_arg in (w_query, w_key, w_value, w_attn, w_inner, w_outer, bias_query, bias_value, bias_attn, gain_one, offset_one, bias_inner, bias_outer, gain_two, offset_two)))
    seq_count = TOKENS // SEQ
    seq_blocks = SEQ // BLOCK
    inputs = tokens.astype(jnp.float32).reshape(seq_count, SEQ, D)
    cotangents = out_grad.astype(jnp.float32).reshape(seq_count, SEQ, D)
    seg_seqs = segment_ids.reshape(seq_count, SEQ)
    random_seqs = jnp.transpose(random_blocks.reshape(HEADS, seq_count, seq_blocks, RANDOM), (1, 2, 0, 3))
    block_offsets = jnp.arange(seq_count, dtype=jnp.int32) * seq_blocks

    def one_sequence(totals, seq_item):
        seq_inputs, seq_cotangent, seq_segments, seq_random, block_offset = seq_item
        plan_arrays = sequence_plan(seq_segments, seq_random - block_offset)
        outputs, backward = jax.vjp(partial(layer_forward, plan_arrays), seq_inputs, params)
        grad_inputs, grad_params = backward(seq_cotangent)
        totals = jax.tree.map(lambda left_sum, right_sum: left_sum + right_sum, totals, grad_params)
        return (totals, (outputs, grad_inputs))
    zero_grads = tuple((jnp.zeros_like(weight_arg) for weight_arg in params))
    totals, (outputs, grad_inputs) = lax.scan(one_sequence, zero_grads, (inputs, cotangents, seg_seqs, random_seqs, block_offsets))
    grad_w_query, grad_w_key, grad_w_value, grad_w_attn, grad_w_inner, grad_w_outer, grad_bias_query, grad_bias_value, grad_bias_attn, grad_gain_one, grad_offset_one, grad_bias_inner, grad_bias_outer, grad_gain_two, grad_offset_two = totals
    return (outputs.reshape(TOKENS, D).astype(jnp.bfloat16), grad_inputs.reshape(TOKENS, D), grad_w_query, grad_w_key, grad_w_value, grad_w_attn, grad_w_inner, grad_w_outer, grad_bias_query, grad_bias_value, grad_bias_attn, grad_gain_one, grad_offset_one, grad_bias_inner, grad_bias_outer, grad_gain_two, grad_offset_two)
```

```python
from functools import partial

import jax
import jax.numpy as jnp
from jax import lax
from jax.experimental import pallas as pl
from jax.experimental.pallas import tpu as pltpu
from jax.sharding import PartitionSpec as P

HEAD_DIM = 64
BLOCK = 64
RANDOM = 3
TILES = 5 + RANDOM
REACH = 2
GROUP = 4

epsilon = 1e-06
masked_value = -1e30
query_scale = 0.125
far_away = -(1 << 24)
f32, bf16 = jnp.float32, jnp.bfloat16


def mm(a, b):
    return jnp.dot(a, b, preferred_element_type=f32)


def mm_nt(a, b):
    return lax.dot_general(a, b, (((1,), (1,)), ((), ())), preferred_element_type=f32)


def mm_tn(a, b):
    return lax.dot_general(a, b, (((0,), (0,)), ((), ())), preferred_element_type=f32)


def head_mask(rows, cols, first):
    lanes = lax.broadcasted_iota(jnp.int32, (rows, cols), 1)
    return (lanes >= first) & (lanes < first + HEAD_DIM)


def stacked_by_head(tile):
    rows, cols = tile.shape
    return jnp.concatenate(
        [
            jnp.where(head_mask(rows, cols, h * HEAD_DIM), tile, jnp.zeros_like(tile))
            for h in range(cols // HEAD_DIM)
        ],
        axis=0,
    )


def own_head_columns(stacked):
    cols = stacked.shape[1]
    total = None
    for h in range(cols // HEAD_DIM):
        part = stacked[h * BLOCK : (h + 1) * BLOCK]
        part = jnp.where(head_mask(BLOCK, cols, h * HEAD_DIM), part, 0.0)
        total = part if total is None else total + part
    return total


def block_rows(row):
    return pl.ds(pl.multiple_of(row * BLOCK, BLOCK), BLOCK)


def gathered(table_ref, fixed_row, random_row):
    tiles = [table_ref[block_rows(fixed_row(t)), :] for t in range(5)]
    low = head_mask(BLOCK, 2 * HEAD_DIM, 0)
    for t in range(RANDOM):
        halves = []
        for pair in range(GROUP // 2):
            cols = pl.ds(pair * 2 * HEAD_DIM, 2 * HEAD_DIM)
            a = table_ref[block_rows(random_row(2 * pair, t)), cols]
            b = table_ref[block_rows(random_row(2 * pair + 1, t)), cols]
            halves.append(jnp.where(low, a, b))
        tiles.append(jnp.concatenate(halves, axis=1))
    return jnp.concatenate(tiles, axis=0)


def row_readers(rows_ref, blocks):
    group, i = pl.program_id(0), pl.program_id(1)

    def fixed_row(t):
        return rows_ref[(group * GROUP * blocks + i) * TILES + t]

    def random_row(h, t):
        return rows_ref[((group * GROUP + h) * blocks + i) * TILES + 5 + t]

    return fixed_row, random_row


def attend_kernel(blocks, rows_ref, q_ref, k_ref, v_ref, base_ref, doc_ref, out_ref, p_ref):
    fixed_row, random_row = row_readers(rows_ref, blocks)
    keys = gathered(k_ref, fixed_row, random_row)
    values = gathered(v_ref, fixed_row, random_row)
    scores = mm_nt(keys, stacked_by_head(q_ref[...]))
    lo = doc_ref[0, 0:1, :]
    hi = doc_ref[0, 1:2, :]
    within = lax.broadcasted_iota(jnp.int32, (BLOCK, GROUP * BLOCK), 0)
    masked = []
    for t in range(TILES):
        place = within + base_ref[0, 0, t : t + 1, :]
        allowed = (place >= lo) & (place < hi)
        masked.append(jnp.where(allowed, scores[t * BLOCK : (t + 1) * BLOCK], masked_value))
    scores = jnp.concatenate(masked, axis=0)
    raised = jnp.exp(scores - jnp.max(scores, axis=0, keepdims=True))
    probs = (raised * (1.0 / jnp.sum(raised, axis=0, keepdims=True))).astype(bf16)
    p_ref[0, 0] = probs
    out_ref[...] = own_head_columns(mm_tn(probs, values)).astype(bf16)


def attend_back_kernel(
    blocks,
    rows_ref,
    q_ref,
    g_ref,
    k_ref,
    v_ref,
    p_ref,
    dq_ref,
    dk_ref,
    dv_ref,
    dk_sum,
    dv_sum,
):
    i = pl.program_id(1)

    @pl.when(i == 0)
    def _():
        dk_sum[...] = jnp.zeros_like(dk_sum)
        dv_sum[...] = jnp.zeros_like(dv_sum)

    fixed_row, random_row = row_readers(rows_ref, blocks)
    keys = gathered(k_ref, fixed_row, random_row)
    values = gathered(v_ref, fixed_row, random_row)
    queries = stacked_by_head(q_ref[...])
    grads = stacked_by_head(g_ref[...])
    probs = p_ref[0, 0]
    grad_probs = mm_nt(values, grads)
    wide = probs.astype(f32)
    balance = jnp.sum(wide * grad_probs, axis=0, keepdims=True)
    grad_scores = (wide * (grad_probs - balance)).astype(bf16)
    dq_ref[...] = (query_scale * own_head_columns(mm_tn(grad_scores, keys))).astype(bf16)
    grad_keys = mm(grad_scores, queries)
    grad_values = mm(probs, grads)
    for total, part in ((dk_sum, grad_keys), (dv_sum, grad_values)):
        for t in range(5):
            total[block_rows(fixed_row(t)), :] += part[t * BLOCK : (t + 1) * BLOCK]
        for t in range(RANDOM):
            rows = part[(5 + t) * BLOCK : (6 + t) * BLOCK]
            for h in range(GROUP):
                first = (h // 2) * 2 * HEAD_DIM
                mine = head_mask(BLOCK, 2 * HEAD_DIM, (h % 2) * HEAD_DIM)
                total[block_rows(random_row(h, t)), pl.ds(first, 2 * HEAD_DIM)] += jnp.where(
                    mine, rows[:, first : first + 2 * HEAD_DIM], 0.0
                )

    @pl.when(i == blocks - 1)
    def _():
        dk_ref[...] = dk_sum[...].astype(bf16)
        dv_ref[...] = dv_sum[...].astype(bf16)


def attend(rows, queries, keys, values, bases, docs):
    tokens, width = queries.shape
    ext = keys.shape[0]
    blocks, cols = tokens // BLOCK, GROUP * HEAD_DIM
    groups = width // cols
    tile = pl.BlockSpec((BLOCK, cols), lambda g, i, r: (i, g))
    table = pl.BlockSpec((ext, cols), lambda g, i, r: (0, g))
    return pl.pallas_call(
        partial(attend_kernel, blocks),
        grid_spec=pltpu.PrefetchScalarGridSpec(
            num_scalar_prefetch=1,
            grid=(groups, blocks),
            in_specs=[
                tile,
                table,
                table,
                pl.BlockSpec((1, 1, TILES, cols), lambda g, i, r: (g, i, 0, 0)),
                pl.BlockSpec((1, 8, cols), lambda g, i, r: (i, 0, 0)),
            ],
            out_specs=[
                tile,
                pl.BlockSpec((1, 1, TILES * BLOCK, cols), lambda g, i, r: (g, i, 0, 0)),
            ],
        ),
        out_shape=[
            jax.ShapeDtypeStruct((tokens, width), bf16),
            jax.ShapeDtypeStruct((groups, blocks, TILES * BLOCK, cols), bf16),
        ],
        compiler_params=pltpu.CompilerParams(vmem_limit_bytes=40 << 20),
        cost_estimate=pl.CostEstimate(
            flops=4 * groups * blocks * TILES * BLOCK * cols * cols,
            bytes_accessed=4 * ext * width + 2 * groups * blocks * TILES * BLOCK * cols,
            transcendentals=groups * blocks * TILES * BLOCK * cols,
        ),
    )(rows, queries, keys, values, bases, docs)


def attend_back(rows, queries, grads, keys, values, probs):
    tokens, width = queries.shape
    ext = keys.shape[0]
    blocks, cols = tokens // BLOCK, GROUP * HEAD_DIM
    groups = width // cols
    tile = pl.BlockSpec((BLOCK, cols), lambda g, i, r: (i, g))
    table = pl.BlockSpec((ext, cols), lambda g, i, r: (0, g))
    return pl.pallas_call(
        partial(attend_back_kernel, blocks),
        grid_spec=pltpu.PrefetchScalarGridSpec(
            num_scalar_prefetch=1,
            grid=(groups, blocks),
            in_specs=[
                tile,
                tile,
                table,
                table,
                pl.BlockSpec((1, 1, TILES * BLOCK, cols), lambda g, i, r: (g, i, 0, 0)),
            ],
            out_specs=[tile, table, table],
            scratch_shapes=[pltpu.VMEM((ext, cols), f32), pltpu.VMEM((ext, cols), f32)],
        ),
        out_shape=[
            jax.ShapeDtypeStruct((tokens, width), bf16),
            jax.ShapeDtypeStruct((ext, width), bf16),
            jax.ShapeDtypeStruct((ext, width), bf16),
        ],
        compiler_params=pltpu.CompilerParams(vmem_limit_bytes=56 << 20),
        cost_estimate=pl.CostEstimate(
            flops=10 * groups * blocks * TILES * BLOCK * cols * cols,
            bytes_accessed=8 * ext * width + 2 * groups * blocks * TILES * BLOCK * cols,
            transcendentals=0,
        ),
    )(rows, queries, grads, keys, values, probs)


def tile_plan(segment_ids, random_blocks, tokens):
    heads, total_blocks, _ = random_blocks.shape
    blocks = tokens // BLOCK
    chunk = lax.axis_index("blk") * lax.axis_size("head") + lax.axis_index("head")
    margin = REACH * tokens
    padded = jnp.concatenate(
        [
            jnp.full((margin,), -1, jnp.int32),
            segment_ids,
            jnp.full((margin,), jnp.iinfo(jnp.int32).max, jnp.int32),
        ]
    )
    near = lax.dynamic_slice_in_dim(padded, chunk * tokens, tokens + 2 * margin)
    own = near[margin : margin + tokens]
    begins = jnp.sum((near[None, :] < own[:, None]).astype(jnp.int32), axis=1)
    ends = jnp.sum((near[None, :] <= own[:, None]).astype(jnp.int32), axis=1)
    docs = jnp.stack([begins, ends]).reshape(2, blocks, BLOCK)
    docs = jnp.tile(jnp.transpose(docs, (1, 0, 2)), (1, 4, GROUP))
    first = begins[::BLOCK] // BLOCK
    here = REACH * blocks + jnp.arange(blocks, dtype=jnp.int32)
    fixed = jnp.stack([here - 1, here, here + 1, first, first + 1], axis=-1)
    picked = lax.dynamic_slice_in_dim(random_blocks, chunk * blocks, blocks, axis=1)
    picked = picked - (chunk - REACH) * blocks
    rows = jnp.concatenate(
        [jnp.broadcast_to(fixed[None], (heads, blocks, 5)), picked], axis=-1
    )
    earlier = jnp.arange(TILES)[None, :] < jnp.arange(TILES)[:, None]
    repeat = jnp.any((rows[..., :, None] == rows[..., None, :]) & earlier, axis=-1)
    bases = jnp.where(repeat, far_away, rows * BLOCK)
    rows = jnp.clip(rows, 0, (1 + 2 * REACH) * blocks - 1)
    bases = bases.reshape(heads // GROUP, GROUP, blocks, TILES)
    bases = jnp.repeat(jnp.transpose(bases, (0, 2, 3, 1)), BLOCK, axis=-1)
    return rows.reshape(-1), bases, docs


def side_pairs(blk, head, far):
    pairs = []
    for b in range(blk):
        for h in range(head):
            down = h < head // 2
            if far and h not in (0, head - 1):
                continue
            source = b - 1 if down else b + 1
            if 0 <= source < blk:
                pairs.append((h * blk + source, h * blk + b))
    return pairs


def widen(tokens_rows, blk, head):
    rows = tokens_rows.shape[0]
    h = lax.axis_index("head")
    line = lax.all_gather(tokens_rows, "head", axis=0, tiled=True)
    low = h < head // 2
    near = lax.dynamic_slice_in_dim(line, jnp.where(low, head - 1, 0) * rows, rows)
    far = lax.dynamic_slice_in_dim(line, jnp.where(low, head - 2, 1) * rows, rows)
    near = lax.ppermute(near, ("head", "blk"), side_pairs(blk, head, False))
    far = lax.ppermute(far, ("head", "blk"), side_pairs(blk, head, True))
    whole = jnp.concatenate([far, near, line, near, far], axis=0)
    return lax.dynamic_slice_in_dim(whole, h * rows, (1 + 2 * REACH) * rows)


def narrow(wide_rows, rows, blk, head):
    h = lax.axis_index("head")
    low = h < head // 2
    frame = jnp.zeros(((head + 2 * REACH) * rows, wide_rows.shape[1]), wide_rows.dtype)
    frame = lax.dynamic_update_slice_in_dim(frame, wide_rows, h * rows, 0)
    near = lax.dynamic_slice_in_dim(frame, jnp.where(low, 1, head + REACH) * rows, rows)
    far = lax.dynamic_slice_in_dim(frame, jnp.where(low, 0, head + REACH + 1) * rows, rows)
    back = [(t, s) for s, t in side_pairs(blk, head, False)]
    near = lax.ppermute(near, ("head", "blk"), back)
    back = [(t, s) for s, t in side_pairs(blk, head, True)]
    far = lax.ppermute(far, ("head", "blk"), back)
    line = frame[REACH * rows : (REACH + head) * rows].reshape(head, rows, -1)
    place = jnp.arange(head, dtype=jnp.int32)[:, None, None]
    line = line + jnp.where(place == jnp.where(low, head - 1, 0), near[None], 0)
    line = line + jnp.where(place == jnp.where(low, head - 2, 1), far[None], 0)
    return lax.psum_scatter(line.reshape(head * rows, -1), "head", scatter_dimension=0, tiled=True)


def layer_norm(values, gain_vec, offset):
    centred = values - jnp.mean(values, axis=-1, keepdims=True)
    spread = jnp.mean(centred * centred, axis=-1, keepdims=True)
    return centred * lax.rsqrt(spread + epsilon) * gain_vec + offset


def whole(shard):
    return lax.all_gather(shard, ("head", "blk"), axis=0, tiled=True)


def shared_out(grad):
    return lax.psum_scatter(grad.astype(bf16), ("head", "blk"), scatter_dimension=0, tiled=True).astype(f32)


def per_device(blk, head, tokens, *rest):
    weights, vectors, (out_grad, segment_ids, random_blocks) = rest[:6], rest[6:15], rest[15:]
    rows = tokens.shape[0]
    w_query, w_key, w_value, w_attn, w_inner, w_outer = [whole(w) for w in weights]
    sizes = [v.shape[0] for v in vectors]
    cuts = [sum(sizes[:n]) for n in range(len(sizes) + 1)]
    table = whole(jnp.concatenate(vectors)[None])
    (
        bias_query,
        bias_value,
        bias_attn,
        gain_one,
        offset_one,
        bias_inner,
        bias_outer,
        gain_two,
        offset_two,
    ) = [table[:, a:b].reshape(-1).astype(f32) for a, b in zip(cuts[:-1], cuts[1:])]

    rows_of, bases, docs = tile_plan(segment_ids, random_blocks, rows)
    wide = widen(tokens, blk, head)
    queries = (query_scale * (mm(tokens, w_query) + bias_query)).astype(bf16)
    keys = mm(wide, w_key).astype(bf16)
    values = (mm(wide, w_value) + bias_value).astype(bf16)
    attended, probs = attend(rows_of, queries, keys, values, bases, docs)

    first_norm, norm_one_back = jax.vjp(
        layer_norm, tokens.astype(f32) + mm(attended, w_attn) + bias_attn, gain_one, offset_one
    )
    first_low = first_norm.astype(bf16)
    inner = mm(first_low, w_inner) + bias_inner
    activated, gelu_back = jax.vjp(partial(jax.nn.gelu, approximate=True), inner)
    activ_low = activated.astype(bf16)
    outer = mm(activ_low, w_outer) + bias_outer
    result, norm_two_back = jax.vjp(layer_norm, first_norm + outer, gain_two, offset_two)

    grad_second, grad_gain_two, grad_offset_two = norm_two_back(out_grad.astype(f32))
    grad_outer = grad_second.astype(bf16)
    grad_inner = gelu_back(mm_nt(grad_outer, w_outer))[0].astype(bf16)
    grad_first = grad_second + mm_nt(grad_inner, w_inner)
    grad_first_sum, grad_gain_one, grad_offset_one = norm_one_back(grad_first)
    grad_attn = grad_first_sum.astype(bf16)
    grad_attended = mm_nt(grad_attn, w_attn).astype(bf16)
    grad_w_outer = shared_out(mm_tn(activ_low, grad_outer))
    grad_w_inner = shared_out(mm_tn(first_low, grad_inner))
    grad_w_attn = shared_out(mm_tn(attended, grad_attn))

    grad_scaled, grad_keyed, grad_valued = attend_back(
        rows_of, queries, grad_attended, keys, values, probs
    )
    grad_wide = mm_nt(grad_keyed, w_key) + mm_nt(grad_valued, w_value)
    grad_tokens = (
        grad_first_sum
        + mm_nt(grad_scaled, w_query)
        + narrow(grad_wide.astype(bf16), rows, blk, head).astype(f32)
    )
    grad_w_query = shared_out(mm_tn(tokens, grad_scaled))
    grad_w_key = shared_out(mm_tn(wide, grad_keyed))
    grad_w_value = shared_out(mm_tn(wide, grad_valued))

    def total(grads):
        return jnp.sum(grads.astype(f32), axis=0)

    sums = (
        total(grad_scaled),
        total(grad_valued),
        total(grad_attn),
        grad_gain_one,
        grad_offset_one,
        total(grad_inner),
        total(grad_outer),
        grad_gain_two,
        grad_offset_two,
    )
    packed = jnp.concatenate([s.reshape(blk * head, -1) for s in sums], axis=1)
    packed = lax.psum_scatter(packed, ("head", "blk"), scatter_dimension=0, tiled=True)
    vector_grads = tuple(packed[0, a:b] for a, b in zip(cuts[:-1], cuts[1:]))
    return (
        result.astype(bf16),
        grad_tokens,
        grad_w_query,
        grad_w_key,
        grad_w_value,
        grad_w_attn,
        grad_w_inner,
        grad_w_outer,
    ) + vector_grads


def solution(mesh):
    row = P(("blk", "head"), None)
    matrix = P(("head", "blk"), None)
    vector = P(("head", "blk"))
    return jax.shard_map(
        partial(per_device, mesh.shape["blk"], mesh.shape["head"]),
        mesh=mesh,
        in_specs=(row,) + (matrix,) * 6 + (vector,) * 9 + (row, P(), P()),
        out_specs=(row, row) + (matrix,) * 6 + (vector,) * 9,
        check_vma=False,
    )
```

```python
from functools import partial

import jax
import jax.numpy as jnp
from jax import lax
from jax.experimental import pallas as pl
from jax.experimental.pallas import tpu as pltpu
from jax.sharding import PartitionSpec as P

HEAD_DIM = 64
BLOCK = 64
RANDOM = 3
TILES = 5 + RANDOM
REACH = 2
GROUP = 4

epsilon = 1e-06
masked_value = -1e30
query_scale = 0.125
far_away = -(1 << 24)
f32, bf16 = jnp.float32, jnp.bfloat16


def mm(a, b):
    return jnp.dot(a, b, preferred_element_type=f32)


def mm_nt(a, b):
    return lax.dot_general(a, b, (((1,), (1,)), ((), ())), preferred_element_type=f32)


def mm_tn(a, b):
    return lax.dot_general(a, b, (((0,), (0,)), ((), ())), preferred_element_type=f32)


def head_mask(rows, cols, first):
    lanes = lax.broadcasted_iota(jnp.int32, (rows, cols), 1)
    return (lanes >= first) & (lanes < first + HEAD_DIM)


def stacked_by_head(tile):
    rows, cols = tile.shape
    return jnp.concatenate(
        [
            jnp.where(head_mask(rows, cols, h * HEAD_DIM), tile, jnp.zeros_like(tile))
            for h in range(cols // HEAD_DIM)
        ],
        axis=0,
    )


def own_head_columns(stacked):
    cols = stacked.shape[1]
    total = None
    for h in range(cols // HEAD_DIM):
        part = stacked[h * BLOCK : (h + 1) * BLOCK]
        part = jnp.where(head_mask(BLOCK, cols, h * HEAD_DIM), part, 0.0)
        total = part if total is None else total + part
    return total


def block_rows(row):
    return pl.ds(pl.multiple_of(row * BLOCK, BLOCK), BLOCK)


def gathered(table_ref, fixed_row, random_row):
    tiles = [table_ref[block_rows(fixed_row(t)), :] for t in range(5)]
    low = head_mask(BLOCK, 2 * HEAD_DIM, 0)
    for t in range(RANDOM):
        halves = []
        for pair in range(GROUP // 2):
            cols = pl.ds(pair * 2 * HEAD_DIM, 2 * HEAD_DIM)
            a = table_ref[block_rows(random_row(2 * pair, t)), cols]
            b = table_ref[block_rows(random_row(2 * pair + 1, t)), cols]
            halves.append(jnp.where(low, a, b))
        tiles.append(jnp.concatenate(halves, axis=1))
    return jnp.concatenate(tiles, axis=0)


def row_readers(rows_ref, blocks):
    group, i = pl.program_id(0), pl.program_id(1)

    def fixed_row(t):
        return rows_ref[(group * GROUP * blocks + i) * TILES + t]

    def random_row(h, t):
        return rows_ref[((group * GROUP + h) * blocks + i) * TILES + 5 + t]

    return fixed_row, random_row


def attend_kernel(blocks, rows_ref, q_ref, k_ref, v_ref, base_ref, doc_ref, out_ref, p_ref):
    fixed_row, random_row = row_readers(rows_ref, blocks)
    keys = gathered(k_ref, fixed_row, random_row)
    values = gathered(v_ref, fixed_row, random_row)
    scores = mm_nt(keys, stacked_by_head(q_ref[...]))
    lo = doc_ref[0, 0:1, :]
    hi = doc_ref[0, 1:2, :]
    within = lax.broadcasted_iota(jnp.int32, (BLOCK, GROUP * BLOCK), 0)
    masked = []
    for t in range(TILES):
        place = within + base_ref[0, 0, t : t + 1, :]
        allowed = (place >= lo) & (place < hi)
        masked.append(jnp.where(allowed, scores[t * BLOCK : (t + 1) * BLOCK], masked_value))
    scores = jnp.concatenate(masked, axis=0)
    raised = jnp.exp(scores - jnp.max(scores, axis=0, keepdims=True))
    probs = (raised * (1.0 / jnp.sum(raised, axis=0, keepdims=True))).astype(bf16)
    p_ref[0, 0] = probs
    out_ref[...] = own_head_columns(mm_tn(probs, values)).astype(bf16)


def attend_back_kernel(
    blocks,
    rows_ref,
    q_ref,
    g_ref,
    k_ref,
    v_ref,
    p_ref,
    dq_ref,
    dk_ref,
    dv_ref,
    dk_sum,
    dv_sum,
):
    i = pl.program_id(1)

    @pl.when(i == 0)
    def _():
        dk_sum[...] = jnp.zeros_like(dk_sum)
        dv_sum[...] = jnp.zeros_like(dv_sum)

    fixed_row, random_row = row_readers(rows_ref, blocks)
    keys = gathered(k_ref, fixed_row, random_row)
    values = gathered(v_ref, fixed_row, random_row)
    queries = stacked_by_head(q_ref[...])
    grads = stacked_by_head(g_ref[...])
    probs = p_ref[0, 0]
    grad_probs = mm_nt(values, grads)
    wide = probs.astype(f32)
    balance = jnp.sum(wide * grad_probs, axis=0, keepdims=True)
    grad_scores = (wide * (grad_probs - balance)).astype(bf16)
    dq_ref[...] = (query_scale * own_head_columns(mm_tn(grad_scores, keys))).astype(bf16)
    grad_keys = mm(grad_scores, queries)
    grad_values = mm(probs, grads)
    for total, part in ((dk_sum, grad_keys), (dv_sum, grad_values)):
        for t in range(5):
            total[block_rows(fixed_row(t)), :] += part[t * BLOCK : (t + 1) * BLOCK]
        for t in range(RANDOM):
            rows = part[(5 + t) * BLOCK : (6 + t) * BLOCK]
            for h in range(GROUP):
                first = (h // 2) * 2 * HEAD_DIM
                mine = head_mask(BLOCK, 2 * HEAD_DIM, (h % 2) * HEAD_DIM)
                total[block_rows(random_row(h, t)), pl.ds(first, 2 * HEAD_DIM)] += jnp.where(
                    mine, rows[:, first : first + 2 * HEAD_DIM], 0.0
                )

    @pl.when(i == blocks - 1)
    def _():
        dk_ref[...] = dk_sum[...].astype(bf16)
        dv_ref[...] = dv_sum[...].astype(bf16)


def attend(rows, queries, keys, values, bases, docs):
    tokens, width = queries.shape
    ext = keys.shape[0]
    blocks, cols = tokens // BLOCK, GROUP * HEAD_DIM
    groups = width // cols
    tile = pl.BlockSpec((BLOCK, cols), lambda g, i, r: (i, g))
    table = pl.BlockSpec((ext, cols), lambda g, i, r: (0, g))
    return pl.pallas_call(
        partial(attend_kernel, blocks),
        grid_spec=pltpu.PrefetchScalarGridSpec(
            num_scalar_prefetch=1,
            grid=(groups, blocks),
            in_specs=[
                tile,
                table,
                table,
                pl.BlockSpec((1, 1, TILES, cols), lambda g, i, r: (g, i, 0, 0)),
                pl.BlockSpec((1, 8, cols), lambda g, i, r: (i, 0, 0)),
            ],
            out_specs=[
                tile,
                pl.BlockSpec((1, 1, TILES * BLOCK, cols), lambda g, i, r: (g, i, 0, 0)),
            ],
        ),
        out_shape=[
            jax.ShapeDtypeStruct((tokens, width), bf16),
            jax.ShapeDtypeStruct((groups, blocks, TILES * BLOCK, cols), bf16),
        ],
        compiler_params=pltpu.CompilerParams(vmem_limit_bytes=40 << 20),
        cost_estimate=pl.CostEstimate(
            flops=4 * groups * blocks * TILES * BLOCK * cols * cols,
            bytes_accessed=4 * ext * width + 2 * groups * blocks * TILES * BLOCK * cols,
            transcendentals=groups * blocks * TILES * BLOCK * cols,
        ),
    )(rows, queries, keys, values, bases, docs)


def attend_back(rows, queries, grads, keys, values, probs):
    tokens, width = queries.shape
    ext = keys.shape[0]
    blocks, cols = tokens // BLOCK, GROUP * HEAD_DIM
    groups = width // cols
    tile = pl.BlockSpec((BLOCK, cols), lambda g, i, r: (i, g))
    table = pl.BlockSpec((ext, cols), lambda g, i, r: (0, g))
    return pl.pallas_call(
        partial(attend_back_kernel, blocks),
        grid_spec=pltpu.PrefetchScalarGridSpec(
            num_scalar_prefetch=1,
            grid=(groups, blocks),
            in_specs=[
                tile,
                tile,
                table,
                table,
                pl.BlockSpec((1, 1, TILES * BLOCK, cols), lambda g, i, r: (g, i, 0, 0)),
            ],
            out_specs=[tile, table, table],
            scratch_shapes=[pltpu.VMEM((ext, cols), f32), pltpu.VMEM((ext, cols), f32)],
        ),
        out_shape=[
            jax.ShapeDtypeStruct((tokens, width), bf16),
            jax.ShapeDtypeStruct((ext, width), bf16),
            jax.ShapeDtypeStruct((ext, width), bf16),
        ],
        compiler_params=pltpu.CompilerParams(vmem_limit_bytes=56 << 20),
        cost_estimate=pl.CostEstimate(
            flops=10 * groups * blocks * TILES * BLOCK * cols * cols,
            bytes_accessed=8 * ext * width + 2 * groups * blocks * TILES * BLOCK * cols,
            transcendentals=0,
        ),
    )(rows, queries, grads, keys, values, probs)


def tile_plan(segment_ids, random_blocks, tokens):
    heads, total_blocks, _ = random_blocks.shape
    blocks = tokens // BLOCK
    chunk = lax.axis_index("blk") * lax.axis_size("head") + lax.axis_index("head")
    margin = REACH * tokens
    padded = jnp.concatenate(
        [
            jnp.full((margin,), -1, jnp.int32),
            segment_ids,
            jnp.full((margin,), jnp.iinfo(jnp.int32).max, jnp.int32),
        ]
    )
    near = lax.dynamic_slice_in_dim(padded, chunk * tokens, tokens + 2 * margin)
    own = near[margin : margin + tokens]
    begins = jnp.sum((near[None, :] < own[:, None]).astype(jnp.int32), axis=1)
    ends = jnp.sum((near[None, :] <= own[:, None]).astype(jnp.int32), axis=1)
    docs = jnp.stack([begins, ends]).reshape(2, blocks, BLOCK)
    docs = jnp.tile(jnp.transpose(docs, (1, 0, 2)), (1, 4, GROUP))
    first = begins[::BLOCK] // BLOCK
    here = REACH * blocks + jnp.arange(blocks, dtype=jnp.int32)
    fixed = jnp.stack([here - 1, here, here + 1, first, first + 1], axis=-1)
    picked = lax.dynamic_slice_in_dim(random_blocks, chunk * blocks, blocks, axis=1)
    picked = picked - (chunk - REACH) * blocks
    rows = jnp.concatenate(
        [jnp.broadcast_to(fixed[None], (heads, blocks, 5)), picked], axis=-1
    )
    earlier = jnp.arange(TILES)[None, :] < jnp.arange(TILES)[:, None]
    repeat = jnp.any((rows[..., :, None] == rows[..., None, :]) & earlier, axis=-1)
    bases = jnp.where(repeat, far_away, rows * BLOCK)
    rows = jnp.clip(rows, 0, (1 + 2 * REACH) * blocks - 1)
    bases = bases.reshape(heads // GROUP, GROUP, blocks, TILES)
    bases = jnp.repeat(jnp.transpose(bases, (0, 2, 3, 1)), BLOCK, axis=-1)
    return rows.reshape(-1), bases, docs


def side_pairs(blk, head, far):
    pairs = []
    for b in range(blk):
        for h in range(head):
            down = h < head // 2
            if far and h not in (0, head - 1):
                continue
            source = b - 1 if down else b + 1
            if 0 <= source < blk:
                pairs.append((h * blk + source, h * blk + b))
    return pairs


def widen(tokens_rows, blk, head):
    rows = tokens_rows.shape[0]
    h = lax.axis_index("head")
    line = lax.all_gather(tokens_rows, "head", axis=0, tiled=True)
    low = h < head // 2
    near = lax.dynamic_slice_in_dim(line, jnp.where(low, head - 1, 0) * rows, rows)
    far = lax.dynamic_slice_in_dim(line, jnp.where(low, head - 2, 1) * rows, rows)
    near = lax.ppermute(near, ("head", "blk"), side_pairs(blk, head, False))
    far = lax.ppermute(far, ("head", "blk"), side_pairs(blk, head, True))
    whole = jnp.concatenate([far, near, line, near, far], axis=0)
    return lax.dynamic_slice_in_dim(whole, h * rows, (1 + 2 * REACH) * rows)


def narrow(wide_rows, rows, blk, head):
    h = lax.axis_index("head")
    low = h < head // 2
    frame = jnp.zeros(((head + 2 * REACH) * rows, wide_rows.shape[1]), wide_rows.dtype)
    frame = lax.dynamic_update_slice_in_dim(frame, wide_rows, h * rows, 0)
    near = lax.dynamic_slice_in_dim(frame, jnp.where(low, 1, head + REACH) * rows, rows)
    far = lax.dynamic_slice_in_dim(frame, jnp.where(low, 0, head + REACH + 1) * rows, rows)
    back = [(t, s) for s, t in side_pairs(blk, head, False)]
    near = lax.ppermute(near, ("head", "blk"), back)
    back = [(t, s) for s, t in side_pairs(blk, head, True)]
    far = lax.ppermute(far, ("head", "blk"), back)
    line = frame[REACH * rows : (REACH + head) * rows].reshape(head, rows, -1)
    place = jnp.arange(head, dtype=jnp.int32)[:, None, None]
    line = line + jnp.where(place == jnp.where(low, head - 1, 0), near[None], 0)
    line = line + jnp.where(place == jnp.where(low, head - 2, 1), far[None], 0)
    return lax.psum_scatter(line.reshape(head * rows, -1), "head", scatter_dimension=0, tiled=True)


LINE = 4
CORES = 2
PIECES = 4
MESH = pl.DeviceIdType.MESH
NEAR_SLOT = (1, 0, 4, 3)
FAR_SLOT = (0, None, None, 4)


def remote(source, target, send, recv, head, blk):
    return pltpu.make_async_remote_copy(
        src_ref=source,
        dst_ref=target,
        send_sem=send,
        recv_sem=recv,
        device_id=(head, blk),
        device_id_type=MESH,
    )


def at_each_head(h, body):
    for hh in range(LINE):
        pl.when(h == hh)(partial(body, hh))


def greet_plane_and_line(h, b, blk):
    barrier = pltpu.get_barrier_semaphore()
    for d in range(1, LINE):
        pl.semaphore_signal(
            barrier, inc=1, device_id=((h + d) % LINE, b), device_id_type=MESH
        )
    for d in range(1, blk):
        pl.semaphore_signal(barrier, inc=1, device_id=(h, (b + d) % blk), device_id_type=MESH)
    pl.semaphore_wait(barrier, LINE - 1 + blk - 1)


def gather_kernel(blk, count, *refs):
    x_ref, shards = refs[0], refs[1 : 1 + count]
    wide, spill, fulls = refs[1 + count], refs[2 + count], refs[3 + count : 3 + 2 * count]
    local, zs, zr, cs, cr, ss, sr, us, ur, ds, dr, ns, nr, fs, fr = refs[3 + 2 * count :]
    h, b = lax.axis_index("head"), lax.axis_index("blk")
    chips = blk // CORES
    chip, core = b // CORES, b % CORES
    sibling = chip * CORES + 1 - core
    rows = x_ref.shape[0] // PIECES

    def piece(ref, p):
        return ref.at[pl.ds(p * rows, rows)]

    def place(hh, j):
        slot = 2 + j - hh
        return wide.at[slot] if 0 <= slot < 5 else spill

    def own(a):
        return pltpu.make_async_copy(shards[a], fulls[a].at[h, b], local.at[a])

    def along(a, d):
        return remote(
            shards[a], fulls[a].at[h, b], zs.at[a, d - 1], zr.at[a, d - 1], (h + d) % LINE, b
        )

    def along_arrives(a, d):
        src = (h - d + LINE) % LINE
        return remote(
            shards[a], fulls[a].at[src, b], zs.at[a, d - 1], zr.at[a, d - 1], (h + d) % LINE, b
        )

    def over(a, e):
        part = fulls[a].at[:, b]
        there = ((chip + e) % chips) * CORES + core
        return remote(part, part, cs.at[a, e - 1], cr.at[a, e - 1], h, there)

    def over_arrives(a, e):
        there = ((chip - e + chips) % chips) * CORES + core
        part = fulls[a].at[:, there]
        return remote(part, part, cs.at[a, e - 1], cr.at[a, e - 1], h, there)

    def across(a, e):
        part = fulls[a].at[:, ((chip - e + chips) % chips) * CORES + core]
        return remote(part, part, ss.at[a, e], sr.at[a, e], h, sibling)

    def across_arrives(a, e):
        part = fulls[a].at[:, ((chip - e + chips) % chips) * CORES + 1 - core]
        return remote(part, part, ss.at[a, e], sr.at[a, e], h, sibling)

    def spread(a):
        for d in range(1, LINE):
            along_arrives(a, d).wait_recv()
        own(a).wait()
        for e in range(1, chips):
            over(a, e).start()
        across(a, 0).start()

    def hand_over(a):
        for e in range(1, chips):
            over_arrives(a, e).wait_recv()
            across(a, e).start()

    def up(hh, j, p):
        source = x_ref if j == hh else place(hh, j)
        return remote(
            piece(source, p), piece(place(hh + 1, j), p), us.at[j, p], ur.at[j, p], (h + 1) % LINE, b
        )

    def up_arrives(hh, j, p):
        target = piece(place(hh, j), p)
        return remote(target, target, us.at[j, p], ur.at[j, p], (h + 1) % LINE, b)

    def down(hh, j, p):
        source = x_ref if j == hh else place(hh, j)
        return remote(
            piece(source, p), piece(place(hh - 1, j), p), ds.at[j, p], dr.at[j, p], (h + 3) % LINE, b
        )

    def down_arrives(hh, j, p):
        target = piece(place(hh, j), p)
        return remote(target, target, ds.at[j, p], dr.at[j, p], (h + 3) % LINE, b)

    def sides(hh, j):
        near, far = (3, 2) if hh < 2 else (0, 1)
        if j == near:
            return [(NEAR_SLOT[hh], ns, nr)]
        if j == far and FAR_SLOT[hh] is not None:
            return [(FAR_SLOT[hh], fs, fr)]
        return []

    def side(hh, j, p, slot, send, recv):
        target = (b + 1) % blk if hh < 2 else (b + blk - 1) % blk
        return remote(
            piece(place(hh, j), p), piece(wide.at[slot], p), send.at[p], recv.at[p], h, target
        )

    def sends_side(hh):
        return b < blk - 1 if hh < 2 else b > 0

    def gets_side(hh):
        return b > 0 if hh < 2 else b < blk - 1

    def side_slots(hh):
        found = [(NEAR_SLOT[hh], ns, nr)]
        if FAR_SLOT[hh] is not None:
            found.append((FAR_SLOT[hh], fs, fr))
        return found

    def fill(n, slot):
        return pltpu.make_async_copy(x_ref, wide.at[slot], local.at[count + 1 + n])

    def own_rows():
        return pltpu.make_async_copy(x_ref, wide.at[2], local.at[count])

    def begin(hh):
        for p in range(PIECES):
            if hh < LINE - 1:
                up(hh, hh, p).start()
            if hh > 0:
                down(hh, hh, p).start()

        @pl.when(jnp.logical_not(gets_side(hh)))
        def _():
            for n, (slot, _, _) in enumerate(side_slots(hh)):
                fill(n, slot).start()

    def pass_on(distance, hh):
        for p in range(PIECES):
            for j, arrives, onward, ends in (
                (hh - distance, up_arrives, up, hh == LINE - 1),
                (hh + distance, down_arrives, down, hh == 0),
            ):
                if not 0 <= j < LINE:
                    continue
                arrives(hh, j, p).wait_recv()
                if not ends:
                    onward(hh, j, p).start()
                for slot, send, recv in sides(hh, j):

                    @pl.when(sends_side(hh))
                    def _(slot=slot, send=send, recv=recv):
                        side(hh, j, p, slot, send, recv).start()

    def finish(hh):
        for p in range(PIECES):
            for j in range(LINE):
                if j <= hh < LINE - 1:
                    up(hh, j, p).wait_send()
                if j >= hh > 0:
                    down(hh, j, p).wait_send()

        @pl.when(sends_side(hh))
        def _():
            for j in range(LINE):
                for slot, send, recv in sides(hh, j):
                    for p in range(PIECES):
                        side(hh, j, p, slot, send, recv).wait_send()

        @pl.when(gets_side(hh))
        def _():
            for slot, send, recv in side_slots(hh):
                for p in range(PIECES):
                    target = piece(wide.at[slot], p)
                    remote(target, target, send.at[p], recv.at[p], h, (b + 1) % blk).wait_recv()

        @pl.when(jnp.logical_not(gets_side(hh)))
        def _():
            for n, (slot, _, _) in enumerate(side_slots(hh)):
                fill(n, slot).wait()

    own_rows().start()
    for a in range(count):
        own(a).start()
    greet_plane_and_line(h, b, blk)
    for a in range(count):
        for d in range(1, LINE):
            along(a, d).start()
    at_each_head(h, begin)
    for a in range(count):
        spread(a)
    at_each_head(h, partial(pass_on, 1))
    for a in range(count - 2):
        hand_over(a)
    at_each_head(h, partial(pass_on, 2))
    hand_over(count - 2)
    at_each_head(h, partial(pass_on, 3))
    hand_over(count - 1)
    for a in range(count):
        for d in range(1, LINE):
            along(a, d).wait_send()
        for e in range(1, chips):
            over(a, e).wait_send()
        for e in range(chips):
            across(a, e).wait_send()
            across_arrives(a, e).wait_recv()
    own_rows().wait()
    at_each_head(h, finish)


def gather(tokens, shards, blk):
    rows, width = tokens.shape
    count, chips = len(shards), blk // CORES
    anywhere = pl.BlockSpec(memory_space=pl.ANY)
    dma = pltpu.SemaphoreType.DMA
    outs = pl.pallas_call(
        partial(gather_kernel, blk, count),
        out_shape=[
            jax.ShapeDtypeStruct((5, rows, width), tokens.dtype),
            jax.ShapeDtypeStruct((rows, width), tokens.dtype),
        ]
        + [jax.ShapeDtypeStruct((LINE, blk) + s.shape, s.dtype) for s in shards],
        in_specs=[anywhere] * (1 + count),
        out_specs=[anywhere] * (2 + count),
        scratch_shapes=[dma((count + 3,))]
        + [dma((count, LINE - 1))] * 2
        + [dma((count, chips - 1))] * 2
        + [dma((count, chips))] * 2
        + [dma((LINE, PIECES))] * 4
        + [dma((PIECES,))] * 4,
        compiler_params=pltpu.CompilerParams(collective_id=0, has_side_effects=True),
    )(tokens, *shards)
    return outs[0], outs[2:]


def reduce_kernel(blk, count, *refs):
    dx_ref, grads = refs[0], refs[1 : 1 + count]
    sum_ref, outs = refs[1 + count], refs[2 + count : 2 + 2 * count]
    rest = refs[2 + 2 * count :]
    held, from_core, from_chip, from_line = (rest[n * count : (n + 1) * count] for n in range(4))
    line, arrived, aside = rest[4 * count : 4 * count + 3]
    load, ss, sr, cs, cr, zs, zr, xl, us, ur, ds, dr, ns, nr, fs, fr = rest[4 * count + 3 :]
    h, b = lax.axis_index("head"), lax.axis_index("blk")
    chips = blk // CORES
    chip, core = b // CORES, b % CORES
    sibling = chip * CORES + 1 - core
    rows = dx_ref.shape[1] // PIECES

    def mine(a, k):
        return pltpu.make_async_copy(grads[a].at[:, k * CORES + core], held[a].at[k], load.at[a, k])

    def across(a, k):
        return remote(
            grads[a].at[:, k * CORES + 1 - core],
            from_core[a].at[k],
            ss.at[a, k],
            sr.at[a, k],
            h,
            sibling,
        )

    def over(a, e):
        k = (chip + e) % chips
        return remote(
            held[a].at[k],
            from_chip[a].at[e - 1],
            cs.at[a, e - 1],
            cr.at[a, e - 1],
            h,
            k * CORES + core,
        )

    def along(a, d):
        there = (h + d) % LINE
        return remote(
            held[a].at[chip, there],
            from_line[a].at[d - 1],
            zs.at[a, d - 1],
            zr.at[a, d - 1],
            there,
            b,
        )

    def add_cores(a, k):
        def one(n, carry):
            held[a][k, n] = (held[a][k, n].astype(f32) + from_core[a][k, n].astype(f32)).astype(
                held[a].dtype
            )
            return carry

        lax.fori_loop(0, LINE, one, 0)

    def to_chips(a):
        for k in range(chips):
            mine(a, k).wait()
            across(a, k).wait_recv()
        for e in range(1, chips):
            add_cores(a, (chip + e) % chips)
            over(a, e).start()
        add_cores(a, chip)

    def to_line(a):
        for e in range(1, chips):
            over(a, e).wait_recv()

        def one(n, carry):
            total = held[a][chip, n].astype(f32)
            for e in range(1, chips):
                total = total + from_chip[a][e - 1, n].astype(f32)
            held[a][chip, n] = total.astype(held[a].dtype)
            return carry

        lax.fori_loop(0, LINE, one, 0)
        for d in range(1, LINE):
            along(a, d).start()

    def to_owner(a):
        for d in range(1, LINE):
            along(a, d).wait_recv()
        total = held[a][chip, h].astype(f32)
        for d in range(1, LINE):
            total = total + from_line[a][d - 1].astype(f32)
        outs[a][...] = total

    def part(p):
        return pl.ds(p * rows, rows)

    def piece(ref, p):
        return ref.at[part(p)]

    def add_rows(target, j, source, n, p):
        def one(step, carry):
            some = pl.ds(p * rows + step * 64, 64)
            target[j, some] = (
                target[j, some].astype(f32) + source[n, some].astype(f32)
            ).astype(target.dtype)
            return carry

        lax.fori_loop(0, rows // 64, one, 0)

    def slot_of(hh, j):
        slot = 2 + j - hh
        return slot if 0 <= slot < 5 else None

    def fetch(hh, j):
        return pltpu.make_async_copy(dx_ref.at[slot_of(hh, j)], line.at[j], xl.at[j])

    def arrival(hh, j, upward):
        return arrived.at[LINE if j == hh and not upward else j]

    def up(hh, j, p):
        return remote(
            piece(line.at[j], p),
            piece(arrival(hh + 1, j, True), p),
            us.at[j, p],
            ur.at[j, p],
            (h + 1) % LINE,
            b,
        )

    def up_arrives(hh, j, p):
        here = piece(arrival(hh, j, True), p)
        return remote(here, here, us.at[j, p], ur.at[j, p], (h + 1) % LINE, b)

    def down(hh, j, p):
        return remote(
            piece(line.at[j], p),
            piece(arrival(hh - 1, j, False), p),
            ds.at[j, p],
            dr.at[j, p],
            (h + 3) % LINE,
            b,
        )

    def down_arrives(hh, j, p):
        here = piece(arrival(hh, j, False), p)
        return remote(here, here, ds.at[j, p], dr.at[j, p], (h + 3) % LINE, b)

    def side_parts(hh):
        near, far = (3, 2) if hh < 2 else (0, 1)
        found = [(NEAR_SLOT[hh], near, 0, ns, nr)]
        if FAR_SLOT[hh] is not None:
            found.append((FAR_SLOT[hh], far, 1, fs, fr))
        return found

    def side(hh, slot, n, send, recv, p):
        target = (b + blk - 1) % blk if hh < 2 else (b + 1) % blk
        return remote(
            piece(dx_ref.at[slot], p), piece(aside.at[n], p), send.at[p], recv.at[p], h, target
        )

    def sends_side(hh):
        return b > 0 if hh < 2 else b < blk - 1

    def gets_side(hh):
        return b < blk - 1 if hh < 2 else b > 0

    def begin(hh):
        @pl.when(sends_side(hh))
        def _():
            for p in range(PIECES):
                for slot, _, n, send, recv in side_parts(hh):
                    side(hh, slot, n, send, recv, p).start()

        for j in range(LINE):
            if slot_of(hh, j) is not None:
                fetch(hh, j).start()
        for j in range(LINE):
            if slot_of(hh, j) is not None:
                fetch(hh, j).wait()
            else:
                line[j] = jnp.zeros(line.shape[1:], line.dtype)
        for p in range(PIECES):
            if hh == 0:
                up(hh, 1, p).start()
            if hh == LINE - 1:
                down(hh, 2, p).start()

    def take_sides(hh):
        for p in range(PIECES):
            for _, j, n, send, recv in side_parts(hh):

                @pl.when(gets_side(hh))
                def _(j=j, n=n, send=send, recv=recv):
                    here = piece(aside.at[n], p)
                    remote(here, here, send.at[p], recv.at[p], h, (b + 1) % blk).wait_recv()
                    add_rows(line, j, aside, n, p)

                if hh == 0:
                    up(hh, j, p).start()
                if hh == LINE - 1:
                    down(hh, j, p).start()

    def pass_on(first, hh):
        if hh == 1:
            moves = [(3, True), (0, False)] if first else [(2, True)]
        elif hh == 2:
            moves = [(0, False), (3, True)] if first else [(1, False)]
        else:
            moves = []
        for p in range(PIECES):
            for j, upward in moves:
                (up_arrives if upward else down_arrives)(hh, j, p).wait_recv()
                add_rows(line, j, arrived, j, p)
                (up if upward else down)(hh, j, p).start()

    def finish(hh):
        for p in range(PIECES):
            sources = []
            if hh > 0:
                up_arrives(hh, hh, p).wait_recv()
                sources.append(hh)
            if hh < LINE - 1:
                down_arrives(hh, hh, p).wait_recv()
                sources.append(LINE)

            def one(step, carry, p=p, sources=tuple(sources)):
                some = pl.ds(p * rows + step * 64, 64)
                total = line[hh, some].astype(f32)
                for n in sources:
                    total = total + arrived[n, some].astype(f32)
                sum_ref[some] = total
                return carry

            lax.fori_loop(0, rows // 64, one, 0)
        for p in range(PIECES):
            for j in range(LINE):
                if j > hh:
                    up(hh, j, p).wait_send()
                if j < hh:
                    down(hh, j, p).wait_send()

        @pl.when(sends_side(hh))
        def _():
            for p in range(PIECES):
                for slot, _, n, send, recv in side_parts(hh):
                    side(hh, slot, n, send, recv, p).wait_send()

    for a in range(count):
        for k in range(chips):
            mine(a, k).start()
    greet_plane_and_line(h, b, blk)
    for a in range(count):
        for k in range(chips):
            across(a, k).start()
    at_each_head(h, begin)
    for a in range(count):
        to_chips(a)
    at_each_head(h, take_sides)
    at_each_head(h, partial(pass_on, True))
    for a in range(count // 2):
        to_line(a)
    at_each_head(h, partial(pass_on, False))
    for a in range(count // 2, count):
        to_line(a)
    at_each_head(h, finish)
    for a in range(count):
        to_owner(a)
    for a in range(count):
        for k in range(chips):
            across(a, k).wait_send()
        for e in range(1, chips):
            over(a, e).wait_send()
        for d in range(1, LINE):
            along(a, d).wait_send()


def reduce_to_owners(wide_grad, grads, blk):
    _, rows, width = wide_grad.shape
    count, chips = len(grads), blk // CORES
    anywhere = pl.BlockSpec(memory_space=pl.ANY)
    inside = pl.BlockSpec(memory_space=pltpu.VMEM)
    dma = pltpu.SemaphoreType.DMA
    shard = [g.shape[2:] for g in grads]
    outs = pl.pallas_call(
        partial(reduce_kernel, blk, count),
        out_shape=[jax.ShapeDtypeStruct((rows, width), f32)]
        + [jax.ShapeDtypeStruct(s, f32) for s in shard],
        in_specs=[anywhere] * (1 + count),
        out_specs=[inside] * (1 + count),
        scratch_shapes=[pltpu.VMEM((chips, LINE) + s, g.dtype) for s, g in zip(shard, grads)]
        + [pltpu.VMEM((chips, LINE) + s, g.dtype) for s, g in zip(shard, grads)]
        + [pltpu.VMEM((chips - 1, LINE) + s, g.dtype) for s, g in zip(shard, grads)]
        + [pltpu.VMEM((LINE - 1,) + s, g.dtype) for s, g in zip(shard, grads)]
        + [
            pltpu.VMEM((LINE, rows, width), bf16),
            pltpu.VMEM((LINE + 1, rows, width), bf16),
            pltpu.VMEM((2, rows, width), bf16),
        ]
        + [dma((count, chips))] * 3
        + [dma((count, chips - 1))] * 2
        + [dma((count, LINE - 1))] * 2
        + [dma((LINE,))]
        + [dma((LINE, PIECES))] * 4
        + [dma((PIECES,))] * 4,
        compiler_params=pltpu.CompilerParams(
            collective_id=1, has_side_effects=True, vmem_limit_bytes=60 << 20
        ),
    )(wide_grad, *grads)
    return outs[0], outs[1:]


def layer_norm(values, gain_vec, offset):
    centred = values - jnp.mean(values, axis=-1, keepdims=True)
    spread = jnp.mean(centred * centred, axis=-1, keepdims=True)
    return centred * lax.rsqrt(spread + epsilon) * gain_vec + offset


def whole(shard):
    return lax.all_gather(shard, ("head", "blk"), axis=0, tiled=True)


def shared_out(grad):
    return lax.psum_scatter(grad.astype(bf16), ("head", "blk"), scatter_dimension=0, tiled=True).astype(f32)


def vectors_of(table, sizes):
    cuts = [sum(sizes[:n]) for n in range(len(sizes) + 1)]
    return [table[..., a:b] for a, b in zip(cuts[:-1], cuts[1:])]


def padded_to(flat, size):
    return jnp.pad(flat, [(0, 0)] * (flat.ndim - 1) + [(0, size - flat.shape[-1])])


def per_device(blk, head, tokens, *rest):
    weights, vectors, (out_grad, segment_ids, random_blocks) = rest[:6], rest[6:15], rest[15:]
    rows = tokens.shape[0]
    by_kernel = head == LINE and blk == LINE * CORES
    sizes = [v.shape[0] for v in vectors]
    if by_kernel:
        packed = padded_to(jnp.concatenate(vectors), 16 * 128).reshape(16, 128)
        order = (0, 1, 2, 3, 4, 5)
        wide, fulls = gather(tokens, [packed] + [weights[n] for n in order], blk)
        wide = wide.reshape(-1, tokens.shape[1])
        w_query, w_key, w_value, w_attn, w_inner, w_outer = [
            w.reshape(-1, w.shape[-1]) for w in fulls[1:]
        ]
        table = fulls[0].reshape(head * blk, -1)
    else:
        wide = widen(tokens, blk, head)
        w_query, w_key, w_value, w_attn, w_inner, w_outer = [whole(w) for w in weights]
        table = whole(jnp.concatenate(vectors)[None])
    (
        bias_query,
        bias_value,
        bias_attn,
        gain_one,
        offset_one,
        bias_inner,
        bias_outer,
        gain_two,
        offset_two,
    ) = [v.reshape(-1).astype(f32) for v in vectors_of(table, sizes)]

    rows_of, bases, docs = tile_plan(segment_ids, random_blocks, rows)
    queries = (query_scale * (mm(tokens, w_query) + bias_query)).astype(bf16)
    keys = mm(wide, w_key).astype(bf16)
    values = (mm(wide, w_value) + bias_value).astype(bf16)
    attended, probs = attend(rows_of, queries, keys, values, bases, docs)

    first_norm, norm_one_back = jax.vjp(
        layer_norm, tokens.astype(f32) + mm(attended, w_attn) + bias_attn, gain_one, offset_one
    )
    first_low = first_norm.astype(bf16)
    inner = mm(first_low, w_inner) + bias_inner
    activated, gelu_back = jax.vjp(partial(jax.nn.gelu, approximate=True), inner)
    activ_low = activated.astype(bf16)
    outer = mm(activ_low, w_outer) + bias_outer
    result, norm_two_back = jax.vjp(layer_norm, first_norm + outer, gain_two, offset_two)

    grad_second, grad_gain_two, grad_offset_two = norm_two_back(out_grad.astype(f32))
    grad_outer = grad_second.astype(bf16)
    grad_inner = gelu_back(mm_nt(grad_outer, w_outer))[0].astype(bf16)
    grad_first = grad_second + mm_nt(grad_inner, w_inner)
    grad_first_sum, grad_gain_one, grad_offset_one = norm_one_back(grad_first)
    grad_attn = grad_first_sum.astype(bf16)
    grad_attended = mm_nt(grad_attn, w_attn).astype(bf16)
    grad_scaled, grad_keyed, grad_valued = attend_back(
        rows_of, queries, grad_attended, keys, values, probs
    )
    def total(grads):
        return jnp.sum(grads.astype(f32), axis=0)

    sums = (
        total(grad_scaled),
        total(grad_valued),
        total(grad_attn),
        grad_gain_one,
        grad_offset_one,
        total(grad_inner),
        total(grad_outer),
        grad_gain_two,
        grad_offset_two,
    )
    packed = jnp.concatenate([s.reshape(blk * head, -1) for s in sums], axis=1)
    grad_wide = (mm_nt(grad_keyed, w_key) + mm_nt(grad_valued, w_value)).astype(bf16)
    grad_rows = grad_first_sum + mm_nt(grad_scaled, w_query)
    matrix_grads = [
        mm_tn(tokens, grad_scaled).astype(bf16),
        mm_tn(wide, grad_keyed).astype(bf16),
        mm_tn(wide, grad_valued).astype(bf16),
        mm_tn(attended, grad_attn).astype(bf16),
        mm_tn(first_low, grad_inner).astype(bf16),
        mm_tn(activ_low, grad_outer).astype(bf16),
    ]
    if by_kernel:
        shares = [g.reshape(head, blk, -1, g.shape[-1]) for g in matrix_grads]
        small = padded_to(packed, 8 * 128).reshape(head, blk, 8, 128)
        wide_sum, sums = reduce_to_owners(
            grad_wide.reshape(-1, rows, grad_wide.shape[-1]), [small] + shares, blk
        )
        matrix_grads = list(sums[1:])
        packed = sums[0].reshape(-1)
    else:
        wide_sum = narrow(grad_wide, rows, blk, head).astype(f32)
        matrix_grads = [shared_out(g) for g in matrix_grads]
        packed = lax.psum_scatter(packed, ("head", "blk"), scatter_dimension=0, tiled=True)[0]
    return (
        (result.astype(bf16), grad_rows + wide_sum)
        + tuple(matrix_grads)
        + tuple(vectors_of(packed, sizes))
    )


def solution(mesh):
    row = P(("blk", "head"), None)
    matrix = P(("head", "blk"), None)
    vector = P(("head", "blk"))
    return jax.shard_map(
        partial(per_device, mesh.shape["blk"], mesh.shape["head"]),
        mesh=mesh,
        in_specs=(row,) + (matrix,) * 6 + (vector,) * 9 + (row, P(), P()),
        out_specs=(row, row) + (matrix,) * 6 + (vector,) * 9,
        check_vma=False,
    )
```

```python
from functools import partial

import jax
import jax.numpy as jnp
from jax import lax
from jax.experimental import pallas as pl
from jax.experimental.pallas import tpu as pltpu
from jax.sharding import PartitionSpec as P

HEAD_DIM = 64
BLOCK = 64
RANDOM = 3
TILES = 5 + RANDOM
REACH = 2
GROUP = 4
FORWARD_BLOCKS = 4
BACKWARD_BLOCKS = 4
ROWS = 256
PIECE = 768

epsilon = 1e-06
masked_value = -1e30
query_scale = 0.125
gelu_scale = 0.7978845608028654
gelu_cubic = 0.044715
far_away = -(1 << 24)
f32, bf16 = jnp.float32, jnp.bfloat16


def mm(a, b):
    return jnp.dot(a, b, preferred_element_type=f32)


def mm_nt(a, b):
    return lax.dot_general(a, b, (((1,), (1,)), ((), ())), preferred_element_type=f32)


def mm_tn(a, b):
    return lax.dot_general(a, b, (((0,), (0,)), ((), ())), preferred_element_type=f32)


def head_mask(rows, cols, first):
    lanes = lax.broadcasted_iota(jnp.int32, (rows, cols), 1)
    return (lanes >= first) & (lanes < first + HEAD_DIM)


def stacked_by_head(tile):
    rows, cols = tile.shape
    return jnp.concatenate(
        [
            jnp.where(head_mask(rows, cols, h * HEAD_DIM), tile, jnp.zeros_like(tile))
            for h in range(cols // HEAD_DIM)
        ],
        axis=0,
    )


def own_head_columns(stacked):
    cols = stacked.shape[1]
    total = None
    for h in range(cols // HEAD_DIM):
        part = stacked[h * BLOCK : (h + 1) * BLOCK]
        part = jnp.where(head_mask(BLOCK, cols, h * HEAD_DIM), part, 0.0)
        total = part if total is None else total + part
    return total


def block_rows(row):
    return pl.ds(pl.multiple_of(row * BLOCK, BLOCK), BLOCK)


def gathered(table_ref, fixed_row, random_row):
    tiles = [table_ref[block_rows(fixed_row(t)), :] for t in range(5)]
    low = head_mask(BLOCK, 2 * HEAD_DIM, 0)
    for t in range(RANDOM):
        halves = []
        for pair in range(GROUP // 2):
            cols = pl.ds(pair * 2 * HEAD_DIM, 2 * HEAD_DIM)
            a = table_ref[block_rows(random_row(2 * pair, t)), cols]
            b = table_ref[block_rows(random_row(2 * pair + 1, t)), cols]
            halves.append(jnp.where(low, a, b))
        tiles.append(jnp.concatenate(halves, axis=1))
    return jnp.concatenate(tiles, axis=0)


def row_readers(rows_ref, blocks, i):
    group = pl.program_id(0)

    def fixed_row(t):
        return rows_ref[(group * GROUP * blocks + i) * TILES + t]

    def random_row(h, t):
        return rows_ref[((group * GROUP + h) * blocks + i) * TILES + 5 + t]

    return fixed_row, random_row


def attend_kernel(blocks, rows_ref, q_ref, k_ref, v_ref, base_ref, doc_ref, out_ref, p_ref):
    within = lax.broadcasted_iota(jnp.int32, (BLOCK, GROUP * BLOCK), 0)
    for u in range(FORWARD_BLOCKS):
        here = pl.ds(u * BLOCK, BLOCK)
        readers = row_readers(rows_ref, blocks, pl.program_id(1) * FORWARD_BLOCKS + u)
        keys = gathered(k_ref, *readers)
        values = gathered(v_ref, *readers)
        scores = mm_nt(keys, stacked_by_head(q_ref[here, :]))
        lo = doc_ref[u, 0:1, :]
        hi = doc_ref[u, 1:2, :]
        masked = []
        for t in range(TILES):
            place = within + base_ref[0, u, t : t + 1, :]
            allowed = (place >= lo) & (place < hi)
            masked.append(jnp.where(allowed, scores[t * BLOCK : (t + 1) * BLOCK], masked_value))
        scores = jnp.concatenate(masked, axis=0)
        raised = jnp.exp(scores - jnp.max(scores, axis=0, keepdims=True))
        probs = (raised * (1.0 / jnp.sum(raised, axis=0, keepdims=True))).astype(bf16)
        p_ref[0, u] = probs
        out_ref[here, :] = own_head_columns(mm_tn(probs, values)).astype(bf16)


def attend_back_kernel(
    blocks,
    rows_ref,
    q_ref,
    g_ref,
    k_ref,
    v_ref,
    p_ref,
    dq_ref,
    dk_ref,
    dv_ref,
    dk_sum,
    dv_sum,
):
    step = pl.program_id(1)

    @pl.when(step == 0)
    def _():
        dk_sum[...] = jnp.zeros_like(dk_sum)
        dv_sum[...] = jnp.zeros_like(dv_sum)

    found = []
    for u in range(BACKWARD_BLOCKS):
        here = pl.ds(u * BLOCK, BLOCK)
        readers = row_readers(rows_ref, blocks, step * BACKWARD_BLOCKS + u)
        keys = gathered(k_ref, *readers)
        values = gathered(v_ref, *readers)
        queries = stacked_by_head(q_ref[here, :])
        grads = stacked_by_head(g_ref[here, :])
        probs = p_ref[0, u]
        grad_probs = mm_nt(values, grads)
        wide = probs.astype(f32)
        balance = jnp.sum(wide * grad_probs, axis=0, keepdims=True)
        grad_scores = (wide * (grad_probs - balance)).astype(bf16)
        dq_ref[here, :] = (query_scale * own_head_columns(mm_tn(grad_scores, keys))).astype(bf16)
        found.append((readers, mm(grad_scores, queries), mm(probs, grads)))
    for (fixed_row, random_row), grad_keys, grad_values in found:
        for total, part in ((dk_sum, grad_keys), (dv_sum, grad_values)):
            for t in range(5):
                total[block_rows(fixed_row(t)), :] += part[t * BLOCK : (t + 1) * BLOCK]
            for t in range(RANDOM):
                rows = part[(5 + t) * BLOCK : (6 + t) * BLOCK]
                for h in range(GROUP):
                    first = (h // 2) * 2 * HEAD_DIM
                    mine = head_mask(BLOCK, 2 * HEAD_DIM, (h % 2) * HEAD_DIM)
                    total[block_rows(random_row(h, t)), pl.ds(first, 2 * HEAD_DIM)] += jnp.where(
                        mine, rows[:, first : first + 2 * HEAD_DIM], 0.0
                    )

    @pl.when(step == blocks // BACKWARD_BLOCKS - 1)
    def _():
        dk_ref[...] = dk_sum[...].astype(bf16)
        dv_ref[...] = dv_sum[...].astype(bf16)


def attend(rows, queries, keys, values, bases, docs):
    tokens, width = queries.shape
    ext = keys.shape[0]
    blocks, cols, some = tokens // BLOCK, GROUP * HEAD_DIM, FORWARD_BLOCKS
    groups = width // cols
    tile = pl.BlockSpec((some * BLOCK, cols), lambda g, i, r: (i, g))
    table = pl.BlockSpec((ext, cols), lambda g, i, r: (0, g))
    return pl.pallas_call(
        partial(attend_kernel, blocks),
        grid_spec=pltpu.PrefetchScalarGridSpec(
            num_scalar_prefetch=1,
            grid=(groups, blocks // some),
            in_specs=[
                tile,
                table,
                table,
                pl.BlockSpec((1, some, TILES, cols), lambda g, i, r: (g, i, 0, 0)),
                pl.BlockSpec((some, 8, cols), lambda g, i, r: (i, 0, 0)),
            ],
            out_specs=[
                tile,
                pl.BlockSpec((1, some, TILES * BLOCK, cols), lambda g, i, r: (g, i, 0, 0)),
            ],
        ),
        out_shape=[
            jax.ShapeDtypeStruct((tokens, width), bf16),
            jax.ShapeDtypeStruct((groups, blocks, TILES * BLOCK, cols), bf16),
        ],
        compiler_params=pltpu.CompilerParams(vmem_limit_bytes=40 << 20),
        name="attend",
    )(rows, queries, keys, values, bases, docs)


def attend_back(rows, queries, grads, keys, values, probs):
    tokens, width = queries.shape
    ext = keys.shape[0]
    blocks, cols, some = tokens // BLOCK, GROUP * HEAD_DIM, BACKWARD_BLOCKS
    groups = width // cols
    tile = pl.BlockSpec((some * BLOCK, cols), lambda g, i, r: (i, g))
    table = pl.BlockSpec((ext, cols), lambda g, i, r: (0, g))
    return pl.pallas_call(
        partial(attend_back_kernel, blocks),
        grid_spec=pltpu.PrefetchScalarGridSpec(
            num_scalar_prefetch=1,
            grid=(groups, blocks // some),
            in_specs=[
                tile,
                tile,
                table,
                table,
                pl.BlockSpec((1, some, TILES * BLOCK, cols), lambda g, i, r: (g, i, 0, 0)),
            ],
            out_specs=[tile, table, table],
            scratch_shapes=[pltpu.VMEM((ext, cols), f32), pltpu.VMEM((ext, cols), f32)],
        ),
        out_shape=[
            jax.ShapeDtypeStruct((tokens, width), bf16),
            jax.ShapeDtypeStruct((ext, width), bf16),
            jax.ShapeDtypeStruct((ext, width), bf16),
        ],
        compiler_params=pltpu.CompilerParams(vmem_limit_bytes=56 << 20),
        name="attend_back",
    )(rows, queries, grads, keys, values, probs)


def normalized(values):
    centred = values - jnp.mean(values, axis=-1, keepdims=True)
    root = lax.rsqrt(jnp.mean(centred * centred, axis=-1, keepdims=True) + epsilon)
    return centred * root, root


def norm_back(grad, normal, root, gain):
    scaled = grad * gain
    along = jnp.mean(scaled * normal, axis=-1, keepdims=True)
    return root * (scaled - jnp.mean(scaled, axis=-1, keepdims=True) - normal * along)


def gelu_and_slope(u):
    square = u * u
    bend = jnp.tanh(gelu_scale * (u + gelu_cubic * (square * u)))
    half = 0.5 * (1.0 + bend)
    slope = half + (0.5 * gelu_scale) * u * (1.0 - bend * bend) * (
        1.0 + (3.0 * gelu_cubic) * square
    )
    return u * half, slope


def middle_kernel(
    att_ref,
    x_ref,
    og_ref,
    wa_ref,
    wi_ref,
    wo_ref,
    vec_ref,
    bi_ref,
    res_ref,
    sum_ref,
    ga_ref,
    dwa_ref,
    dwi_ref,
    dwo_ref,
    dvec_ref,
    dbi_ref,
    normal,
    root,
    low,
    act,
    slope,
    inner,
):
    step, half = pl.program_id(0), pl.num_programs(0) // 2
    tokens, width = x_ref.shape
    slices = [pl.ds(t * ROWS, ROWS) for t in range(tokens // ROWS)]
    bias_attn, gain_one, offset_one, bias_outer, gain_two, offset_two = (
        vec_ref[n : n + 1, :] for n in range(6)
    )

    def row_sum(total, values):
        part = jnp.sum(values, axis=0, keepdims=True)
        return part if total is None else total + part

    @pl.when(step == 0)
    def _():
        for s in slices:
            values = x_ref[s, :].astype(f32) + mm(att_ref[s, :], wa_ref[...]) + bias_attn
            flat, scale = normalized(values)
            normal[s, :] = flat
            root[s, :] = jnp.broadcast_to(scale, (ROWS, 128))
            first = flat * gain_one + offset_one
            low[s, :] = first.astype(bf16)
            sum_ref[s, :] = first + bias_outer

    @pl.when(step < half)
    def _():
        for s in slices:
            active, bend = gelu_and_slope(mm(low[s, :], wi_ref[...]) + bi_ref[0])
            active = active.astype(bf16)
            act[step, s, :] = active
            slope[step, s, :] = bend.astype(bf16)
            sum_ref[s, :] += mm(active, wo_ref[...])

    @pl.when(step == half)
    def _():
        outer_sum, gain_sum, offset_sum = None, None, None
        for s in slices:
            flat, scale = normalized(sum_ref[s, :])
            res_ref[s, :] = (flat * gain_two + offset_two).astype(bf16)
            grad = og_ref[s, :].astype(f32)
            gain_sum = row_sum(gain_sum, grad * flat)
            offset_sum = row_sum(offset_sum, grad)
            second = norm_back(grad, flat, scale, gain_two)
            sum_ref[s, :] = second
            second = second.astype(bf16)
            ga_ref[s, :] = second
            outer_sum = row_sum(outer_sum, second.astype(f32))
        dvec_ref[3:4, :] = outer_sum
        dvec_ref[4:5, :] = gain_sum
        dvec_ref[5:6, :] = offset_sum
        dvec_ref[6:8, :] = jnp.zeros((2, width), f32)

    @pl.when(step >= half)
    def _():
        now = step - half
        total = None
        for s in slices:
            grad = mm_nt(ga_ref[s, :], wo_ref[...]) * slope[now, s, :].astype(f32)
            grad = grad.astype(bf16)
            inner[s, :] = grad
            total = row_sum(total, grad.astype(f32))
            sum_ref[s, :] += mm_nt(grad, wi_ref[...])
        dbi_ref[0] = total
        for n in range(width // 256):
            some = pl.ds(n * 256, 256)
            dwi_ref[some, :] = mm_tn(low[:, some], inner[...]).astype(bf16)
        for n in range(PIECE // 256):
            some = pl.ds(n * 256, 256)
            dwo_ref[some, :] = mm_tn(act[now, :, some], ga_ref[...]).astype(bf16)

    @pl.when(step == 2 * half - 1)
    def _():
        attn_sum, gain_sum, offset_sum = None, None, None
        for s in slices:
            grad, flat = sum_ref[s, :], normal[s, :]
            gain_sum = row_sum(gain_sum, grad * flat)
            offset_sum = row_sum(offset_sum, grad)
            grad = norm_back(grad, flat, root[s, 0:1], gain_one)
            sum_ref[s, :] = grad
            grad = grad.astype(bf16)
            inner[s, :width] = grad
            attn_sum = row_sum(attn_sum, grad.astype(f32))
            ga_ref[s, :] = mm_nt(grad, wa_ref[...]).astype(bf16)
        dvec_ref[0:1, :] = attn_sum
        dvec_ref[1:2, :] = gain_sum
        dvec_ref[2:3, :] = offset_sum
        for n in range(width // 256):
            some = pl.ds(n * 256, 256)
            dwa_ref[some, :] = mm_tn(att_ref[:, some], inner[:, :width]).astype(bf16)


def middle(attended, tokens, out_grad, w_attn, w_inner, w_outer, vectors, bias_inner):
    rows, width = tokens.shape
    steps = w_inner.shape[1] // PIECE
    one = pl.Buffered(1)
    still = pl.BlockSpec((rows, width), lambda i: (0, 0), pipeline_mode=one)
    square = pl.BlockSpec((width, width), lambda i: (0, 0), pipeline_mode=one)
    few = pl.BlockSpec((8, width), lambda i: (0, 0))
    later = lambda i: jnp.maximum(i - steps, 0)
    return pl.pallas_call(
        middle_kernel,
        grid=(2 * steps,),
        in_specs=[
            still,
            still,
            still,
            square,
            pl.BlockSpec((width, PIECE), lambda i: (0, i % steps)),
            pl.BlockSpec((PIECE, width), lambda i: (i % steps, 0)),
            few,
            pl.BlockSpec((1, 1, PIECE), lambda i: (i % steps, 0, 0)),
        ],
        out_specs=[
            still,
            still,
            still,
            square,
            pl.BlockSpec((width, PIECE), lambda i: (0, later(i))),
            pl.BlockSpec((PIECE, width), lambda i: (later(i), 0)),
            few,
            pl.BlockSpec((1, 1, PIECE), lambda i: (later(i), 0, 0)),
        ],
        out_shape=[
            jax.ShapeDtypeStruct((rows, width), bf16),
            jax.ShapeDtypeStruct((rows, width), f32),
            jax.ShapeDtypeStruct((rows, width), bf16),
            jax.ShapeDtypeStruct(w_attn.shape, bf16),
            jax.ShapeDtypeStruct(w_inner.shape, bf16),
            jax.ShapeDtypeStruct(w_outer.shape, bf16),
            jax.ShapeDtypeStruct((8, width), f32),
            jax.ShapeDtypeStruct((steps, 1, PIECE), f32),
        ],
        scratch_shapes=[
            pltpu.VMEM((rows, width), f32),
            pltpu.VMEM((rows, 128), f32),
            pltpu.VMEM((rows, width), bf16),
            pltpu.VMEM((steps, rows, PIECE), bf16),
            pltpu.VMEM((steps, rows, PIECE), bf16),
            pltpu.VMEM((rows, PIECE), bf16),
        ],
        compiler_params=pltpu.CompilerParams(vmem_limit_bytes=60 << 20),
        name="middle",
    )(attended, tokens, out_grad, w_attn, w_inner, w_outer, vectors, bias_inner)


def tile_plan(segment_ids, random_blocks, tokens):
    heads, total_blocks, _ = random_blocks.shape
    blocks = tokens // BLOCK
    chunk = lax.axis_index("blk") * lax.axis_size("head") + lax.axis_index("head")
    margin = REACH * tokens
    padded = jnp.concatenate(
        [
            jnp.full((margin,), -1, jnp.int32),
            segment_ids,
            jnp.full((margin,), jnp.iinfo(jnp.int32).max, jnp.int32),
        ]
    )
    near = lax.dynamic_slice_in_dim(padded, chunk * tokens, tokens + 2 * margin)
    own = near[margin : margin + tokens]
    begins = jnp.sum((near[None, :] < own[:, None]).astype(jnp.int32), axis=1)
    ends = jnp.sum((near[None, :] <= own[:, None]).astype(jnp.int32), axis=1)
    docs = jnp.stack([begins, ends]).reshape(2, blocks, BLOCK)
    docs = jnp.tile(jnp.transpose(docs, (1, 0, 2)), (1, 4, GROUP))
    first = begins[::BLOCK] // BLOCK
    here = REACH * blocks + jnp.arange(blocks, dtype=jnp.int32)
    fixed = jnp.stack([here - 1, here, here + 1, first, first + 1], axis=-1)
    picked = lax.dynamic_slice_in_dim(random_blocks, chunk * blocks, blocks, axis=1)
    picked = picked - (chunk - REACH) * blocks
    rows = jnp.concatenate(
        [jnp.broadcast_to(fixed[None], (heads, blocks, 5)), picked], axis=-1
    )
    earlier = jnp.arange(TILES)[None, :] < jnp.arange(TILES)[:, None]
    repeat = jnp.any((rows[..., :, None] == rows[..., None, :]) & earlier, axis=-1)
    bases = jnp.where(repeat, far_away, rows * BLOCK)
    rows = jnp.clip(rows, 0, (1 + 2 * REACH) * blocks - 1)
    bases = bases.reshape(heads // GROUP, GROUP, blocks, TILES)
    bases = jnp.repeat(jnp.transpose(bases, (0, 2, 3, 1)), BLOCK, axis=-1)
    return rows.reshape(-1), bases, docs


def side_pairs(blk, head, far):
    pairs = []
    for b in range(blk):
        for h in range(head):
            down = h < head // 2
            if far and h not in (0, head - 1):
                continue
            source = b - 1 if down else b + 1
            if 0 <= source < blk:
                pairs.append((h * blk + source, h * blk + b))
    return pairs


def widen(tokens_rows, blk, head):
    rows = tokens_rows.shape[0]
    h = lax.axis_index("head")
    line = lax.all_gather(tokens_rows, "head", axis=0, tiled=True)
    low = h < head // 2
    near = lax.dynamic_slice_in_dim(line, jnp.where(low, head - 1, 0) * rows, rows)
    far = lax.dynamic_slice_in_dim(line, jnp.where(low, head - 2, 1) * rows, rows)
    near = lax.ppermute(near, ("head", "blk"), side_pairs(blk, head, False))
    far = lax.ppermute(far, ("head", "blk"), side_pairs(blk, head, True))
    whole = jnp.concatenate([far, near, line, near, far], axis=0)
    return lax.dynamic_slice_in_dim(whole, h * rows, (1 + 2 * REACH) * rows)


def narrow(wide_rows, rows, blk, head):
    h = lax.axis_index("head")
    low = h < head // 2
    frame = jnp.zeros(((head + 2 * REACH) * rows, wide_rows.shape[1]), wide_rows.dtype)
    frame = lax.dynamic_update_slice_in_dim(frame, wide_rows, h * rows, 0)
    near = lax.dynamic_slice_in_dim(frame, jnp.where(low, 1, head + REACH) * rows, rows)
    far = lax.dynamic_slice_in_dim(frame, jnp.where(low, 0, head + REACH + 1) * rows, rows)
    back = [(t, s) for s, t in side_pairs(blk, head, False)]
    near = lax.ppermute(near, ("head", "blk"), back)
    back = [(t, s) for s, t in side_pairs(blk, head, True)]
    far = lax.ppermute(far, ("head", "blk"), back)
    line = frame[REACH * rows : (REACH + head) * rows].reshape(head, rows, -1)
    place = jnp.arange(head, dtype=jnp.int32)[:, None, None]
    line = line + jnp.where(place == jnp.where(low, head - 1, 0), near[None], 0)
    line = line + jnp.where(place == jnp.where(low, head - 2, 1), far[None], 0)
    return lax.psum_scatter(line.reshape(head * rows, -1), "head", scatter_dimension=0, tiled=True)


LINE = 4
CORES = 2
PIECES = 4
MESH = pl.DeviceIdType.MESH
NEAR_SLOT = (1, 0, 4, 3)
FAR_SLOT = (0, None, None, 4)


def remote(source, target, send, recv, head, blk):
    return pltpu.make_async_remote_copy(
        src_ref=source,
        dst_ref=target,
        send_sem=send,
        recv_sem=recv,
        device_id=(head, blk),
        device_id_type=MESH,
    )


def at_each_head(h, body):
    for hh in range(LINE):
        pl.when(h == hh)(partial(body, hh))


def greet_plane_and_line(h, b, blk):
    barrier = pltpu.get_barrier_semaphore()
    for d in range(1, LINE):
        pl.semaphore_signal(
            barrier, inc=1, device_id=((h + d) % LINE, b), device_id_type=MESH
        )
    for d in range(1, blk):
        pl.semaphore_signal(barrier, inc=1, device_id=(h, (b + d) % blk), device_id_type=MESH)
    pl.semaphore_wait(barrier, LINE - 1 + blk - 1)


def gather_kernel(blk, count, *refs):
    x_ref, shards = refs[0], refs[1 : 1 + count]
    wide, spill, fulls = refs[1 + count], refs[2 + count], refs[3 + count : 3 + 2 * count]
    local, zs, zr, cs, cr, ss, sr, us, ur, ds, dr, ns, nr, fs, fr = refs[3 + 2 * count :]
    h, b = lax.axis_index("head"), lax.axis_index("blk")
    chips = blk // CORES
    chip, core = b // CORES, b % CORES
    sibling = chip * CORES + 1 - core
    rows = x_ref.shape[0] // PIECES

    def piece(ref, p):
        return ref.at[pl.ds(p * rows, rows)]

    def place(hh, j):
        slot = 2 + j - hh
        return wide.at[slot] if 0 <= slot < 5 else spill

    def own(a):
        return pltpu.make_async_copy(shards[a], fulls[a].at[h, b], local.at[a])

    def along(a, d):
        return remote(
            shards[a], fulls[a].at[h, b], zs.at[a, d - 1], zr.at[a, d - 1], (h + d) % LINE, b
        )

    def along_arrives(a, d):
        src = (h - d + LINE) % LINE
        return remote(
            shards[a], fulls[a].at[src, b], zs.at[a, d - 1], zr.at[a, d - 1], (h + d) % LINE, b
        )

    def over(a, e):
        part = fulls[a].at[:, b]
        there = ((chip + e) % chips) * CORES + core
        return remote(part, part, cs.at[a, e - 1], cr.at[a, e - 1], h, there)

    def over_arrives(a, e):
        there = ((chip - e + chips) % chips) * CORES + core
        part = fulls[a].at[:, there]
        return remote(part, part, cs.at[a, e - 1], cr.at[a, e - 1], h, there)

    def across(a, e):
        part = fulls[a].at[:, ((chip - e + chips) % chips) * CORES + core]
        return remote(part, part, ss.at[a, e], sr.at[a, e], h, sibling)

    def across_arrives(a, e):
        part = fulls[a].at[:, ((chip - e + chips) % chips) * CORES + 1 - core]
        return remote(part, part, ss.at[a, e], sr.at[a, e], h, sibling)

    def spread(a):
        for d in range(1, LINE):
            along_arrives(a, d).wait_recv()
        own(a).wait()
        for e in range(1, chips):
            over(a, e).start()
        across(a, 0).start()

    def hand_over(a):
        for e in range(1, chips):
            over_arrives(a, e).wait_recv()
            across(a, e).start()

    def up(hh, j, p):
        source = x_ref if j == hh else place(hh, j)
        return remote(
            piece(source, p), piece(place(hh + 1, j), p), us.at[j, p], ur.at[j, p], (h + 1) % LINE, b
        )

    def up_arrives(hh, j, p):
        target = piece(place(hh, j), p)
        return remote(target, target, us.at[j, p], ur.at[j, p], (h + 1) % LINE, b)

    def down(hh, j, p):
        source = x_ref if j == hh else place(hh, j)
        return remote(
            piece(source, p), piece(place(hh - 1, j), p), ds.at[j, p], dr.at[j, p], (h + 3) % LINE, b
        )

    def down_arrives(hh, j, p):
        target = piece(place(hh, j), p)
        return remote(target, target, ds.at[j, p], dr.at[j, p], (h + 3) % LINE, b)

    def sides(hh, j):
        near, far = (3, 2) if hh < 2 else (0, 1)
        if j == near:
            return [(NEAR_SLOT[hh], ns, nr)]
        if j == far and FAR_SLOT[hh] is not None:
            return [(FAR_SLOT[hh], fs, fr)]
        return []

    def side(hh, j, p, slot, send, recv):
        target = (b + 1) % blk if hh < 2 else (b + blk - 1) % blk
        return remote(
            piece(place(hh, j), p), piece(wide.at[slot], p), send.at[p], recv.at[p], h, target
        )

    def sends_side(hh):
        return b < blk - 1 if hh < 2 else b > 0

    def gets_side(hh):
        return b > 0 if hh < 2 else b < blk - 1

    def side_slots(hh):
        found = [(NEAR_SLOT[hh], ns, nr)]
        if FAR_SLOT[hh] is not None:
            found.append((FAR_SLOT[hh], fs, fr))
        return found

    def fill(n, slot):
        return pltpu.make_async_copy(x_ref, wide.at[slot], local.at[count + 1 + n])

    def own_rows():
        return pltpu.make_async_copy(x_ref, wide.at[2], local.at[count])

    def begin(hh):
        for p in range(PIECES):
            if hh < LINE - 1:
                up(hh, hh, p).start()
            if hh > 0:
                down(hh, hh, p).start()

        @pl.when(jnp.logical_not(gets_side(hh)))
        def _():
            for n, (slot, _, _) in enumerate(side_slots(hh)):
                fill(n, slot).start()

    def pass_on(distance, hh):
        for p in range(PIECES):
            for j, arrives, onward, ends in (
                (hh - distance, up_arrives, up, hh == LINE - 1),
                (hh + distance, down_arrives, down, hh == 0),
            ):
                if not 0 <= j < LINE:
                    continue
                arrives(hh, j, p).wait_recv()
                if not ends:
                    onward(hh, j, p).start()
                for slot, send, recv in sides(hh, j):

                    @pl.when(sends_side(hh))
                    def _(slot=slot, send=send, recv=recv):
                        side(hh, j, p, slot, send, recv).start()

    def finish(hh):
        for p in range(PIECES):
            for j in range(LINE):
                if j <= hh < LINE - 1:
                    up(hh, j, p).wait_send()
                if j >= hh > 0:
                    down(hh, j, p).wait_send()

        @pl.when(sends_side(hh))
        def _():
            for j in range(LINE):
                for slot, send, recv in sides(hh, j):
                    for p in range(PIECES):
                        side(hh, j, p, slot, send, recv).wait_send()

        @pl.when(gets_side(hh))
        def _():
            for slot, send, recv in side_slots(hh):
                for p in range(PIECES):
                    target = piece(wide.at[slot], p)
                    remote(target, target, send.at[p], recv.at[p], h, (b + 1) % blk).wait_recv()

        @pl.when(jnp.logical_not(gets_side(hh)))
        def _():
            for n, (slot, _, _) in enumerate(side_slots(hh)):
                fill(n, slot).wait()

    own_rows().start()
    for a in range(count):
        own(a).start()
    greet_plane_and_line(h, b, blk)
    for a in range(count):
        for d in range(1, LINE):
            along(a, d).start()
    at_each_head(h, begin)
    for a in range(count):
        spread(a)
    at_each_head(h, partial(pass_on, 1))
    for a in range(count - 2):
        hand_over(a)
    at_each_head(h, partial(pass_on, 2))
    hand_over(count - 2)
    at_each_head(h, partial(pass_on, 3))
    hand_over(count - 1)
    for a in range(count):
        for d in range(1, LINE):
            along(a, d).wait_send()
        for e in range(1, chips):
            over(a, e).wait_send()
        for e in range(chips):
            across(a, e).wait_send()
            across_arrives(a, e).wait_recv()
    own_rows().wait()
    at_each_head(h, finish)


def gather(tokens, shards, blk):
    rows, width = tokens.shape
    count, chips = len(shards), blk // CORES
    anywhere = pl.BlockSpec(memory_space=pl.ANY)
    dma = pltpu.SemaphoreType.DMA
    outs = pl.pallas_call(
        partial(gather_kernel, blk, count),
        out_shape=[
            jax.ShapeDtypeStruct((5, rows, width), tokens.dtype),
            jax.ShapeDtypeStruct((rows, width), tokens.dtype),
        ]
        + [jax.ShapeDtypeStruct((LINE, blk) + s.shape, s.dtype) for s in shards],
        in_specs=[anywhere] * (1 + count),
        out_specs=[anywhere] * (2 + count),
        scratch_shapes=[dma((count + 3,))]
        + [dma((count, LINE - 1))] * 2
        + [dma((count, chips - 1))] * 2
        + [dma((count, chips))] * 2
        + [dma((LINE, PIECES))] * 4
        + [dma((PIECES,))] * 4,
        compiler_params=pltpu.CompilerParams(collective_id=0, has_side_effects=True),
    )(tokens, *shards)
    return outs[0], outs[2:]


def reduce_kernel(blk, count, *refs):
    dx_ref, grads = refs[0], refs[1 : 1 + count]
    sum_ref, outs = refs[1 + count], refs[2 + count : 2 + 2 * count]
    rest = refs[2 + 2 * count :]
    held, from_core, from_chip, from_line = (rest[n * count : (n + 1) * count] for n in range(4))
    line, arrived, aside = rest[4 * count : 4 * count + 3]
    load, ss, sr, cs, cr, zs, zr, xl, us, ur, ds, dr, ns, nr, fs, fr = rest[4 * count + 3 :]
    h, b = lax.axis_index("head"), lax.axis_index("blk")
    chips = blk // CORES
    chip, core = b // CORES, b % CORES
    sibling = chip * CORES + 1 - core
    rows = dx_ref.shape[1] // PIECES

    def mine(a, k):
        return pltpu.make_async_copy(grads[a].at[:, k * CORES + core], held[a].at[k], load.at[a, k])

    def across(a, k):
        return remote(
            grads[a].at[:, k * CORES + 1 - core],
            from_core[a].at[k],
            ss.at[a, k],
            sr.at[a, k],
            h,
            sibling,
        )

    def over(a, e):
        k = (chip + e) % chips
        return remote(
            held[a].at[k],
            from_chip[a].at[e - 1],
            cs.at[a, e - 1],
            cr.at[a, e - 1],
            h,
            k * CORES + core,
        )

    def along(a, d):
        there = (h + d) % LINE
        return remote(
            held[a].at[chip, there],
            from_line[a].at[d - 1],
            zs.at[a, d - 1],
            zr.at[a, d - 1],
            there,
            b,
        )

    def add_cores(a, k):
        def one(n, carry):
            held[a][k, n] = (held[a][k, n].astype(f32) + from_core[a][k, n].astype(f32)).astype(
                held[a].dtype
            )
            return carry

        lax.fori_loop(0, LINE, one, 0)

    def to_chips(a):
        for k in range(chips):
            mine(a, k).wait()
            across(a, k).wait_recv()
        for e in range(1, chips):
            add_cores(a, (chip + e) % chips)
            over(a, e).start()
        add_cores(a, chip)

    def to_line(a):
        for e in range(1, chips):
            over(a, e).wait_recv()

        def one(n, carry):
            total = held[a][chip, n].astype(f32)
            for e in range(1, chips):
                total = total + from_chip[a][e - 1, n].astype(f32)
            held[a][chip, n] = total.astype(held[a].dtype)
            return carry

        lax.fori_loop(0, LINE, one, 0)
        for d in range(1, LINE):
            along(a, d).start()

    def to_owner(a):
        for d in range(1, LINE):
            along(a, d).wait_recv()
        total = held[a][chip, h].astype(f32)
        for d in range(1, LINE):
            total = total + from_line[a][d - 1].astype(f32)
        outs[a][...] = total

    def part(p):
        return pl.ds(p * rows, rows)

    def piece(ref, p):
        return ref.at[part(p)]

    def add_rows(target, j, source, n, p):
        def one(step, carry):
            some = pl.ds(p * rows + step * 64, 64)
            target[j, some] = (
                target[j, some].astype(f32) + source[n, some].astype(f32)
            ).astype(target.dtype)
            return carry

        lax.fori_loop(0, rows // 64, one, 0)

    def slot_of(hh, j):
        slot = 2 + j - hh
        return slot if 0 <= slot < 5 else None

    def fetch(hh, j):
        return pltpu.make_async_copy(dx_ref.at[slot_of(hh, j)], line.at[j], xl.at[j])

    def arrival(hh, j, upward):
        return arrived.at[LINE if j == hh and not upward else j]

    def up(hh, j, p):
        return remote(
            piece(line.at[j], p),
            piece(arrival(hh + 1, j, True), p),
            us.at[j, p],
            ur.at[j, p],
            (h + 1) % LINE,
            b,
        )

    def up_arrives(hh, j, p):
        here = piece(arrival(hh, j, True), p)
        return remote(here, here, us.at[j, p], ur.at[j, p], (h + 1) % LINE, b)

    def down(hh, j, p):
        return remote(
            piece(line.at[j], p),
            piece(arrival(hh - 1, j, False), p),
            ds.at[j, p],
            dr.at[j, p],
            (h + 3) % LINE,
            b,
        )

    def down_arrives(hh, j, p):
        here = piece(arrival(hh, j, False), p)
        return remote(here, here, ds.at[j, p], dr.at[j, p], (h + 3) % LINE, b)

    def side_parts(hh):
        near, far = (3, 2) if hh < 2 else (0, 1)
        found = [(NEAR_SLOT[hh], near, 0, ns, nr)]
        if FAR_SLOT[hh] is not None:
            found.append((FAR_SLOT[hh], far, 1, fs, fr))
        return found

    def side(hh, slot, n, send, recv, p):
        target = (b + blk - 1) % blk if hh < 2 else (b + 1) % blk
        return remote(
            piece(dx_ref.at[slot], p), piece(aside.at[n], p), send.at[p], recv.at[p], h, target
        )

    def sends_side(hh):
        return b > 0 if hh < 2 else b < blk - 1

    def gets_side(hh):
        return b < blk - 1 if hh < 2 else b > 0

    def begin(hh):
        @pl.when(sends_side(hh))
        def _():
            for p in range(PIECES):
                for slot, _, n, send, recv in side_parts(hh):
                    side(hh, slot, n, send, recv, p).start()

        for j in range(LINE):
            if slot_of(hh, j) is not None:
                fetch(hh, j).start()
        for j in range(LINE):
            if slot_of(hh, j) is not None:
                fetch(hh, j).wait()
            else:
                line[j] = jnp.zeros(line.shape[1:], line.dtype)
        for p in range(PIECES):
            if hh == 0:
                up(hh, 1, p).start()
            if hh == LINE - 1:
                down(hh, 2, p).start()

    def take_sides(hh):
        for p in range(PIECES):
            for _, j, n, send, recv in side_parts(hh):

                @pl.when(gets_side(hh))
                def _(j=j, n=n, send=send, recv=recv):
                    here = piece(aside.at[n], p)
                    remote(here, here, send.at[p], recv.at[p], h, (b + 1) % blk).wait_recv()
                    add_rows(line, j, aside, n, p)

                if hh == 0:
                    up(hh, j, p).start()
                if hh == LINE - 1:
                    down(hh, j, p).start()

    def pass_on(first, hh):
        if hh == 1:
            moves = [(3, True), (0, False)] if first else [(2, True)]
        elif hh == 2:
            moves = [(0, False), (3, True)] if first else [(1, False)]
        else:
            moves = []
        for p in range(PIECES):
            for j, upward in moves:
                (up_arrives if upward else down_arrives)(hh, j, p).wait_recv()
                add_rows(line, j, arrived, j, p)
                (up if upward else down)(hh, j, p).start()

    def finish(hh):
        for p in range(PIECES):
            sources = []
            if hh > 0:
                up_arrives(hh, hh, p).wait_recv()
                sources.append(hh)
            if hh < LINE - 1:
                down_arrives(hh, hh, p).wait_recv()
                sources.append(LINE)

            def one(step, carry, p=p, sources=tuple(sources)):
                some = pl.ds(p * rows + step * 64, 64)
                total = line[hh, some].astype(f32)
                for n in sources:
                    total = total + arrived[n, some].astype(f32)
                sum_ref[some] = total
                return carry

            lax.fori_loop(0, rows // 64, one, 0)
        for p in range(PIECES):
            for j in range(LINE):
                if j > hh:
                    up(hh, j, p).wait_send()
                if j < hh:
                    down(hh, j, p).wait_send()

        @pl.when(sends_side(hh))
        def _():
            for p in range(PIECES):
                for slot, _, n, send, recv in side_parts(hh):
                    side(hh, slot, n, send, recv, p).wait_send()

    for a in range(count):
        for k in range(chips):
            mine(a, k).start()
    greet_plane_and_line(h, b, blk)
    for a in range(count):
        for k in range(chips):
            across(a, k).start()
    at_each_head(h, begin)
    for a in range(count):
        to_chips(a)
    at_each_head(h, take_sides)
    at_each_head(h, partial(pass_on, True))
    at_each_head(h, partial(pass_on, False))
    for a in range(count):
        to_line(a)
    at_each_head(h, finish)
    for a in range(count):
        to_owner(a)
    for a in range(count):
        for k in range(chips):
            across(a, k).wait_send()
        for e in range(1, chips):
            over(a, e).wait_send()
        for d in range(1, LINE):
            along(a, d).wait_send()


def reduce_to_owners(wide_grad, grads, blk):
    _, rows, width = wide_grad.shape
    count, chips = len(grads), blk // CORES
    anywhere = pl.BlockSpec(memory_space=pl.ANY)
    inside = pl.BlockSpec(memory_space=pltpu.VMEM)
    dma = pltpu.SemaphoreType.DMA
    shard = [g.shape[2:] for g in grads]
    outs = pl.pallas_call(
        partial(reduce_kernel, blk, count),
        out_shape=[jax.ShapeDtypeStruct((rows, width), f32)]
        + [jax.ShapeDtypeStruct(s, f32) for s in shard],
        in_specs=[anywhere] * (1 + count),
        out_specs=[inside] * (1 + count),
        scratch_shapes=[pltpu.VMEM((chips, LINE) + s, g.dtype) for s, g in zip(shard, grads)]
        + [pltpu.VMEM((chips, LINE) + s, g.dtype) for s, g in zip(shard, grads)]
        + [pltpu.VMEM((chips - 1, LINE) + s, g.dtype) for s, g in zip(shard, grads)]
        + [pltpu.VMEM((LINE - 1,) + s, g.dtype) for s, g in zip(shard, grads)]
        + [
            pltpu.VMEM((LINE, rows, width), bf16),
            pltpu.VMEM((LINE + 1, rows, width), bf16),
            pltpu.VMEM((2, rows, width), bf16),
        ]
        + [dma((count, chips))] * 3
        + [dma((count, chips - 1))] * 2
        + [dma((count, LINE - 1))] * 2
        + [dma((LINE,))]
        + [dma((LINE, PIECES))] * 4
        + [dma((PIECES,))] * 4,
        compiler_params=pltpu.CompilerParams(
            collective_id=1, has_side_effects=True, vmem_limit_bytes=60 << 20
        ),
    )(wide_grad, *grads)
    return outs[0], outs[1:]


def whole(shard):
    return lax.all_gather(shard, ("head", "blk"), axis=0, tiled=True)


def shared_out(grad):
    return lax.psum_scatter(grad.astype(bf16), ("head", "blk"), scatter_dimension=0, tiled=True).astype(f32)


def vectors_of(table, sizes):
    cuts = [sum(sizes[:n]) for n in range(len(sizes) + 1)]
    return [table[..., a:b] for a, b in zip(cuts[:-1], cuts[1:])]


def padded_to(flat, size):
    return jnp.pad(flat, [(0, 0)] * (flat.ndim - 1) + [(0, size - flat.shape[-1])])


def per_device(blk, head, tokens, *rest):
    weights, vectors, (out_grad, segment_ids, random_blocks) = rest[:6], rest[6:15], rest[15:]
    rows = tokens.shape[0]
    by_kernel = head == LINE and blk == LINE * CORES
    sizes = [v.shape[0] for v in vectors]
    if by_kernel:
        packed = padded_to(jnp.concatenate(vectors), 16 * 128).reshape(16, 128)
        order = (0, 1, 2, 3, 4, 5)
        wide, fulls = gather(tokens, [packed] + [weights[n] for n in order], blk)
        wide = wide.reshape(-1, tokens.shape[1])
        w_query, w_key, w_value, w_attn, w_inner, w_outer = [
            w.reshape(-1, w.shape[-1]) for w in fulls[1:]
        ]
        table = fulls[0].reshape(head * blk, -1)
    else:
        wide = widen(tokens, blk, head)
        w_query, w_key, w_value, w_attn, w_inner, w_outer = [whole(w) for w in weights]
        table = whole(jnp.concatenate(vectors)[None])
    (
        bias_query,
        bias_value,
        bias_attn,
        gain_one,
        offset_one,
        bias_inner,
        bias_outer,
        gain_two,
        offset_two,
    ) = [v.reshape(-1).astype(f32) for v in vectors_of(table, sizes)]

    rows_of, bases, docs = tile_plan(segment_ids, random_blocks, rows)
    queries = (query_scale * (mm(tokens, w_query) + bias_query)).astype(bf16)
    keys = mm(wide, w_key).astype(bf16)
    values = (mm(wide, w_value) + bias_value).astype(bf16)
    attended, probs = attend(rows_of, queries, keys, values, bases, docs)

    rows_vec = jnp.stack(
        [bias_attn, gain_one, offset_one, bias_outer, gain_two, offset_two, gain_two, gain_two]
    )
    result, grad_first_sum, grad_attended, grad_w_attn, grad_w_inner, grad_w_outer, sums_d, sums_ff = (
        middle(
            attended,
            tokens,
            out_grad,
            w_attn,
            w_inner,
            w_outer,
            rows_vec,
            bias_inner.reshape(-1, 1, PIECE),
        )
    )

    grad_scaled, grad_keyed, grad_valued = attend_back(
        rows_of, queries, grad_attended, keys, values, probs
    )
    def total(grads):
        return jnp.sum(grads.astype(f32), axis=0)

    sums = (
        total(grad_scaled),
        total(grad_valued),
        sums_d[0],
        sums_d[1],
        sums_d[2],
        sums_ff,
        sums_d[3],
        sums_d[4],
        sums_d[5],
    )
    packed = jnp.concatenate([s.reshape(blk * head, -1) for s in sums], axis=1)
    grad_wide = (mm_nt(grad_keyed, w_key) + mm_nt(grad_valued, w_value)).astype(bf16)
    grad_rows = grad_first_sum + mm_nt(grad_scaled, w_query)
    matrix_grads = [
        mm_tn(tokens, grad_scaled).astype(bf16),
        mm_tn(wide, grad_keyed).astype(bf16),
        mm_tn(wide, grad_valued).astype(bf16),
        grad_w_attn,
        grad_w_inner,
        grad_w_outer,
    ]
    if by_kernel:
        shares = [g.reshape(head, blk, -1, g.shape[-1]) for g in matrix_grads]
        small = padded_to(packed, 8 * 128).reshape(head, blk, 8, 128)
        wide_sum, sums = reduce_to_owners(
            grad_wide.reshape(-1, rows, grad_wide.shape[-1]), [small] + shares, blk
        )
        matrix_grads = list(sums[1:])
        packed = sums[0].reshape(-1)
    else:
        wide_sum = narrow(grad_wide, rows, blk, head).astype(f32)
        matrix_grads = [shared_out(g) for g in matrix_grads]
        packed = lax.psum_scatter(packed, ("head", "blk"), scatter_dimension=0, tiled=True)[0]
    return (
        (result, grad_rows + wide_sum)
        + tuple(matrix_grads)
        + tuple(vectors_of(packed, sizes))
    )


def solution(mesh):
    row = P(("blk", "head"), None)
    matrix = P(("head", "blk"), None)
    vector = P(("head", "blk"))
    return jax.shard_map(
        partial(per_device, mesh.shape["blk"], mesh.shape["head"]),
        mesh=mesh,
        in_specs=(row,) + (matrix,) * 6 + (vector,) * 9 + (row, P(), P()),
        out_specs=(row, row) + (matrix,) * 6 + (vector,) * 9,
        check_vma=False,
    )
```

```python
from functools import partial

import jax
import jax.numpy as jnp
from jax import lax
from jax.experimental import pallas as pl
from jax.experimental.pallas import tpu as pltpu
from jax.sharding import PartitionSpec as P

HEAD_DIM = 64
BLOCK = 64
RANDOM = 3
TILES = 5 + RANDOM
REACH = 2
GROUP = 4
FORWARD_BLOCKS = 4
BACKWARD_BLOCKS = 4
ROWS = 256
PIECE = 768

epsilon = 1e-06
masked_value = -1e30
query_scale = 0.125
gelu_scale = 0.7978845608028654
gelu_cubic = 0.044715
far_away = -(1 << 24)
f32, bf16 = jnp.float32, jnp.bfloat16


def mm(a, b):
    return jnp.dot(a, b, preferred_element_type=f32)


def mm_nt(a, b):
    return lax.dot_general(a, b, (((1,), (1,)), ((), ())), preferred_element_type=f32)


def mm_tn(a, b):
    return lax.dot_general(a, b, (((0,), (0,)), ((), ())), preferred_element_type=f32)


def head_mask(rows, cols, first):
    lanes = lax.broadcasted_iota(jnp.int32, (rows, cols), 1)
    return (lanes >= first) & (lanes < first + HEAD_DIM)


def stacked_by_head(tile):
    rows, cols = tile.shape
    return jnp.concatenate(
        [
            jnp.where(head_mask(rows, cols, h * HEAD_DIM), tile, jnp.zeros_like(tile))
            for h in range(cols // HEAD_DIM)
        ],
        axis=0,
    )


def own_head_columns(stacked):
    cols = stacked.shape[1]
    total = None
    for h in range(cols // HEAD_DIM):
        part = stacked[h * BLOCK : (h + 1) * BLOCK]
        part = jnp.where(head_mask(BLOCK, cols, h * HEAD_DIM), part, 0.0)
        total = part if total is None else total + part
    return total


def block_rows(row):
    return pl.ds(pl.multiple_of(row * BLOCK, BLOCK), BLOCK)


def gathered(table_ref, fixed_row, random_row):
    tiles = [table_ref[block_rows(fixed_row(t)), :] for t in range(5)]
    low = head_mask(BLOCK, 2 * HEAD_DIM, 0)
    for t in range(RANDOM):
        halves = []
        for pair in range(GROUP // 2):
            cols = pl.ds(pair * 2 * HEAD_DIM, 2 * HEAD_DIM)
            a = table_ref[block_rows(random_row(2 * pair, t)), cols]
            b = table_ref[block_rows(random_row(2 * pair + 1, t)), cols]
            halves.append(jnp.where(low, a, b))
        tiles.append(jnp.concatenate(halves, axis=1))
    return jnp.concatenate(tiles, axis=0)


def row_readers(rows_ref, blocks, i):
    group = pl.program_id(0)

    def fixed_row(t):
        return rows_ref[(group * GROUP * blocks + i) * TILES + t]

    def random_row(h, t):
        return rows_ref[((group * GROUP + h) * blocks + i) * TILES + 5 + t]

    return fixed_row, random_row


def attend_kernel(blocks, rows_ref, q_ref, k_ref, v_ref, base_ref, doc_ref, out_ref, p_ref):
    within = lax.broadcasted_iota(jnp.int32, (BLOCK, GROUP * BLOCK), 0)
    for u in range(FORWARD_BLOCKS):
        here = pl.ds(u * BLOCK, BLOCK)
        readers = row_readers(rows_ref, blocks, pl.program_id(1) * FORWARD_BLOCKS + u)
        keys = gathered(k_ref, *readers)
        values = gathered(v_ref, *readers)
        scores = mm_nt(keys, stacked_by_head(q_ref[here, :]))
        lo = doc_ref[u, 0:1, :]
        hi = doc_ref[u, 1:2, :]
        masked = []
        for t in range(TILES):
            place = within + base_ref[0, u, t : t + 1, :]
            allowed = (place >= lo) & (place < hi)
            masked.append(jnp.where(allowed, scores[t * BLOCK : (t + 1) * BLOCK], masked_value))
        scores = jnp.concatenate(masked, axis=0)
        raised = jnp.exp(scores - jnp.max(scores, axis=0, keepdims=True))
        probs = (raised * (1.0 / jnp.sum(raised, axis=0, keepdims=True))).astype(bf16)
        p_ref[0, u] = probs
        out_ref[here, :] = own_head_columns(mm_tn(probs, values)).astype(bf16)


def attend_back_kernel(
    blocks,
    rows_ref,
    q_ref,
    g_ref,
    k_ref,
    v_ref,
    p_ref,
    dq_ref,
    dk_ref,
    dv_ref,
    dk_sum,
    dv_sum,
):
    step = pl.program_id(1)

    @pl.when(step == 0)
    def _():
        dk_sum[...] = jnp.zeros_like(dk_sum)
        dv_sum[...] = jnp.zeros_like(dv_sum)

    found = []
    for u in range(BACKWARD_BLOCKS):
        here = pl.ds(u * BLOCK, BLOCK)
        readers = row_readers(rows_ref, blocks, step * BACKWARD_BLOCKS + u)
        keys = gathered(k_ref, *readers)
        values = gathered(v_ref, *readers)
        queries = stacked_by_head(q_ref[here, :])
        grads = stacked_by_head(g_ref[here, :])
        probs = p_ref[0, u]
        grad_probs = mm_nt(values, grads)
        wide = probs.astype(f32)
        balance = jnp.sum(wide * grad_probs, axis=0, keepdims=True)
        grad_scores = (wide * (grad_probs - balance)).astype(bf16)
        dq_ref[here, :] = (query_scale * own_head_columns(mm_tn(grad_scores, keys))).astype(bf16)
        found.append((readers, mm(grad_scores, queries), mm(probs, grads)))
    for (fixed_row, random_row), grad_keys, grad_values in found:
        for total, part in ((dk_sum, grad_keys), (dv_sum, grad_values)):
            for t in range(5):
                total[block_rows(fixed_row(t)), :] += part[t * BLOCK : (t + 1) * BLOCK]
            for t in range(RANDOM):
                rows = part[(5 + t) * BLOCK : (6 + t) * BLOCK]
                for h in range(GROUP):
                    first = (h // 2) * 2 * HEAD_DIM
                    mine = head_mask(BLOCK, 2 * HEAD_DIM, (h % 2) * HEAD_DIM)
                    total[block_rows(random_row(h, t)), pl.ds(first, 2 * HEAD_DIM)] += jnp.where(
                        mine, rows[:, first : first + 2 * HEAD_DIM], 0.0
                    )

    @pl.when(step == blocks // BACKWARD_BLOCKS - 1)
    def _():
        dk_ref[...] = dk_sum[...].astype(bf16)
        dv_ref[...] = dv_sum[...].astype(bf16)


def attend(rows, queries, keys, values, bases, docs):
    tokens, width = queries.shape
    ext = keys.shape[0]
    blocks, cols, some = tokens // BLOCK, GROUP * HEAD_DIM, FORWARD_BLOCKS
    groups = width // cols
    tile = pl.BlockSpec((some * BLOCK, cols), lambda g, i, r: (i, g))
    table = pl.BlockSpec((ext, cols), lambda g, i, r: (0, g))
    return pl.pallas_call(
        partial(attend_kernel, blocks),
        grid_spec=pltpu.PrefetchScalarGridSpec(
            num_scalar_prefetch=1,
            grid=(groups, blocks // some),
            in_specs=[
                tile,
                table,
                table,
                pl.BlockSpec((1, some, TILES, cols), lambda g, i, r: (g, i, 0, 0)),
                pl.BlockSpec((some, 8, cols), lambda g, i, r: (i, 0, 0)),
            ],
            out_specs=[
                tile,
                pl.BlockSpec((1, some, TILES * BLOCK, cols), lambda g, i, r: (g, i, 0, 0)),
            ],
        ),
        out_shape=[
            jax.ShapeDtypeStruct((tokens, width), bf16),
            jax.ShapeDtypeStruct((groups, blocks, TILES * BLOCK, cols), bf16),
        ],
        compiler_params=pltpu.CompilerParams(vmem_limit_bytes=40 << 20),
        name="attend",
    )(rows, queries, keys, values, bases, docs)


def attend_back(rows, queries, grads, keys, values, probs):
    tokens, width = queries.shape
    ext = keys.shape[0]
    blocks, cols, some = tokens // BLOCK, GROUP * HEAD_DIM, BACKWARD_BLOCKS
    groups = width // cols
    tile = pl.BlockSpec((some * BLOCK, cols), lambda g, i, r: (i, g))
    table = pl.BlockSpec((ext, cols), lambda g, i, r: (0, g))
    return pl.pallas_call(
        partial(attend_back_kernel, blocks),
        grid_spec=pltpu.PrefetchScalarGridSpec(
            num_scalar_prefetch=1,
            grid=(groups, blocks // some),
            in_specs=[
                tile,
                tile,
                table,
                table,
                pl.BlockSpec((1, some, TILES * BLOCK, cols), lambda g, i, r: (g, i, 0, 0)),
            ],
            out_specs=[tile, table, table],
            scratch_shapes=[pltpu.VMEM((ext, cols), f32), pltpu.VMEM((ext, cols), f32)],
        ),
        out_shape=[
            jax.ShapeDtypeStruct((tokens, width), bf16),
            jax.ShapeDtypeStruct((ext, width), bf16),
            jax.ShapeDtypeStruct((ext, width), bf16),
        ],
        compiler_params=pltpu.CompilerParams(vmem_limit_bytes=56 << 20),
        cost_estimate=pl.CostEstimate(
            flops=10 * groups * blocks * TILES * BLOCK * cols * cols,
            bytes_accessed=100 << 20,
            transcendentals=0,
        ),
        name="attend_back",
    )(rows, queries, grads, keys, values, probs)


def normalized(values):
    centred = values - jnp.mean(values, axis=-1, keepdims=True)
    root = lax.rsqrt(jnp.mean(centred * centred, axis=-1, keepdims=True) + epsilon)
    return centred * root, root


def norm_back(grad, normal, root, gain):
    scaled = grad * gain
    along = jnp.mean(scaled * normal, axis=-1, keepdims=True)
    return root * (scaled - jnp.mean(scaled, axis=-1, keepdims=True) - normal * along)


def gelu_and_slope(u):
    square = u * u
    bend = jnp.tanh(gelu_scale * (u + gelu_cubic * (square * u)))
    half = 0.5 * (1.0 + bend)
    slope = half + (0.5 * gelu_scale) * u * (1.0 - bend * bend) * (
        1.0 + (3.0 * gelu_cubic) * square
    )
    return u * half, slope


def middle_kernel(
    att_ref,
    x_ref,
    og_ref,
    wa_ref,
    wi_ref,
    wo_ref,
    vec_ref,
    bi_ref,
    res_ref,
    sum_ref,
    ga_ref,
    dwa_ref,
    dwi_ref,
    dwo_ref,
    dvec_ref,
    dbi_ref,
    normal,
    root,
    low,
    act,
    slope,
    inner,
):
    step, half = pl.program_id(0), pl.num_programs(0) // 2
    tokens, width = x_ref.shape
    slices = [pl.ds(t * ROWS, ROWS) for t in range(tokens // ROWS)]
    bias_attn, gain_one, offset_one, bias_outer, gain_two, offset_two = (
        vec_ref[n : n + 1, :] for n in range(6)
    )

    def row_sum(total, values):
        part = jnp.sum(values, axis=0, keepdims=True)
        return part if total is None else total + part

    @pl.when(step == 0)
    def _():
        for s in slices:
            values = x_ref[s, :].astype(f32) + mm(att_ref[s, :], wa_ref[...]) + bias_attn
            flat, scale = normalized(values)
            normal[s, :] = flat
            root[s, :] = jnp.broadcast_to(scale, (ROWS, 128))
            first = flat * gain_one + offset_one
            low[s, :] = first.astype(bf16)
            sum_ref[s, :] = first + bias_outer

    @pl.when(step < half)
    def _():
        for s in slices:
            active, bend = gelu_and_slope(mm(low[s, :], wi_ref[...]) + bi_ref[0])
            active = active.astype(bf16)
            act[step, s, :] = active
            slope[step, s, :] = bend.astype(bf16)
            sum_ref[s, :] += mm(active, wo_ref[...])

    @pl.when(step == half)
    def _():
        outer_sum, gain_sum, offset_sum = None, None, None
        for s in slices:
            flat, scale = normalized(sum_ref[s, :])
            res_ref[s, :] = (flat * gain_two + offset_two).astype(bf16)
            grad = og_ref[s, :].astype(f32)
            gain_sum = row_sum(gain_sum, grad * flat)
            offset_sum = row_sum(offset_sum, grad)
            second = norm_back(grad, flat, scale, gain_two)
            sum_ref[s, :] = second
            second = second.astype(bf16)
            ga_ref[s, :] = second
            outer_sum = row_sum(outer_sum, second.astype(f32))
        dvec_ref[3:4, :] = outer_sum
        dvec_ref[4:5, :] = gain_sum
        dvec_ref[5:6, :] = offset_sum
        dvec_ref[6:8, :] = jnp.zeros((2, width), f32)

    @pl.when(step >= half)
    def _():
        now = step - half
        total = None
        for s in slices:
            grad = mm_nt(ga_ref[s, :], wo_ref[...]) * slope[now, s, :].astype(f32)
            grad = grad.astype(bf16)
            inner[s, :] = grad
            total = row_sum(total, grad.astype(f32))
            sum_ref[s, :] += mm_nt(grad, wi_ref[...])
        dbi_ref[0] = total
        for n in range(width // 256):
            some = pl.ds(n * 256, 256)
            dwi_ref[some, :] = mm_tn(low[:, some], inner[...]).astype(bf16)
        for n in range(PIECE // 256):
            some = pl.ds(n * 256, 256)
            dwo_ref[some, :] = mm_tn(act[now, :, some], ga_ref[...]).astype(bf16)

    @pl.when(step == 2 * half - 1)
    def _():
        attn_sum, gain_sum, offset_sum = None, None, None
        for s in slices:
            grad, flat = sum_ref[s, :], normal[s, :]
            gain_sum = row_sum(gain_sum, grad * flat)
            offset_sum = row_sum(offset_sum, grad)
            grad = norm_back(grad, flat, root[s, 0:1], gain_one)
            sum_ref[s, :] = grad
            grad = grad.astype(bf16)
            inner[s, :width] = grad
            attn_sum = row_sum(attn_sum, grad.astype(f32))
            ga_ref[s, :] = mm_nt(grad, wa_ref[...]).astype(bf16)
        dvec_ref[0:1, :] = attn_sum
        dvec_ref[1:2, :] = gain_sum
        dvec_ref[2:3, :] = offset_sum
        for n in range(width // 256):
            some = pl.ds(n * 256, 256)
            dwa_ref[some, :] = mm_tn(att_ref[:, some], inner[:, :width]).astype(bf16)


def middle(attended, tokens, out_grad, w_attn, w_inner, w_outer, vectors, bias_inner):
    rows, width = tokens.shape
    steps = w_inner.shape[1] // PIECE
    one = pl.Buffered(1)
    still = pl.BlockSpec((rows, width), lambda i: (0, 0), pipeline_mode=one)
    square = pl.BlockSpec((width, width), lambda i: (0, 0), pipeline_mode=one)
    few = pl.BlockSpec((8, width), lambda i: (0, 0))
    later = lambda i: jnp.maximum(i - steps, 0)
    return pl.pallas_call(
        middle_kernel,
        grid=(2 * steps,),
        in_specs=[
            still,
            still,
            still,
            square,
            pl.BlockSpec((width, PIECE), lambda i: (0, i % steps)),
            pl.BlockSpec((PIECE, width), lambda i: (i % steps, 0)),
            few,
            pl.BlockSpec((1, 1, PIECE), lambda i: (i % steps, 0, 0)),
        ],
        out_specs=[
            still,
            still,
            still,
            square,
            pl.BlockSpec((width, PIECE), lambda i: (0, later(i))),
            pl.BlockSpec((PIECE, width), lambda i: (later(i), 0)),
            few,
            pl.BlockSpec((1, 1, PIECE), lambda i: (later(i), 0, 0)),
        ],
        out_shape=[
            jax.ShapeDtypeStruct((rows, width), bf16),
            jax.ShapeDtypeStruct((rows, width), f32),
            jax.ShapeDtypeStruct((rows, width), bf16),
            jax.ShapeDtypeStruct(w_attn.shape, bf16),
            jax.ShapeDtypeStruct(w_inner.shape, bf16),
            jax.ShapeDtypeStruct(w_outer.shape, bf16),
            jax.ShapeDtypeStruct((8, width), f32),
            jax.ShapeDtypeStruct((steps, 1, PIECE), f32),
        ],
        scratch_shapes=[
            pltpu.VMEM((rows, width), f32),
            pltpu.VMEM((rows, 128), f32),
            pltpu.VMEM((rows, width), bf16),
            pltpu.VMEM((steps, rows, PIECE), bf16),
            pltpu.VMEM((steps, rows, PIECE), bf16),
            pltpu.VMEM((rows, PIECE), bf16),
        ],
        compiler_params=pltpu.CompilerParams(vmem_limit_bytes=60 << 20),
        name="middle",
    )(attended, tokens, out_grad, w_attn, w_inner, w_outer, vectors, bias_inner)


def project_kernel(wide_ref, wk_ref, wv_ref, wq_ref, vec_ref, k_ref, v_ref, q_ref):
    rows = wide_ref.shape[0]
    slices = [pl.ds(t * ROWS, ROWS) for t in range(rows // ROWS)]
    for s in slices:
        k_ref[s, :] = mm(wide_ref[s, :], wk_ref[...]).astype(bf16)
        v_ref[s, :] = (mm(wide_ref[s, :], wv_ref[...]) + vec_ref[7:8, :]).astype(bf16)

    @pl.when(pl.program_id(0) == REACH)
    def _():
        for s in slices:
            queries = mm(wide_ref[s, :], wq_ref[...]) + vec_ref[6:7, :]
            q_ref[s, :] = (query_scale * queries).astype(bf16)


def project(wide, w_key, w_value, w_query, vectors, rows):
    width = wide.shape[1]
    one = pl.Buffered(1)
    tile = pl.BlockSpec((rows, width), lambda i: (i, 0))
    still = pl.BlockSpec((rows, width), lambda i: (0, 0), pipeline_mode=one)
    square = pl.BlockSpec((width, width), lambda i: (0, 0), pipeline_mode=one)
    table = jax.ShapeDtypeStruct(wide.shape, bf16)
    return pl.pallas_call(
        project_kernel,
        grid=(1 + 2 * REACH,),
        in_specs=[tile, square, square, square, pl.BlockSpec((8, width), lambda i: (0, 0))],
        out_specs=[tile, tile, still],
        out_shape=[table, table, jax.ShapeDtypeStruct((rows, width), bf16)],
        compiler_params=pltpu.CompilerParams(vmem_limit_bytes=40 << 20),
        name="project",
    )(wide, w_key, w_value, w_query, vectors)


def project_back_kernel(
    wide_ref,
    dk_ref,
    dv_ref,
    dq_ref,
    wk_ref,
    wv_ref,
    wq_ref,
    first_ref,
    dx_ref,
    rows_ref,
    dwk_ref,
    dwv_ref,
    dwq_ref,
    sums_ref,
    key_sum,
    value_sum,
):
    step = pl.program_id(0)
    rows, width = dx_ref.shape
    slices = [pl.ds(t * ROWS, ROWS) for t in range(rows // ROWS)]
    columns = [pl.ds(n * 256, 256) for n in range(width // 256)]

    def summed(ref):
        return jnp.sum(ref[...].astype(f32), axis=0, keepdims=True)

    @pl.when(step == 0)
    def _():
        key_sum[...] = jnp.zeros_like(key_sum)
        value_sum[...] = jnp.zeros_like(value_sum)
        sums_ref[...] = jnp.zeros_like(sums_ref)

    for s in slices:
        dx_ref[s, :] = (
            mm_nt(dk_ref[s, :], wk_ref[...]) + mm_nt(dv_ref[s, :], wv_ref[...])
        ).astype(bf16)
    for c in columns:
        key_sum[c, :] += mm_tn(wide_ref[:, c], dk_ref[...])
        value_sum[c, :] += mm_tn(wide_ref[:, c], dv_ref[...])
    sums_ref[0:1, :] += summed(dv_ref)

    @pl.when(step == REACH)
    def _():
        for s in slices:
            rows_ref[s, :] = first_ref[s, :] + mm_nt(dq_ref[s, :], wq_ref[...])
        for c in columns:
            dwq_ref[c, :] = mm_tn(wide_ref[:, c], dq_ref[...]).astype(bf16)
        sums_ref[1:2, :] = summed(dq_ref)

    @pl.when(step == pl.num_programs(0) - 1)
    def _():
        dwk_ref[...] = key_sum[...].astype(bf16)
        dwv_ref[...] = value_sum[...].astype(bf16)


def project_back(wide, grad_keyed, grad_valued, grad_scaled, w_key, w_value, w_query, grad_first):
    rows, width = grad_scaled.shape
    one = pl.Buffered(1)
    tile = pl.BlockSpec((rows, width), lambda i: (i, 0))
    still = pl.BlockSpec((rows, width), lambda i: (0, 0), pipeline_mode=one)
    square = pl.BlockSpec((width, width), lambda i: (0, 0), pipeline_mode=one)
    few = pl.BlockSpec((8, width), lambda i: (0, 0))
    matrix = jax.ShapeDtypeStruct((width, width), bf16)
    steps = wide.shape[0] // rows
    return pl.pallas_call(
        project_back_kernel,
        grid=(steps,),
        in_specs=[tile, tile, tile, still, square, square, square, still],
        out_specs=[tile, still, square, square, square, few],
        out_shape=[
            jax.ShapeDtypeStruct(wide.shape, bf16),
            jax.ShapeDtypeStruct((rows, width), f32),
            matrix,
            matrix,
            matrix,
            jax.ShapeDtypeStruct((8, width), f32),
        ],
        scratch_shapes=[pltpu.VMEM((width, width), f32)] * 2,
        compiler_params=pltpu.CompilerParams(vmem_limit_bytes=56 << 20),
        cost_estimate=pl.CostEstimate(
            flops=8 * wide.shape[0] * width * width, bytes_accessed=40 << 20, transcendentals=0
        ),
        name="project_back",
    )(wide, grad_keyed, grad_valued, grad_scaled, w_key, w_value, w_query, grad_first)


def tile_plan(segment_ids, random_blocks, tokens):
    heads, total_blocks, _ = random_blocks.shape
    blocks = tokens // BLOCK
    chunk = lax.axis_index("blk") * lax.axis_size("head") + lax.axis_index("head")
    margin = REACH * tokens
    padded = jnp.concatenate(
        [
            jnp.full((margin,), -1, jnp.int32),
            segment_ids,
            jnp.full((margin,), jnp.iinfo(jnp.int32).max, jnp.int32),
        ]
    )
    near = lax.dynamic_slice_in_dim(padded, chunk * tokens, tokens + 2 * margin)
    own = near[margin : margin + tokens]
    before, after = near[: margin + tokens], near[margin:]
    begins = jnp.sum((before[None, :] < own[:, None]).astype(jnp.int32), axis=1)
    ends = margin + jnp.sum((after[None, :] <= own[:, None]).astype(jnp.int32), axis=1)
    docs = jnp.stack([begins, ends]).reshape(2, blocks, BLOCK)
    docs = jnp.tile(jnp.transpose(docs, (1, 0, 2)), (1, 4, GROUP))
    first = begins[::BLOCK] // BLOCK
    here = REACH * blocks + jnp.arange(blocks, dtype=jnp.int32)
    fixed = jnp.stack([here - 1, here, here + 1, first, first + 1], axis=-1)
    picked = lax.dynamic_slice_in_dim(random_blocks, chunk * blocks, blocks, axis=1)
    picked = picked - (chunk - REACH) * blocks
    rows = jnp.concatenate(
        [jnp.broadcast_to(fixed[None], (heads, blocks, 5)), picked], axis=-1
    )
    earlier = jnp.arange(TILES)[None, :] < jnp.arange(TILES)[:, None]
    repeat = jnp.any((rows[..., :, None] == rows[..., None, :]) & earlier, axis=-1)
    bases = jnp.where(repeat, far_away, rows * BLOCK)
    rows = jnp.clip(rows, 0, (1 + 2 * REACH) * blocks - 1)
    bases = bases.reshape(heads // GROUP, GROUP, blocks, TILES)
    bases = jnp.repeat(jnp.transpose(bases, (0, 2, 3, 1)), BLOCK, axis=-1)
    return rows.reshape(-1), bases, docs


def side_pairs(blk, head, far):
    pairs = []
    for b in range(blk):
        for h in range(head):
            down = h < head // 2
            if far and h not in (0, head - 1):
                continue
            source = b - 1 if down else b + 1
            if 0 <= source < blk:
                pairs.append((h * blk + source, h * blk + b))
    return pairs


def widen(tokens_rows, blk, head):
    rows = tokens_rows.shape[0]
    h = lax.axis_index("head")
    line = lax.all_gather(tokens_rows, "head", axis=0, tiled=True)
    low = h < head // 2
    near = lax.dynamic_slice_in_dim(line, jnp.where(low, head - 1, 0) * rows, rows)
    far = lax.dynamic_slice_in_dim(line, jnp.where(low, head - 2, 1) * rows, rows)
    near = lax.ppermute(near, ("head", "blk"), side_pairs(blk, head, False))
    far = lax.ppermute(far, ("head", "blk"), side_pairs(blk, head, True))
    whole = jnp.concatenate([far, near, line, near, far], axis=0)
    return lax.dynamic_slice_in_dim(whole, h * rows, (1 + 2 * REACH) * rows)


def narrow(wide_rows, rows, blk, head):
    h = lax.axis_index("head")
    low = h < head // 2
    frame = jnp.zeros(((head + 2 * REACH) * rows, wide_rows.shape[1]), wide_rows.dtype)
    frame = lax.dynamic_update_slice_in_dim(frame, wide_rows, h * rows, 0)
    near = lax.dynamic_slice_in_dim(frame, jnp.where(low, 1, head + REACH) * rows, rows)
    far = lax.dynamic_slice_in_dim(frame, jnp.where(low, 0, head + REACH + 1) * rows, rows)
    back = [(t, s) for s, t in side_pairs(blk, head, False)]
    near = lax.ppermute(near, ("head", "blk"), back)
    back = [(t, s) for s, t in side_pairs(blk, head, True)]
    far = lax.ppermute(far, ("head", "blk"), back)
    line = frame[REACH * rows : (REACH + head) * rows].reshape(head, rows, -1)
    place = jnp.arange(head, dtype=jnp.int32)[:, None, None]
    line = line + jnp.where(place == jnp.where(low, head - 1, 0), near[None], 0)
    line = line + jnp.where(place == jnp.where(low, head - 2, 1), far[None], 0)
    return lax.psum_scatter(line.reshape(head * rows, -1), "head", scatter_dimension=0, tiled=True)


LINE = 4
CORES = 2
PIECES = 4
PIECES_BACK = 8
MESH = pl.DeviceIdType.MESH
NEAR_SLOT = (1, 0, 4, 3)
FAR_SLOT = (0, None, None, 4)


def remote(source, target, send, recv, head, blk):
    return pltpu.make_async_remote_copy(
        src_ref=source,
        dst_ref=target,
        send_sem=send,
        recv_sem=recv,
        device_id=(head, blk),
        device_id_type=MESH,
    )


def at_each_head(h, body):
    for hh in range(LINE):
        pl.when(h == hh)(partial(body, hh))


def greet_plane_and_line(h, b, blk):
    barrier = pltpu.get_barrier_semaphore()
    for d in range(1, LINE):
        pl.semaphore_signal(
            barrier, inc=1, device_id=((h + d) % LINE, b), device_id_type=MESH
        )
    for d in range(1, blk):
        pl.semaphore_signal(barrier, inc=1, device_id=(h, (b + d) % blk), device_id_type=MESH)
    pl.semaphore_wait(barrier, LINE - 1 + blk - 1)


def gather_kernel(blk, count, *refs):
    x_ref, shards = refs[0], refs[1 : 1 + count]
    wide, spill, fulls = refs[1 + count], refs[2 + count], refs[3 + count : 3 + 2 * count]
    local, zs, zr, cs, cr, ss, sr, us, ur, ds, dr, ns, nr, fs, fr = refs[3 + 2 * count :]
    h, b = lax.axis_index("head"), lax.axis_index("blk")
    chips = blk // CORES
    chip, core = b // CORES, b % CORES
    sibling = chip * CORES + 1 - core
    rows = x_ref.shape[0] // PIECES

    def piece(ref, p):
        return ref.at[pl.ds(p * rows, rows)]

    def place(hh, j):
        slot = 2 + j - hh
        return wide.at[slot] if 0 <= slot < 5 else spill

    def own(a):
        return pltpu.make_async_copy(shards[a], fulls[a].at[h, b], local.at[a])

    def along(a, d):
        return remote(
            shards[a], fulls[a].at[h, b], zs.at[a, d - 1], zr.at[a, d - 1], (h + d) % LINE, b
        )

    def along_arrives(a, d):
        src = (h - d + LINE) % LINE
        return remote(
            shards[a], fulls[a].at[src, b], zs.at[a, d - 1], zr.at[a, d - 1], (h + d) % LINE, b
        )

    def over(a, e):
        part = fulls[a].at[:, b]
        there = ((chip + e) % chips) * CORES + core
        return remote(part, part, cs.at[a, e - 1], cr.at[a, e - 1], h, there)

    def over_arrives(a, e):
        there = ((chip - e + chips) % chips) * CORES + core
        part = fulls[a].at[:, there]
        return remote(part, part, cs.at[a, e - 1], cr.at[a, e - 1], h, there)

    def across(a, e):
        part = fulls[a].at[:, ((chip - e + chips) % chips) * CORES + core]
        return remote(part, part, ss.at[a, e], sr.at[a, e], h, sibling)

    def across_arrives(a, e):
        part = fulls[a].at[:, ((chip - e + chips) % chips) * CORES + 1 - core]
        return remote(part, part, ss.at[a, e], sr.at[a, e], h, sibling)

    def spread(a):
        for d in range(1, LINE):
            along_arrives(a, d).wait_recv()
        own(a).wait()
        for e in range(1, chips):
            over(a, e).start()
        across(a, 0).start()

    def hand_over(a):
        for e in range(1, chips):
            over_arrives(a, e).wait_recv()
            across(a, e).start()

    def up(hh, j, p):
        source = x_ref if j == hh else place(hh, j)
        return remote(
            piece(source, p), piece(place(hh + 1, j), p), us.at[j, p], ur.at[j, p], (h + 1) % LINE, b
        )

    def up_arrives(hh, j, p):
        target = piece(place(hh, j), p)
        return remote(target, target, us.at[j, p], ur.at[j, p], (h + 1) % LINE, b)

    def down(hh, j, p):
        source = x_ref if j == hh else place(hh, j)
        return remote(
            piece(source, p), piece(place(hh - 1, j), p), ds.at[j, p], dr.at[j, p], (h + 3) % LINE, b
        )

    def down_arrives(hh, j, p):
        target = piece(place(hh, j), p)
        return remote(target, target, ds.at[j, p], dr.at[j, p], (h + 3) % LINE, b)

    def sides(hh, j):
        near, far = (3, 2) if hh < 2 else (0, 1)
        if j == near:
            return [(NEAR_SLOT[hh], ns, nr)]
        if j == far and FAR_SLOT[hh] is not None:
            return [(FAR_SLOT[hh], fs, fr)]
        return []

    def side(hh, j, p, slot, send, recv):
        target = (b + 1) % blk if hh < 2 else (b + blk - 1) % blk
        return remote(
            piece(place(hh, j), p), piece(wide.at[slot], p), send.at[p], recv.at[p], h, target
        )

    def sends_side(hh):
        return b < blk - 1 if hh < 2 else b > 0

    def gets_side(hh):
        return b > 0 if hh < 2 else b < blk - 1

    def side_slots(hh):
        found = [(NEAR_SLOT[hh], ns, nr)]
        if FAR_SLOT[hh] is not None:
            found.append((FAR_SLOT[hh], fs, fr))
        return found

    def fill(n, slot):
        return pltpu.make_async_copy(x_ref, wide.at[slot], local.at[count + 1 + n])

    def own_rows():
        return pltpu.make_async_copy(x_ref, wide.at[2], local.at[count])

    def begin(hh):
        for p in range(PIECES):
            if hh < LINE - 1:
                up(hh, hh, p).start()
            if hh > 0:
                down(hh, hh, p).start()

        @pl.when(jnp.logical_not(gets_side(hh)))
        def _():
            for n, (slot, _, _) in enumerate(side_slots(hh)):
                fill(n, slot).start()

    def pass_on(distance, hh):
        for p in range(PIECES):
            for j, arrives, onward, ends in (
                (hh - distance, up_arrives, up, hh == LINE - 1),
                (hh + distance, down_arrives, down, hh == 0),
            ):
                if not 0 <= j < LINE:
                    continue
                arrives(hh, j, p).wait_recv()
                if not ends:
                    onward(hh, j, p).start()
                for slot, send, recv in sides(hh, j):

                    @pl.when(sends_side(hh))
                    def _(slot=slot, send=send, recv=recv):
                        side(hh, j, p, slot, send, recv).start()

    def finish(hh):
        for p in range(PIECES):
            for j in range(LINE):
                if j <= hh < LINE - 1:
                    up(hh, j, p).wait_send()
                if j >= hh > 0:
                    down(hh, j, p).wait_send()

        @pl.when(sends_side(hh))
        def _():
            for j in range(LINE):
                for slot, send, recv in sides(hh, j):
                    for p in range(PIECES):
                        side(hh, j, p, slot, send, recv).wait_send()

        @pl.when(gets_side(hh))
        def _():
            for slot, send, recv in side_slots(hh):
                for p in range(PIECES):
                    target = piece(wide.at[slot], p)
                    remote(target, target, send.at[p], recv.at[p], h, (b + 1) % blk).wait_recv()

        @pl.when(jnp.logical_not(gets_side(hh)))
        def _():
            for n, (slot, _, _) in enumerate(side_slots(hh)):
                fill(n, slot).wait()

    own_rows().start()
    for a in range(count):
        own(a).start()
    greet_plane_and_line(h, b, blk)
    for a in range(count):
        for d in range(1, LINE):
            along(a, d).start()
    at_each_head(h, begin)
    for a in range(count):
        spread(a)
    at_each_head(h, partial(pass_on, 1))
    for a in range(count - 2):
        hand_over(a)
    at_each_head(h, partial(pass_on, 2))
    hand_over(count - 2)
    at_each_head(h, partial(pass_on, 3))
    hand_over(count - 1)
    for a in range(count):
        for d in range(1, LINE):
            along(a, d).wait_send()
        for e in range(1, chips):
            over(a, e).wait_send()
        for e in range(chips):
            across(a, e).wait_send()
            across_arrives(a, e).wait_recv()
    own_rows().wait()
    at_each_head(h, finish)


def gather(tokens, shards, blk):
    rows, width = tokens.shape
    count, chips = len(shards), blk // CORES
    anywhere = pl.BlockSpec(memory_space=pl.ANY)
    dma = pltpu.SemaphoreType.DMA
    outs = pl.pallas_call(
        partial(gather_kernel, blk, count),
        out_shape=[
            jax.ShapeDtypeStruct((5, rows, width), tokens.dtype),
            jax.ShapeDtypeStruct((rows, width), tokens.dtype),
        ]
        + [jax.ShapeDtypeStruct((LINE, blk) + s.shape, s.dtype) for s in shards],
        in_specs=[anywhere] * (1 + count),
        out_specs=[anywhere] * (2 + count),
        scratch_shapes=[dma((count + 3,))]
        + [dma((count, LINE - 1))] * 2
        + [dma((count, chips - 1))] * 2
        + [dma((count, chips))] * 2
        + [dma((LINE, PIECES))] * 4
        + [dma((PIECES,))] * 4,
        compiler_params=pltpu.CompilerParams(collective_id=0, has_side_effects=True),
        name="gather",
    )(tokens, *shards)
    return outs[0], outs[2:]


def pair_kernel(blk, *refs):
    grads, outs, (held, arrived), (load, send, recv) = (
        refs[:3],
        refs[3:7],
        (refs[7:10], refs[10:13]),
        refs[13:],
    )
    h, b = lax.axis_index("head"), lax.axis_index("blk")
    chips = blk // CORES
    chip, core = b // CORES, b % CORES
    sibling = chip * CORES + 1 - core

    def mine(a, e):
        there = ((chip + e) % chips) * CORES + core
        return pltpu.make_async_copy(grads[a].at[:, there], held[a].at[e], load.at[a, e])

    def across(a, e):
        there = ((chip + e) % chips) * CORES + 1 - core
        return remote(
            grads[a].at[:, there], arrived[a].at[e], send.at[a, e], recv.at[a, e], h, sibling
        )

    order = [e % chips for e in range(1, chips + 1)]
    for e in order:
        for a in range(3):
            mine(a, e).start()
    barrier = pltpu.get_barrier_semaphore()
    pl.semaphore_signal(barrier, inc=1, device_id=(h, sibling), device_id_type=MESH)
    pl.semaphore_wait(barrier, 1)
    for e in order:
        for a in range(3):
            across(a, e).start()
    for e in order:
        for a in range(3):
            mine(a, e).wait()
            across(a, e).wait_recv()

        def one(n, carry, e=e):
            attn, inner, outer = (
                held[a][e, n].astype(f32) + arrived[a][e, n].astype(f32) for a in range(3)
            )
            parts = [inner[:, m * 768 : (m + 1) * 768] for m in range(4)]
            spare = jnp.zeros((8, 768), f32)
            outs[e][n, 0:48] = jnp.concatenate([attn, parts[0]], axis=0).astype(bf16)
            outs[e][n, 48:96] = jnp.concatenate(parts[1:3], axis=0).astype(bf16)
            outs[e][n, 96:128] = jnp.concatenate([parts[3], spare], axis=0).astype(bf16)
            outs[e][n, 128:224] = outer.astype(bf16)
            return carry

        lax.fori_loop(0, LINE, one, 0)
    for e in order:
        for a in range(3):
            across(a, e).wait_send()


def pair_sums(grads, blk):
    chips = blk // CORES
    shard = [g.shape[2:] for g in grads]
    dma = pltpu.SemaphoreType.DMA
    inside = pl.BlockSpec(memory_space=pltpu.VMEM)
    return pl.pallas_call(
        partial(pair_kernel, blk),
        out_shape=[jax.ShapeDtypeStruct((LINE, 224, 768), bf16)] * chips,
        in_specs=[pl.BlockSpec(memory_space=pl.ANY)] * 3,
        out_specs=[inside] * chips,
        scratch_shapes=[pltpu.VMEM((chips, LINE) + s, bf16) for s in shard] * 2
        + [dma((3, chips))] * 3,
        compiler_params=pltpu.CompilerParams(
            collective_id=2, has_side_effects=True, vmem_limit_bytes=56 << 20
        ),
        name="pair_sums",
    )(*grads)


def over_plane(sums, blk, head):
    chips = blk // CORES
    received = [sums[0]]
    for e in range(1, chips):
        pairs = [
            (
                h * blk + k * CORES + c,
                h * blk + ((k + e) % chips) * CORES + c,
            )
            for h in range(head)
            for k in range(chips)
            for c in range(CORES)
        ]
        received.append(lax.ppermute(sums[e], ("head", "blk"), pairs))
    return received


def unpacked(packed):
    parts = [packed[n * 24 : (n + 1) * 24] for n in range(1, 5)]
    return packed[:24], jnp.concatenate(parts, axis=1), packed[128:]


def reduce_kernel(blk, count, *refs):
    dx_ref, grads, early = refs[0], refs[1 : 1 + count], refs[1 + count : 1 + count + blk // CORES]
    rest = refs[1 + count + blk // CORES :]
    sum_ref, outs, early_ref = rest[0], rest[1 : 1 + count], rest[1 + count]
    early_sum, early_in, es, er = rest[2 + count : 6 + count]
    rest = rest[6 + count :]
    held, from_core, from_chip, from_line = (rest[n * count : (n + 1) * count] for n in range(4))
    line, arrived, aside = rest[4 * count : 4 * count + 3]
    load, ss, sr, cs, cr, zs, zr, xl, us, ur, ds, dr, ns, nr, fs, fr = rest[4 * count + 3 :]
    h, b = lax.axis_index("head"), lax.axis_index("blk")
    chips = blk // CORES
    chip, core = b // CORES, b % CORES
    sibling = chip * CORES + 1 - core
    rows = dx_ref.shape[1] // PIECES_BACK

    def mine(a, k):
        return pltpu.make_async_copy(grads[a].at[:, k * CORES + core], held[a].at[k], load.at[a, k])

    def across(a, k):
        return remote(
            grads[a].at[:, k * CORES + 1 - core],
            from_core[a].at[k],
            ss.at[a, k],
            sr.at[a, k],
            h,
            sibling,
        )

    def over(a, e):
        k = (chip + e) % chips
        return remote(
            held[a].at[k],
            from_chip[a].at[e - 1],
            cs.at[a, e - 1],
            cr.at[a, e - 1],
            h,
            k * CORES + core,
        )

    def along(a, d):
        there = (h + d) % LINE
        return remote(
            held[a].at[chip, there],
            from_line[a].at[d - 1],
            zs.at[a, d - 1],
            zr.at[a, d - 1],
            there,
            b,
        )

    def add_cores(a, k):
        def one(n, carry):
            held[a][k, n] = (held[a][k, n].astype(f32) + from_core[a][k, n].astype(f32)).astype(
                held[a].dtype
            )
            return carry

        lax.fori_loop(0, LINE, one, 0)

    def to_chips(a):
        for k in range(chips):
            mine(a, k).wait()
            across(a, k).wait_recv()
        for e in range(1, chips):
            add_cores(a, (chip + e) % chips)
            over(a, e).start()
        add_cores(a, chip)

    def to_line(a):
        for e in range(1, chips):
            over(a, e).wait_recv()

        def one(n, carry):
            total = held[a][chip, n].astype(f32)
            for e in range(1, chips):
                total = total + from_chip[a][e - 1, n].astype(f32)
            held[a][chip, n] = total.astype(held[a].dtype)
            return carry

        lax.fori_loop(0, LINE, one, 0)
        for d in range(1, LINE):
            along(a, d).start()

    def to_owner(a):
        for d in range(1, LINE):
            along(a, d).wait_recv()
        total = held[a][chip, h].astype(f32)
        for d in range(1, LINE):
            total = total + from_line[a][d - 1].astype(f32)
        outs[a][...] = total

    def early_along(d):
        there = (h + d) % LINE
        return remote(
            early_sum.at[there], early_in.at[d - 1], es.at[d - 1], er.at[d - 1], there, b
        )

    def early_to_line():
        def one(n, carry):
            total = early[0][n].astype(f32)
            for ref in early[1:]:
                total = total + ref[n].astype(f32)
            early_sum[n] = total.astype(bf16)
            return carry

        lax.fori_loop(0, LINE, one, 0)
        for d in range(1, LINE):
            early_along(d).start()

    def early_to_owner():
        for d in range(1, LINE):
            early_along(d).wait_recv()
        total = early_sum[h].astype(f32)
        for d in range(1, LINE):
            total = total + early_in[d - 1].astype(f32)
        early_ref[...] = total

    def part(p):
        return pl.ds(p * rows, rows)

    def piece(ref, p):
        return ref.at[part(p)]

    def add_rows(target, j, source, n, p):
        def one(step, carry):
            some = pl.ds(p * rows + step * 64, 64)
            target[j, some] = (
                target[j, some].astype(f32) + source[n, some].astype(f32)
            ).astype(target.dtype)
            return carry

        lax.fori_loop(0, rows // 64, one, 0)

    def slot_of(hh, j):
        slot = 2 + j - hh
        return slot if 0 <= slot < 5 else None

    def fetch(hh, j):
        return pltpu.make_async_copy(dx_ref.at[slot_of(hh, j)], line.at[j], xl.at[j])

    def arrival(hh, j, upward):
        return arrived.at[LINE if j == hh and not upward else j]

    def up(hh, j, p):
        return remote(
            piece(line.at[j], p),
            piece(arrival(hh + 1, j, True), p),
            us.at[j, p],
            ur.at[j, p],
            (h + 1) % LINE,
            b,
        )

    def up_arrives(hh, j, p):
        here = piece(arrival(hh, j, True), p)
        return remote(here, here, us.at[j, p], ur.at[j, p], (h + 1) % LINE, b)

    def down(hh, j, p):
        return remote(
            piece(line.at[j], p),
            piece(arrival(hh - 1, j, False), p),
            ds.at[j, p],
            dr.at[j, p],
            (h + 3) % LINE,
            b,
        )

    def down_arrives(hh, j, p):
        here = piece(arrival(hh, j, False), p)
        return remote(here, here, ds.at[j, p], dr.at[j, p], (h + 3) % LINE, b)

    def side_parts(hh):
        near, far = (3, 2) if hh < 2 else (0, 1)
        found = [(NEAR_SLOT[hh], near, 0, ns, nr)]
        if FAR_SLOT[hh] is not None:
            found.append((FAR_SLOT[hh], far, 1, fs, fr))
        return found

    def side(hh, slot, n, send, recv, p):
        target = (b + blk - 1) % blk if hh < 2 else (b + 1) % blk
        return remote(
            piece(dx_ref.at[slot], p), piece(aside.at[n], p), send.at[p], recv.at[p], h, target
        )

    def sends_side(hh):
        return b > 0 if hh < 2 else b < blk - 1

    def gets_side(hh):
        return b < blk - 1 if hh < 2 else b > 0

    def begin(hh):
        @pl.when(sends_side(hh))
        def _():
            for p in range(PIECES_BACK):
                for slot, _, n, send, recv in side_parts(hh):
                    side(hh, slot, n, send, recv, p).start()

        for j in range(LINE):
            if slot_of(hh, j) is not None:
                fetch(hh, j).start()
        for j in range(LINE):
            if slot_of(hh, j) is not None:
                fetch(hh, j).wait()
            else:
                line[j] = jnp.zeros(line.shape[1:], line.dtype)
        for p in range(PIECES_BACK):
            if hh == 0:
                up(hh, 1, p).start()
            if hh == LINE - 1:
                down(hh, 2, p).start()

    def take_sides(hh):
        for p in range(PIECES_BACK):
            for _, j, n, send, recv in side_parts(hh):

                @pl.when(gets_side(hh))
                def _(j=j, n=n, send=send, recv=recv):
                    here = piece(aside.at[n], p)
                    remote(here, here, send.at[p], recv.at[p], h, (b + 1) % blk).wait_recv()
                    add_rows(line, j, aside, n, p)

                if hh == 0:
                    up(hh, j, p).start()
                if hh == LINE - 1:
                    down(hh, j, p).start()

    def pass_on(hh):
        moves = []
        if hh == 1:
            moves = [(3, True), (2, True), (0, False)]
        if hh == 2:
            moves = [(0, False), (1, False), (3, True)]
        for p in range(PIECES_BACK):
            for j, upward in moves:
                (up_arrives if upward else down_arrives)(hh, j, p).wait_recv()
                add_rows(line, j, arrived, j, p)
                (up if upward else down)(hh, j, p).start()

    def finish(hh):
        for p in range(PIECES_BACK):
            sources = []
            if hh > 0:
                up_arrives(hh, hh, p).wait_recv()
                sources.append(hh)
            if hh < LINE - 1:
                down_arrives(hh, hh, p).wait_recv()
                sources.append(LINE)

            def one(step, carry, p=p, sources=tuple(sources)):
                some = pl.ds(p * rows + step * 64, 64)
                total = line[hh, some].astype(f32)
                for n in sources:
                    total = total + arrived[n, some].astype(f32)
                sum_ref[some] = total
                return carry

            lax.fori_loop(0, rows // 64, one, 0)
        for p in range(PIECES_BACK):
            for j in range(LINE):
                if j > hh:
                    up(hh, j, p).wait_send()
                if j < hh:
                    down(hh, j, p).wait_send()

        @pl.when(sends_side(hh))
        def _():
            for p in range(PIECES_BACK):
                for slot, _, n, send, recv in side_parts(hh):
                    side(hh, slot, n, send, recv, p).wait_send()

    for a in range(count):
        for k in range(chips):
            mine(a, k).start()
    greet_plane_and_line(h, b, blk)
    for a in range(count):
        for k in range(chips):
            across(a, k).start()
    at_each_head(h, begin)
    at_each_head(h, take_sides)
    early_to_line()
    for a in range(count):
        to_chips(a)
    at_each_head(h, pass_on)
    for a in range(count):
        to_line(a)
    at_each_head(h, finish)
    early_to_owner()
    for d in range(1, LINE):
        early_along(d).wait_send()
    for a in range(count):
        to_owner(a)
    for a in range(count):
        for k in range(chips):
            across(a, k).wait_send()
        for e in range(1, chips):
            over(a, e).wait_send()
        for d in range(1, LINE):
            along(a, d).wait_send()


def reduce_to_owners(wide_grad, grads, early, blk):
    _, rows, width = wide_grad.shape
    count, chips = len(grads), blk // CORES
    anywhere = pl.BlockSpec(memory_space=pl.ANY)
    inside = pl.BlockSpec(memory_space=pltpu.VMEM)
    dma = pltpu.SemaphoreType.DMA
    shard = [g.shape[2:] for g in grads]
    outs = pl.pallas_call(
        partial(reduce_kernel, blk, count),
        out_shape=[jax.ShapeDtypeStruct((rows, width), f32)]
        + [jax.ShapeDtypeStruct(s, f32) for s in shard]
        + [jax.ShapeDtypeStruct(early[0].shape[1:], f32)],
        in_specs=[anywhere] * (1 + count) + [inside] * chips,
        out_specs=[inside] * (2 + count),
        scratch_shapes=[
            pltpu.VMEM(early[0].shape, bf16),
            pltpu.VMEM((LINE - 1,) + early[0].shape[1:], bf16),
            dma((LINE - 1,)),
            dma((LINE - 1,)),
        ]
        + [pltpu.VMEM((chips, LINE) + s, g.dtype) for s, g in zip(shard, grads)]
        + [pltpu.VMEM((chips, LINE) + s, g.dtype) for s, g in zip(shard, grads)]
        + [pltpu.VMEM((chips - 1, LINE) + s, g.dtype) for s, g in zip(shard, grads)]
        + [pltpu.VMEM((LINE - 1,) + s, g.dtype) for s, g in zip(shard, grads)]
        + [
            pltpu.VMEM((LINE, rows, width), bf16),
            pltpu.VMEM((LINE + 1, rows, width), bf16),
            pltpu.VMEM((2, rows, width), bf16),
        ]
        + [dma((count, chips))] * 3
        + [dma((count, chips - 1))] * 2
        + [dma((count, LINE - 1))] * 2
        + [dma((LINE,))]
        + [dma((LINE, PIECES_BACK))] * 4
        + [dma((PIECES_BACK,))] * 4,
        compiler_params=pltpu.CompilerParams(
            collective_id=1, has_side_effects=True, vmem_limit_bytes=60 << 20
        ),
        name="reduce_to_owners",
    )(wide_grad, *grads, *early)
    return outs[0], outs[1:-1], outs[-1]


def whole(shard):
    return lax.all_gather(shard, ("head", "blk"), axis=0, tiled=True)


def shared_out(grad):
    return lax.psum_scatter(grad.astype(bf16), ("head", "blk"), scatter_dimension=0, tiled=True).astype(f32)


def padded_to(flat, size):
    return jnp.pad(flat, [(0, 0)] * (flat.ndim - 1) + [(0, size - flat.shape[-1])])


def per_device(blk, head, tokens, *rest):
    weights, vectors, (out_grad, segment_ids, random_blocks) = rest[:6], rest[6:15], rest[15:]
    rows = tokens.shape[0]
    by_kernel = head == LINE and blk == LINE * CORES
    short = [vectors[n] for n in (2, 3, 4, 6, 7, 8, 0, 1)]
    if by_kernel:
        packed = jnp.concatenate(
            [
                padded_to(jnp.stack(short), 128),
                padded_to(vectors[5][None], 128),
                jnp.zeros((7, 128), bf16),
            ]
        )
        wide, fulls = gather(tokens, [packed] + list(weights), blk)
        wide = wide.reshape(-1, tokens.shape[1])
        w_query, w_key, w_value, w_attn, w_inner, w_outer = [
            w.reshape(-1, w.shape[-1]) for w in fulls[1:]
        ]
        table = fulls[0].reshape(head * blk, 16, 128)
    else:
        wide = widen(tokens, blk, head)
        w_query, w_key, w_value, w_attn, w_inner, w_outer = [whole(w) for w in weights]
        packed = jnp.concatenate(
            [padded_to(jnp.stack(short), 128), padded_to(vectors[5][None], 128)]
        )
        table = whole(packed[None])
    short_rows = jnp.transpose(table[:, :8, : short[0].shape[0]], (1, 0, 2)).astype(f32)
    short_rows = short_rows.reshape(8, -1)
    bias_inner = table[:, 8, : vectors[5].shape[0]].astype(f32).reshape(-1, 1, PIECE)

    rows_of, bases, docs = tile_plan(segment_ids, random_blocks, rows)
    keys, values, queries = project(wide, w_key, w_value, w_query, short_rows, rows)
    attended, probs = attend(rows_of, queries, keys, values, bases, docs)

    result, grad_first_sum, grad_attended, grad_w_attn, grad_w_inner, grad_w_outer, sums_d, sums_ff = (
        middle(
            attended,
            tokens,
            out_grad,
            w_attn,
            w_inner,
            w_outer,
            short_rows,
            bias_inner,
        )
    )

    early_grads = [grad_w_attn, grad_w_inner, grad_w_outer]
    if by_kernel:
        early = over_plane(
            pair_sums([g.reshape(head, blk, -1, g.shape[-1]) for g in early_grads], blk), blk, head
        )
    grad_scaled, grad_keyed, grad_valued = attend_back(
        rows_of, queries, grad_attended, keys, values, probs
    )
    grad_wide, grad_rows, grad_w_key, grad_w_value, grad_w_query, sums_qv = project_back(
        wide, grad_keyed, grad_valued, grad_scaled, w_key, w_value, w_query, grad_first_sum
    )
    late_grads = [grad_w_query, grad_w_key, grad_w_value]
    sums = jnp.concatenate([sums_d[:6], sums_qv[1:2], sums_qv[0:1]])
    sums = jnp.transpose(sums.reshape(8, head * blk, -1), (1, 0, 2))
    packed = jnp.concatenate(
        [
            padded_to(sums, 128),
            padded_to(sums_ff.reshape(head * blk, 1, -1), 128),
            jnp.zeros((head * blk, 7, 128), f32),
        ],
        axis=1,
    )
    if by_kernel:
        shares = [g.reshape(head, blk, -1, g.shape[-1]) for g in late_grads]
        small = packed.reshape(head, blk, 16, 128)
        wide_sum, late, early_sum = reduce_to_owners(
            grad_wide.reshape(-1, rows, grad_wide.shape[-1]), [small] + shares, early, blk
        )
        matrix_grads = tuple(late[1:]) + unpacked(early_sum)
        packed = late[0]
    else:
        wide_sum = narrow(grad_wide, rows, blk, head).astype(f32)
        matrix_grads = tuple(shared_out(g) for g in late_grads + early_grads)
        packed = lax.psum_scatter(packed, ("head", "blk"), scatter_dimension=0, tiled=True)[0]
    order = (6, 7, 0, 1, 2, 8, 3, 4, 5)
    vector_grads = tuple(packed[n, : v.shape[0]] for n, v in zip(order, vectors))
    return (result, grad_rows + wide_sum) + matrix_grads + vector_grads


def solution(mesh):
    row = P(("blk", "head"), None)
    matrix = P(("head", "blk"), None)
    vector = P(("head", "blk"))
    return jax.shard_map(
        partial(per_device, mesh.shape["blk"], mesh.shape["head"]),
        mesh=mesh,
        in_specs=(row,) + (matrix,) * 6 + (vector,) * 9 + (row, P(), P()),
        out_specs=(row, row) + (matrix,) * 6 + (vector,) * 9,
        check_vma=False,
    )
```

```python
from functools import partial

import jax
import jax.numpy as jnp
from jax import lax
from jax.experimental import pallas as pl
from jax.experimental.pallas import tpu as pltpu
from jax.sharding import PartitionSpec as P

HEAD_DIM = 64
BLOCK = 64
RANDOM = 3
TILES = 5 + RANDOM
REACH = 2
GROUP = 4
FORWARD_BLOCKS = 4
BACKWARD_BLOCKS = 4
ROWS = 256
PIECE = 768

epsilon = 1e-06
masked_value = -1e30
query_scale = 0.125
gelu_scale = 0.7978845608028654
gelu_cubic = 0.044715
far_away = -(1 << 24)
f32, bf16 = jnp.float32, jnp.bfloat16


def mm(a, b):
    return jnp.dot(a, b, preferred_element_type=f32)


def mm_nt(a, b):
    return lax.dot_general(a, b, (((1,), (1,)), ((), ())), preferred_element_type=f32)


def mm_tn(a, b):
    return lax.dot_general(a, b, (((0,), (0,)), ((), ())), preferred_element_type=f32)


def head_mask(rows, cols, first):
    lanes = lax.broadcasted_iota(jnp.int32, (rows, cols), 1)
    return (lanes >= first) & (lanes < first + HEAD_DIM)


def stacked_by_head(tile):
    rows, cols = tile.shape
    return jnp.concatenate(
        [
            jnp.where(head_mask(rows, cols, h * HEAD_DIM), tile, jnp.zeros_like(tile))
            for h in range(cols // HEAD_DIM)
        ],
        axis=0,
    )


def own_head_columns(stacked):
    cols = stacked.shape[1]
    total = None
    for h in range(cols // HEAD_DIM):
        part = stacked[h * BLOCK : (h + 1) * BLOCK]
        part = jnp.where(head_mask(BLOCK, cols, h * HEAD_DIM), part, 0.0)
        total = part if total is None else total + part
    return total


def block_rows(row):
    return pl.ds(pl.multiple_of(row * BLOCK, BLOCK), BLOCK)


def gathered(table_ref, fixed_row, random_row):
    tiles = [table_ref[block_rows(fixed_row(t)), :] for t in range(5)]
    low = head_mask(BLOCK, 2 * HEAD_DIM, 0)
    for t in range(RANDOM):
        halves = []
        for pair in range(GROUP // 2):
            cols = pl.ds(pair * 2 * HEAD_DIM, 2 * HEAD_DIM)
            a = table_ref[block_rows(random_row(2 * pair, t)), cols]
            b = table_ref[block_rows(random_row(2 * pair + 1, t)), cols]
            halves.append(jnp.where(low, a, b))
        tiles.append(jnp.concatenate(halves, axis=1))
    return jnp.concatenate(tiles, axis=0)


def row_readers(rows_ref, blocks, i):
    group = pl.program_id(0)

    def fixed_row(t):
        return rows_ref[(group * GROUP * blocks + i) * TILES + t]

    def random_row(h, t):
        return rows_ref[((group * GROUP + h) * blocks + i) * TILES + 5 + t]

    return fixed_row, random_row


def attend_kernel(blocks, rows_ref, q_ref, k_ref, v_ref, base_ref, doc_ref, out_ref, p_ref):
    within = lax.broadcasted_iota(jnp.int32, (BLOCK, GROUP * BLOCK), 0)
    for u in range(FORWARD_BLOCKS):
        here = pl.ds(u * BLOCK, BLOCK)
        readers = row_readers(rows_ref, blocks, pl.program_id(1) * FORWARD_BLOCKS + u)
        keys = gathered(k_ref, *readers)
        values = gathered(v_ref, *readers)
        scores = mm_nt(keys, stacked_by_head(q_ref[here, :]))
        lo = doc_ref[u, 0:1, :]
        hi = doc_ref[u, 1:2, :]
        masked = []
        for t in range(TILES):
            place = within + base_ref[0, u, t : t + 1, :]
            allowed = (place >= lo) & (place < hi)
            masked.append(jnp.where(allowed, scores[t * BLOCK : (t + 1) * BLOCK], masked_value))
        scores = jnp.concatenate(masked, axis=0)
        raised = jnp.exp(scores - jnp.max(scores, axis=0, keepdims=True))
        probs = (raised * (1.0 / jnp.sum(raised, axis=0, keepdims=True))).astype(bf16)
        p_ref[0, u] = probs
        out_ref[here, :] = own_head_columns(mm_tn(probs, values)).astype(bf16)


def attend_back_kernel(
    blocks,
    rows_ref,
    q_ref,
    g_ref,
    k_ref,
    v_ref,
    p_ref,
    dq_ref,
    dk_ref,
    dv_ref,
    dk_sum,
    dv_sum,
):
    step = pl.program_id(1)

    @pl.when(step == 0)
    def _():
        dk_sum[...] = jnp.zeros_like(dk_sum)
        dv_sum[...] = jnp.zeros_like(dv_sum)

    found = []
    for u in range(BACKWARD_BLOCKS):
        here = pl.ds(u * BLOCK, BLOCK)
        readers = row_readers(rows_ref, blocks, step * BACKWARD_BLOCKS + u)
        keys = gathered(k_ref, *readers)
        values = gathered(v_ref, *readers)
        queries = stacked_by_head(q_ref[here, :])
        grads = stacked_by_head(g_ref[here, :])
        probs = p_ref[0, u]
        grad_probs = mm_nt(values, grads)
        wide = probs.astype(f32)
        balance = jnp.sum(wide * grad_probs, axis=0, keepdims=True)
        grad_scores = (wide * (grad_probs - balance)).astype(bf16)
        dq_ref[here, :] = (query_scale * own_head_columns(mm_tn(grad_scores, keys))).astype(bf16)
        found.append((readers, mm(grad_scores, queries), mm(probs, grads)))
    for (fixed_row, random_row), grad_keys, grad_values in found:
        for total, part in ((dk_sum, grad_keys), (dv_sum, grad_values)):
            for t in range(5):
                total[block_rows(fixed_row(t)), :] += part[t * BLOCK : (t + 1) * BLOCK]
            for t in range(RANDOM):
                rows = part[(5 + t) * BLOCK : (6 + t) * BLOCK]
                for h in range(GROUP):
                    first = (h // 2) * 2 * HEAD_DIM
                    mine = head_mask(BLOCK, 2 * HEAD_DIM, (h % 2) * HEAD_DIM)
                    total[block_rows(random_row(h, t)), pl.ds(first, 2 * HEAD_DIM)] += jnp.where(
                        mine, rows[:, first : first + 2 * HEAD_DIM], 0.0
                    )

    @pl.when(step == blocks // BACKWARD_BLOCKS - 1)
    def _():
        dk_ref[...] = dk_sum[...].astype(bf16)
        dv_ref[...] = dv_sum[...].astype(bf16)


def attend(rows, queries, keys, values, bases, docs):
    tokens, width = queries.shape
    ext = keys.shape[0]
    blocks, cols, some = tokens // BLOCK, GROUP * HEAD_DIM, FORWARD_BLOCKS
    groups = width // cols
    tile = pl.BlockSpec((some * BLOCK, cols), lambda g, i, r: (i, g))
    table = pl.BlockSpec((ext, cols), lambda g, i, r: (0, g))
    return pl.pallas_call(
        partial(attend_kernel, blocks),
        grid_spec=pltpu.PrefetchScalarGridSpec(
            num_scalar_prefetch=1,
            grid=(groups, blocks // some),
            in_specs=[
                tile,
                table,
                table,
                pl.BlockSpec((1, some, TILES, cols), lambda g, i, r: (g, i, 0, 0)),
                pl.BlockSpec((some, 8, cols), lambda g, i, r: (i, 0, 0)),
            ],
            out_specs=[
                tile,
                pl.BlockSpec((1, some, TILES * BLOCK, cols), lambda g, i, r: (g, i, 0, 0)),
            ],
        ),
        out_shape=[
            jax.ShapeDtypeStruct((tokens, width), bf16),
            jax.ShapeDtypeStruct((groups, blocks, TILES * BLOCK, cols), bf16),
        ],
        compiler_params=pltpu.CompilerParams(vmem_limit_bytes=40 << 20),
        name="attend",
    )(rows, queries, keys, values, bases, docs)


def attend_back(rows, queries, grads, keys, values, probs):
    tokens, width = queries.shape
    ext = keys.shape[0]
    blocks, cols, some = tokens // BLOCK, GROUP * HEAD_DIM, BACKWARD_BLOCKS
    groups = width // cols
    tile = pl.BlockSpec((some * BLOCK, cols), lambda g, i, r: (i, g))
    table = pl.BlockSpec((ext, cols), lambda g, i, r: (0, g))
    return pl.pallas_call(
        partial(attend_back_kernel, blocks),
        grid_spec=pltpu.PrefetchScalarGridSpec(
            num_scalar_prefetch=1,
            grid=(groups, blocks // some),
            in_specs=[
                tile,
                tile,
                table,
                table,
                pl.BlockSpec((1, some, TILES * BLOCK, cols), lambda g, i, r: (g, i, 0, 0)),
            ],
            out_specs=[tile, table, table],
            scratch_shapes=[pltpu.VMEM((ext, cols), f32), pltpu.VMEM((ext, cols), f32)],
        ),
        out_shape=[
            jax.ShapeDtypeStruct((tokens, width), bf16),
            jax.ShapeDtypeStruct((ext, width), bf16),
            jax.ShapeDtypeStruct((ext, width), bf16),
        ],
        compiler_params=pltpu.CompilerParams(vmem_limit_bytes=56 << 20),
        cost_estimate=pl.CostEstimate(
            flops=10 * groups * blocks * TILES * BLOCK * cols * cols,
            bytes_accessed=100 << 20,
            transcendentals=0,
        ),
        name="attend_back",
    )(rows, queries, grads, keys, values, probs)


def normalized(values):
    centred = values - jnp.mean(values, axis=-1, keepdims=True)
    root = lax.rsqrt(jnp.mean(centred * centred, axis=-1, keepdims=True) + epsilon)
    return centred * root, root


def norm_back(grad, normal, root, gain):
    scaled = grad * gain
    along = jnp.mean(scaled * normal, axis=-1, keepdims=True)
    return root * (scaled - jnp.mean(scaled, axis=-1, keepdims=True) - normal * along)


def gelu_and_slope(u):
    square = u * u
    bend = jnp.tanh(gelu_scale * (u + gelu_cubic * (square * u)))
    half = 0.5 * (1.0 + bend)
    slope = half + (0.5 * gelu_scale) * u * (1.0 - bend * bend) * (
        1.0 + (3.0 * gelu_cubic) * square
    )
    return u * half, slope


def middle_kernel(
    att_ref,
    x_ref,
    og_ref,
    wa_ref,
    wi_ref,
    wo_ref,
    vec_ref,
    bi_ref,
    res_ref,
    sum_ref,
    ga_ref,
    dwa_ref,
    dwi_ref,
    dwo_ref,
    dvec_ref,
    dbi_ref,
    normal,
    root,
    low,
    act,
    slope,
    inner,
):
    step, half = pl.program_id(0), pl.num_programs(0) // 2
    tokens, width = x_ref.shape
    slices = [pl.ds(t * ROWS, ROWS) for t in range(tokens // ROWS)]
    bias_attn, gain_one, offset_one, bias_outer, gain_two, offset_two = (
        vec_ref[n : n + 1, :] for n in range(6)
    )

    def row_sum(total, values):
        part = jnp.sum(values, axis=0, keepdims=True)
        return part if total is None else total + part

    @pl.when(step == 0)
    def _():
        for s in slices:
            values = x_ref[s, :].astype(f32) + mm(att_ref[s, :], wa_ref[...]) + bias_attn
            flat, scale = normalized(values)
            normal[s, :] = flat
            root[s, :] = jnp.broadcast_to(scale, (ROWS, 128))
            first = flat * gain_one + offset_one
            low[s, :] = first.astype(bf16)
            sum_ref[s, :] = first + bias_outer

    @pl.when(step < half)
    def _():
        for s in slices:
            active, bend = gelu_and_slope(mm(low[s, :], wi_ref[...]) + bi_ref[0])
            active = active.astype(bf16)
            act[step, s, :] = active
            slope[step, s, :] = bend.astype(bf16)
            sum_ref[s, :] += mm(active, wo_ref[...])

    @pl.when(step == half)
    def _():
        outer_sum, gain_sum, offset_sum = None, None, None
        for s in slices:
            flat, scale = normalized(sum_ref[s, :])
            res_ref[s, :] = (flat * gain_two + offset_two).astype(bf16)
            grad = og_ref[s, :].astype(f32)
            gain_sum = row_sum(gain_sum, grad * flat)
            offset_sum = row_sum(offset_sum, grad)
            second = norm_back(grad, flat, scale, gain_two)
            sum_ref[s, :] = second
            second = second.astype(bf16)
            ga_ref[s, :] = second
            outer_sum = row_sum(outer_sum, second.astype(f32))
        dvec_ref[3:4, :] = outer_sum
        dvec_ref[4:5, :] = gain_sum
        dvec_ref[5:6, :] = offset_sum
        dvec_ref[6:8, :] = jnp.zeros((2, width), f32)

    @pl.when(step >= half)
    def _():
        now = step - half
        total = None
        for s in slices:
            grad = mm_nt(ga_ref[s, :], wo_ref[...]) * slope[now, s, :].astype(f32)
            grad = grad.astype(bf16)
            inner[s, :] = grad
            total = row_sum(total, grad.astype(f32))
            sum_ref[s, :] += mm_nt(grad, wi_ref[...])
        dbi_ref[0] = total
        for n in range(width // 256):
            some = pl.ds(n * 256, 256)
            dwi_ref[some, :] = mm_tn(low[:, some], inner[...]).astype(bf16)
        for n in range(PIECE // 256):
            some = pl.ds(n * 256, 256)
            dwo_ref[some, :] = mm_tn(act[now, :, some], ga_ref[...]).astype(bf16)

    @pl.when(step == 2 * half - 1)
    def _():
        attn_sum, gain_sum, offset_sum = None, None, None
        for s in slices:
            grad, flat = sum_ref[s, :], normal[s, :]
            gain_sum = row_sum(gain_sum, grad * flat)
            offset_sum = row_sum(offset_sum, grad)
            grad = norm_back(grad, flat, root[s, 0:1], gain_one)
            sum_ref[s, :] = grad
            grad = grad.astype(bf16)
            inner[s, :width] = grad
            attn_sum = row_sum(attn_sum, grad.astype(f32))
            ga_ref[s, :] = mm_nt(grad, wa_ref[...]).astype(bf16)
        dvec_ref[0:1, :] = attn_sum
        dvec_ref[1:2, :] = gain_sum
        dvec_ref[2:3, :] = offset_sum
        for n in range(width // 256):
            some = pl.ds(n * 256, 256)
            dwa_ref[some, :] = mm_tn(att_ref[:, some], inner[:, :width]).astype(bf16)


def middle(attended, tokens, out_grad, w_attn, w_inner, w_outer, vectors, bias_inner):
    rows, width = tokens.shape
    steps = w_inner.shape[1] // PIECE
    one = pl.Buffered(1)
    still = pl.BlockSpec((rows, width), lambda i: (0, 0), pipeline_mode=one)
    square = pl.BlockSpec((width, width), lambda i: (0, 0), pipeline_mode=one)
    few = pl.BlockSpec((8, width), lambda i: (0, 0))
    later = lambda i: jnp.maximum(i - steps, 0)
    return pl.pallas_call(
        middle_kernel,
        grid=(2 * steps,),
        in_specs=[
            still,
            still,
            still,
            square,
            pl.BlockSpec((width, PIECE), lambda i: (0, i % steps)),
            pl.BlockSpec((PIECE, width), lambda i: (i % steps, 0)),
            few,
            pl.BlockSpec((1, 1, PIECE), lambda i: (i % steps, 0, 0)),
        ],
        out_specs=[
            still,
            still,
            still,
            square,
            pl.BlockSpec((width, PIECE), lambda i: (0, later(i))),
            pl.BlockSpec((PIECE, width), lambda i: (later(i), 0)),
            few,
            pl.BlockSpec((1, 1, PIECE), lambda i: (later(i), 0, 0)),
        ],
        out_shape=[
            jax.ShapeDtypeStruct((rows, width), bf16),
            jax.ShapeDtypeStruct((rows, width), f32),
            jax.ShapeDtypeStruct((rows, width), bf16),
            jax.ShapeDtypeStruct(w_attn.shape, bf16),
            jax.ShapeDtypeStruct(w_inner.shape, bf16),
            jax.ShapeDtypeStruct(w_outer.shape, bf16),
            jax.ShapeDtypeStruct((8, width), f32),
            jax.ShapeDtypeStruct((steps, 1, PIECE), f32),
        ],
        scratch_shapes=[
            pltpu.VMEM((rows, width), f32),
            pltpu.VMEM((rows, 128), f32),
            pltpu.VMEM((rows, width), bf16),
            pltpu.VMEM((steps, rows, PIECE), bf16),
            pltpu.VMEM((steps, rows, PIECE), bf16),
            pltpu.VMEM((rows, PIECE), bf16),
        ],
        compiler_params=pltpu.CompilerParams(vmem_limit_bytes=60 << 20),
        name="middle",
    )(attended, tokens, out_grad, w_attn, w_inner, w_outer, vectors, bias_inner)


def project_kernel(wide_ref, wk_ref, wv_ref, wq_ref, vec_ref, k_ref, v_ref, q_ref):
    rows = wide_ref.shape[0]
    slices = [pl.ds(t * ROWS, ROWS) for t in range(rows // ROWS)]
    for s in slices:
        k_ref[s, :] = mm(wide_ref[s, :], wk_ref[...]).astype(bf16)
        v_ref[s, :] = (mm(wide_ref[s, :], wv_ref[...]) + vec_ref[7:8, :]).astype(bf16)

    @pl.when(pl.program_id(0) == REACH)
    def _():
        for s in slices:
            queries = mm(wide_ref[s, :], wq_ref[...]) + vec_ref[6:7, :]
            q_ref[s, :] = (query_scale * queries).astype(bf16)


def project(wide, w_key, w_value, w_query, vectors, rows):
    width = wide.shape[1]
    one = pl.Buffered(1)
    tile = pl.BlockSpec((rows, width), lambda i: (i, 0))
    still = pl.BlockSpec((rows, width), lambda i: (0, 0), pipeline_mode=one)
    square = pl.BlockSpec((width, width), lambda i: (0, 0), pipeline_mode=one)
    table = jax.ShapeDtypeStruct(wide.shape, bf16)
    return pl.pallas_call(
        project_kernel,
        grid=(1 + 2 * REACH,),
        in_specs=[tile, square, square, square, pl.BlockSpec((8, width), lambda i: (0, 0))],
        out_specs=[tile, tile, still],
        out_shape=[table, table, jax.ShapeDtypeStruct((rows, width), bf16)],
        compiler_params=pltpu.CompilerParams(vmem_limit_bytes=40 << 20),
        name="project",
    )(wide, w_key, w_value, w_query, vectors)


def tokens_back_kernel(
    dk_ref, dv_ref, dq_ref, wk_ref, wv_ref, wq_ref, first_ref, dx_ref, rows_ref, sums_ref
):
    step = pl.program_id(0)
    rows = dx_ref.shape[0]
    slices = [pl.ds(t * ROWS, ROWS) for t in range(rows // ROWS)]

    def summed(ref):
        return jnp.sum(ref[...].astype(f32), axis=0, keepdims=True)

    @pl.when(step == 0)
    def _():
        sums_ref[...] = jnp.zeros_like(sums_ref)

    for s in slices:
        dx_ref[s, :] = (
            mm_nt(dk_ref[s, :], wk_ref[...]) + mm_nt(dv_ref[s, :], wv_ref[...])
        ).astype(bf16)
    sums_ref[7:8, :] += summed(dv_ref)

    @pl.when(step == REACH)
    def _():
        for s in slices:
            rows_ref[s, :] = first_ref[s, :] + mm_nt(dq_ref[s, :], wq_ref[...])
        sums_ref[6:7, :] = summed(dq_ref)


def tokens_back(grad_keyed, grad_valued, grad_scaled, w_key, w_value, w_query, grad_first):
    rows, width = grad_scaled.shape
    one = pl.Buffered(1)
    tile = pl.BlockSpec((rows, width), lambda i: (i, 0))
    still = pl.BlockSpec((rows, width), lambda i: (0, 0), pipeline_mode=one)
    square = pl.BlockSpec((width, width), lambda i: (0, 0), pipeline_mode=one)
    few = pl.BlockSpec((8, width), lambda i: (0, 0))
    return pl.pallas_call(
        tokens_back_kernel,
        grid=(1 + 2 * REACH,),
        in_specs=[tile, tile, still, square, square, square, still],
        out_specs=[tile, still, few],
        out_shape=[
            jax.ShapeDtypeStruct(grad_keyed.shape, bf16),
            jax.ShapeDtypeStruct((rows, width), f32),
            jax.ShapeDtypeStruct((8, width), f32),
        ],
        compiler_params=pltpu.CompilerParams(vmem_limit_bytes=40 << 20),
        cost_estimate=pl.CostEstimate(
            flops=4 * grad_keyed.shape[0] * width * width,
            bytes_accessed=30 << 20,
            transcendentals=0,
        ),
        name="tokens_back",
    )(grad_keyed, grad_valued, grad_scaled, w_key, w_value, w_query, grad_first)


def tile_plan(segment_ids, random_blocks, tokens):
    heads, total_blocks, _ = random_blocks.shape
    blocks = tokens // BLOCK
    chunk = lax.axis_index("blk") * lax.axis_size("head") + lax.axis_index("head")
    margin = REACH * tokens
    padded = jnp.concatenate(
        [
            jnp.full((margin,), -1, jnp.int32),
            segment_ids,
            jnp.full((margin,), jnp.iinfo(jnp.int32).max, jnp.int32),
        ]
    )
    near = lax.dynamic_slice_in_dim(padded, chunk * tokens, tokens + 2 * margin)
    own = near[margin : margin + tokens]
    before, after = near[: margin + tokens], near[margin:]
    begins = jnp.sum((before[None, :] < own[:, None]).astype(jnp.int32), axis=1)
    ends = margin + jnp.sum((after[None, :] <= own[:, None]).astype(jnp.int32), axis=1)
    docs = jnp.stack([begins, ends]).reshape(2, blocks, BLOCK)
    docs = jnp.tile(jnp.transpose(docs, (1, 0, 2)), (1, 4, GROUP))
    first = begins[::BLOCK] // BLOCK
    here = REACH * blocks + jnp.arange(blocks, dtype=jnp.int32)
    fixed = jnp.stack([here - 1, here, here + 1, first, first + 1], axis=-1)
    picked = lax.dynamic_slice_in_dim(random_blocks, chunk * blocks, blocks, axis=1)
    picked = picked - (chunk - REACH) * blocks
    rows = jnp.concatenate(
        [jnp.broadcast_to(fixed[None], (heads, blocks, 5)), picked], axis=-1
    )
    earlier = jnp.arange(TILES)[None, :] < jnp.arange(TILES)[:, None]
    repeat = jnp.any((rows[..., :, None] == rows[..., None, :]) & earlier, axis=-1)
    bases = jnp.where(repeat, far_away, rows * BLOCK)
    rows = jnp.clip(rows, 0, (1 + 2 * REACH) * blocks - 1)
    bases = bases.reshape(heads // GROUP, GROUP, blocks, TILES)
    bases = jnp.repeat(jnp.transpose(bases, (0, 2, 3, 1)), BLOCK, axis=-1)
    return rows.reshape(-1), bases, docs


def side_pairs(blk, head, far):
    pairs = []
    for b in range(blk):
        for h in range(head):
            down = h < head // 2
            if far and h not in (0, head - 1):
                continue
            source = b - 1 if down else b + 1
            if 0 <= source < blk:
                pairs.append((h * blk + source, h * blk + b))
    return pairs


def widen(tokens_rows, blk, head):
    rows = tokens_rows.shape[0]
    h = lax.axis_index("head")
    line = lax.all_gather(tokens_rows, "head", axis=0, tiled=True)
    low = h < head // 2
    near = lax.dynamic_slice_in_dim(line, jnp.where(low, head - 1, 0) * rows, rows)
    far = lax.dynamic_slice_in_dim(line, jnp.where(low, head - 2, 1) * rows, rows)
    near = lax.ppermute(near, ("head", "blk"), side_pairs(blk, head, False))
    far = lax.ppermute(far, ("head", "blk"), side_pairs(blk, head, True))
    whole = jnp.concatenate([far, near, line, near, far], axis=0)
    return lax.dynamic_slice_in_dim(whole, h * rows, (1 + 2 * REACH) * rows)


def narrow(wide_rows, rows, blk, head):
    h = lax.axis_index("head")
    low = h < head // 2
    frame = jnp.zeros(((head + 2 * REACH) * rows, wide_rows.shape[1]), wide_rows.dtype)
    frame = lax.dynamic_update_slice_in_dim(frame, wide_rows, h * rows, 0)
    near = lax.dynamic_slice_in_dim(frame, jnp.where(low, 1, head + REACH) * rows, rows)
    far = lax.dynamic_slice_in_dim(frame, jnp.where(low, 0, head + REACH + 1) * rows, rows)
    back = [(t, s) for s, t in side_pairs(blk, head, False)]
    near = lax.ppermute(near, ("head", "blk"), back)
    back = [(t, s) for s, t in side_pairs(blk, head, True)]
    far = lax.ppermute(far, ("head", "blk"), back)
    line = frame[REACH * rows : (REACH + head) * rows].reshape(head, rows, -1)
    place = jnp.arange(head, dtype=jnp.int32)[:, None, None]
    line = line + jnp.where(place == jnp.where(low, head - 1, 0), near[None], 0)
    line = line + jnp.where(place == jnp.where(low, head - 2, 1), far[None], 0)
    return lax.psum_scatter(line.reshape(head * rows, -1), "head", scatter_dimension=0, tiled=True)


LINE = 4
CORES = 2
PIECES = 4
PIECES_BACK = 8
MESH = pl.DeviceIdType.MESH
NEAR_SLOT = (1, 0, 4, 3)
FAR_SLOT = (0, None, None, 4)


def remote(source, target, send, recv, head, blk):
    return pltpu.make_async_remote_copy(
        src_ref=source,
        dst_ref=target,
        send_sem=send,
        recv_sem=recv,
        device_id=(head, blk),
        device_id_type=MESH,
    )


def at_each_head(h, body):
    for hh in range(LINE):
        pl.when(h == hh)(partial(body, hh))


def greet_plane_and_line(h, b, blk):
    barrier = pltpu.get_barrier_semaphore()
    for d in range(1, LINE):
        pl.semaphore_signal(
            barrier, inc=1, device_id=((h + d) % LINE, b), device_id_type=MESH
        )
    for d in range(1, blk):
        pl.semaphore_signal(barrier, inc=1, device_id=(h, (b + d) % blk), device_id_type=MESH)
    pl.semaphore_wait(barrier, LINE - 1 + blk - 1)


def gather_kernel(blk, count, *refs):
    x_ref, shards = refs[0], refs[1 : 1 + count]
    wide, spill, fulls = refs[1 + count], refs[2 + count], refs[3 + count : 3 + 2 * count]
    local, zs, zr, cs, cr, ss, sr, us, ur, ds, dr, ns, nr, fs, fr = refs[3 + 2 * count :]
    h, b = lax.axis_index("head"), lax.axis_index("blk")
    chips = blk // CORES
    chip, core = b // CORES, b % CORES
    sibling = chip * CORES + 1 - core
    rows = x_ref.shape[0] // PIECES

    def piece(ref, p):
        return ref.at[pl.ds(p * rows, rows)]

    def place(hh, j):
        slot = 2 + j - hh
        return wide.at[slot] if 0 <= slot < 5 else spill

    def own(a):
        return pltpu.make_async_copy(shards[a], fulls[a].at[h, b], local.at[a])

    def along(a, d):
        return remote(
            shards[a], fulls[a].at[h, b], zs.at[a, d - 1], zr.at[a, d - 1], (h + d) % LINE, b
        )

    def along_arrives(a, d):
        src = (h - d + LINE) % LINE
        return remote(
            shards[a], fulls[a].at[src, b], zs.at[a, d - 1], zr.at[a, d - 1], (h + d) % LINE, b
        )

    def over(a, e):
        part = fulls[a].at[:, b]
        there = ((chip + e) % chips) * CORES + core
        return remote(part, part, cs.at[a, e - 1], cr.at[a, e - 1], h, there)

    def over_arrives(a, e):
        there = ((chip - e + chips) % chips) * CORES + core
        part = fulls[a].at[:, there]
        return remote(part, part, cs.at[a, e - 1], cr.at[a, e - 1], h, there)

    def across(a, e):
        part = fulls[a].at[:, ((chip - e + chips) % chips) * CORES + core]
        return remote(part, part, ss.at[a, e], sr.at[a, e], h, sibling)

    def across_arrives(a, e):
        part = fulls[a].at[:, ((chip - e + chips) % chips) * CORES + 1 - core]
        return remote(part, part, ss.at[a, e], sr.at[a, e], h, sibling)

    def spread(a):
        for d in range(1, LINE):
            along_arrives(a, d).wait_recv()
        own(a).wait()
        for e in range(1, chips):
            over(a, e).start()
        across(a, 0).start()

    def hand_over(a):
        for e in range(1, chips):
            over_arrives(a, e).wait_recv()
            across(a, e).start()

    def up(hh, j, p):
        source = x_ref if j == hh else place(hh, j)
        return remote(
            piece(source, p), piece(place(hh + 1, j), p), us.at[j, p], ur.at[j, p], (h + 1) % LINE, b
        )

    def up_arrives(hh, j, p):
        target = piece(place(hh, j), p)
        return remote(target, target, us.at[j, p], ur.at[j, p], (h + 1) % LINE, b)

    def down(hh, j, p):
        source = x_ref if j == hh else place(hh, j)
        return remote(
            piece(source, p), piece(place(hh - 1, j), p), ds.at[j, p], dr.at[j, p], (h + 3) % LINE, b
        )

    def down_arrives(hh, j, p):
        target = piece(place(hh, j), p)
        return remote(target, target, ds.at[j, p], dr.at[j, p], (h + 3) % LINE, b)

    def sides(hh, j):
        near, far = (3, 2) if hh < 2 else (0, 1)
        if j == near:
            return [(NEAR_SLOT[hh], ns, nr)]
        if j == far and FAR_SLOT[hh] is not None:
            return [(FAR_SLOT[hh], fs, fr)]
        return []

    def side(hh, j, p, slot, send, recv):
        target = (b + 1) % blk if hh < 2 else (b + blk - 1) % blk
        return remote(
            piece(place(hh, j), p), piece(wide.at[slot], p), send.at[p], recv.at[p], h, target
        )

    def sends_side(hh):
        return b < blk - 1 if hh < 2 else b > 0

    def gets_side(hh):
        return b > 0 if hh < 2 else b < blk - 1

    def side_slots(hh):
        found = [(NEAR_SLOT[hh], ns, nr)]
        if FAR_SLOT[hh] is not None:
            found.append((FAR_SLOT[hh], fs, fr))
        return found

    def fill(n, slot):
        return pltpu.make_async_copy(x_ref, wide.at[slot], local.at[count + 1 + n])

    def own_rows():
        return pltpu.make_async_copy(x_ref, wide.at[2], local.at[count])

    def begin(hh):
        for p in range(PIECES):
            if hh < LINE - 1:
                up(hh, hh, p).start()
            if hh > 0:
                down(hh, hh, p).start()

        @pl.when(jnp.logical_not(gets_side(hh)))
        def _():
            for n, (slot, _, _) in enumerate(side_slots(hh)):
                fill(n, slot).start()

    def pass_on(distance, hh):
        for p in range(PIECES):
            for j, arrives, onward, ends in (
                (hh - distance, up_arrives, up, hh == LINE - 1),
                (hh + distance, down_arrives, down, hh == 0),
            ):
                if not 0 <= j < LINE:
                    continue
                arrives(hh, j, p).wait_recv()
                if not ends:
                    onward(hh, j, p).start()
                for slot, send, recv in sides(hh, j):

                    @pl.when(sends_side(hh))
                    def _(slot=slot, send=send, recv=recv):
                        side(hh, j, p, slot, send, recv).start()

    def finish(hh):
        for p in range(PIECES):
            for j in range(LINE):
                if j <= hh < LINE - 1:
                    up(hh, j, p).wait_send()
                if j >= hh > 0:
                    down(hh, j, p).wait_send()

        @pl.when(sends_side(hh))
        def _():
            for j in range(LINE):
                for slot, send, recv in sides(hh, j):
                    for p in range(PIECES):
                        side(hh, j, p, slot, send, recv).wait_send()

        @pl.when(gets_side(hh))
        def _():
            for slot, send, recv in side_slots(hh):
                for p in range(PIECES):
                    target = piece(wide.at[slot], p)
                    remote(target, target, send.at[p], recv.at[p], h, (b + 1) % blk).wait_recv()

        @pl.when(jnp.logical_not(gets_side(hh)))
        def _():
            for n, (slot, _, _) in enumerate(side_slots(hh)):
                fill(n, slot).wait()

    own_rows().start()
    for a in range(count):
        own(a).start()
    greet_plane_and_line(h, b, blk)
    for a in range(count):
        for d in range(1, LINE):
            along(a, d).start()
    at_each_head(h, begin)
    for a in range(count):
        spread(a)
    at_each_head(h, partial(pass_on, 1))
    for a in range(count - 2):
        hand_over(a)
    at_each_head(h, partial(pass_on, 2))
    hand_over(count - 2)
    at_each_head(h, partial(pass_on, 3))
    hand_over(count - 1)
    for a in range(count):
        for d in range(1, LINE):
            along(a, d).wait_send()
        for e in range(1, chips):
            over(a, e).wait_send()
        for e in range(chips):
            across(a, e).wait_send()
            across_arrives(a, e).wait_recv()
    own_rows().wait()
    at_each_head(h, finish)


def gather(tokens, shards, blk):
    rows, width = tokens.shape
    count, chips = len(shards), blk // CORES
    anywhere = pl.BlockSpec(memory_space=pl.ANY)
    dma = pltpu.SemaphoreType.DMA
    outs = pl.pallas_call(
        partial(gather_kernel, blk, count),
        out_shape=[
            jax.ShapeDtypeStruct((5, rows, width), tokens.dtype),
            jax.ShapeDtypeStruct((rows, width), tokens.dtype),
        ]
        + [jax.ShapeDtypeStruct((LINE, blk) + s.shape, s.dtype) for s in shards],
        in_specs=[anywhere] * (1 + count),
        out_specs=[anywhere] * (2 + count),
        scratch_shapes=[dma((count + 3,))]
        + [dma((count, LINE - 1))] * 2
        + [dma((count, chips - 1))] * 2
        + [dma((count, chips))] * 2
        + [dma((LINE, PIECES))] * 4
        + [dma((PIECES,))] * 4,
        compiler_params=pltpu.CompilerParams(collective_id=0, has_side_effects=True),
        name="gather",
    )(tokens, *shards)
    return outs[0], outs[2:]


def pair_kernel(blk, *refs):
    grads, outs, (held, arrived), (load, send, recv) = (
        refs[:3],
        refs[3:7],
        (refs[7:10], refs[10:13]),
        refs[13:],
    )
    h, b = lax.axis_index("head"), lax.axis_index("blk")
    chips = blk // CORES
    chip, core = b // CORES, b % CORES
    sibling = chip * CORES + 1 - core

    def mine(a, e):
        there = ((chip + e) % chips) * CORES + core
        return pltpu.make_async_copy(grads[a].at[:, there], held[a].at[e], load.at[a, e])

    def across(a, e):
        there = ((chip + e) % chips) * CORES + 1 - core
        return remote(
            grads[a].at[:, there], arrived[a].at[e], send.at[a, e], recv.at[a, e], h, sibling
        )

    order = [e % chips for e in range(1, chips + 1)]
    for e in order:
        for a in range(3):
            mine(a, e).start()
    barrier = pltpu.get_barrier_semaphore()
    pl.semaphore_signal(barrier, inc=1, device_id=(h, sibling), device_id_type=MESH)
    pl.semaphore_wait(barrier, 1)
    for e in order:
        for a in range(3):
            across(a, e).start()
    for e in order:
        for a in range(3):
            mine(a, e).wait()
            across(a, e).wait_recv()

        def one(n, carry, e=e):
            attn, inner, outer = (
                held[a][e, n].astype(f32) + arrived[a][e, n].astype(f32) for a in range(3)
            )
            parts = [inner[:, m * 768 : (m + 1) * 768] for m in range(4)]
            spare = jnp.zeros((8, 768), f32)
            outs[e][n, 0:48] = jnp.concatenate([attn, parts[0]], axis=0).astype(bf16)
            outs[e][n, 48:96] = jnp.concatenate(parts[1:3], axis=0).astype(bf16)
            outs[e][n, 96:128] = jnp.concatenate([parts[3], spare], axis=0).astype(bf16)
            outs[e][n, 128:224] = outer.astype(bf16)
            return carry

        lax.fori_loop(0, LINE, one, 0)
    for e in order:
        for a in range(3):
            across(a, e).wait_send()


def pair_sums(grads, blk):
    chips = blk // CORES
    shard = [g.shape[2:] for g in grads]
    dma = pltpu.SemaphoreType.DMA
    inside = pl.BlockSpec(memory_space=pltpu.VMEM)
    return pl.pallas_call(
        partial(pair_kernel, blk),
        out_shape=[jax.ShapeDtypeStruct((LINE, 224, 768), bf16)] * chips,
        in_specs=[pl.BlockSpec(memory_space=pl.ANY)] * 3,
        out_specs=[inside] * chips,
        scratch_shapes=[pltpu.VMEM((chips, LINE) + s, bf16) for s in shard] * 2
        + [dma((3, chips))] * 3,
        compiler_params=pltpu.CompilerParams(
            collective_id=2, has_side_effects=True, vmem_limit_bytes=56 << 20
        ),
        name="pair_sums",
    )(*grads)


def over_plane(sums, blk, head):
    chips = blk // CORES
    received = [sums[0]]
    for e in range(1, chips):
        pairs = [
            (
                h * blk + k * CORES + c,
                h * blk + ((k + e) % chips) * CORES + c,
            )
            for h in range(head)
            for k in range(chips)
            for c in range(CORES)
        ]
        received.append(lax.ppermute(sums[e], ("head", "blk"), pairs))
    return received


def reduce_kernel(blk, count, *refs):
    dx_ref, small_ref, wide_ref, sides_refs = refs[0], refs[1], refs[2], refs[3:6]
    early = refs[6 : 6 + blk // CORES]
    rest = refs[6 + blk // CORES :]
    sum_ref, outs, early_outs = rest[0], rest[1 : 1 + count], rest[1 + count : 4 + count]
    early_sum, early_in, es, er = rest[4 + count : 8 + count]
    totals, (wide_in, key_in, value_in, fed) = rest[8 + count : 11 + count], rest[11 + count : 15 + count]
    rest = rest[15 + count :]
    held, from_core, from_chip, from_line = (rest[n * count : (n + 1) * count] for n in range(4))
    line, arrived, aside = rest[4 * count : 4 * count + 3]
    load, ss, sr, cs, cr, zs, zr, xl, us, ur, ds, dr, ns, nr, fs, fr = rest[4 * count + 3 :]
    grads = (small_ref,) + tuple(totals)
    h, b = lax.axis_index("head"), lax.axis_index("blk")
    chips = blk // CORES
    chip, core = b // CORES, b % CORES
    sibling = chip * CORES + 1 - core
    rows = dx_ref.shape[1] // PIECES_BACK

    feed_rows = wide_in.shape[1]
    feeds = wide_ref.shape[0] // feed_rows
    per_chunk = feeds // (1 + 2 * REACH)
    query_ref, key_ref, value_ref = sides_refs

    def feed(step, slot):
        some = pl.ds(step * feed_rows, feed_rows)
        return [
            pltpu.make_async_copy(source.at[some], target.at[slot], fed.at[n, slot])
            for n, (source, target) in enumerate(
                ((wide_ref, wide_in), (key_ref, key_in), (value_ref, value_in))
            )
        ]

    def add_product(total, left, right, fresh):
        half = left.shape[1] // 2
        for n in range(2):
            lines = LINE // 2
            part = mm_tn(left[:, n * half : (n + 1) * half], right)
            part = part.reshape((lines,) + total.shape[1:])
            here = pl.ds(n * lines, lines)
            total[here] = part if fresh else total[here] + part

    def weigh():
        for copy in feed(0, 0):
            copy.start()
        for n in (1, 2):
            totals[n][...] = jnp.zeros_like(totals[n])

        def one(step, carry):
            slot = step % 2

            @pl.when(step + 1 < feeds)
            def _():
                for copy in feed(step + 1, 1 - slot):
                    copy.start()

            for copy in feed(step, slot):
                copy.wait()
            add_product(totals[1], wide_in[slot], key_in[slot], False)
            add_product(totals[2], wide_in[slot], value_in[slot], False)
            return carry

        lax.fori_loop(0, feeds, one, 0)
        for n in range(per_chunk):
            copies = [
                pltpu.make_async_copy(
                    wide_ref.at[pl.ds((REACH * per_chunk + n) * feed_rows, feed_rows)],
                    wide_in.at[0],
                    fed.at[0, 0],
                ),
                pltpu.make_async_copy(
                    query_ref.at[pl.ds(n * feed_rows, feed_rows)], key_in.at[0], fed.at[1, 0]
                ),
            ]
            for copy in copies:
                copy.start()
            for copy in copies:
                copy.wait()
            add_product(totals[0], wide_in[0], key_in[0], n == 0)

    def mine(a, k):
        return pltpu.make_async_copy(grads[a].at[:, k * CORES + core], held[a].at[k], load.at[a, k])

    def across(a, k):
        return remote(
            grads[a].at[:, k * CORES + 1 - core],
            from_core[a].at[k],
            ss.at[a, k],
            sr.at[a, k],
            h,
            sibling,
        )

    def over(a, e):
        k = (chip + e) % chips
        return remote(
            held[a].at[k],
            from_chip[a].at[e - 1],
            cs.at[a, e - 1],
            cr.at[a, e - 1],
            h,
            k * CORES + core,
        )

    def along(a, d):
        there = (h + d) % LINE
        return remote(
            held[a].at[chip, there],
            from_line[a].at[d - 1],
            zs.at[a, d - 1],
            zr.at[a, d - 1],
            there,
            b,
        )

    def add_cores(a, k):
        def one(n, carry):
            own = held[a][k, n] if a == 0 else grads[a][n, k * CORES + core]
            held[a][k, n] = (own + from_core[a][k, n]).astype(held[a].dtype)
            return carry

        lax.fori_loop(0, LINE, one, 0)

    def to_chips(a):
        for k in range(chips):
            if a == 0:
                mine(a, k).wait()
            across(a, k).wait_recv()
        for e in range(1, chips):
            add_cores(a, (chip + e) % chips)
            over(a, e).start()
        add_cores(a, chip)

    def to_line(a):
        for e in range(1, chips):
            over(a, e).wait_recv()

        def one(n, carry):
            total = held[a][chip, n].astype(f32)
            for e in range(1, chips):
                total = total + from_chip[a][e - 1, n].astype(f32)
            held[a][chip, n] = total.astype(held[a].dtype)
            return carry

        lax.fori_loop(0, LINE, one, 0)
        for d in range(1, LINE):
            along(a, d).start()

    def to_owner(a):
        for d in range(1, LINE):
            along(a, d).wait_recv()
        total = held[a][chip, h].astype(f32)
        for d in range(1, LINE):
            total = total + from_line[a][d - 1].astype(f32)
        outs[a][...] = total

    def early_along(d):
        there = (h + d) % LINE
        return remote(
            early_sum.at[there], early_in.at[d - 1], es.at[d - 1], er.at[d - 1], there, b
        )

    def early_to_line():
        def one(n, carry):
            total = early[0][n].astype(f32)
            for ref in early[1:]:
                total = total + ref[n].astype(f32)
            early_sum[n] = total.astype(bf16)
            return carry

        lax.fori_loop(0, LINE, one, 0)
        for d in range(1, LINE):
            early_along(d).start()

    def early_to_owner():
        for d in range(1, LINE):
            early_along(d).wait_recv()
        total = early_sum[h].astype(f32)
        for d in range(1, LINE):
            total = total + early_in[d - 1].astype(f32)
        attn_ref, inner_ref, outer_ref = early_outs
        attn_ref[...] = total[:24]
        for n in range(4):
            inner_ref[:, n * 768 : (n + 1) * 768] = total[24 * (n + 1) : 24 * (n + 2)]
        outer_ref[...] = total[128:]

    def part(p):
        return pl.ds(p * rows, rows)

    def piece(ref, p):
        return ref.at[part(p)]

    def add_rows(target, j, source, n, p):
        def one(step, carry):
            some = pl.ds(p * rows + step * 64, 64)
            target[j, some] = (
                target[j, some].astype(f32) + source[n, some].astype(f32)
            ).astype(target.dtype)
            return carry

        lax.fori_loop(0, rows // 64, one, 0)

    def slot_of(hh, j):
        slot = 2 + j - hh
        return slot if 0 <= slot < 5 else None

    def fetch(hh, j):
        return pltpu.make_async_copy(dx_ref.at[slot_of(hh, j)], line.at[j], xl.at[j])

    def arrival(hh, j, upward):
        return arrived.at[LINE if j == hh and not upward else j]

    def up(hh, j, p):
        return remote(
            piece(line.at[j], p),
            piece(arrival(hh + 1, j, True), p),
            us.at[j, p],
            ur.at[j, p],
            (h + 1) % LINE,
            b,
        )

    def up_arrives(hh, j, p):
        here = piece(arrival(hh, j, True), p)
        return remote(here, here, us.at[j, p], ur.at[j, p], (h + 1) % LINE, b)

    def down(hh, j, p):
        return remote(
            piece(line.at[j], p),
            piece(arrival(hh - 1, j, False), p),
            ds.at[j, p],
            dr.at[j, p],
            (h + 3) % LINE,
            b,
        )

    def down_arrives(hh, j, p):
        here = piece(arrival(hh, j, False), p)
        return remote(here, here, ds.at[j, p], dr.at[j, p], (h + 3) % LINE, b)

    def side_parts(hh):
        near, far = (3, 2) if hh < 2 else (0, 1)
        found = [(NEAR_SLOT[hh], near, 0, ns, nr)]
        if FAR_SLOT[hh] is not None:
            found.append((FAR_SLOT[hh], far, 1, fs, fr))
        return found

    def side(hh, slot, n, send, recv, p):
        target = (b + blk - 1) % blk if hh < 2 else (b + 1) % blk
        return remote(
            piece(dx_ref.at[slot], p), piece(aside.at[n], p), send.at[p], recv.at[p], h, target
        )

    def sends_side(hh):
        return b > 0 if hh < 2 else b < blk - 1

    def gets_side(hh):
        return b < blk - 1 if hh < 2 else b > 0

    def begin(hh):
        @pl.when(sends_side(hh))
        def _():
            for p in range(PIECES_BACK):
                for slot, _, n, send, recv in side_parts(hh):
                    side(hh, slot, n, send, recv, p).start()

        for j in range(LINE):
            if slot_of(hh, j) is not None:
                fetch(hh, j).start()
        for j in range(LINE):
            if slot_of(hh, j) is not None:
                fetch(hh, j).wait()
            else:
                line[j] = jnp.zeros(line.shape[1:], line.dtype)
        for p in range(PIECES_BACK):
            if hh == 0:
                up(hh, 1, p).start()
            if hh == LINE - 1:
                down(hh, 2, p).start()

    def take_sides(hh):
        for p in range(PIECES_BACK):
            for _, j, n, send, recv in side_parts(hh):

                @pl.when(gets_side(hh))
                def _(j=j, n=n, send=send, recv=recv):
                    here = piece(aside.at[n], p)
                    remote(here, here, send.at[p], recv.at[p], h, (b + 1) % blk).wait_recv()
                    add_rows(line, j, aside, n, p)

                if hh == 0:
                    up(hh, j, p).start()
                if hh == LINE - 1:
                    down(hh, j, p).start()

    def pass_on(hh):
        moves = []
        if hh == 1:
            moves = [(3, True), (2, True), (0, False)]
        if hh == 2:
            moves = [(0, False), (1, False), (3, True)]
        for p in range(PIECES_BACK):
            for j, upward in moves:
                (up_arrives if upward else down_arrives)(hh, j, p).wait_recv()
                add_rows(line, j, arrived, j, p)
                (up if upward else down)(hh, j, p).start()

    def finish(hh):
        for p in range(PIECES_BACK):
            sources = []
            if hh > 0:
                up_arrives(hh, hh, p).wait_recv()
                sources.append(hh)
            if hh < LINE - 1:
                down_arrives(hh, hh, p).wait_recv()
                sources.append(LINE)

            def one(step, carry, p=p, sources=tuple(sources)):
                some = pl.ds(p * rows + step * 64, 64)
                total = line[hh, some].astype(f32)
                for n in sources:
                    total = total + arrived[n, some].astype(f32)
                sum_ref[some] = total
                return carry

            lax.fori_loop(0, rows // 64, one, 0)
        for p in range(PIECES_BACK):
            for j in range(LINE):
                if j > hh:
                    up(hh, j, p).wait_send()
                if j < hh:
                    down(hh, j, p).wait_send()

        @pl.when(sends_side(hh))
        def _():
            for p in range(PIECES_BACK):
                for slot, _, n, send, recv in side_parts(hh):
                    side(hh, slot, n, send, recv, p).wait_send()

    for k in range(chips):
        mine(0, k).start()
    greet_plane_and_line(h, b, blk)
    at_each_head(h, begin)
    early_to_line()
    weigh()
    for a in range(count):
        for k in range(chips):
            across(a, k).start()
    at_each_head(h, take_sides)
    for a in range(count):
        to_chips(a)
    at_each_head(h, pass_on)
    for a in range(count):
        to_line(a)
    at_each_head(h, finish)
    early_to_owner()
    for d in range(1, LINE):
        early_along(d).wait_send()
    for a in range(count):
        to_owner(a)
    for a in range(count):
        for k in range(chips):
            across(a, k).wait_send()
        for e in range(1, chips):
            over(a, e).wait_send()
        for d in range(1, LINE):
            along(a, d).wait_send()


def reduce_to_owners(wide_grad, small, wide, projected, early, blk):
    _, rows, width = wide_grad.shape
    count, chips = 4, blk // CORES
    anywhere = pl.BlockSpec(memory_space=pl.ANY)
    inside = pl.BlockSpec(memory_space=pltpu.VMEM)
    dma = pltpu.SemaphoreType.DMA
    square = (width // (LINE * blk), width)
    shard = [small.shape[2:]] + [square] * 3
    kinds = [f32] + [bf16] * 3
    early_shapes = ((24, 768), (24, 3072), (96, 768))
    outs = pl.pallas_call(
        partial(reduce_kernel, blk, count),
        out_shape=[jax.ShapeDtypeStruct((rows, width), f32)]
        + [jax.ShapeDtypeStruct(s, f32) for s in shard]
        + [jax.ShapeDtypeStruct(s, f32) for s in early_shapes],
        in_specs=[anywhere] * 6 + [inside] * chips,
        out_specs=[inside] * (4 + count),
        scratch_shapes=[
            pltpu.VMEM(early[0].shape, bf16),
            pltpu.VMEM((LINE - 1,) + early[0].shape[1:], bf16),
            dma((LINE - 1,)),
            dma((LINE - 1,)),
        ]
        + [pltpu.VMEM((LINE, blk) + square, f32)] * 3
        + [pltpu.VMEM((2, rows // 2, width), bf16)] * 3
        + [dma((3, 2))]
        + [pltpu.VMEM((chips, LINE) + s, t) for s, t in zip(shard, kinds)]
        + [pltpu.VMEM((chips, LINE) + s, f32) for s in shard]
        + [pltpu.VMEM((chips - 1, LINE) + s, t) for s, t in zip(shard, kinds)]
        + [pltpu.VMEM((LINE - 1,) + s, t) for s, t in zip(shard, kinds)]
        + [
            pltpu.VMEM((LINE, rows, width), bf16),
            pltpu.VMEM((LINE + 1, rows, width), bf16),
            pltpu.VMEM((2, rows, width), bf16),
        ]
        + [dma((count, chips))] * 3
        + [dma((count, chips - 1))] * 2
        + [dma((count, LINE - 1))] * 2
        + [dma((LINE,))]
        + [dma((LINE, PIECES_BACK))] * 4
        + [dma((PIECES_BACK,))] * 4,
        compiler_params=pltpu.CompilerParams(
            collective_id=1, has_side_effects=True, vmem_limit_bytes=62 << 20
        ),
        name="reduce_to_owners",
    )(wide_grad, small, wide, *projected, *early)
    return outs[0], outs[1:-3], outs[-3:]


def whole(shard):
    return lax.all_gather(shard, ("head", "blk"), axis=0, tiled=True)


def shared_out(grad):
    return lax.psum_scatter(grad.astype(bf16), ("head", "blk"), scatter_dimension=0, tiled=True).astype(f32)


def padded_to(flat, size):
    return jnp.pad(flat, [(0, 0)] * (flat.ndim - 1) + [(0, size - flat.shape[-1])])


def per_device(blk, head, tokens, *rest):
    weights, vectors, (out_grad, segment_ids, random_blocks) = rest[:6], rest[6:15], rest[15:]
    rows = tokens.shape[0]
    by_kernel = head == LINE and blk == LINE * CORES
    short = [vectors[n] for n in (2, 3, 4, 6, 7, 8, 0, 1)]
    if by_kernel:
        packed = jnp.concatenate(
            [
                padded_to(jnp.stack(short), 128),
                padded_to(vectors[5][None], 128),
                jnp.zeros((7, 128), bf16),
            ]
        )
        wide, fulls = gather(tokens, [packed] + list(weights), blk)
        wide = wide.reshape(-1, tokens.shape[1])
        w_query, w_key, w_value, w_attn, w_inner, w_outer = [
            w.reshape(-1, w.shape[-1]) for w in fulls[1:]
        ]
        table = fulls[0].reshape(head * blk, 16, 128)
    else:
        wide = widen(tokens, blk, head)
        w_query, w_key, w_value, w_attn, w_inner, w_outer = [whole(w) for w in weights]
        packed = jnp.concatenate(
            [padded_to(jnp.stack(short), 128), padded_to(vectors[5][None], 128)]
        )
        table = whole(packed[None])
    short_rows = jnp.transpose(table[:, :8, : short[0].shape[0]], (1, 0, 2)).astype(f32)
    short_rows = short_rows.reshape(8, -1)
    bias_inner = table[:, 8, : vectors[5].shape[0]].astype(f32).reshape(-1, 1, PIECE)

    rows_of, bases, docs = tile_plan(segment_ids, random_blocks, rows)
    keys, values, queries = project(wide, w_key, w_value, w_query, short_rows, rows)
    attended, probs = attend(rows_of, queries, keys, values, bases, docs)

    result, grad_first_sum, grad_attended, grad_w_attn, grad_w_inner, grad_w_outer, sums_d, sums_ff = (
        middle(
            attended,
            tokens,
            out_grad,
            w_attn,
            w_inner,
            w_outer,
            short_rows,
            bias_inner,
        )
    )

    early_grads = [grad_w_attn, grad_w_inner, grad_w_outer]
    if by_kernel:
        early = over_plane(
            pair_sums([g.reshape(head, blk, -1, g.shape[-1]) for g in early_grads], blk), blk, head
        )
    grad_scaled, grad_keyed, grad_valued = attend_back(
        rows_of, queries, grad_attended, keys, values, probs
    )
    grad_wide, grad_rows, sums_qv = tokens_back(
        grad_keyed, grad_valued, grad_scaled, w_key, w_value, w_query, grad_first_sum
    )
    sums = jnp.concatenate([sums_d[:6], sums_qv[6:]])
    sums = jnp.transpose(sums.reshape(8, head * blk, -1), (1, 0, 2))
    packed = jnp.concatenate(
        [
            padded_to(sums, 128),
            padded_to(sums_ff.reshape(head * blk, 1, -1), 128),
            jnp.zeros((head * blk, 7, 128), f32),
        ],
        axis=1,
    )
    if by_kernel:
        wide_sum, late, early_sum = reduce_to_owners(
            grad_wide.reshape(-1, rows, grad_wide.shape[-1]),
            packed.reshape(head, blk, 16, 128),
            wide,
            (grad_scaled, grad_keyed, grad_valued),
            early,
            blk,
        )
        matrix_grads = tuple(late[1:]) + tuple(early_sum)
        packed = late[0]
    else:
        wide_sum = narrow(grad_wide, rows, blk, head).astype(f32)
        late_grads = [mm_tn(tokens, grad_scaled), mm_tn(wide, grad_keyed), mm_tn(wide, grad_valued)]
        matrix_grads = tuple(shared_out(g) for g in late_grads + early_grads)
        packed = lax.psum_scatter(packed, ("head", "blk"), scatter_dimension=0, tiled=True)[0]
    order = (6, 7, 0, 1, 2, 8, 3, 4, 5)
    vector_grads = tuple(packed[n, : v.shape[0]] for n, v in zip(order, vectors))
    return (result, grad_rows + wide_sum) + matrix_grads + vector_grads


def solution(mesh):
    row = P(("blk", "head"), None)
    matrix = P(("head", "blk"), None)
    vector = P(("head", "blk"))
    return jax.shard_map(
        partial(per_device, mesh.shape["blk"], mesh.shape["head"]),
        mesh=mesh,
        in_specs=(row,) + (matrix,) * 6 + (vector,) * 9 + (row, P(), P()),
        out_specs=(row, row) + (matrix,) * 6 + (vector,) * 9,
        check_vma=False,
    )
```

```python
from functools import partial

import jax
import jax.numpy as jnp
from jax import lax
from jax.experimental import pallas as pl
from jax.experimental.pallas import tpu as pltpu
from jax.sharding import PartitionSpec as P

HEAD_DIM = 64
BLOCK = 64
RANDOM = 3
TILES = 5 + RANDOM
REACH = 2
GROUP = 4
FORWARD_BLOCKS = 8
BACKWARD_BLOCKS = 8
ROWS = 256
PIECE = 768

epsilon = 1e-06
masked_value = -1e30
query_scale = 0.125
gelu_scale = 0.7978845608028654
gelu_cubic = 0.044715
far_away = -(1 << 24)
f32, bf16 = jnp.float32, jnp.bfloat16


def mm(a, b):
    return jnp.dot(a, b, preferred_element_type=f32)


def mm_nt(a, b):
    return lax.dot_general(a, b, (((1,), (1,)), ((), ())), preferred_element_type=f32)


def mm_tn(a, b):
    return lax.dot_general(a, b, (((0,), (0,)), ((), ())), preferred_element_type=f32)


def head_mask(rows, cols, first):
    lanes = lax.broadcasted_iota(jnp.int32, (rows, cols), 1)
    return (lanes >= first) & (lanes < first + HEAD_DIM)


def stacked_by_head(tile):
    rows, cols = tile.shape
    return jnp.concatenate(
        [
            jnp.where(head_mask(rows, cols, h * HEAD_DIM), tile, jnp.zeros_like(tile))
            for h in range(cols // HEAD_DIM)
        ],
        axis=0,
    )


def own_head_columns(stacked):
    cols = stacked.shape[1]
    total = None
    for h in range(cols // HEAD_DIM):
        part = stacked[h * BLOCK : (h + 1) * BLOCK]
        part = jnp.where(head_mask(BLOCK, cols, h * HEAD_DIM), part, 0.0)
        total = part if total is None else total + part
    return total


def block_rows(row):
    return pl.ds(pl.multiple_of(row * BLOCK, BLOCK), BLOCK)


def gathered(table_ref, fixed_row, random_row):
    tiles = [table_ref[block_rows(fixed_row(t)), :] for t in range(5)]
    low = head_mask(BLOCK, 2 * HEAD_DIM, 0)
    for t in range(RANDOM):
        halves = []
        for pair in range(GROUP // 2):
            cols = pl.ds(pair * 2 * HEAD_DIM, 2 * HEAD_DIM)
            a = table_ref[block_rows(random_row(2 * pair, t)), cols]
            b = table_ref[block_rows(random_row(2 * pair + 1, t)), cols]
            halves.append(jnp.where(low, a, b))
        tiles.append(jnp.concatenate(halves, axis=1))
    return jnp.concatenate(tiles, axis=0)


def row_readers(rows_ref, blocks, i):
    group = pl.program_id(0)

    def fixed_row(t):
        return rows_ref[(group * GROUP * blocks + i) * TILES + t]

    def random_row(h, t):
        return rows_ref[((group * GROUP + h) * blocks + i) * TILES + 5 + t]

    return fixed_row, random_row


def attend_kernel(blocks, rows_ref, q_ref, k_ref, v_ref, base_ref, doc_ref, out_ref, p_ref):
    within = lax.broadcasted_iota(jnp.int32, (BLOCK, GROUP * BLOCK), 0)
    for u in range(FORWARD_BLOCKS):
        here = pl.ds(u * BLOCK, BLOCK)
        readers = row_readers(rows_ref, blocks, pl.program_id(1) * FORWARD_BLOCKS + u)
        keys = gathered(k_ref, *readers)
        values = gathered(v_ref, *readers)
        scores = mm_nt(keys, stacked_by_head(q_ref[here, :]))
        lo = doc_ref[u, 0:1, :]
        hi = doc_ref[u, 1:2, :]
        masked = []
        for t in range(TILES):
            place = within + base_ref[0, u, t : t + 1, :]
            allowed = (place >= lo) & (place < hi)
            masked.append(jnp.where(allowed, scores[t * BLOCK : (t + 1) * BLOCK], masked_value))
        scores = jnp.concatenate(masked, axis=0)
        raised = jnp.exp(scores - jnp.max(scores, axis=0, keepdims=True))
        probs = (raised * (1.0 / jnp.sum(raised, axis=0, keepdims=True))).astype(bf16)
        p_ref[0, u] = probs
        out_ref[here, :] = own_head_columns(mm_tn(probs, values)).astype(bf16)


def attend_back_kernel(
    blocks,
    rows_ref,
    q_ref,
    g_ref,
    k_ref,
    v_ref,
    p_ref,
    dq_ref,
    dk_ref,
    dv_ref,
    sums_ref,
    dk_sum,
    dv_sum,
):
    step = pl.program_id(1)

    @pl.when(step == 0)
    def _():
        sums_ref[...] = jnp.zeros_like(sums_ref)
        dk_sum[...] = jnp.zeros_like(dk_sum)
        dv_sum[...] = jnp.zeros_like(dv_sum)

    found = []
    for u in range(BACKWARD_BLOCKS):
        here = pl.ds(u * BLOCK, BLOCK)
        readers = row_readers(rows_ref, blocks, step * BACKWARD_BLOCKS + u)
        keys = gathered(k_ref, *readers)
        values = gathered(v_ref, *readers)
        queries = stacked_by_head(q_ref[here, :])
        grads = stacked_by_head(g_ref[here, :])
        probs = p_ref[0, u]
        grad_probs = mm_nt(values, grads)
        wide = probs.astype(f32)
        balance = jnp.sum(wide * grad_probs, axis=0, keepdims=True)
        grad_scores = (wide * (grad_probs - balance)).astype(bf16)
        dq_ref[here, :] = (query_scale * own_head_columns(mm_tn(grad_scores, keys))).astype(bf16)
        found.append((readers, mm(grad_scores, queries), mm(probs, grads)))
    for (fixed_row, random_row), grad_keys, grad_values in found:
        for total, part in ((dk_sum, grad_keys), (dv_sum, grad_values)):
            for t in range(5):
                total[block_rows(fixed_row(t)), :] += part[t * BLOCK : (t + 1) * BLOCK]
            for t in range(RANDOM):
                rows = part[(5 + t) * BLOCK : (6 + t) * BLOCK]
                for h in range(GROUP):
                    first = (h // 2) * 2 * HEAD_DIM
                    mine = head_mask(BLOCK, 2 * HEAD_DIM, (h % 2) * HEAD_DIM)
                    total[block_rows(random_row(h, t)), pl.ds(first, 2 * HEAD_DIM)] += jnp.where(
                        mine, rows[:, first : first + 2 * HEAD_DIM], 0.0
                    )

    sums_ref[6:7, :] += jnp.sum(dq_ref[...].astype(f32), axis=0, keepdims=True)

    @pl.when(step == blocks // BACKWARD_BLOCKS - 1)
    def _():
        dk_ref[...] = dk_sum[...].astype(bf16)
        dv_ref[...] = dv_sum[...].astype(bf16)
        sums_ref[7:8, :] = jnp.sum(dv_ref[...].astype(f32), axis=0, keepdims=True)


def attend(rows, queries, keys, values, bases, docs):
    tokens, width = queries.shape
    ext = keys.shape[0]
    blocks, cols, some = tokens // BLOCK, GROUP * HEAD_DIM, FORWARD_BLOCKS
    groups = width // cols
    tile = pl.BlockSpec((some * BLOCK, cols), lambda g, i, r: (i, g))
    table = pl.BlockSpec((ext, cols), lambda g, i, r: (0, g))
    return pl.pallas_call(
        partial(attend_kernel, blocks),
        grid_spec=pltpu.PrefetchScalarGridSpec(
            num_scalar_prefetch=1,
            grid=(groups, blocks // some),
            in_specs=[
                tile,
                table,
                table,
                pl.BlockSpec((1, some, TILES, cols), lambda g, i, r: (g, i, 0, 0)),
                pl.BlockSpec((some, 8, cols), lambda g, i, r: (i, 0, 0)),
            ],
            out_specs=[
                tile,
                pl.BlockSpec((1, some, TILES * BLOCK, cols), lambda g, i, r: (g, i, 0, 0)),
            ],
        ),
        out_shape=[
            jax.ShapeDtypeStruct((tokens, width), bf16),
            jax.ShapeDtypeStruct((groups, blocks, TILES * BLOCK, cols), bf16),
        ],
        compiler_params=pltpu.CompilerParams(vmem_limit_bytes=40 << 20),
        name="attend",
    )(rows, queries, keys, values, bases, docs)


def attend_back(rows, queries, grads, keys, values, probs):
    tokens, width = queries.shape
    ext = keys.shape[0]
    blocks, cols, some = tokens // BLOCK, GROUP * HEAD_DIM, BACKWARD_BLOCKS
    groups = width // cols
    tile = pl.BlockSpec((some * BLOCK, cols), lambda g, i, r: (i, g))
    table = pl.BlockSpec((ext, cols), lambda g, i, r: (0, g))
    return pl.pallas_call(
        partial(attend_back_kernel, blocks),
        grid_spec=pltpu.PrefetchScalarGridSpec(
            num_scalar_prefetch=1,
            grid=(groups, blocks // some),
            in_specs=[
                tile,
                tile,
                table,
                table,
                pl.BlockSpec((1, some, TILES * BLOCK, cols), lambda g, i, r: (g, i, 0, 0)),
            ],
            out_specs=[tile, table, table, pl.BlockSpec((8, cols), lambda g, i, r: (0, g))],
            scratch_shapes=[pltpu.VMEM((ext, cols), f32), pltpu.VMEM((ext, cols), f32)],
        ),
        out_shape=[
            jax.ShapeDtypeStruct((tokens, width), bf16),
            jax.ShapeDtypeStruct((ext, width), bf16),
            jax.ShapeDtypeStruct((ext, width), bf16),
            jax.ShapeDtypeStruct((8, width), f32),
        ],
        compiler_params=pltpu.CompilerParams(vmem_limit_bytes=56 << 20),
        cost_estimate=pl.CostEstimate(
            flops=10 * groups * blocks * TILES * BLOCK * cols * cols,
            bytes_accessed=100 << 20,
            transcendentals=0,
        ),
        name="attend_back",
    )(rows, queries, grads, keys, values, probs)


def normalized(values):
    centred = values - jnp.mean(values, axis=-1, keepdims=True)
    root = lax.rsqrt(jnp.mean(centred * centred, axis=-1, keepdims=True) + epsilon)
    return centred * root, root


def norm_back(grad, normal, root, gain):
    scaled = grad * gain
    along = jnp.mean(scaled * normal, axis=-1, keepdims=True)
    return root * (scaled - jnp.mean(scaled, axis=-1, keepdims=True) - normal * along)


def gelu_and_slope(u):
    square = u * u
    bend = jnp.tanh(gelu_scale * (u + gelu_cubic * (square * u)))
    half = 0.5 * (1.0 + bend)
    slope = half + (0.5 * gelu_scale) * u * (1.0 - bend * bend) * (
        1.0 + (3.0 * gelu_cubic) * square
    )
    return u * half, slope


def middle_kernel(
    att_ref,
    x_ref,
    og_ref,
    wa_ref,
    wi_ref,
    wo_ref,
    vec_ref,
    bi_ref,
    res_ref,
    sum_ref,
    ga_ref,
    dwa_ref,
    dwi_ref,
    dwo_ref,
    dvec_ref,
    dbi_ref,
    normal,
    root,
    low,
    act,
    slope,
    inner,
):
    step, half = pl.program_id(0), pl.num_programs(0) // 2
    tokens, width = x_ref.shape
    slices = [pl.ds(t * ROWS, ROWS) for t in range(tokens // ROWS)]
    bias_attn, gain_one, offset_one, bias_outer, gain_two, offset_two = (
        vec_ref[n : n + 1, :] for n in range(6)
    )

    def row_sum(total, values):
        part = jnp.sum(values, axis=0, keepdims=True)
        return part if total is None else total + part

    @pl.when(step == 0)
    def _():
        for s in slices:
            values = x_ref[s, :].astype(f32) + mm(att_ref[s, :], wa_ref[...]) + bias_attn
            flat, scale = normalized(values)
            normal[s, :] = flat
            root[s, :] = jnp.broadcast_to(scale, (ROWS, 128))
            first = flat * gain_one + offset_one
            low[s, :] = first.astype(bf16)
            sum_ref[s, :] = first + bias_outer

    @pl.when(step < half)
    def _():
        for s in slices:
            active, bend = gelu_and_slope(mm(low[s, :], wi_ref[...]) + bi_ref[0])
            active = active.astype(bf16)
            act[step, s, :] = active
            slope[step, s, :] = bend.astype(bf16)
            sum_ref[s, :] += mm(active, wo_ref[...])

    @pl.when(step == half)
    def _():
        outer_sum, gain_sum, offset_sum = None, None, None
        for s in slices:
            flat, scale = normalized(sum_ref[s, :])
            res_ref[s, :] = (flat * gain_two + offset_two).astype(bf16)
            grad = og_ref[s, :].astype(f32)
            gain_sum = row_sum(gain_sum, grad * flat)
            offset_sum = row_sum(offset_sum, grad)
            second = norm_back(grad, flat, scale, gain_two)
            sum_ref[s, :] = second
            second = second.astype(bf16)
            ga_ref[s, :] = second
            outer_sum = row_sum(outer_sum, second.astype(f32))
        dvec_ref[3:4, :] = outer_sum
        dvec_ref[4:5, :] = gain_sum
        dvec_ref[5:6, :] = offset_sum
        dvec_ref[6:8, :] = jnp.zeros((2, width), f32)

    @pl.when(step >= half)
    def _():
        now = step - half
        total = None
        for s in slices:
            grad = mm_nt(ga_ref[s, :], wo_ref[...]) * slope[now, s, :].astype(f32)
            grad = grad.astype(bf16)
            inner[s, :] = grad
            total = row_sum(total, grad.astype(f32))
            sum_ref[s, :] += mm_nt(grad, wi_ref[...])
        dbi_ref[0] = total
        for n in range(width // 256):
            some = pl.ds(n * 256, 256)
            dwi_ref[some, :] = mm_tn(low[:, some], inner[...]).astype(bf16)
        for n in range(PIECE // 256):
            some = pl.ds(n * 256, 256)
            dwo_ref[some, :] = mm_tn(act[now, :, some], ga_ref[...]).astype(bf16)

    @pl.when(step == 2 * half - 1)
    def _():
        attn_sum, gain_sum, offset_sum = None, None, None
        for s in slices:
            grad, flat = sum_ref[s, :], normal[s, :]
            gain_sum = row_sum(gain_sum, grad * flat)
            offset_sum = row_sum(offset_sum, grad)
            grad = norm_back(grad, flat, root[s, 0:1], gain_one)
            sum_ref[s, :] = grad
            grad = grad.astype(bf16)
            inner[s, :width] = grad
            attn_sum = row_sum(attn_sum, grad.astype(f32))
            ga_ref[s, :] = mm_nt(grad, wa_ref[...]).astype(bf16)
        dvec_ref[0:1, :] = attn_sum
        dvec_ref[1:2, :] = gain_sum
        dvec_ref[2:3, :] = offset_sum
        for n in range(width // 256):
            some = pl.ds(n * 256, 256)
            dwa_ref[some, :] = mm_tn(att_ref[:, some], inner[:, :width]).astype(bf16)


def middle(attended, tokens, out_grad, w_attn, w_inner, w_outer, vectors, bias_inner):
    rows, width = tokens.shape
    steps = w_inner.shape[1] // PIECE
    one = pl.Buffered(1)
    still = pl.BlockSpec((rows, width), lambda i: (0, 0), pipeline_mode=one)
    square = pl.BlockSpec((width, width), lambda i: (0, 0), pipeline_mode=one)
    few = pl.BlockSpec((8, width), lambda i: (0, 0))
    later = lambda i: jnp.maximum(i - steps, 0)
    return pl.pallas_call(
        middle_kernel,
        grid=(2 * steps,),
        in_specs=[
            still,
            still,
            still,
            square,
            pl.BlockSpec((width, PIECE), lambda i: (0, i % steps)),
            pl.BlockSpec((PIECE, width), lambda i: (i % steps, 0)),
            few,
            pl.BlockSpec((1, 1, PIECE), lambda i: (i % steps, 0, 0)),
        ],
        out_specs=[
            still,
            still,
            still,
            square,
            pl.BlockSpec((width, PIECE), lambda i: (0, later(i))),
            pl.BlockSpec((PIECE, width), lambda i: (later(i), 0)),
            few,
            pl.BlockSpec((1, 1, PIECE), lambda i: (later(i), 0, 0)),
        ],
        out_shape=[
            jax.ShapeDtypeStruct((rows, width), bf16),
            jax.ShapeDtypeStruct((rows, width), f32),
            jax.ShapeDtypeStruct((rows, width), bf16),
            jax.ShapeDtypeStruct(w_attn.shape, bf16),
            jax.ShapeDtypeStruct(w_inner.shape, bf16),
            jax.ShapeDtypeStruct(w_outer.shape, bf16),
            jax.ShapeDtypeStruct((8, width), f32),
            jax.ShapeDtypeStruct((steps, 1, PIECE), f32),
        ],
        scratch_shapes=[
            pltpu.VMEM((rows, width), f32),
            pltpu.VMEM((rows, 128), f32),
            pltpu.VMEM((rows, width), bf16),
            pltpu.VMEM((steps, rows, PIECE), bf16),
            pltpu.VMEM((steps, rows, PIECE), bf16),
            pltpu.VMEM((rows, PIECE), bf16),
        ],
        compiler_params=pltpu.CompilerParams(vmem_limit_bytes=60 << 20),
        name="middle",
    )(attended, tokens, out_grad, w_attn, w_inner, w_outer, vectors, bias_inner)


def project_kernel(wide_ref, wk_ref, wv_ref, wq_ref, vec_ref, k_ref, v_ref, q_ref):
    rows = wide_ref.shape[0]
    slices = [pl.ds(t * ROWS, ROWS) for t in range(rows // ROWS)]
    for s in slices:
        k_ref[s, :] = mm(wide_ref[s, :], wk_ref[...]).astype(bf16)
        v_ref[s, :] = (mm(wide_ref[s, :], wv_ref[...]) + vec_ref[7:8, :]).astype(bf16)

    @pl.when(pl.program_id(0) == REACH)
    def _():
        for s in slices:
            queries = mm(wide_ref[s, :], wq_ref[...]) + vec_ref[6:7, :]
            q_ref[s, :] = (query_scale * queries).astype(bf16)


def project(wide, w_key, w_value, w_query, vectors, rows):
    width = wide.shape[1]
    one = pl.Buffered(1)
    tile = pl.BlockSpec((rows, width), lambda i: (i, 0))
    still = pl.BlockSpec((rows, width), lambda i: (0, 0), pipeline_mode=one)
    square = pl.BlockSpec((width, width), lambda i: (0, 0), pipeline_mode=one)
    table = jax.ShapeDtypeStruct(wide.shape, bf16)
    return pl.pallas_call(
        project_kernel,
        grid=(1 + 2 * REACH,),
        in_specs=[tile, square, square, square, pl.BlockSpec((8, width), lambda i: (0, 0))],
        out_specs=[tile, tile, still],
        out_shape=[table, table, jax.ShapeDtypeStruct((rows, width), bf16)],
        compiler_params=pltpu.CompilerParams(vmem_limit_bytes=60 << 20),
        name="project",
    )(wide, w_key, w_value, w_query, vectors)


def tile_plan(segment_ids, random_blocks, tokens):
    heads, total_blocks, _ = random_blocks.shape
    blocks = tokens // BLOCK
    chunk = lax.axis_index("blk") * lax.axis_size("head") + lax.axis_index("head")
    margin = REACH * tokens
    padded = jnp.concatenate(
        [
            jnp.full((margin,), -1, jnp.int32),
            segment_ids,
            jnp.full((margin,), jnp.iinfo(jnp.int32).max, jnp.int32),
        ]
    )
    near = lax.dynamic_slice_in_dim(padded, chunk * tokens, tokens + 2 * margin)
    own = near[margin : margin + tokens]
    before, after = near[: margin + tokens], near[margin:]
    begins = jnp.sum((before[None, :] < own[:, None]).astype(jnp.int32), axis=1)
    ends = margin + jnp.sum((after[None, :] <= own[:, None]).astype(jnp.int32), axis=1)
    docs = jnp.stack([begins, ends]).reshape(2, blocks, BLOCK)
    docs = jnp.tile(jnp.transpose(docs, (1, 0, 2)), (1, 4, GROUP))
    first = begins[::BLOCK] // BLOCK
    here = REACH * blocks + jnp.arange(blocks, dtype=jnp.int32)
    fixed = jnp.stack([here - 1, here, here + 1, first, first + 1], axis=-1)
    picked = lax.dynamic_slice_in_dim(random_blocks, chunk * blocks, blocks, axis=1)
    picked = picked - (chunk - REACH) * blocks
    rows = jnp.concatenate(
        [jnp.broadcast_to(fixed[None], (heads, blocks, 5)), picked], axis=-1
    )
    earlier = jnp.arange(TILES)[None, :] < jnp.arange(TILES)[:, None]
    repeat = jnp.any((rows[..., :, None] == rows[..., None, :]) & earlier, axis=-1)
    bases = jnp.where(repeat, far_away, rows * BLOCK)
    rows = jnp.clip(rows, 0, (1 + 2 * REACH) * blocks - 1)
    bases = bases.reshape(heads // GROUP, GROUP, blocks, TILES)
    bases = jnp.repeat(jnp.transpose(bases, (0, 2, 3, 1)), BLOCK, axis=-1)
    return rows.reshape(-1), bases, docs


def side_pairs(blk, head, far):
    pairs = []
    for b in range(blk):
        for h in range(head):
            down = h < head // 2
            if far and h not in (0, head - 1):
                continue
            source = b - 1 if down else b + 1
            if 0 <= source < blk:
                pairs.append((h * blk + source, h * blk + b))
    return pairs


def widen(tokens_rows, blk, head):
    rows = tokens_rows.shape[0]
    h = lax.axis_index("head")
    line = lax.all_gather(tokens_rows, "head", axis=0, tiled=True)
    low = h < head // 2
    near = lax.dynamic_slice_in_dim(line, jnp.where(low, head - 1, 0) * rows, rows)
    far = lax.dynamic_slice_in_dim(line, jnp.where(low, head - 2, 1) * rows, rows)
    near = lax.ppermute(near, ("head", "blk"), side_pairs(blk, head, False))
    far = lax.ppermute(far, ("head", "blk"), side_pairs(blk, head, True))
    whole = jnp.concatenate([far, near, line, near, far], axis=0)
    return lax.dynamic_slice_in_dim(whole, h * rows, (1 + 2 * REACH) * rows)


def narrow(wide_rows, rows, blk, head):
    h = lax.axis_index("head")
    low = h < head // 2
    frame = jnp.zeros(((head + 2 * REACH) * rows, wide_rows.shape[1]), wide_rows.dtype)
    frame = lax.dynamic_update_slice_in_dim(frame, wide_rows, h * rows, 0)
    near = lax.dynamic_slice_in_dim(frame, jnp.where(low, 1, head + REACH) * rows, rows)
    far = lax.dynamic_slice_in_dim(frame, jnp.where(low, 0, head + REACH + 1) * rows, rows)
    back = [(t, s) for s, t in side_pairs(blk, head, False)]
    near = lax.ppermute(near, ("head", "blk"), back)
    back = [(t, s) for s, t in side_pairs(blk, head, True)]
    far = lax.ppermute(far, ("head", "blk"), back)
    line = frame[REACH * rows : (REACH + head) * rows].reshape(head, rows, -1)
    place = jnp.arange(head, dtype=jnp.int32)[:, None, None]
    line = line + jnp.where(place == jnp.where(low, head - 1, 0), near[None], 0)
    line = line + jnp.where(place == jnp.where(low, head - 2, 1), far[None], 0)
    return lax.psum_scatter(line.reshape(head * rows, -1), "head", scatter_dimension=0, tiled=True)


LINE = 4
CORES = 2
PIECES = 4
PIECES_BACK = 8
MESH = pl.DeviceIdType.MESH
NEAR_SLOT = (1, 0, 4, 3)
FAR_SLOT = (0, None, None, 4)
WORK_ORDER = ((3, 1, 0, 4, 2), (0, 4, 3, 1, 2), (4, 0, 1, 3, 2), (1, 3, 4, 0, 2))


def remote(source, target, send, recv, head, blk):
    return pltpu.make_async_remote_copy(
        src_ref=source,
        dst_ref=target,
        send_sem=send,
        recv_sem=recv,
        device_id=(head, blk),
        device_id_type=MESH,
    )


def at_each_head(h, body):
    for hh in range(LINE):
        pl.when(h == hh)(partial(body, hh))


def greet_plane_and_line(h, b, blk):
    barrier = pltpu.get_barrier_semaphore()
    for d in range(1, LINE):
        pl.semaphore_signal(
            barrier, inc=1, device_id=((h + d) % LINE, b), device_id_type=MESH
        )
    for d in range(1, blk):
        pl.semaphore_signal(barrier, inc=1, device_id=(h, (b + d) % blk), device_id_type=MESH)
    pl.semaphore_wait(barrier, LINE - 1 + blk - 1)


def gather_kernel(blk, count, *refs):
    x_ref, shards = refs[0], refs[1 : 1 + count]
    wide, spill, fulls = refs[1 + count], refs[2 + count], refs[3 + count : 3 + 2 * count]
    local, zs, zr, cs, cr, ss, sr, us, ur, ds, dr, ns, nr, fs, fr = refs[3 + 2 * count :]
    h, b = lax.axis_index("head"), lax.axis_index("blk")
    chips = blk // CORES
    chip, core = b // CORES, b % CORES
    sibling = chip * CORES + 1 - core
    rows = x_ref.shape[0] // PIECES

    def piece(ref, p):
        return ref.at[pl.ds(p * rows, rows)]

    def place(hh, j):
        slot = 2 + j - hh
        return wide.at[slot] if 0 <= slot < 5 else spill

    def own(a):
        return pltpu.make_async_copy(shards[a], fulls[a].at[h, b], local.at[a])

    def along(a, d):
        return remote(
            shards[a], fulls[a].at[h, b], zs.at[a, d - 1], zr.at[a, d - 1], (h + d) % LINE, b
        )

    def along_arrives(a, d):
        src = (h - d + LINE) % LINE
        return remote(
            shards[a], fulls[a].at[src, b], zs.at[a, d - 1], zr.at[a, d - 1], (h + d) % LINE, b
        )

    def over(a, e):
        part = fulls[a].at[:, b]
        there = ((chip + e) % chips) * CORES + core
        return remote(part, part, cs.at[a, e - 1], cr.at[a, e - 1], h, there)

    def over_arrives(a, e):
        there = ((chip - e + chips) % chips) * CORES + core
        part = fulls[a].at[:, there]
        return remote(part, part, cs.at[a, e - 1], cr.at[a, e - 1], h, there)

    def across(a, e):
        part = fulls[a].at[:, ((chip - e + chips) % chips) * CORES + core]
        return remote(part, part, ss.at[a, e], sr.at[a, e], h, sibling)

    def across_arrives(a, e):
        part = fulls[a].at[:, ((chip - e + chips) % chips) * CORES + 1 - core]
        return remote(part, part, ss.at[a, e], sr.at[a, e], h, sibling)

    def spread(a):
        for d in range(1, LINE):
            along_arrives(a, d).wait_recv()
        own(a).wait()
        for e in range(1, chips):
            over(a, e).start()
        across(a, 0).start()

    def hand_over(a):
        for e in range(1, chips):
            over_arrives(a, e).wait_recv()
            across(a, e).start()

    def up(hh, j, p):
        source = x_ref if j == hh else place(hh, j)
        return remote(
            piece(source, p), piece(place(hh + 1, j), p), us.at[j, p], ur.at[j, p], (h + 1) % LINE, b
        )

    def up_arrives(hh, j, p):
        target = piece(place(hh, j), p)
        return remote(target, target, us.at[j, p], ur.at[j, p], (h + 1) % LINE, b)

    def down(hh, j, p):
        source = x_ref if j == hh else place(hh, j)
        return remote(
            piece(source, p), piece(place(hh - 1, j), p), ds.at[j, p], dr.at[j, p], (h + 3) % LINE, b
        )

    def down_arrives(hh, j, p):
        target = piece(place(hh, j), p)
        return remote(target, target, ds.at[j, p], dr.at[j, p], (h + 3) % LINE, b)

    def sides(hh, j):
        near, far = (3, 2) if hh < 2 else (0, 1)
        if j == near:
            return [(NEAR_SLOT[hh], ns, nr)]
        if j == far and FAR_SLOT[hh] is not None:
            return [(FAR_SLOT[hh], fs, fr)]
        return []

    def side(hh, j, p, slot, send, recv):
        target = (b + 1) % blk if hh < 2 else (b + blk - 1) % blk
        return remote(
            piece(place(hh, j), p), piece(wide.at[slot], p), send.at[p], recv.at[p], h, target
        )

    def sends_side(hh):
        return b < blk - 1 if hh < 2 else b > 0

    def gets_side(hh):
        return b > 0 if hh < 2 else b < blk - 1

    def side_slots(hh):
        found = [(NEAR_SLOT[hh], ns, nr)]
        if FAR_SLOT[hh] is not None:
            found.append((FAR_SLOT[hh], fs, fr))
        return found

    def fill(n, slot):
        return pltpu.make_async_copy(x_ref, wide.at[slot], local.at[count + 1 + n])

    def own_rows():
        return pltpu.make_async_copy(x_ref, wide.at[2], local.at[count])

    def begin(hh):
        for p in range(PIECES):
            if hh < LINE - 1:
                up(hh, hh, p).start()
            if hh > 0:
                down(hh, hh, p).start()

        @pl.when(jnp.logical_not(gets_side(hh)))
        def _():
            for n, (slot, _, _) in enumerate(side_slots(hh)):
                fill(n, slot).start()

    def pass_on(distance, hh):
        for p in range(PIECES):
            for j, arrives, onward, ends in (
                (hh - distance, up_arrives, up, hh == LINE - 1),
                (hh + distance, down_arrives, down, hh == 0),
            ):
                if not 0 <= j < LINE:
                    continue
                arrives(hh, j, p).wait_recv()
                if not ends:
                    onward(hh, j, p).start()
                for slot, send, recv in sides(hh, j):

                    @pl.when(sends_side(hh))
                    def _(slot=slot, send=send, recv=recv):
                        side(hh, j, p, slot, send, recv).start()

    def finish(hh):
        for p in range(PIECES):
            for j in range(LINE):
                if j <= hh < LINE - 1:
                    up(hh, j, p).wait_send()
                if j >= hh > 0:
                    down(hh, j, p).wait_send()

        @pl.when(sends_side(hh))
        def _():
            for j in range(LINE):
                for slot, send, recv in sides(hh, j):
                    for p in range(PIECES):
                        side(hh, j, p, slot, send, recv).wait_send()

        @pl.when(gets_side(hh))
        def _():
            for slot, send, recv in side_slots(hh):
                for p in range(PIECES):
                    target = piece(wide.at[slot], p)
                    remote(target, target, send.at[p], recv.at[p], h, (b + 1) % blk).wait_recv()

        @pl.when(jnp.logical_not(gets_side(hh)))
        def _():
            for n, (slot, _, _) in enumerate(side_slots(hh)):
                fill(n, slot).wait()

    own_rows().start()
    for a in range(count):
        own(a).start()
    greet_plane_and_line(h, b, blk)
    for a in range(count):
        for d in range(1, LINE):
            along(a, d).start()
    at_each_head(h, begin)
    for a in range(count):
        spread(a)
    at_each_head(h, partial(pass_on, 1))
    for a in range(count - 2):
        hand_over(a)
    at_each_head(h, partial(pass_on, 2))
    hand_over(count - 2)
    at_each_head(h, partial(pass_on, 3))
    hand_over(count - 1)
    for a in range(count):
        for d in range(1, LINE):
            along(a, d).wait_send()
        for e in range(1, chips):
            over(a, e).wait_send()
        for e in range(chips):
            across(a, e).wait_send()
            across_arrives(a, e).wait_recv()
    own_rows().wait()
    at_each_head(h, finish)


def gather(tokens, shards, blk):
    rows, width = tokens.shape
    count, chips = len(shards), blk // CORES
    anywhere = pl.BlockSpec(memory_space=pl.ANY)
    dma = pltpu.SemaphoreType.DMA
    outs = pl.pallas_call(
        partial(gather_kernel, blk, count),
        out_shape=[
            jax.ShapeDtypeStruct((5, rows, width), tokens.dtype),
            jax.ShapeDtypeStruct((rows, width), tokens.dtype),
        ]
        + [jax.ShapeDtypeStruct((LINE, blk) + s.shape, s.dtype) for s in shards],
        in_specs=[anywhere] * (1 + count),
        out_specs=[anywhere] * (2 + count),
        scratch_shapes=[dma((count + 3,))]
        + [dma((count, LINE - 1))] * 2
        + [dma((count, chips - 1))] * 2
        + [dma((count, chips))] * 2
        + [dma((LINE, PIECES))] * 4
        + [dma((PIECES,))] * 4,
        compiler_params=pltpu.CompilerParams(collective_id=0, has_side_effects=True),
        name="gather",
    )(tokens, *shards)
    return outs[0], outs[2:]


def pair_kernel(blk, *refs):
    chips = blk // CORES
    grads, firsts, seconds = refs[:3], refs[3 : 3 + chips], refs[3 + chips : 3 + 2 * chips]
    rest = refs[3 + 2 * chips :]
    held, arrived, (load, send, recv) = rest[:3], rest[3:6], rest[6:]
    h, b = lax.axis_index("head"), lax.axis_index("blk")
    chip, core = b // CORES, b % CORES
    sibling = chip * CORES + 1 - core

    def mine(a, e):
        there = ((chip + e) % chips) * CORES + core
        return pltpu.make_async_copy(grads[a].at[:, there], held[a].at[e], load.at[a, e])

    def across(a, e):
        there = ((chip + e) % chips) * CORES + 1 - core
        return remote(
            grads[a].at[:, there], arrived[a].at[e], send.at[a, e], recv.at[a, e], h, sibling
        )

    order = [e % chips for e in range(1, chips + 1)]
    for e in order:
        for a in range(3):
            mine(a, e).start()
    barrier = pltpu.get_barrier_semaphore()
    pl.semaphore_signal(barrier, inc=1, device_id=(h, sibling), device_id_type=MESH)
    pl.semaphore_wait(barrier, 1)
    for e in order:
        for a in range(3):
            across(a, e).start()
    for e in order:
        for a in range(3):
            mine(a, e).wait()
            across(a, e).wait_recv()

        def one(n, carry, e=e):
            attn, inner, outer = (
                held[a][e, n].astype(f32) + arrived[a][e, n].astype(f32) for a in range(3)
            )
            parts = [inner[:, m * 768 : (m + 1) * 768] for m in range(4)]
            spare = jnp.zeros((8, 768), f32)
            firsts[e][n, 0:48] = jnp.concatenate([attn, parts[0]], axis=0).astype(bf16)
            firsts[e][n, 48:96] = jnp.concatenate(parts[1:3], axis=0).astype(bf16)
            seconds[e][n, 0:32] = jnp.concatenate([parts[3], spare], axis=0).astype(bf16)
            seconds[e][n, 32:128] = outer.astype(bf16)
            return carry

        lax.fori_loop(0, LINE, one, 0)
    for e in order:
        for a in range(3):
            across(a, e).wait_send()


def pair_sums(grads, blk):
    chips = blk // CORES
    shard = [g.shape[2:] for g in grads]
    dma = pltpu.SemaphoreType.DMA
    inside = pl.BlockSpec(memory_space=pltpu.VMEM)
    outs = pl.pallas_call(
        partial(pair_kernel, blk),
        out_shape=[jax.ShapeDtypeStruct((LINE, 96, 768), bf16)] * chips
        + [jax.ShapeDtypeStruct((LINE, 128, 768), bf16)] * chips,
        in_specs=[pl.BlockSpec(memory_space=pl.ANY)] * 3,
        out_specs=[inside] * 2 * chips,
        scratch_shapes=[pltpu.VMEM((chips, LINE) + s, bf16) for s in shard] * 2
        + [dma((3, chips))] * 3,
        compiler_params=pltpu.CompilerParams(
            collective_id=2, has_side_effects=True, vmem_limit_bytes=56 << 20
        ),
        name="pair_sums",
    )(*grads)
    return outs[:chips], outs[chips:]


def over_plane(sums, blk, head):
    chips = blk // CORES
    received = [sums[0]]
    for e in range(1, chips):
        pairs = [
            (
                h * blk + k * CORES + c,
                h * blk + ((k + e) % chips) * CORES + c,
            )
            for h in range(head)
            for k in range(chips)
            for c in range(CORES)
        ]
        received.append(lax.ppermute(sums[e], ("head", "blk"), pairs))
    return received


def reduce_kernel(blk, count, *refs):
    small_ref, wide_ref, query_ref, key_ref, value_ref = refs[:5]
    weights, first_ref = refs[5:8], refs[8]
    chips = blk // CORES
    early, packed = refs[9 : 9 + chips], refs[9 + chips : 9 + 2 * chips]
    rest = refs[9 + 2 * chips :]
    sum_ref, outs, early_outs = rest[0], rest[1 : 1 + count], rest[1 + count : 4 + count]
    early_sum, early_in, es, er = rest[4 + count : 8 + count]
    totals, (wide_in, key_in, value_in, fed) = rest[8 + count : 11 + count], rest[11 + count : 15 + count]
    rest = rest[15 + count :]
    weight_in, early_here, loaded = rest[:3], rest[3 : 3 + chips], rest[3 + chips]
    rest = rest[4 + chips :]
    extra = count
    held, from_core, rest = rest[: count + 1], rest[count + 1 : 2 * count + 1], rest[2 * count + 1 :]
    from_chip, from_line, rest = rest[: count + 1], rest[count + 1 : 2 * count + 2], rest[2 * count + 2 :]
    frame, arrived, aside = rest[:3]
    load, ss, sr, cs, cr, zs, zr, us, ur, ds, dr, ns, nr, fs, fr = rest[3:]
    grads = (small_ref,) + tuple(totals)
    h, b = lax.axis_index("head"), lax.axis_index("blk")
    chip, core = b // CORES, b % CORES
    sibling = chip * CORES + 1 - core
    chunk_rows = sum_ref.shape[0]
    rows = chunk_rows // PIECES_BACK

    feed_rows = wide_in.shape[1]
    halves = chunk_rows // feed_rows
    slots = 1 + 2 * REACH

    def slot_at(n):
        slot = REACH
        for hh in range(LINE):
            for k in range(slots):
                slot = jnp.where((h == hh) & (n == k), WORK_ORDER[hh][k], slot)
        return slot

    def feed(slot, half):
        some = pl.ds(slot * chunk_rows + half * feed_rows, feed_rows)
        return [
            pltpu.make_async_copy(source.at[some], target.at[half], fed.at[n, half])
            for n, (source, target) in enumerate(
                ((wide_ref, wide_in), (key_ref, key_in), (value_ref, value_in))
            )
        ]

    def feed_queries(half):
        some = pl.ds(half * feed_rows, feed_rows)
        wide_some = pl.ds(REACH * chunk_rows + half * feed_rows, feed_rows)
        return [
            pltpu.make_async_copy(wide_ref.at[wide_some], wide_in.at[half], fed.at[0, half]),
            pltpu.make_async_copy(query_ref.at[some], key_in.at[half], fed.at[1, half]),
        ]

    def start(copies):
        for copy in copies:
            copy.start()

    def wait(copies):
        for copy in copies:
            copy.wait()

    def standing():
        pairs = list(zip(weights, weight_in)) + list(zip(early, early_here)) + [(first_ref, sum_ref)]
        return [
            pltpu.make_async_copy(source, target, loaded.at[n])
            for n, (source, target) in enumerate(pairs)
        ]

    def add_product(total, left, right, fresh):
        half = left.shape[1] // 2
        for n in range(2):
            lines = LINE // 2
            part = mm_tn(left[:, n * half : (n + 1) * half], right)
            part = part.reshape((lines,) + total.shape[1:])
            here = pl.ds(n * lines, lines)
            total[here] = part if fresh else total[here] + part

    def work(n, carry):
        slot = slot_at(n)
        for half in range(halves):
            if half + 1 < halves:
                start(feed(slot, half + 1))
            else:

                @pl.when(n + 1 < slots)
                def _():
                    start(feed(slot_at(n + 1), 0))

            wait(feed(slot, half))
            for t in range(feed_rows // ROWS):
                s = pl.ds(t * ROWS, ROWS)
                grad = mm_nt(key_in[half, s], weight_in[1][...]) + mm_nt(
                    value_in[half, s], weight_in[2][...]
                )
                frame[slot, pl.ds(half * feed_rows + t * ROWS, ROWS)] = grad.astype(bf16)
            add_product(totals[1], wide_in[half], key_in[half], False)
            add_product(totals[2], wide_in[half], value_in[half], False)
        for hh in range(LINE):
            for k in range(slots):
                pl.when((h == hh) & (n == k))(partial(send_off, hh, WORK_ORDER[hh][k]))
        return carry

    def query_work():
        start(feed_queries(0))
        for half in range(halves):
            if half + 1 < halves:
                start(feed_queries(half + 1))
            wait(feed_queries(half))
            for t in range(feed_rows // ROWS):
                s = pl.ds(t * ROWS, ROWS)
                here = pl.ds(half * feed_rows + t * ROWS, ROWS)
                sum_ref[here] += mm_nt(key_in[half, s], weight_in[0][...])
            add_product(totals[0], wide_in[half], key_in[half], half == 0)

    def mine(a, k):
        return pltpu.make_async_copy(grads[a].at[:, k * CORES + core], held[a].at[k], load.at[a, k])

    def mine_packed(e):
        target = held[extra].at[(chip + e) % chips]
        return pltpu.make_async_copy(packed[e], target, load.at[extra, e])

    def across(a, k):
        return remote(
            grads[a].at[:, k * CORES + 1 - core],
            from_core[a].at[k],
            ss.at[a, k],
            sr.at[a, k],
            h,
            sibling,
        )

    def over(a, e):
        k = (chip + e) % chips
        return remote(
            held[a].at[k],
            from_chip[a].at[e - 1],
            cs.at[a, e - 1],
            cr.at[a, e - 1],
            h,
            k * CORES + core,
        )

    def along(a, d):
        there = (h + d) % LINE
        return remote(
            held[a].at[chip, there],
            from_line[a].at[d - 1],
            zs.at[a, d - 1],
            zr.at[a, d - 1],
            there,
            b,
        )

    def add_cores(a, k):
        def one(n, carry):
            own = held[a][k, n] if a == 0 else grads[a][n, k * CORES + core]
            held[a][k, n] = (own + from_core[a][k, n]).astype(held[a].dtype)
            return carry

        lax.fori_loop(0, LINE, one, 0)

    def to_chips(a):
        for k in range(chips):
            if a == 0:
                mine(a, k).wait()
            across(a, k).wait_recv()
        for e in range(1, chips):
            add_cores(a, (chip + e) % chips)
            over(a, e).start()
        add_cores(a, chip)

    def to_line(a):
        for e in range(1, chips):
            over(a, e).wait_recv()

        def one(n, carry):
            total = held[a][chip, n].astype(f32)
            for e in range(1, chips):
                total = total + from_chip[a][e - 1, n].astype(f32)
            held[a][chip, n] = total.astype(held[a].dtype)
            return carry

        lax.fori_loop(0, LINE, one, 0)
        for d in range(1, LINE):
            along(a, d).start()

    def to_owner(a):
        for d in range(1, LINE):
            along(a, d).wait_recv()
        total = held[a][chip, h].astype(f32)
        for d in range(1, LINE):
            total = total + from_line[a][d - 1].astype(f32)
        outs[a][...] = total

    def early_along(d):
        there = (h + d) % LINE
        return remote(
            early_sum.at[there], early_in.at[d - 1], es.at[d - 1], er.at[d - 1], there, b
        )

    def early_to_line():
        def one(n, carry):
            total = early_here[0][n].astype(f32)
            for ref in early_here[1:]:
                total = total + ref[n].astype(f32)
            early_sum[n] = total.astype(bf16)
            return carry

        lax.fori_loop(0, LINE, one, 0)
        for d in range(1, LINE):
            early_along(d).start()

    def early_to_owner():
        for d in range(1, LINE):
            early_along(d).wait_recv()
        total = early_sum[h].astype(f32)
        for d in range(1, LINE):
            total = total + early_in[d - 1].astype(f32)
        attn_ref, inner_ref, outer_ref = early_outs
        inner_ref[:, 3 * 768 :] = total[:24]
        outer_ref[...] = total[32:]
        for d in range(1, LINE):
            along(extra, d).wait_recv()
        total = held[extra][chip, h].astype(f32)
        for d in range(1, LINE):
            total = total + from_line[extra][d - 1].astype(f32)
        attn_ref[...] = total[:24]
        for n in range(3):
            inner_ref[:, n * 768 : (n + 1) * 768] = total[24 * (n + 1) : 24 * (n + 2)]

    def part(p):
        return pl.ds(p * rows, rows)

    def piece(ref, p):
        return ref.at[part(p)]

    def add_rows(target, j, source, n, p):
        def one(step, carry):
            some = pl.ds(p * rows + step * 64, 64)
            target[j, some] = (
                target[j, some].astype(f32) + source[n, some].astype(f32)
            ).astype(target.dtype)
            return carry

        lax.fori_loop(0, rows // 64, one, 0)

    def slot_of(hh, j):
        slot = 2 + j - hh
        return slot if 0 <= slot < slots else slots

    def arrival(hh, j, upward):
        return arrived.at[LINE if j == hh and not upward else j]

    def up(hh, j, p):
        return remote(
            piece(frame.at[slot_of(hh, j)], p),
            piece(arrival(hh + 1, j, True), p),
            us.at[j, p],
            ur.at[j, p],
            (h + 1) % LINE,
            b,
        )

    def up_arrives(hh, j, p):
        here = piece(arrival(hh, j, True), p)
        return remote(here, here, us.at[j, p], ur.at[j, p], (h + 1) % LINE, b)

    def down(hh, j, p):
        return remote(
            piece(frame.at[slot_of(hh, j)], p),
            piece(arrival(hh - 1, j, False), p),
            ds.at[j, p],
            dr.at[j, p],
            (h + 3) % LINE,
            b,
        )

    def down_arrives(hh, j, p):
        here = piece(arrival(hh, j, False), p)
        return remote(here, here, ds.at[j, p], dr.at[j, p], (h + 3) % LINE, b)

    def side_parts(hh):
        near, far = (3, 2) if hh < 2 else (0, 1)
        found = [(NEAR_SLOT[hh], near, 0, ns, nr)]
        if FAR_SLOT[hh] is not None:
            found.append((FAR_SLOT[hh], far, 1, fs, fr))
        return found

    def side(hh, slot, n, send, recv, p):
        target = (b + blk - 1) % blk if hh < 2 else (b + 1) % blk
        return remote(
            piece(frame.at[slot], p), piece(aside.at[n], p), send.at[p], recv.at[p], h, target
        )

    def sends_side(hh):
        return b > 0 if hh < 2 else b < blk - 1

    def gets_side(hh):
        return b < blk - 1 if hh < 2 else b > 0

    def send_off(hh, slot):
        @pl.when(sends_side(hh))
        def _():
            for p in range(PIECES_BACK):
                for side_slot, _, n, send, recv in side_parts(hh):
                    if side_slot == slot:
                        side(hh, slot, n, send, recv, p).start()

        for p in range(PIECES_BACK):
            if hh == 0 and slot == slot_of(0, 1):
                up(hh, 1, p).start()
            if hh == LINE - 1 and slot == slot_of(LINE - 1, 2):
                down(hh, 2, p).start()

    def take_sides(hh):
        for p in range(PIECES_BACK):
            for _, j, n, send, recv in side_parts(hh):

                @pl.when(gets_side(hh))
                def _(j=j, n=n, send=send, recv=recv):
                    here = piece(aside.at[n], p)
                    remote(here, here, send.at[p], recv.at[p], h, (b + 1) % blk).wait_recv()
                    add_rows(frame, slot_of(hh, j), aside, n, p)

                if hh == 0:
                    up(hh, j, p).start()
                if hh == LINE - 1:
                    down(hh, j, p).start()

    def pass_on(hh):
        moves = []
        if hh == 1:
            moves = [(3, True), (2, True), (0, False)]
        if hh == 2:
            moves = [(0, False), (1, False), (3, True)]
        for p in range(PIECES_BACK):
            for j, upward in moves:
                (up_arrives if upward else down_arrives)(hh, j, p).wait_recv()
                add_rows(frame, slot_of(hh, j), arrived, j, p)
                (up if upward else down)(hh, j, p).start()

    def finish(hh):
        for p in range(PIECES_BACK):
            sources = []
            if hh > 0:
                up_arrives(hh, hh, p).wait_recv()
                sources.append(hh)
            if hh < LINE - 1:
                down_arrives(hh, hh, p).wait_recv()
                sources.append(LINE)

            def one(step, carry, p=p, sources=tuple(sources)):
                some = pl.ds(p * rows + step * 64, 64)
                total = sum_ref[some] + frame[REACH, some].astype(f32)
                for n in sources:
                    total = total + arrived[n, some].astype(f32)
                sum_ref[some] = total
                return carry

            lax.fori_loop(0, rows // 64, one, 0)
        for p in range(PIECES_BACK):
            for j in range(LINE):
                if j > hh:
                    up(hh, j, p).wait_send()
                if j < hh:
                    down(hh, j, p).wait_send()

        @pl.when(sends_side(hh))
        def _():
            for p in range(PIECES_BACK):
                for slot, _, n, send, recv in side_parts(hh):
                    side(hh, slot, n, send, recv, p).wait_send()

    start(feed(slot_at(0), 0))
    start(standing())
    for k in range(chips):
        mine(0, k).start()
        mine_packed(k).start()
    frame[slots] = jnp.zeros(frame.shape[1:], frame.dtype)
    for n in (1, 2):
        totals[n][...] = jnp.zeros_like(totals[n])
    greet_plane_and_line(h, b, blk)
    wait(standing())
    early_to_line()
    lax.fori_loop(0, slots, work, 0)
    query_work()
    for e in range(chips):
        mine_packed(e).wait()
    for e in range(1, chips):
        over(extra, e).start()
    for a in range(count):
        for k in range(chips):
            across(a, k).start()
    at_each_head(h, take_sides)
    for a in range(count):
        to_chips(a)
    at_each_head(h, pass_on)
    for a in range(count + 1):
        to_line(a)
    at_each_head(h, finish)
    early_to_owner()
    for d in range(1, LINE):
        early_along(d).wait_send()
    for a in range(count):
        to_owner(a)
    for a in range(count):
        for k in range(chips):
            across(a, k).wait_send()
    for a in range(count + 1):
        for e in range(1, chips):
            over(a, e).wait_send()
        for d in range(1, LINE):
            along(a, d).wait_send()


def reduce_to_owners(small, wide, projected, weights, first, early, packed, blk):
    rows, width = first.shape
    count, chips = 4, blk // CORES
    anywhere = pl.BlockSpec(memory_space=pl.ANY)
    inside = pl.BlockSpec(memory_space=pltpu.VMEM)
    dma = pltpu.SemaphoreType.DMA
    square = (width // (LINE * blk), width)
    shard = [small.shape[2:]] + [square] * 3
    kinds = [f32] + [bf16] * 4
    travels = shard + [packed[0].shape[1:]]
    early_shapes = ((24, 768), (24, 3072), (96, 768))
    outs = pl.pallas_call(
        partial(reduce_kernel, blk, count),
        out_shape=[jax.ShapeDtypeStruct((rows, width), f32)]
        + [jax.ShapeDtypeStruct(s, f32) for s in shard]
        + [jax.ShapeDtypeStruct(s, f32) for s in early_shapes],
        in_specs=[anywhere] * (9 + 2 * chips),
        out_specs=[inside] * (4 + count),
        scratch_shapes=[
            pltpu.VMEM(early[0].shape, bf16),
            pltpu.VMEM((LINE - 1,) + early[0].shape[1:], bf16),
            dma((LINE - 1,)),
            dma((LINE - 1,)),
        ]
        + [pltpu.VMEM((LINE, blk) + square, f32)] * 3
        + [pltpu.VMEM((2, rows // 2, width), bf16)] * 3
        + [dma((3, 2))]
        + [pltpu.VMEM((width, width), bf16)] * 3
        + [pltpu.VMEM(early[0].shape, bf16)] * chips
        + [dma((4 + chips,))]
        + [pltpu.VMEM((chips, LINE) + s, t) for s, t in zip(travels, kinds)]
        + [pltpu.VMEM((chips, LINE) + s, f32) for s in shard]
        + [pltpu.VMEM((chips - 1, LINE) + s, t) for s, t in zip(travels, kinds)]
        + [pltpu.VMEM((LINE - 1,) + s, t) for s, t in zip(travels, kinds)]
        + [
            pltpu.VMEM((2 + 2 * REACH, rows, width), bf16),
            pltpu.VMEM((LINE + 1, rows, width), bf16),
            pltpu.VMEM((2, rows, width), bf16),
        ]
        + [dma((count + 1, chips))] * 3
        + [dma((count + 1, chips - 1))] * 2
        + [dma((count + 1, LINE - 1))] * 2
        + [dma((LINE, PIECES_BACK))] * 4
        + [dma((PIECES_BACK,))] * 4,
        compiler_params=pltpu.CompilerParams(
            collective_id=1, has_side_effects=True, vmem_limit_bytes=62 << 20
        ),
        name="reduce_to_owners",
    )(small, wide, *projected, *weights, first, *early, *packed)
    return outs[0], outs[1:-3], outs[-3:]


def whole(shard):
    return lax.all_gather(shard, ("head", "blk"), axis=0, tiled=True)


def shared_out(grad):
    return lax.psum_scatter(grad.astype(bf16), ("head", "blk"), scatter_dimension=0, tiled=True).astype(f32)


def padded_to(flat, size):
    return jnp.pad(flat, [(0, 0)] * (flat.ndim - 1) + [(0, size - flat.shape[-1])])


def per_device(blk, head, tokens, *rest):
    weights, vectors, (out_grad, segment_ids, random_blocks) = rest[:6], rest[6:15], rest[15:]
    rows = tokens.shape[0]
    by_kernel = head == LINE and blk == LINE * CORES
    short = [vectors[n] for n in (2, 3, 4, 6, 7, 8, 0, 1)]
    if by_kernel:
        packed = jnp.concatenate(
            [
                padded_to(jnp.stack(short), 128),
                padded_to(vectors[5][None], 128),
                jnp.zeros((7, 128), bf16),
            ]
        )
        wide, fulls = gather(tokens, [packed] + list(weights), blk)
        wide = wide.reshape(-1, tokens.shape[1])
        w_query, w_key, w_value, w_attn, w_inner, w_outer = [
            w.reshape(-1, w.shape[-1]) for w in fulls[1:]
        ]
        table = fulls[0].reshape(head * blk, 16, 128)
    else:
        wide = widen(tokens, blk, head)
        w_query, w_key, w_value, w_attn, w_inner, w_outer = [whole(w) for w in weights]
        packed = jnp.concatenate(
            [padded_to(jnp.stack(short), 128), padded_to(vectors[5][None], 128)]
        )
        table = whole(packed[None])
    short_rows = jnp.transpose(table[:, :8, : short[0].shape[0]], (1, 0, 2)).astype(f32)
    short_rows = short_rows.reshape(8, -1)
    bias_inner = table[:, 8, : vectors[5].shape[0]].astype(f32).reshape(-1, 1, PIECE)

    rows_of, bases, docs = tile_plan(segment_ids, random_blocks, rows)
    keys, values, queries = project(wide, w_key, w_value, w_query, short_rows, rows)
    attended, probs = attend(rows_of, queries, keys, values, bases, docs)

    result, grad_first_sum, grad_attended, grad_w_attn, grad_w_inner, grad_w_outer, sums_d, sums_ff = (
        middle(
            attended,
            tokens,
            out_grad,
            w_attn,
            w_inner,
            w_outer,
            short_rows,
            bias_inner,
        )
    )

    early_grads = [grad_w_attn, grad_w_inner, grad_w_outer]
    if by_kernel:
        halves, early = pair_sums([g.reshape(head, blk, -1, g.shape[-1]) for g in early_grads], blk)
        early = over_plane(early, blk, head)
    grad_scaled, grad_keyed, grad_valued, sums_qv = attend_back(
        rows_of, queries, grad_attended, keys, values, probs
    )
    sums = jnp.concatenate([sums_d[:6], sums_qv[6:]])
    sums = jnp.transpose(sums.reshape(8, head * blk, -1), (1, 0, 2))
    packed = jnp.concatenate(
        [
            padded_to(sums, 128),
            padded_to(sums_ff.reshape(head * blk, 1, -1), 128),
            jnp.zeros((head * blk, 7, 128), f32),
        ],
        axis=1,
    )
    if by_kernel:
        grad_tokens, late, early_sum = reduce_to_owners(
            packed.reshape(head, blk, 16, 128),
            wide,
            (grad_scaled, grad_keyed, grad_valued),
            (w_query, w_key, w_value),
            grad_first_sum,
            early,
            halves,
            blk,
        )
        matrix_grads = tuple(late[1:]) + tuple(early_sum)
        packed = late[0]
    else:
        grad_wide = (mm_nt(grad_keyed, w_key) + mm_nt(grad_valued, w_value)).astype(bf16)
        grad_tokens = (
            grad_first_sum
            + mm_nt(grad_scaled, w_query)
            + narrow(grad_wide, rows, blk, head).astype(f32)
        )
        late_grads = [mm_tn(tokens, grad_scaled), mm_tn(wide, grad_keyed), mm_tn(wide, grad_valued)]
        matrix_grads = tuple(shared_out(g) for g in late_grads + early_grads)
        packed = lax.psum_scatter(packed, ("head", "blk"), scatter_dimension=0, tiled=True)[0]
    order = (6, 7, 0, 1, 2, 8, 3, 4, 5)
    vector_grads = tuple(packed[n, : v.shape[0]] for n, v in zip(order, vectors))
    return (result, grad_tokens) + matrix_grads + vector_grads


def solution(mesh):
    row = P(("blk", "head"), None)
    matrix = P(("head", "blk"), None)
    vector = P(("head", "blk"))
    return jax.shard_map(
        partial(per_device, mesh.shape["blk"], mesh.shape["head"]),
        mesh=mesh,
        in_specs=(row,) + (matrix,) * 6 + (vector,) * 9 + (row, P(), P()),
        out_specs=(row, row) + (matrix,) * 6 + (vector,) * 9,
        check_vma=False,
    )
```

```python
from functools import partial

import jax
import jax.numpy as jnp
from jax import lax
from jax.experimental import pallas as pl
from jax.experimental.pallas import tpu as pltpu
from jax.sharding import PartitionSpec as P

HEAD_DIM = 64
BLOCK = 64
RANDOM = 3
TILES = 5 + RANDOM
REACH = 2
GROUP = 4
FORWARD_BLOCKS = 8
BACKWARD_BLOCKS = 8
ROWS = 256
PIECE = 768

epsilon = 1e-06
masked_value = -1e30
query_scale = 0.125
gelu_scale = 0.7978845608028654
gelu_cubic = 0.044715
far_away = -(1 << 24)
f32, bf16 = jnp.float32, jnp.bfloat16


def mm(a, b):
    return jnp.dot(a, b, preferred_element_type=f32)


def mm_nt(a, b):
    return lax.dot_general(a, b, (((1,), (1,)), ((), ())), preferred_element_type=f32)


def mm_tn(a, b):
    return lax.dot_general(a, b, (((0,), (0,)), ((), ())), preferred_element_type=f32)


def head_mask(rows, cols, first):
    lanes = lax.broadcasted_iota(jnp.int32, (rows, cols), 1)
    return (lanes >= first) & (lanes < first + HEAD_DIM)


def stacked_by_head(tile):
    rows, cols = tile.shape
    return jnp.concatenate(
        [
            jnp.where(head_mask(rows, cols, h * HEAD_DIM), tile, jnp.zeros_like(tile))
            for h in range(cols // HEAD_DIM)
        ],
        axis=0,
    )


def own_head_columns(stacked):
    cols = stacked.shape[1]
    total = None
    for h in range(cols // HEAD_DIM):
        part = stacked[h * BLOCK : (h + 1) * BLOCK]
        part = jnp.where(head_mask(BLOCK, cols, h * HEAD_DIM), part, 0.0)
        total = part if total is None else total + part
    return total


def block_rows(row):
    return pl.ds(pl.multiple_of(row * BLOCK, BLOCK), BLOCK)


def gathered(table_ref, fixed_row, random_row):
    tiles = [table_ref[block_rows(fixed_row(t)), :] for t in range(5)]
    low = head_mask(BLOCK, 2 * HEAD_DIM, 0)
    for t in range(RANDOM):
        halves = []
        for pair in range(GROUP // 2):
            cols = pl.ds(pair * 2 * HEAD_DIM, 2 * HEAD_DIM)
            a = table_ref[block_rows(random_row(2 * pair, t)), cols]
            b = table_ref[block_rows(random_row(2 * pair + 1, t)), cols]
            halves.append(jnp.where(low, a, b))
        tiles.append(jnp.concatenate(halves, axis=1))
    return jnp.concatenate(tiles, axis=0)


def row_readers(rows_ref, blocks, i):
    group = pl.program_id(0)

    def fixed_row(t):
        return rows_ref[(group * GROUP * blocks + i) * TILES + t]

    def random_row(h, t):
        return rows_ref[((group * GROUP + h) * blocks + i) * TILES + 5 + t]

    return fixed_row, random_row


def attend_kernel(blocks, rows_ref, q_ref, k_ref, v_ref, base_ref, doc_ref, out_ref, p_ref):
    within = lax.broadcasted_iota(jnp.int32, (BLOCK, GROUP * BLOCK), 0)
    for u in range(FORWARD_BLOCKS):
        here = pl.ds(u * BLOCK, BLOCK)
        readers = row_readers(rows_ref, blocks, pl.program_id(1) * FORWARD_BLOCKS + u)
        keys = gathered(k_ref, *readers)
        values = gathered(v_ref, *readers)
        scores = mm_nt(keys, stacked_by_head(q_ref[here, :]))
        lo = doc_ref[u, 0:1, :]
        hi = doc_ref[u, 1:2, :]
        masked = []
        for t in range(TILES):
            place = within + base_ref[0, u, t : t + 1, :]
            allowed = (place >= lo) & (place < hi)
            masked.append(jnp.where(allowed, scores[t * BLOCK : (t + 1) * BLOCK], masked_value))
        scores = jnp.concatenate(masked, axis=0)
        raised = jnp.exp(scores - jnp.max(scores, axis=0, keepdims=True))
        probs = (raised * (1.0 / jnp.sum(raised, axis=0, keepdims=True))).astype(bf16)
        p_ref[0, u] = probs
        out_ref[here, :] = own_head_columns(mm_tn(probs, values)).astype(bf16)


def attend_back_kernel(
    blocks,
    rows_ref,
    q_ref,
    g_ref,
    k_ref,
    v_ref,
    p_ref,
    dq_ref,
    dk_ref,
    dv_ref,
    sums_ref,
    dk_sum,
    dv_sum,
):
    step = pl.program_id(1)

    @pl.when(step == 0)
    def _():
        sums_ref[...] = jnp.zeros_like(sums_ref)
        dk_sum[...] = jnp.zeros_like(dk_sum)
        dv_sum[...] = jnp.zeros_like(dv_sum)

    found = []
    for u in range(BACKWARD_BLOCKS):
        here = pl.ds(u * BLOCK, BLOCK)
        readers = row_readers(rows_ref, blocks, step * BACKWARD_BLOCKS + u)
        keys = gathered(k_ref, *readers)
        values = gathered(v_ref, *readers)
        queries = stacked_by_head(q_ref[here, :])
        grads = stacked_by_head(g_ref[here, :])
        probs = p_ref[0, u]
        grad_probs = mm_nt(values, grads)
        wide = probs.astype(f32)
        balance = jnp.sum(wide * grad_probs, axis=0, keepdims=True)
        grad_scores = (wide * (grad_probs - balance)).astype(bf16)
        dq_ref[here, :] = (query_scale * own_head_columns(mm_tn(grad_scores, keys))).astype(bf16)
        found.append((readers, mm(grad_scores, queries), mm(probs, grads)))
    for (fixed_row, random_row), grad_keys, grad_values in found:
        for total, part in ((dk_sum, grad_keys), (dv_sum, grad_values)):
            for t in range(5):
                total[block_rows(fixed_row(t)), :] += part[t * BLOCK : (t + 1) * BLOCK]
            for t in range(RANDOM):
                rows = part[(5 + t) * BLOCK : (6 + t) * BLOCK]
                for h in range(GROUP):
                    first = (h // 2) * 2 * HEAD_DIM
                    mine = head_mask(BLOCK, 2 * HEAD_DIM, (h % 2) * HEAD_DIM)
                    total[block_rows(random_row(h, t)), pl.ds(first, 2 * HEAD_DIM)] += jnp.where(
                        mine, rows[:, first : first + 2 * HEAD_DIM], 0.0
                    )

    sums_ref[6:7, :] += jnp.sum(dq_ref[...].astype(f32), axis=0, keepdims=True)

    @pl.when(step == blocks // BACKWARD_BLOCKS - 1)
    def _():
        dk_ref[...] = dk_sum[...].astype(bf16)
        dv_ref[...] = dv_sum[...].astype(bf16)
        sums_ref[7:8, :] = jnp.sum(dv_ref[...].astype(f32), axis=0, keepdims=True)


def attend(rows, queries, keys, values, bases, docs):
    tokens, width = queries.shape
    ext = keys.shape[0]
    blocks, cols, some = tokens // BLOCK, GROUP * HEAD_DIM, FORWARD_BLOCKS
    groups = width // cols
    tile = pl.BlockSpec((some * BLOCK, cols), lambda g, i, r: (i, g))
    table = pl.BlockSpec((ext, cols), lambda g, i, r: (0, g))
    return pl.pallas_call(
        partial(attend_kernel, blocks),
        grid_spec=pltpu.PrefetchScalarGridSpec(
            num_scalar_prefetch=1,
            grid=(groups, blocks // some),
            in_specs=[
                tile,
                table,
                table,
                pl.BlockSpec((1, some, TILES, cols), lambda g, i, r: (g, i, 0, 0)),
                pl.BlockSpec((some, 8, cols), lambda g, i, r: (i, 0, 0)),
            ],
            out_specs=[
                tile,
                pl.BlockSpec((1, some, TILES * BLOCK, cols), lambda g, i, r: (g, i, 0, 0)),
            ],
        ),
        out_shape=[
            jax.ShapeDtypeStruct((tokens, width), bf16),
            jax.ShapeDtypeStruct((groups, blocks, TILES * BLOCK, cols), bf16),
        ],
        compiler_params=pltpu.CompilerParams(vmem_limit_bytes=60 << 20),
        name="attend",
    )(rows, queries, keys, values, bases, docs)


def attend_back(rows, queries, grads, keys, values, probs):
    tokens, width = queries.shape
    ext = keys.shape[0]
    blocks, cols, some = tokens // BLOCK, GROUP * HEAD_DIM, BACKWARD_BLOCKS
    groups = width // cols
    tile = pl.BlockSpec((some * BLOCK, cols), lambda g, i, r: (i, g))
    table = pl.BlockSpec((ext, cols), lambda g, i, r: (0, g))
    return pl.pallas_call(
        partial(attend_back_kernel, blocks),
        grid_spec=pltpu.PrefetchScalarGridSpec(
            num_scalar_prefetch=1,
            grid=(groups, blocks // some),
            in_specs=[
                tile,
                tile,
                table,
                table,
                pl.BlockSpec((1, some, TILES * BLOCK, cols), lambda g, i, r: (g, i, 0, 0)),
            ],
            out_specs=[tile, table, table, pl.BlockSpec((8, cols), lambda g, i, r: (0, g))],
            scratch_shapes=[pltpu.VMEM((ext, cols), f32), pltpu.VMEM((ext, cols), f32)],
        ),
        out_shape=[
            jax.ShapeDtypeStruct((tokens, width), bf16),
            jax.ShapeDtypeStruct((ext, width), bf16),
            jax.ShapeDtypeStruct((ext, width), bf16),
            jax.ShapeDtypeStruct((8, width), f32),
        ],
        compiler_params=pltpu.CompilerParams(vmem_limit_bytes=56 << 20),
        cost_estimate=pl.CostEstimate(
            flops=10 * groups * blocks * TILES * BLOCK * cols * cols,
            bytes_accessed=100 << 20,
            transcendentals=0,
        ),
        name="attend_back",
    )(rows, queries, grads, keys, values, probs)


def normalized(values):
    centred = values - jnp.mean(values, axis=-1, keepdims=True)
    root = lax.rsqrt(jnp.mean(centred * centred, axis=-1, keepdims=True) + epsilon)
    return centred * root, root


def norm_back(grad, normal, root, gain):
    scaled = grad * gain
    along = jnp.mean(scaled * normal, axis=-1, keepdims=True)
    return root * (scaled - jnp.mean(scaled, axis=-1, keepdims=True) - normal * along)


def gelu_and_slope(u):
    square = u * u
    bend = jnp.tanh(gelu_scale * (u + gelu_cubic * (square * u)))
    half = 0.5 * (1.0 + bend)
    slope = half + (0.5 * gelu_scale) * u * (1.0 - bend * bend) * (
        1.0 + (3.0 * gelu_cubic) * square
    )
    return u * half, slope


def middle_kernel(
    att_ref,
    x_ref,
    og_ref,
    wa_ref,
    wi_ref,
    wo_ref,
    vec_ref,
    bi_ref,
    res_ref,
    sum_ref,
    ga_ref,
    dwa_ref,
    dwi_ref,
    dwo_ref,
    dvec_ref,
    dbi_ref,
    normal,
    root,
    low,
    act,
    slope,
    inner,
):
    step, half = pl.program_id(0), pl.num_programs(0) // 2
    tokens, width = x_ref.shape
    slices = [pl.ds(t * ROWS, ROWS) for t in range(tokens // ROWS)]
    bias_attn, gain_one, offset_one, bias_outer, gain_two, offset_two = (
        vec_ref[n : n + 1, :] for n in range(6)
    )

    def row_sum(total, values):
        part = jnp.sum(values, axis=0, keepdims=True)
        return part if total is None else total + part

    @pl.when(step == 0)
    def _():
        for s in slices:
            values = x_ref[s, :].astype(f32) + mm(att_ref[s, :], wa_ref[...]) + bias_attn
            flat, scale = normalized(values)
            normal[s, :] = flat
            root[s, :] = jnp.broadcast_to(scale, (ROWS, 128))
            first = flat * gain_one + offset_one
            low[s, :] = first.astype(bf16)
            sum_ref[s, :] = first + bias_outer

    @pl.when(step < half)
    def _():
        for s in slices:
            active, bend = gelu_and_slope(mm(low[s, :], wi_ref[...]) + bi_ref[0])
            active = active.astype(bf16)
            act[step, s, :] = active
            slope[step, s, :] = bend.astype(bf16)
            sum_ref[s, :] += mm(active, wo_ref[...])

    @pl.when(step == half)
    def _():
        outer_sum, gain_sum, offset_sum = None, None, None
        for s in slices:
            flat, scale = normalized(sum_ref[s, :])
            res_ref[s, :] = (flat * gain_two + offset_two).astype(bf16)
            grad = og_ref[s, :].astype(f32)
            gain_sum = row_sum(gain_sum, grad * flat)
            offset_sum = row_sum(offset_sum, grad)
            second = norm_back(grad, flat, scale, gain_two)
            sum_ref[s, :] = second
            second = second.astype(bf16)
            ga_ref[s, :] = second
            outer_sum = row_sum(outer_sum, second.astype(f32))
        dvec_ref[3:4, :] = outer_sum
        dvec_ref[4:5, :] = gain_sum
        dvec_ref[5:6, :] = offset_sum
        dvec_ref[6:8, :] = jnp.zeros((2, width), f32)

    @pl.when(step >= half)
    def _():
        now = step - half
        total = None
        for s in slices:
            grad = mm_nt(ga_ref[s, :], wo_ref[...]) * slope[now, s, :].astype(f32)
            grad = grad.astype(bf16)
            inner[s, :] = grad
            total = row_sum(total, grad.astype(f32))
            sum_ref[s, :] += mm_nt(grad, wi_ref[...])
        dbi_ref[0] = total
        for n in range(width // 256):
            some = pl.ds(n * 256, 256)
            dwi_ref[some, :] = mm_tn(low[:, some], inner[...]).astype(bf16)
        for n in range(PIECE // 256):
            some = pl.ds(n * 256, 256)
            dwo_ref[some, :] = mm_tn(act[now, :, some], ga_ref[...]).astype(bf16)

    @pl.when(step == 2 * half - 1)
    def _():
        attn_sum, gain_sum, offset_sum = None, None, None
        for s in slices:
            grad, flat = sum_ref[s, :], normal[s, :]
            gain_sum = row_sum(gain_sum, grad * flat)
            offset_sum = row_sum(offset_sum, grad)
            grad = norm_back(grad, flat, root[s, 0:1], gain_one)
            sum_ref[s, :] = grad
            grad = grad.astype(bf16)
            inner[s, :width] = grad
            attn_sum = row_sum(attn_sum, grad.astype(f32))
            ga_ref[s, :] = mm_nt(grad, wa_ref[...]).astype(bf16)
        dvec_ref[0:1, :] = attn_sum
        dvec_ref[1:2, :] = gain_sum
        dvec_ref[2:3, :] = offset_sum
        for n in range(width // 256):
            some = pl.ds(n * 256, 256)
            dwa_ref[some, :] = mm_tn(att_ref[:, some], inner[:, :width]).astype(bf16)


def middle(attended, tokens, out_grad, w_attn, w_inner, w_outer, vectors, bias_inner):
    rows, width = tokens.shape
    steps = w_inner.shape[1] // PIECE
    one = pl.Buffered(1)
    still = pl.BlockSpec((rows, width), lambda i: (0, 0), pipeline_mode=one)
    square = pl.BlockSpec((width, width), lambda i: (0, 0), pipeline_mode=one)
    few = pl.BlockSpec((8, width), lambda i: (0, 0))
    later = lambda i: jnp.maximum(i - steps, 0)
    return pl.pallas_call(
        middle_kernel,
        grid=(2 * steps,),
        in_specs=[
            still,
            still,
            still,
            square,
            pl.BlockSpec((width, PIECE), lambda i: (0, i % steps)),
            pl.BlockSpec((PIECE, width), lambda i: (i % steps, 0)),
            few,
            pl.BlockSpec((1, 1, PIECE), lambda i: (i % steps, 0, 0)),
        ],
        out_specs=[
            still,
            still,
            still,
            square,
            pl.BlockSpec((width, PIECE), lambda i: (0, later(i))),
            pl.BlockSpec((PIECE, width), lambda i: (later(i), 0)),
            few,
            pl.BlockSpec((1, 1, PIECE), lambda i: (later(i), 0, 0)),
        ],
        out_shape=[
            jax.ShapeDtypeStruct((rows, width), bf16),
            jax.ShapeDtypeStruct((rows, width), f32),
            jax.ShapeDtypeStruct((rows, width), bf16),
            jax.ShapeDtypeStruct(w_attn.shape, bf16),
            jax.ShapeDtypeStruct(w_inner.shape, bf16),
            jax.ShapeDtypeStruct(w_outer.shape, bf16),
            jax.ShapeDtypeStruct((8, width), f32),
            jax.ShapeDtypeStruct((steps, 1, PIECE), f32),
        ],
        scratch_shapes=[
            pltpu.VMEM((rows, width), f32),
            pltpu.VMEM((rows, 128), f32),
            pltpu.VMEM((rows, width), bf16),
            pltpu.VMEM((steps, rows, PIECE), bf16),
            pltpu.VMEM((steps, rows, PIECE), bf16),
            pltpu.VMEM((rows, PIECE), bf16),
        ],
        compiler_params=pltpu.CompilerParams(vmem_limit_bytes=60 << 20),
        name="middle",
    )(attended, tokens, out_grad, w_attn, w_inner, w_outer, vectors, bias_inner)


def project_kernel(wide_ref, wk_ref, wv_ref, wq_ref, vec_ref, k_ref, v_ref, q_ref):
    rows = wide_ref.shape[0]
    slices = [pl.ds(t * ROWS, ROWS) for t in range(rows // ROWS)]
    for s in slices:
        k_ref[s, :] = mm(wide_ref[s, :], wk_ref[...]).astype(bf16)
        v_ref[s, :] = (mm(wide_ref[s, :], wv_ref[...]) + vec_ref[7:8, :]).astype(bf16)

    @pl.when(pl.program_id(0) == REACH)
    def _():
        for s in slices:
            queries = mm(wide_ref[s, :], wq_ref[...]) + vec_ref[6:7, :]
            q_ref[s, :] = (query_scale * queries).astype(bf16)


def project(wide, w_key, w_value, w_query, vectors, rows):
    width = wide.shape[1]
    one = pl.Buffered(1)
    tile = pl.BlockSpec((rows, width), lambda i: (i, 0))
    still = pl.BlockSpec((rows, width), lambda i: (0, 0), pipeline_mode=one)
    square = pl.BlockSpec((width, width), lambda i: (0, 0), pipeline_mode=one)
    table = jax.ShapeDtypeStruct(wide.shape, bf16)
    return pl.pallas_call(
        project_kernel,
        grid=(1 + 2 * REACH,),
        in_specs=[tile, square, square, square, pl.BlockSpec((8, width), lambda i: (0, 0))],
        out_specs=[tile, tile, still],
        out_shape=[table, table, jax.ShapeDtypeStruct((rows, width), bf16)],
        compiler_params=pltpu.CompilerParams(vmem_limit_bytes=60 << 20),
        name="project",
    )(wide, w_key, w_value, w_query, vectors)


def tile_plan(segment_ids, random_blocks, tokens):
    heads, total_blocks, _ = random_blocks.shape
    blocks = tokens // BLOCK
    chunk = lax.axis_index("blk") * lax.axis_size("head") + lax.axis_index("head")
    margin = REACH * tokens
    padded = jnp.concatenate(
        [
            jnp.full((margin,), -1, jnp.int32),
            segment_ids,
            jnp.full((margin,), jnp.iinfo(jnp.int32).max, jnp.int32),
        ]
    )
    near = lax.dynamic_slice_in_dim(padded, chunk * tokens, tokens + 2 * margin)
    own = near[margin : margin + tokens]
    before, after = near[: margin + tokens], near[margin:]
    begins = jnp.sum((before[None, :] < own[:, None]).astype(jnp.int32), axis=1)
    ends = margin + jnp.sum((after[None, :] <= own[:, None]).astype(jnp.int32), axis=1)
    docs = jnp.stack([begins, ends]).reshape(2, blocks, BLOCK)
    docs = jnp.tile(jnp.transpose(docs, (1, 0, 2)), (1, 4, GROUP))
    first = begins[::BLOCK] // BLOCK
    here = REACH * blocks + jnp.arange(blocks, dtype=jnp.int32)
    fixed = jnp.stack([here - 1, here, here + 1, first, first + 1], axis=-1)
    picked = lax.dynamic_slice_in_dim(random_blocks, chunk * blocks, blocks, axis=1)
    picked = picked - (chunk - REACH) * blocks
    rows = jnp.concatenate(
        [jnp.broadcast_to(fixed[None], (heads, blocks, 5)), picked], axis=-1
    )
    earlier = jnp.arange(TILES)[None, :] < jnp.arange(TILES)[:, None]
    repeat = jnp.any((rows[..., :, None] == rows[..., None, :]) & earlier, axis=-1)
    bases = jnp.where(repeat, far_away, rows * BLOCK)
    rows = jnp.clip(rows, 0, (1 + 2 * REACH) * blocks - 1)
    bases = bases.reshape(heads // GROUP, GROUP, blocks, TILES)
    bases = jnp.repeat(jnp.transpose(bases, (0, 2, 3, 1)), BLOCK, axis=-1)
    return rows.reshape(-1), bases, docs


def side_pairs(blk, head, far):
    pairs = []
    for b in range(blk):
        for h in range(head):
            down = h < head // 2
            if far and h not in (0, head - 1):
                continue
            source = b - 1 if down else b + 1
            if 0 <= source < blk:
                pairs.append((h * blk + source, h * blk + b))
    return pairs


def widen(tokens_rows, blk, head):
    rows = tokens_rows.shape[0]
    h = lax.axis_index("head")
    line = lax.all_gather(tokens_rows, "head", axis=0, tiled=True)
    low = h < head // 2
    near = lax.dynamic_slice_in_dim(line, jnp.where(low, head - 1, 0) * rows, rows)
    far = lax.dynamic_slice_in_dim(line, jnp.where(low, head - 2, 1) * rows, rows)
    near = lax.ppermute(near, ("head", "blk"), side_pairs(blk, head, False))
    far = lax.ppermute(far, ("head", "blk"), side_pairs(blk, head, True))
    whole = jnp.concatenate([far, near, line, near, far], axis=0)
    return lax.dynamic_slice_in_dim(whole, h * rows, (1 + 2 * REACH) * rows)


def narrow(wide_rows, rows, blk, head):
    h = lax.axis_index("head")
    low = h < head // 2
    frame = jnp.zeros(((head + 2 * REACH) * rows, wide_rows.shape[1]), wide_rows.dtype)
    frame = lax.dynamic_update_slice_in_dim(frame, wide_rows, h * rows, 0)
    near = lax.dynamic_slice_in_dim(frame, jnp.where(low, 1, head + REACH) * rows, rows)
    far = lax.dynamic_slice_in_dim(frame, jnp.where(low, 0, head + REACH + 1) * rows, rows)
    back = [(t, s) for s, t in side_pairs(blk, head, False)]
    near = lax.ppermute(near, ("head", "blk"), back)
    back = [(t, s) for s, t in side_pairs(blk, head, True)]
    far = lax.ppermute(far, ("head", "blk"), back)
    line = frame[REACH * rows : (REACH + head) * rows].reshape(head, rows, -1)
    place = jnp.arange(head, dtype=jnp.int32)[:, None, None]
    line = line + jnp.where(place == jnp.where(low, head - 1, 0), near[None], 0)
    line = line + jnp.where(place == jnp.where(low, head - 2, 1), far[None], 0)
    return lax.psum_scatter(line.reshape(head * rows, -1), "head", scatter_dimension=0, tiled=True)


LINE = 4
CORES = 2
PIECES = 4
PIECES_BACK = 8
MESH = pl.DeviceIdType.MESH
NEAR_SLOT = (1, 0, 4, 3)
FAR_SLOT = (0, None, None, 4)
WORK_ORDER = ((3, 1, 0, 4, 2), (0, 4, 3, 1, 2), (4, 0, 1, 3, 2), (1, 3, 4, 0, 2))


def remote(source, target, send, recv, head, blk):
    return pltpu.make_async_remote_copy(
        src_ref=source,
        dst_ref=target,
        send_sem=send,
        recv_sem=recv,
        device_id=(head, blk),
        device_id_type=MESH,
    )


def at_each_head(h, body):
    for hh in range(LINE):
        pl.when(h == hh)(partial(body, hh))


def greet_plane_and_line(h, b, blk):
    barrier = pltpu.get_barrier_semaphore()
    for d in range(1, LINE):
        pl.semaphore_signal(
            barrier, inc=1, device_id=((h + d) % LINE, b), device_id_type=MESH
        )
    for d in range(1, blk):
        pl.semaphore_signal(barrier, inc=1, device_id=(h, (b + d) % blk), device_id_type=MESH)
    pl.semaphore_wait(barrier, LINE - 1 + blk - 1)


def gather_kernel(blk, count, *refs):
    x_ref, shards = refs[0], refs[1 : 1 + count]
    wide, spill, fulls = refs[1 + count], refs[2 + count], refs[3 + count : 3 + 2 * count]
    local, zs, zr, cs, cr, ss, sr, us, ur, ds, dr, ns, nr, fs, fr = refs[3 + 2 * count :]
    h, b = lax.axis_index("head"), lax.axis_index("blk")
    chips = blk // CORES
    chip, core = b // CORES, b % CORES
    sibling = chip * CORES + 1 - core
    rows = x_ref.shape[0] // PIECES

    def piece(ref, p):
        return ref.at[pl.ds(p * rows, rows)]

    def place(hh, j):
        slot = 2 + j - hh
        return wide.at[slot] if 0 <= slot < 5 else spill

    def own(a):
        return pltpu.make_async_copy(shards[a], fulls[a].at[h, b], local.at[a])

    def along(a, d):
        return remote(
            shards[a], fulls[a].at[h, b], zs.at[a, d - 1], zr.at[a, d - 1], (h + d) % LINE, b
        )

    def along_arrives(a, d):
        src = (h - d + LINE) % LINE
        return remote(
            shards[a], fulls[a].at[src, b], zs.at[a, d - 1], zr.at[a, d - 1], (h + d) % LINE, b
        )

    def over(a, e):
        part = fulls[a].at[:, b]
        there = ((chip + e) % chips) * CORES + core
        return remote(part, part, cs.at[a, e - 1], cr.at[a, e - 1], h, there)

    def over_arrives(a, e):
        there = ((chip - e + chips) % chips) * CORES + core
        part = fulls[a].at[:, there]
        return remote(part, part, cs.at[a, e - 1], cr.at[a, e - 1], h, there)

    def across(a, e):
        part = fulls[a].at[:, ((chip - e + chips) % chips) * CORES + core]
        return remote(part, part, ss.at[a, e], sr.at[a, e], h, sibling)

    def across_arrives(a, e):
        part = fulls[a].at[:, ((chip - e + chips) % chips) * CORES + 1 - core]
        return remote(part, part, ss.at[a, e], sr.at[a, e], h, sibling)

    def spread(a):
        for d in range(1, LINE):
            along_arrives(a, d).wait_recv()
        own(a).wait()
        for e in range(1, chips):
            over(a, e).start()
        across(a, 0).start()

    def hand_over(a):
        for e in range(1, chips):
            over_arrives(a, e).wait_recv()
            across(a, e).start()

    def up(hh, j, p):
        source = x_ref if j == hh else place(hh, j)
        return remote(
            piece(source, p), piece(place(hh + 1, j), p), us.at[j, p], ur.at[j, p], (h + 1) % LINE, b
        )

    def up_arrives(hh, j, p):
        target = piece(place(hh, j), p)
        return remote(target, target, us.at[j, p], ur.at[j, p], (h + 1) % LINE, b)

    def down(hh, j, p):
        source = x_ref if j == hh else place(hh, j)
        return remote(
            piece(source, p), piece(place(hh - 1, j), p), ds.at[j, p], dr.at[j, p], (h + 3) % LINE, b
        )

    def down_arrives(hh, j, p):
        target = piece(place(hh, j), p)
        return remote(target, target, ds.at[j, p], dr.at[j, p], (h + 3) % LINE, b)

    def sides(hh, j):
        near, far = (3, 2) if hh < 2 else (0, 1)
        if j == near:
            return [(NEAR_SLOT[hh], ns, nr)]
        if j == far and FAR_SLOT[hh] is not None:
            return [(FAR_SLOT[hh], fs, fr)]
        return []

    def side(hh, j, p, slot, send, recv):
        target = (b + 1) % blk if hh < 2 else (b + blk - 1) % blk
        return remote(
            piece(place(hh, j), p), piece(wide.at[slot], p), send.at[p], recv.at[p], h, target
        )

    def sends_side(hh):
        return b < blk - 1 if hh < 2 else b > 0

    def gets_side(hh):
        return b > 0 if hh < 2 else b < blk - 1

    def side_slots(hh):
        found = [(NEAR_SLOT[hh], ns, nr)]
        if FAR_SLOT[hh] is not None:
            found.append((FAR_SLOT[hh], fs, fr))
        return found

    def fill(n, slot):
        return pltpu.make_async_copy(x_ref, wide.at[slot], local.at[count + 1 + n])

    def own_rows():
        return pltpu.make_async_copy(x_ref, wide.at[2], local.at[count])

    def begin(hh):
        for p in range(PIECES):
            if hh < LINE - 1:
                up(hh, hh, p).start()
            if hh > 0:
                down(hh, hh, p).start()

        @pl.when(jnp.logical_not(gets_side(hh)))
        def _():
            for n, (slot, _, _) in enumerate(side_slots(hh)):
                fill(n, slot).start()

    def pass_on(distance, hh):
        for p in range(PIECES):
            for j, arrives, onward, ends in (
                (hh - distance, up_arrives, up, hh == LINE - 1),
                (hh + distance, down_arrives, down, hh == 0),
            ):
                if not 0 <= j < LINE:
                    continue
                arrives(hh, j, p).wait_recv()
                if not ends:
                    onward(hh, j, p).start()
                for slot, send, recv in sides(hh, j):

                    @pl.when(sends_side(hh))
                    def _(slot=slot, send=send, recv=recv):
                        side(hh, j, p, slot, send, recv).start()

    def finish(hh):
        for p in range(PIECES):
            for j in range(LINE):
                if j <= hh < LINE - 1:
                    up(hh, j, p).wait_send()
                if j >= hh > 0:
                    down(hh, j, p).wait_send()

        @pl.when(sends_side(hh))
        def _():
            for j in range(LINE):
                for slot, send, recv in sides(hh, j):
                    for p in range(PIECES):
                        side(hh, j, p, slot, send, recv).wait_send()

        @pl.when(gets_side(hh))
        def _():
            for slot, send, recv in side_slots(hh):
                for p in range(PIECES):
                    target = piece(wide.at[slot], p)
                    remote(target, target, send.at[p], recv.at[p], h, (b + 1) % blk).wait_recv()

        @pl.when(jnp.logical_not(gets_side(hh)))
        def _():
            for n, (slot, _, _) in enumerate(side_slots(hh)):
                fill(n, slot).wait()

    own_rows().start()
    for a in range(count):
        own(a).start()
    greet_plane_and_line(h, b, blk)
    for a in range(count):
        for d in range(1, LINE):
            along(a, d).start()
    at_each_head(h, begin)
    for a in range(count):
        spread(a)
    at_each_head(h, partial(pass_on, 1))
    for a in range(count - 2):
        hand_over(a)
    at_each_head(h, partial(pass_on, 2))
    hand_over(count - 2)
    at_each_head(h, partial(pass_on, 3))
    hand_over(count - 1)
    for a in range(count):
        for d in range(1, LINE):
            along(a, d).wait_send()
        for e in range(1, chips):
            over(a, e).wait_send()
        for e in range(chips):
            across(a, e).wait_send()
            across_arrives(a, e).wait_recv()
    own_rows().wait()
    at_each_head(h, finish)


def gather(tokens, shards, blk):
    rows, width = tokens.shape
    count, chips = len(shards), blk // CORES
    anywhere = pl.BlockSpec(memory_space=pl.ANY)
    dma = pltpu.SemaphoreType.DMA
    outs = pl.pallas_call(
        partial(gather_kernel, blk, count),
        out_shape=[
            jax.ShapeDtypeStruct((5, rows, width), tokens.dtype),
            jax.ShapeDtypeStruct((rows, width), tokens.dtype),
        ]
        + [jax.ShapeDtypeStruct((LINE, blk) + s.shape, s.dtype) for s in shards],
        in_specs=[anywhere] * (1 + count),
        out_specs=[anywhere] * (2 + count),
        scratch_shapes=[dma((count + 3,))]
        + [dma((count, LINE - 1))] * 2
        + [dma((count, chips - 1))] * 2
        + [dma((count, chips))] * 2
        + [dma((LINE, PIECES))] * 4
        + [dma((PIECES,))] * 4,
        compiler_params=pltpu.CompilerParams(collective_id=0, has_side_effects=True),
        name="gather",
    )(tokens, *shards)
    return outs[0], outs[2:]


def pair_kernel(blk, *refs):
    chips = blk // CORES
    grads, outs, rest = refs[:2], refs[2 : 2 + chips], refs[2 + chips :]
    held, arrived, (load, send, recv) = rest[:2], rest[2:4], rest[4:]
    h, b = lax.axis_index("head"), lax.axis_index("blk")
    chip, core = b // CORES, b % CORES
    sibling = chip * CORES + 1 - core

    def part(a, there):
        if a == 0:
            return grads[a].at[:, there, :, pl.ds(3 * 768, 768)]
        return grads[a].at[:, there]

    def mine(a, e):
        there = ((chip + e) % chips) * CORES + core
        return pltpu.make_async_copy(part(a, there), held[a].at[e], load.at[a, e])

    def across(a, e):
        there = ((chip + e) % chips) * CORES + 1 - core
        return remote(
            part(a, there), arrived[a].at[e], send.at[a, e], recv.at[a, e], h, sibling
        )

    order = [e % chips for e in range(1, chips + 1)]
    for e in order:
        for a in range(2):
            mine(a, e).start()
    barrier = pltpu.get_barrier_semaphore()
    pl.semaphore_signal(barrier, inc=1, device_id=(h, sibling), device_id_type=MESH)
    pl.semaphore_wait(barrier, 1)
    for e in order:
        for a in range(2):
            across(a, e).start()
    for e in order:
        for a in range(2):
            mine(a, e).wait()
            across(a, e).wait_recv()

        def one(n, carry, e=e):
            inner, outer = (
                held[a][e, n].astype(f32) + arrived[a][e, n].astype(f32) for a in range(2)
            )
            spare = jnp.zeros((8, 768), f32)
            outs[e][n, 0:32] = jnp.concatenate([inner, spare], axis=0).astype(bf16)
            outs[e][n, 32:128] = outer.astype(bf16)
            return carry

        lax.fori_loop(0, LINE, one, 0)
    for e in order:
        for a in range(2):
            across(a, e).wait_send()


def pair_sums(grads, blk):
    chips = blk // CORES
    shard = [(24, 768), (96, 768)]
    dma = pltpu.SemaphoreType.DMA
    inside = pl.BlockSpec(memory_space=pltpu.VMEM)
    return pl.pallas_call(
        partial(pair_kernel, blk),
        out_shape=[jax.ShapeDtypeStruct((LINE, 128, 768), bf16)] * chips,
        in_specs=[pl.BlockSpec(memory_space=pl.ANY)] * 2,
        out_specs=[inside] * chips,
        scratch_shapes=[pltpu.VMEM((chips, LINE) + s, bf16) for s in shard] * 2
        + [dma((2, chips))] * 3,
        compiler_params=pltpu.CompilerParams(
            collective_id=2, has_side_effects=True, vmem_limit_bytes=56 << 20
        ),
        name="pair_sums",
    )(*grads)


def over_plane(sums, blk, head):
    chips = blk // CORES
    received = [sums[0]]
    for e in range(1, chips):
        pairs = [
            (
                h * blk + k * CORES + c,
                h * blk + ((k + e) % chips) * CORES + c,
            )
            for h in range(head)
            for k in range(chips)
            for c in range(CORES)
        ]
        received.append(lax.ppermute(sums[e], ("head", "blk"), pairs))
    return received


def reduce_kernel(blk, count, *refs):
    small_ref, wide_ref, query_ref, key_ref, value_ref = refs[:5]
    weights, first_ref = refs[5:8], refs[8]
    chips = blk // CORES
    early, raw = refs[9 : 9 + chips], refs[9 + chips : 11 + chips]
    rest = refs[11 + chips :]
    sum_ref, outs, early_outs = rest[0], rest[1 : 1 + count], rest[1 + count : 4 + count]
    early_sum, early_in, es, er = rest[4 + count : 8 + count]
    totals, (wide_in, key_in, value_in, fed) = rest[8 + count : 11 + count], rest[11 + count : 15 + count]
    rest = rest[15 + count :]
    weight_in, early_here, loaded = rest[:3], rest[3 : 3 + chips], rest[3 + chips]
    rest = rest[4 + chips :]
    extra = count
    held, from_core, rest = rest[: count + 1], rest[count + 1 : 2 * count + 1], rest[2 * count + 1 :]
    from_chip, from_line, rest = rest[: count + 1], rest[count + 1 : 2 * count + 2], rest[2 * count + 2 :]
    raw_own, raw_in, (rl, rs, rr), rest = rest[:2], rest[2:4], rest[4:7], rest[7:]
    frame, arrived, aside = rest[:3]
    load, ss, sr, cs, cr, zs, zr, us, ur, ds, dr, ns, nr, fs, fr = rest[3:]
    grads = (small_ref,) + tuple(totals)
    h, b = lax.axis_index("head"), lax.axis_index("blk")
    chip, core = b // CORES, b % CORES
    sibling = chip * CORES + 1 - core
    chunk_rows = sum_ref.shape[0]
    rows = chunk_rows // PIECES_BACK

    feed_rows = wide_in.shape[1]
    halves = chunk_rows // feed_rows
    slots = 1 + 2 * REACH

    def slot_at(n):
        slot = REACH
        for hh in range(LINE):
            for k in range(slots):
                slot = jnp.where((h == hh) & (n == k), WORK_ORDER[hh][k], slot)
        return slot

    def feed(slot, half):
        some = pl.ds(slot * chunk_rows + half * feed_rows, feed_rows)
        return [
            pltpu.make_async_copy(source.at[some], target.at[half], fed.at[n, half])
            for n, (source, target) in enumerate(
                ((wide_ref, wide_in), (key_ref, key_in), (value_ref, value_in))
            )
        ]

    def feed_queries(half):
        some = pl.ds(half * feed_rows, feed_rows)
        wide_some = pl.ds(REACH * chunk_rows + half * feed_rows, feed_rows)
        return [
            pltpu.make_async_copy(wide_ref.at[wide_some], wide_in.at[half], fed.at[0, half]),
            pltpu.make_async_copy(query_ref.at[some], key_in.at[half], fed.at[1, half]),
        ]

    def start(copies):
        for copy in copies:
            copy.start()

    def wait(copies):
        for copy in copies:
            copy.wait()

    def standing():
        pairs = list(zip(weights, weight_in)) + list(zip(early, early_here)) + [(first_ref, sum_ref)]
        return [
            pltpu.make_async_copy(source, target, loaded.at[n])
            for n, (source, target) in enumerate(pairs)
        ]

    def add_product(total, left, right, fresh):
        half = left.shape[1] // 2
        for n in range(2):
            lines = LINE // 2
            part = mm_tn(left[:, n * half : (n + 1) * half], right)
            part = part.reshape((lines,) + total.shape[1:])
            here = pl.ds(n * lines, lines)
            total[here] = part if fresh else total[here] + part

    def work(n, carry):
        slot = slot_at(n)
        for half in range(halves):
            if half + 1 < halves:
                start(feed(slot, half + 1))
            else:

                @pl.when(n + 1 < slots)
                def _():
                    start(feed(slot_at(n + 1), 0))

            wait(feed(slot, half))
            for t in range(feed_rows // ROWS):
                s = pl.ds(t * ROWS, ROWS)
                grad = mm_nt(key_in[half, s], weight_in[1][...]) + mm_nt(
                    value_in[half, s], weight_in[2][...]
                )
                frame[slot, pl.ds(half * feed_rows + t * ROWS, ROWS)] = grad.astype(bf16)
            add_product(totals[1], wide_in[half], key_in[half], False)
            add_product(totals[2], wide_in[half], value_in[half], False)
        for hh in range(LINE):
            for k in range(slots):
                pl.when((h == hh) & (n == k))(partial(send_off, hh, WORK_ORDER[hh][k]))
        return carry

    def query_work():
        start(feed_queries(0))
        for half in range(halves):
            if half + 1 < halves:
                start(feed_queries(half + 1))
            wait(feed_queries(half))
            for t in range(feed_rows // ROWS):
                s = pl.ds(t * ROWS, ROWS)
                here = pl.ds(half * feed_rows + t * ROWS, ROWS)
                sum_ref[here] += mm_nt(key_in[half, s], weight_in[0][...])
            add_product(totals[0], wide_in[half], key_in[half], half == 0)

    def mine(a, k):
        return pltpu.make_async_copy(grads[a].at[:, k * CORES + core], held[a].at[k], load.at[a, k])

    def raw_part(n, there):
        return raw[n].at[:, there, :, pl.ds(0, raw_own[n].shape[3])]

    def mine_raw(n, k):
        there = k * CORES + core
        return pltpu.make_async_copy(raw_part(n, there), raw_own[n].at[k], rl.at[n, k])

    def across_raw(n, k):
        there = k * CORES + 1 - core
        return remote(raw_part(n, there), raw_in[n].at[k], rs.at[n, k], rr.at[n, k], h, sibling)

    def pack_raw(k):
        for n in range(2):
            mine_raw(n, k).wait()
            across_raw(n, k).wait_recv()

        def one(m, carry):
            attn, inner = (
                raw_own[n][k, m].astype(f32) + raw_in[n][k, m].astype(f32) for n in range(2)
            )
            parts = [attn] + [inner[:, c * 768 : (c + 1) * 768] for c in range(3)]
            for c in range(2):
                both = jnp.concatenate(parts[2 * c : 2 * c + 2], axis=0)
                held[extra][k, m, 48 * c : 48 * (c + 1)] = both.astype(bf16)
            return carry

        lax.fori_loop(0, LINE, one, 0)

    def across(a, k):
        return remote(
            grads[a].at[:, k * CORES + 1 - core],
            from_core[a].at[k],
            ss.at[a, k],
            sr.at[a, k],
            h,
            sibling,
        )

    def over(a, e):
        k = (chip + e) % chips
        return remote(
            held[a].at[k],
            from_chip[a].at[e - 1],
            cs.at[a, e - 1],
            cr.at[a, e - 1],
            h,
            k * CORES + core,
        )

    def along(a, d):
        there = (h + d) % LINE
        return remote(
            held[a].at[chip, there],
            from_line[a].at[d - 1],
            zs.at[a, d - 1],
            zr.at[a, d - 1],
            there,
            b,
        )

    def add_cores(a, k):
        def one(n, carry):
            own = held[a][k, n] if a == 0 else grads[a][n, k * CORES + core]
            held[a][k, n] = (own + from_core[a][k, n]).astype(held[a].dtype)
            return carry

        lax.fori_loop(0, LINE, one, 0)

    def to_chips(a):
        for k in range(chips):
            if a == 0:
                mine(a, k).wait()
            across(a, k).wait_recv()
        for e in range(1, chips):
            add_cores(a, (chip + e) % chips)
            over(a, e).start()
        add_cores(a, chip)

    def to_line(a):
        for e in range(1, chips):
            over(a, e).wait_recv()

        def one(n, carry):
            total = held[a][chip, n].astype(f32)
            for e in range(1, chips):
                total = total + from_chip[a][e - 1, n].astype(f32)
            held[a][chip, n] = total.astype(held[a].dtype)
            return carry

        lax.fori_loop(0, LINE, one, 0)
        for d in range(1, LINE):
            along(a, d).start()

    def to_owner(a):
        for d in range(1, LINE):
            along(a, d).wait_recv()
        total = held[a][chip, h].astype(f32)
        for d in range(1, LINE):
            total = total + from_line[a][d - 1].astype(f32)
        outs[a][...] = total

    def early_along(d):
        there = (h + d) % LINE
        return remote(
            early_sum.at[there], early_in.at[d - 1], es.at[d - 1], er.at[d - 1], there, b
        )

    def early_to_line():
        def one(n, carry):
            total = early_here[0][n].astype(f32)
            for ref in early_here[1:]:
                total = total + ref[n].astype(f32)
            early_sum[n] = total.astype(bf16)
            return carry

        lax.fori_loop(0, LINE, one, 0)
        for d in range(1, LINE):
            early_along(d).start()

    def early_to_owner():
        for d in range(1, LINE):
            early_along(d).wait_recv()
        total = early_sum[h].astype(f32)
        for d in range(1, LINE):
            total = total + early_in[d - 1].astype(f32)
        attn_ref, inner_ref, outer_ref = early_outs
        inner_ref[:, 3 * 768 :] = total[:24]
        outer_ref[...] = total[32:]
        for d in range(1, LINE):
            along(extra, d).wait_recv()
        total = held[extra][chip, h].astype(f32)
        for d in range(1, LINE):
            total = total + from_line[extra][d - 1].astype(f32)
        attn_ref[...] = total[:24]
        for n in range(3):
            inner_ref[:, n * 768 : (n + 1) * 768] = total[24 * (n + 1) : 24 * (n + 2)]

    def part(p):
        return pl.ds(p * rows, rows)

    def piece(ref, p):
        return ref.at[part(p)]

    def add_rows(target, j, source, n, p):
        def one(step, carry):
            some = pl.ds(p * rows + step * 64, 64)
            target[j, some] = (
                target[j, some].astype(f32) + source[n, some].astype(f32)
            ).astype(target.dtype)
            return carry

        lax.fori_loop(0, rows // 64, one, 0)

    def slot_of(hh, j):
        slot = 2 + j - hh
        return slot if 0 <= slot < slots else slots

    def arrival(hh, j, upward):
        return arrived.at[LINE if j == hh and not upward else j]

    def up(hh, j, p):
        return remote(
            piece(frame.at[slot_of(hh, j)], p),
            piece(arrival(hh + 1, j, True), p),
            us.at[j, p],
            ur.at[j, p],
            (h + 1) % LINE,
            b,
        )

    def up_arrives(hh, j, p):
        here = piece(arrival(hh, j, True), p)
        return remote(here, here, us.at[j, p], ur.at[j, p], (h + 1) % LINE, b)

    def down(hh, j, p):
        return remote(
            piece(frame.at[slot_of(hh, j)], p),
            piece(arrival(hh - 1, j, False), p),
            ds.at[j, p],
            dr.at[j, p],
            (h + 3) % LINE,
            b,
        )

    def down_arrives(hh, j, p):
        here = piece(arrival(hh, j, False), p)
        return remote(here, here, ds.at[j, p], dr.at[j, p], (h + 3) % LINE, b)

    def side_parts(hh):
        near, far = (3, 2) if hh < 2 else (0, 1)
        found = [(NEAR_SLOT[hh], near, 0, ns, nr)]
        if FAR_SLOT[hh] is not None:
            found.append((FAR_SLOT[hh], far, 1, fs, fr))
        return found

    def side(hh, slot, n, send, recv, p):
        target = (b + blk - 1) % blk if hh < 2 else (b + 1) % blk
        return remote(
            piece(frame.at[slot], p), piece(aside.at[n], p), send.at[p], recv.at[p], h, target
        )

    def sends_side(hh):
        return b > 0 if hh < 2 else b < blk - 1

    def gets_side(hh):
        return b < blk - 1 if hh < 2 else b > 0

    def send_off(hh, slot):
        @pl.when(sends_side(hh))
        def _():
            for p in range(PIECES_BACK):
                for side_slot, _, n, send, recv in side_parts(hh):
                    if side_slot == slot:
                        side(hh, slot, n, send, recv, p).start()

        for p in range(PIECES_BACK):
            if hh == 0 and slot == slot_of(0, 1):
                up(hh, 1, p).start()
            if hh == LINE - 1 and slot == slot_of(LINE - 1, 2):
                down(hh, 2, p).start()

    def take_sides(hh):
        for p in range(PIECES_BACK):
            for _, j, n, send, recv in side_parts(hh):

                @pl.when(gets_side(hh))
                def _(j=j, n=n, send=send, recv=recv):
                    here = piece(aside.at[n], p)
                    remote(here, here, send.at[p], recv.at[p], h, (b + 1) % blk).wait_recv()
                    add_rows(frame, slot_of(hh, j), aside, n, p)

                if hh == 0:
                    up(hh, j, p).start()
                if hh == LINE - 1:
                    down(hh, j, p).start()

    def pass_on(hh):
        moves = []
        if hh == 1:
            moves = [(3, True), (2, True), (0, False)]
        if hh == 2:
            moves = [(0, False), (1, False), (3, True)]
        for p in range(PIECES_BACK):
            for j, upward in moves:
                (up_arrives if upward else down_arrives)(hh, j, p).wait_recv()
                add_rows(frame, slot_of(hh, j), arrived, j, p)
                (up if upward else down)(hh, j, p).start()

    def finish(hh):
        for p in range(PIECES_BACK):
            sources = []
            if hh > 0:
                up_arrives(hh, hh, p).wait_recv()
                sources.append(hh)
            if hh < LINE - 1:
                down_arrives(hh, hh, p).wait_recv()
                sources.append(LINE)

            def one(step, carry, p=p, sources=tuple(sources)):
                some = pl.ds(p * rows + step * 64, 64)
                total = sum_ref[some] + frame[REACH, some].astype(f32)
                for n in sources:
                    total = total + arrived[n, some].astype(f32)
                sum_ref[some] = total
                return carry

            lax.fori_loop(0, rows // 64, one, 0)
        for p in range(PIECES_BACK):
            for j in range(LINE):
                if j > hh:
                    up(hh, j, p).wait_send()
                if j < hh:
                    down(hh, j, p).wait_send()

        @pl.when(sends_side(hh))
        def _():
            for p in range(PIECES_BACK):
                for slot, _, n, send, recv in side_parts(hh):
                    side(hh, slot, n, send, recv, p).wait_send()

    start(feed(slot_at(0), 0))
    start(standing())
    for k in range(chips):
        mine(0, k).start()
        for n in range(2):
            mine_raw(n, k).start()
    frame[slots] = jnp.zeros(frame.shape[1:], frame.dtype)
    for n in (1, 2):
        totals[n][...] = jnp.zeros_like(totals[n])
    greet_plane_and_line(h, b, blk)
    for k in range(chips):
        for n in range(2):
            across_raw(n, k).start()
    wait(standing())
    early_to_line()
    lax.fori_loop(0, slots, work, 0)
    query_work()
    for e in range(1, chips):
        pack_raw((chip + e) % chips)
        over(extra, e).start()
    pack_raw(chip)
    for a in range(count):
        for k in range(chips):
            across(a, k).start()
    at_each_head(h, take_sides)
    for a in range(count):
        to_chips(a)
    at_each_head(h, pass_on)
    for a in range(count + 1):
        to_line(a)
    at_each_head(h, finish)
    early_to_owner()
    for d in range(1, LINE):
        early_along(d).wait_send()
    for a in range(count):
        to_owner(a)
    for a in range(count):
        for k in range(chips):
            across(a, k).wait_send()
    for a in range(count + 1):
        for e in range(1, chips):
            over(a, e).wait_send()
        for d in range(1, LINE):
            along(a, d).wait_send()
    for k in range(chips):
        for n in range(2):
            across_raw(n, k).wait_send()


def reduce_to_owners(small, wide, projected, weights, first, early, raw, blk):
    rows, width = first.shape
    count, chips = 4, blk // CORES
    anywhere = pl.BlockSpec(memory_space=pl.ANY)
    inside = pl.BlockSpec(memory_space=pltpu.VMEM)
    dma = pltpu.SemaphoreType.DMA
    square = (width // (LINE * blk), width)
    shard = [small.shape[2:]] + [square] * 3
    kinds = [f32] + [bf16] * 4
    travels = shard + [(96, 768)]
    early_shapes = ((24, 768), (24, 3072), (96, 768))
    outs = pl.pallas_call(
        partial(reduce_kernel, blk, count),
        out_shape=[jax.ShapeDtypeStruct((rows, width), f32)]
        + [jax.ShapeDtypeStruct(s, f32) for s in shard]
        + [jax.ShapeDtypeStruct(s, f32) for s in early_shapes],
        in_specs=[anywhere] * (11 + chips),
        out_specs=[inside] * (4 + count),
        scratch_shapes=[
            pltpu.VMEM(early[0].shape, bf16),
            pltpu.VMEM((LINE - 1,) + early[0].shape[1:], bf16),
            dma((LINE - 1,)),
            dma((LINE - 1,)),
        ]
        + [pltpu.VMEM((LINE, blk) + square, f32)] * 3
        + [pltpu.VMEM((2, rows // 2, width), bf16)] * 3
        + [dma((3, 2))]
        + [pltpu.VMEM((width, width), bf16)] * 3
        + [pltpu.VMEM(early[0].shape, bf16)] * chips
        + [dma((4 + chips,))]
        + [pltpu.VMEM((chips, LINE) + s, t) for s, t in zip(travels, kinds)]
        + [pltpu.VMEM((chips, LINE) + s, f32) for s in shard]
        + [pltpu.VMEM((chips - 1, LINE) + s, t) for s, t in zip(travels, kinds)]
        + [pltpu.VMEM((LINE - 1,) + s, t) for s, t in zip(travels, kinds)]
        + [pltpu.VMEM((chips, LINE, 24, size), bf16) for size in (768, 3 * 768)] * 2
        + [dma((2, chips))] * 3
        + [
            pltpu.VMEM((2 + 2 * REACH, rows, width), bf16),
            pltpu.VMEM((LINE + 1, rows, width), bf16),
            pltpu.VMEM((2, rows, width), bf16),
        ]
        + [dma((count + 1, chips))] * 3
        + [dma((count + 1, chips - 1))] * 2
        + [dma((count + 1, LINE - 1))] * 2
        + [dma((LINE, PIECES_BACK))] * 4
        + [dma((PIECES_BACK,))] * 4,
        compiler_params=pltpu.CompilerParams(
            collective_id=1, has_side_effects=True, vmem_limit_bytes=62 << 20
        ),
        name="reduce_to_owners",
    )(small, wide, *projected, *weights, first, *early, *raw)
    return outs[0], outs[1:-3], outs[-3:]


def whole(shard):
    return lax.all_gather(shard, ("head", "blk"), axis=0, tiled=True)


def shared_out(grad):
    return lax.psum_scatter(grad.astype(bf16), ("head", "blk"), scatter_dimension=0, tiled=True).astype(f32)


def padded_to(flat, size):
    return jnp.pad(flat, [(0, 0)] * (flat.ndim - 1) + [(0, size - flat.shape[-1])])


def per_device(blk, head, tokens, *rest):
    weights, vectors, (out_grad, segment_ids, random_blocks) = rest[:6], rest[6:15], rest[15:]
    rows = tokens.shape[0]
    by_kernel = head == LINE and blk == LINE * CORES
    short = [vectors[n] for n in (2, 3, 4, 6, 7, 8, 0, 1)]
    if by_kernel:
        packed = jnp.concatenate(
            [
                padded_to(jnp.stack(short), 128),
                padded_to(vectors[5][None], 128),
                jnp.zeros((7, 128), bf16),
            ]
        )
        wide, fulls = gather(tokens, [packed] + list(weights), blk)
        wide = wide.reshape(-1, tokens.shape[1])
        w_query, w_key, w_value, w_attn, w_inner, w_outer = [
            w.reshape(-1, w.shape[-1]) for w in fulls[1:]
        ]
        table = fulls[0].reshape(head * blk, 16, 128)
    else:
        wide = widen(tokens, blk, head)
        w_query, w_key, w_value, w_attn, w_inner, w_outer = [whole(w) for w in weights]
        packed = jnp.concatenate(
            [padded_to(jnp.stack(short), 128), padded_to(vectors[5][None], 128)]
        )
        table = whole(packed[None])
    short_rows = jnp.transpose(table[:, :8, : short[0].shape[0]], (1, 0, 2)).astype(f32)
    short_rows = short_rows.reshape(8, -1)
    bias_inner = table[:, 8, : vectors[5].shape[0]].astype(f32).reshape(-1, 1, PIECE)

    rows_of, bases, docs = tile_plan(segment_ids, random_blocks, rows)
    keys, values, queries = project(wide, w_key, w_value, w_query, short_rows, rows)
    attended, probs = attend(rows_of, queries, keys, values, bases, docs)

    result, grad_first_sum, grad_attended, grad_w_attn, grad_w_inner, grad_w_outer, sums_d, sums_ff = (
        middle(
            attended,
            tokens,
            out_grad,
            w_attn,
            w_inner,
            w_outer,
            short_rows,
            bias_inner,
        )
    )

    early_grads = [grad_w_attn, grad_w_inner, grad_w_outer]
    if by_kernel:
        raw = [g.reshape(head, blk, -1, g.shape[-1]) for g in early_grads]
        early = over_plane(pair_sums(raw[1:], blk), blk, head)
    grad_scaled, grad_keyed, grad_valued, sums_qv = attend_back(
        rows_of, queries, grad_attended, keys, values, probs
    )
    sums = jnp.concatenate([sums_d[:6], sums_qv[6:]])
    sums = jnp.transpose(sums.reshape(8, head * blk, -1), (1, 0, 2))
    packed = jnp.concatenate(
        [
            padded_to(sums, 128),
            padded_to(sums_ff.reshape(head * blk, 1, -1), 128),
            jnp.zeros((head * blk, 7, 128), f32),
        ],
        axis=1,
    )
    if by_kernel:
        grad_tokens, late, early_sum = reduce_to_owners(
            packed.reshape(head, blk, 16, 128),
            wide,
            (grad_scaled, grad_keyed, grad_valued),
            (w_query, w_key, w_value),
            grad_first_sum,
            early,
            raw[:2],
            blk,
        )
        matrix_grads = tuple(late[1:]) + tuple(early_sum)
        packed = late[0]
    else:
        grad_wide = (mm_nt(grad_keyed, w_key) + mm_nt(grad_valued, w_value)).astype(bf16)
        grad_tokens = (
            grad_first_sum
            + mm_nt(grad_scaled, w_query)
            + narrow(grad_wide, rows, blk, head).astype(f32)
        )
        late_grads = [mm_tn(tokens, grad_scaled), mm_tn(wide, grad_keyed), mm_tn(wide, grad_valued)]
        matrix_grads = tuple(shared_out(g) for g in late_grads + early_grads)
        packed = lax.psum_scatter(packed, ("head", "blk"), scatter_dimension=0, tiled=True)[0]
    order = (6, 7, 0, 1, 2, 8, 3, 4, 5)
    vector_grads = tuple(packed[n, : v.shape[0]] for n, v in zip(order, vectors))
    return (result, grad_tokens) + matrix_grads + vector_grads


def solution(mesh):
    row = P(("blk", "head"), None)
    matrix = P(("head", "blk"), None)
    vector = P(("head", "blk"))
    return jax.shard_map(
        partial(per_device, mesh.shape["blk"], mesh.shape["head"]),
        mesh=mesh,
        in_specs=(row,) + (matrix,) * 6 + (vector,) * 9 + (row, P(), P()),
        out_specs=(row, row) + (matrix,) * 6 + (vector,) * 9,
        check_vma=False,
    )
```

```python
from functools import partial

import jax
import jax.numpy as jnp
from jax import lax
from jax.experimental import pallas as pl
from jax.experimental.pallas import tpu as pltpu
from jax.sharding import PartitionSpec as P

HEAD_DIM = 64
BLOCK = 64
RANDOM = 3
TILES = 5 + RANDOM
REACH = 2
GROUP = 4
FORWARD_BLOCKS = 8
BACKWARD_BLOCKS = 8
ROWS = 256
PIECE = 768

epsilon = 1e-06
masked_value = -1e30
query_scale = 0.125
gelu_scale = 0.7978845608028654
gelu_cubic = 0.044715
far_away = -(1 << 24)
repeated = 1 << 20
f32, bf16 = jnp.float32, jnp.bfloat16


def mm(a, b):
    return jnp.dot(a, b, preferred_element_type=f32)


def mm_nt(a, b):
    return lax.dot_general(a, b, (((1,), (1,)), ((), ())), preferred_element_type=f32)


def mm_tn(a, b):
    return lax.dot_general(a, b, (((0,), (0,)), ((), ())), preferred_element_type=f32)


def head_mask(rows, cols, first):
    lanes = lax.broadcasted_iota(jnp.int32, (rows, cols), 1)
    return (lanes >= first) & (lanes < first + HEAD_DIM)


def stacked_by_head(tile):
    rows, cols = tile.shape
    return jnp.concatenate(
        [
            jnp.where(head_mask(rows, cols, h * HEAD_DIM), tile, jnp.zeros_like(tile))
            for h in range(cols // HEAD_DIM)
        ],
        axis=0,
    )


def own_head_columns(stacked):
    cols = stacked.shape[1]
    total = None
    for h in range(cols // HEAD_DIM):
        part = stacked[h * BLOCK : (h + 1) * BLOCK]
        part = jnp.where(head_mask(BLOCK, cols, h * HEAD_DIM), part, 0.0)
        total = part if total is None else total + part
    return total


def block_rows(row):
    return pl.ds(pl.multiple_of(row * BLOCK, BLOCK), BLOCK)


def gathered(table_ref, fixed_row, random_row):
    tiles = [table_ref[block_rows(fixed_row(t)), :] for t in range(5)]
    low = head_mask(BLOCK, 2 * HEAD_DIM, 0)
    for t in range(RANDOM):
        halves = []
        for pair in range(GROUP // 2):
            cols = pl.ds(pair * 2 * HEAD_DIM, 2 * HEAD_DIM)
            a = table_ref[block_rows(random_row(2 * pair, t)), cols]
            b = table_ref[block_rows(random_row(2 * pair + 1, t)), cols]
            halves.append(jnp.where(low, a, b))
        tiles.append(jnp.concatenate(halves, axis=1))
    return jnp.concatenate(tiles, axis=0)


def row_readers(rows_ref, blocks, i):
    group = pl.program_id(0)

    def fixed_code(t):
        return rows_ref[(group * GROUP * blocks + i) * TILES + t]

    def random_code(h, t):
        return rows_ref[((group * GROUP + h) * blocks + i) * TILES + 5 + t]

    def fixed_row(t):
        return fixed_code(t) % repeated

    def random_row(h, t):
        return random_code(h, t) % repeated

    return (fixed_row, random_row), (fixed_code, random_code)


def first_place(code):
    return jnp.where(code >= repeated, far_away, code * BLOCK)


def attend_kernel(blocks, rows_ref, q_ref, k_ref, v_ref, doc_ref, out_ref, p_ref):
    head_of = lax.broadcasted_iota(jnp.int32, (1, GROUP * BLOCK), 1) // BLOCK
    within = lax.broadcasted_iota(jnp.int32, (BLOCK, GROUP * BLOCK), 0)
    for u in range(FORWARD_BLOCKS):
        here = pl.ds(u * BLOCK, BLOCK)
        readers, (fixed_code, random_code) = row_readers(
            rows_ref, blocks, pl.program_id(1) * FORWARD_BLOCKS + u
        )
        keys = gathered(k_ref, *readers)
        values = gathered(v_ref, *readers)
        scores = mm_nt(keys, stacked_by_head(q_ref[here, :]))
        lo = doc_ref[u, 0:1, :]
        hi = doc_ref[u, 1:2, :]
        masked = []
        for t in range(TILES):
            if t < 5:
                base = first_place(fixed_code(t))
            else:
                base = first_place(random_code(0, t - 5))
                for n in range(1, GROUP):
                    base = jnp.where(head_of == n, first_place(random_code(n, t - 5)), base)
            place = within + base
            allowed = (place >= lo) & (place < hi)
            masked.append(jnp.where(allowed, scores[t * BLOCK : (t + 1) * BLOCK], masked_value))
        scores = jnp.concatenate(masked, axis=0)
        raised = jnp.exp(scores - jnp.max(scores, axis=0, keepdims=True))
        probs = (raised * (1.0 / jnp.sum(raised, axis=0, keepdims=True))).astype(bf16)
        p_ref[0, u] = probs
        out_ref[here, :] = own_head_columns(mm_tn(probs, values)).astype(bf16)


def attend_back_kernel(
    blocks,
    rows_ref,
    q_ref,
    g_ref,
    k_ref,
    v_ref,
    p_ref,
    dq_ref,
    dk_ref,
    dv_ref,
    sums_ref,
    dk_sum,
    dv_sum,
):
    step = pl.program_id(1)

    @pl.when(step == 0)
    def _():
        sums_ref[...] = jnp.zeros_like(sums_ref)
        dk_sum[...] = jnp.zeros_like(dk_sum)
        dv_sum[...] = jnp.zeros_like(dv_sum)

    found = []
    for u in range(BACKWARD_BLOCKS):
        here = pl.ds(u * BLOCK, BLOCK)
        readers, _ = row_readers(rows_ref, blocks, step * BACKWARD_BLOCKS + u)
        keys = gathered(k_ref, *readers)
        values = gathered(v_ref, *readers)
        queries = stacked_by_head(q_ref[here, :])
        grads = stacked_by_head(g_ref[here, :])
        probs = p_ref[0, u]
        grad_probs = mm_nt(values, grads)
        wide = probs.astype(f32)
        balance = jnp.sum(wide * grad_probs, axis=0, keepdims=True)
        grad_scores = (wide * (grad_probs - balance)).astype(bf16)
        dq_ref[here, :] = (query_scale * own_head_columns(mm_tn(grad_scores, keys))).astype(bf16)
        found.append((readers, mm(grad_scores, queries), mm(probs, grads)))
    for (fixed_row, random_row), grad_keys, grad_values in found:
        for total, part in ((dk_sum, grad_keys), (dv_sum, grad_values)):
            for t in range(5):
                total[block_rows(fixed_row(t)), :] += part[t * BLOCK : (t + 1) * BLOCK]
            for t in range(RANDOM):
                rows = part[(5 + t) * BLOCK : (6 + t) * BLOCK]
                for h in range(GROUP):
                    first = (h // 2) * 2 * HEAD_DIM
                    mine = head_mask(BLOCK, 2 * HEAD_DIM, (h % 2) * HEAD_DIM)
                    total[block_rows(random_row(h, t)), pl.ds(first, 2 * HEAD_DIM)] += jnp.where(
                        mine, rows[:, first : first + 2 * HEAD_DIM], 0.0
                    )

    sums_ref[6:7, :] += jnp.sum(dq_ref[...].astype(f32), axis=0, keepdims=True)

    @pl.when(step == blocks // BACKWARD_BLOCKS - 1)
    def _():
        dk_ref[...] = dk_sum[...].astype(bf16)
        dv_ref[...] = dv_sum[...].astype(bf16)
        sums_ref[7:8, :] = jnp.sum(dv_ref[...].astype(f32), axis=0, keepdims=True)


def attend(rows, queries, keys, values, docs):
    tokens, width = queries.shape
    ext = keys.shape[0]
    blocks, cols, some = tokens // BLOCK, GROUP * HEAD_DIM, FORWARD_BLOCKS
    groups = width // cols
    tile = pl.BlockSpec((some * BLOCK, cols), lambda g, i, r: (i, g))
    table = pl.BlockSpec((ext, cols), lambda g, i, r: (0, g))
    return pl.pallas_call(
        partial(attend_kernel, blocks),
        grid_spec=pltpu.PrefetchScalarGridSpec(
            num_scalar_prefetch=1,
            grid=(groups, blocks // some),
            in_specs=[
                tile,
                table,
                table,
                pl.BlockSpec((some, 8, cols), lambda g, i, r: (i, 0, 0)),
            ],
            out_specs=[
                tile,
                pl.BlockSpec((1, some, TILES * BLOCK, cols), lambda g, i, r: (g, i, 0, 0)),
            ],
        ),
        out_shape=[
            jax.ShapeDtypeStruct((tokens, width), bf16),
            jax.ShapeDtypeStruct((groups, blocks, TILES * BLOCK, cols), bf16),
        ],
        compiler_params=pltpu.CompilerParams(vmem_limit_bytes=60 << 20),
        name="attend",
    )(rows, queries, keys, values, docs)


def attend_back(rows, queries, grads, keys, values, probs):
    tokens, width = queries.shape
    ext = keys.shape[0]
    blocks, cols, some = tokens // BLOCK, GROUP * HEAD_DIM, BACKWARD_BLOCKS
    groups = width // cols
    tile = pl.BlockSpec((some * BLOCK, cols), lambda g, i, r: (i, g))
    table = pl.BlockSpec((ext, cols), lambda g, i, r: (0, g))
    return pl.pallas_call(
        partial(attend_back_kernel, blocks),
        grid_spec=pltpu.PrefetchScalarGridSpec(
            num_scalar_prefetch=1,
            grid=(groups, blocks // some),
            in_specs=[
                tile,
                tile,
                table,
                table,
                pl.BlockSpec((1, some, TILES * BLOCK, cols), lambda g, i, r: (g, i, 0, 0)),
            ],
            out_specs=[tile, table, table, pl.BlockSpec((8, cols), lambda g, i, r: (0, g))],
            scratch_shapes=[pltpu.VMEM((ext, cols), f32), pltpu.VMEM((ext, cols), f32)],
        ),
        out_shape=[
            jax.ShapeDtypeStruct((tokens, width), bf16),
            jax.ShapeDtypeStruct((ext, width), bf16),
            jax.ShapeDtypeStruct((ext, width), bf16),
            jax.ShapeDtypeStruct((8, width), f32),
        ],
        compiler_params=pltpu.CompilerParams(vmem_limit_bytes=56 << 20),
        cost_estimate=pl.CostEstimate(
            flops=10 * groups * blocks * TILES * BLOCK * cols * cols,
            bytes_accessed=100 << 20,
            transcendentals=0,
        ),
        name="attend_back",
    )(rows, queries, grads, keys, values, probs)


def normalized(values):
    centred = values - jnp.mean(values, axis=-1, keepdims=True)
    root = lax.rsqrt(jnp.mean(centred * centred, axis=-1, keepdims=True) + epsilon)
    return centred * root, root


def norm_back(grad, normal, root, gain):
    scaled = grad * gain
    along = jnp.mean(scaled * normal, axis=-1, keepdims=True)
    return root * (scaled - jnp.mean(scaled, axis=-1, keepdims=True) - normal * along)


def gelu_and_slope(u):
    square = u * u
    bend = jnp.tanh(gelu_scale * (u + gelu_cubic * (square * u)))
    half = 0.5 * (1.0 + bend)
    slope = half + (0.5 * gelu_scale) * u * (1.0 - bend * bend) * (
        1.0 + (3.0 * gelu_cubic) * square
    )
    return u * half, slope


def middle_kernel(
    att_ref,
    x_ref,
    og_ref,
    wa_ref,
    wi_ref,
    wo_ref,
    vec_ref,
    bi_ref,
    res_ref,
    sum_ref,
    ga_ref,
    dwa_ref,
    dwi_ref,
    dwo_ref,
    dvec_ref,
    dbi_ref,
    normal,
    root,
    low,
    act,
    slope,
    inner,
):
    step, half = pl.program_id(0), pl.num_programs(0) // 2
    tokens, width = x_ref.shape
    slices = [pl.ds(t * ROWS, ROWS) for t in range(tokens // ROWS)]
    bias_attn, gain_one, offset_one, bias_outer, gain_two, offset_two = (
        vec_ref[n : n + 1, :] for n in range(6)
    )

    def row_sum(total, values):
        part = jnp.sum(values, axis=0, keepdims=True)
        return part if total is None else total + part

    @pl.when(step == 0)
    def _():
        for s in slices:
            values = x_ref[s, :].astype(f32) + mm(att_ref[s, :], wa_ref[...]) + bias_attn
            flat, scale = normalized(values)
            normal[s, :] = flat
            root[s, :] = jnp.broadcast_to(scale, (ROWS, 128))
            first = flat * gain_one + offset_one
            low[s, :] = first.astype(bf16)
            sum_ref[s, :] = first + bias_outer

    @pl.when(step < half)
    def _():
        for s in slices:
            active, bend = gelu_and_slope(mm(low[s, :], wi_ref[...]) + bi_ref[0])
            active = active.astype(bf16)
            act[step, s, :] = active
            slope[step, s, :] = bend.astype(bf16)
            sum_ref[s, :] += mm(active, wo_ref[...])

    @pl.when(step == half)
    def _():
        outer_sum, gain_sum, offset_sum = None, None, None
        for s in slices:
            flat, scale = normalized(sum_ref[s, :])
            res_ref[s, :] = (flat * gain_two + offset_two).astype(bf16)
            grad = og_ref[s, :].astype(f32)
            gain_sum = row_sum(gain_sum, grad * flat)
            offset_sum = row_sum(offset_sum, grad)
            second = norm_back(grad, flat, scale, gain_two)
            sum_ref[s, :] = second
            second = second.astype(bf16)
            ga_ref[s, :] = second
            outer_sum = row_sum(outer_sum, second.astype(f32))
        dvec_ref[3:4, :] = outer_sum
        dvec_ref[4:5, :] = gain_sum
        dvec_ref[5:6, :] = offset_sum
        dvec_ref[6:8, :] = jnp.zeros((2, width), f32)

    @pl.when(step >= half)
    def _():
        now = step - half
        total = None
        for s in slices:
            grad = mm_nt(ga_ref[s, :], wo_ref[...]) * slope[now, s, :].astype(f32)
            grad = grad.astype(bf16)
            inner[s, :] = grad
            total = row_sum(total, grad.astype(f32))
            sum_ref[s, :] += mm_nt(grad, wi_ref[...])
        dbi_ref[0] = total
        for n in range(width // 256):
            some = pl.ds(n * 256, 256)
            dwi_ref[some, :] = mm_tn(low[:, some], inner[...]).astype(bf16)
        for n in range(PIECE // 256):
            some = pl.ds(n * 256, 256)
            dwo_ref[some, :] = mm_tn(act[now, :, some], ga_ref[...]).astype(bf16)

    @pl.when(step == 2 * half - 1)
    def _():
        attn_sum, gain_sum, offset_sum = None, None, None
        for s in slices:
            grad, flat = sum_ref[s, :], normal[s, :]
            gain_sum = row_sum(gain_sum, grad * flat)
            offset_sum = row_sum(offset_sum, grad)
            grad = norm_back(grad, flat, root[s, 0:1], gain_one)
            sum_ref[s, :] = grad
            grad = grad.astype(bf16)
            inner[s, :width] = grad
            attn_sum = row_sum(attn_sum, grad.astype(f32))
            ga_ref[s, :] = mm_nt(grad, wa_ref[...]).astype(bf16)
        dvec_ref[0:1, :] = attn_sum
        dvec_ref[1:2, :] = gain_sum
        dvec_ref[2:3, :] = offset_sum
        for n in range(width // 256):
            some = pl.ds(n * 256, 256)
            dwa_ref[some, :] = mm_tn(att_ref[:, some], inner[:, :width]).astype(bf16)


def middle(attended, tokens, out_grad, w_attn, w_inner, w_outer, vectors, bias_inner):
    rows, width = tokens.shape
    steps = w_inner.shape[1] // PIECE
    one = pl.Buffered(1)
    still = pl.BlockSpec((rows, width), lambda i: (0, 0), pipeline_mode=one)
    square = pl.BlockSpec((width, width), lambda i: (0, 0), pipeline_mode=one)
    few = pl.BlockSpec((8, width), lambda i: (0, 0))
    later = lambda i: jnp.maximum(i - steps, 0)
    return pl.pallas_call(
        middle_kernel,
        grid=(2 * steps,),
        in_specs=[
            still,
            still,
            still,
            square,
            pl.BlockSpec((width, PIECE), lambda i: (0, i % steps)),
            pl.BlockSpec((PIECE, width), lambda i: (i % steps, 0)),
            few,
            pl.BlockSpec((1, 1, PIECE), lambda i: (i % steps, 0, 0)),
        ],
        out_specs=[
            still,
            still,
            still,
            square,
            pl.BlockSpec((width, PIECE), lambda i: (0, later(i))),
            pl.BlockSpec((PIECE, width), lambda i: (later(i), 0)),
            few,
            pl.BlockSpec((1, 1, PIECE), lambda i: (later(i), 0, 0)),
        ],
        out_shape=[
            jax.ShapeDtypeStruct((rows, width), bf16),
            jax.ShapeDtypeStruct((rows, width), f32),
            jax.ShapeDtypeStruct((rows, width), bf16),
            jax.ShapeDtypeStruct(w_attn.shape, bf16),
            jax.ShapeDtypeStruct(w_inner.shape, bf16),
            jax.ShapeDtypeStruct(w_outer.shape, bf16),
            jax.ShapeDtypeStruct((8, width), f32),
            jax.ShapeDtypeStruct((steps, 1, PIECE), f32),
        ],
        scratch_shapes=[
            pltpu.VMEM((rows, width), f32),
            pltpu.VMEM((rows, 128), f32),
            pltpu.VMEM((rows, width), bf16),
            pltpu.VMEM((steps, rows, PIECE), bf16),
            pltpu.VMEM((steps, rows, PIECE), bf16),
            pltpu.VMEM((rows, PIECE), bf16),
        ],
        compiler_params=pltpu.CompilerParams(vmem_limit_bytes=60 << 20),
        name="middle",
    )(attended, tokens, out_grad, w_attn, w_inner, w_outer, vectors, bias_inner)


def project_kernel(wide_ref, wk_ref, wv_ref, wq_ref, vec_ref, k_ref, v_ref, q_ref):
    rows = wide_ref.shape[0]
    slices = [pl.ds(t * ROWS, ROWS) for t in range(rows // ROWS)]
    for s in slices:
        k_ref[s, :] = mm(wide_ref[s, :], wk_ref[...]).astype(bf16)
        v_ref[s, :] = (mm(wide_ref[s, :], wv_ref[...]) + vec_ref[7:8, :]).astype(bf16)

    @pl.when(pl.program_id(0) == REACH)
    def _():
        for s in slices:
            queries = mm(wide_ref[s, :], wq_ref[...]) + vec_ref[6:7, :]
            q_ref[s, :] = (query_scale * queries).astype(bf16)


def project(wide, w_key, w_value, w_query, vectors, rows):
    width = wide.shape[1]
    one = pl.Buffered(1)
    tile = pl.BlockSpec((rows, width), lambda i: (i, 0))
    still = pl.BlockSpec((rows, width), lambda i: (0, 0), pipeline_mode=one)
    square = pl.BlockSpec((width, width), lambda i: (0, 0), pipeline_mode=one)
    table = jax.ShapeDtypeStruct(wide.shape, bf16)
    return pl.pallas_call(
        project_kernel,
        grid=(1 + 2 * REACH,),
        in_specs=[tile, square, square, square, pl.BlockSpec((8, width), lambda i: (0, 0))],
        out_specs=[tile, tile, still],
        out_shape=[table, table, jax.ShapeDtypeStruct((rows, width), bf16)],
        compiler_params=pltpu.CompilerParams(vmem_limit_bytes=60 << 20),
        name="project",
    )(wide, w_key, w_value, w_query, vectors)


def tile_plan(segment_ids, random_blocks, tokens):
    heads, total_blocks, _ = random_blocks.shape
    blocks = tokens // BLOCK
    chunk = lax.axis_index("blk") * lax.axis_size("head") + lax.axis_index("head")
    margin = REACH * tokens
    padded = jnp.concatenate(
        [
            jnp.full((margin,), -1, jnp.int32),
            segment_ids,
            jnp.full((margin,), jnp.iinfo(jnp.int32).max, jnp.int32),
        ]
    )
    near = lax.dynamic_slice_in_dim(padded, chunk * tokens, tokens + 2 * margin)
    own = near[margin : margin + tokens]
    before, after = near[: margin + tokens], near[margin:]
    begins = jnp.sum((before[None, :] < own[:, None]).astype(jnp.int32), axis=1)
    ends = margin + jnp.sum((after[None, :] <= own[:, None]).astype(jnp.int32), axis=1)
    docs = jnp.stack([begins, ends]).reshape(2, blocks, BLOCK)
    docs = jnp.tile(jnp.transpose(docs, (1, 0, 2)), (1, 4, GROUP))
    first = begins[::BLOCK] // BLOCK
    here = REACH * blocks + jnp.arange(blocks, dtype=jnp.int32)
    fixed = jnp.stack([here - 1, here, here + 1, first, first + 1], axis=-1)
    picked = lax.dynamic_slice_in_dim(random_blocks, chunk * blocks, blocks, axis=1)
    picked = picked - (chunk - REACH) * blocks
    rows = jnp.concatenate(
        [jnp.broadcast_to(fixed[None], (heads, blocks, 5)), picked], axis=-1
    )
    earlier = jnp.arange(TILES)[None, :] < jnp.arange(TILES)[:, None]
    repeat = jnp.any((rows[..., :, None] == rows[..., None, :]) & earlier, axis=-1)
    rows = jnp.clip(rows, 0, (1 + 2 * REACH) * blocks - 1)
    return (rows + jnp.where(repeat, repeated, 0)).reshape(-1), docs


def side_pairs(blk, head, far):
    pairs = []
    for b in range(blk):
        for h in range(head):
            down = h < head // 2
            if far and h not in (0, head - 1):
                continue
            source = b - 1 if down else b + 1
            if 0 <= source < blk:
                pairs.append((h * blk + source, h * blk + b))
    return pairs


def widen(tokens_rows, blk, head):
    rows = tokens_rows.shape[0]
    h = lax.axis_index("head")
    line = lax.all_gather(tokens_rows, "head", axis=0, tiled=True)
    low = h < head // 2
    near = lax.dynamic_slice_in_dim(line, jnp.where(low, head - 1, 0) * rows, rows)
    far = lax.dynamic_slice_in_dim(line, jnp.where(low, head - 2, 1) * rows, rows)
    near = lax.ppermute(near, ("head", "blk"), side_pairs(blk, head, False))
    far = lax.ppermute(far, ("head", "blk"), side_pairs(blk, head, True))
    whole = jnp.concatenate([far, near, line, near, far], axis=0)
    return lax.dynamic_slice_in_dim(whole, h * rows, (1 + 2 * REACH) * rows)


def narrow(wide_rows, rows, blk, head):
    h = lax.axis_index("head")
    low = h < head // 2
    frame = jnp.zeros(((head + 2 * REACH) * rows, wide_rows.shape[1]), wide_rows.dtype)
    frame = lax.dynamic_update_slice_in_dim(frame, wide_rows, h * rows, 0)
    near = lax.dynamic_slice_in_dim(frame, jnp.where(low, 1, head + REACH) * rows, rows)
    far = lax.dynamic_slice_in_dim(frame, jnp.where(low, 0, head + REACH + 1) * rows, rows)
    back = [(t, s) for s, t in side_pairs(blk, head, False)]
    near = lax.ppermute(near, ("head", "blk"), back)
    back = [(t, s) for s, t in side_pairs(blk, head, True)]
    far = lax.ppermute(far, ("head", "blk"), back)
    line = frame[REACH * rows : (REACH + head) * rows].reshape(head, rows, -1)
    place = jnp.arange(head, dtype=jnp.int32)[:, None, None]
    line = line + jnp.where(place == jnp.where(low, head - 1, 0), near[None], 0)
    line = line + jnp.where(place == jnp.where(low, head - 2, 1), far[None], 0)
    return lax.psum_scatter(line.reshape(head * rows, -1), "head", scatter_dimension=0, tiled=True)


LINE = 4
CORES = 2
PIECES = 4
PIECES_BACK = 8
MESH = pl.DeviceIdType.MESH
NEAR_SLOT = (1, 0, 4, 3)
FAR_SLOT = (0, None, None, 4)
WORK_ORDER = ((3, 1, 0, 4, 2), (0, 4, 3, 1, 2), (4, 0, 1, 3, 2), (1, 3, 4, 0, 2))


def remote(source, target, send, recv, head, blk):
    return pltpu.make_async_remote_copy(
        src_ref=source,
        dst_ref=target,
        send_sem=send,
        recv_sem=recv,
        device_id=(head, blk),
        device_id_type=MESH,
    )


def at_each_head(h, body):
    for hh in range(LINE):
        pl.when(h == hh)(partial(body, hh))


def greet_plane_and_line(h, b, blk):
    barrier = pltpu.get_barrier_semaphore()
    for d in range(1, LINE):
        pl.semaphore_signal(
            barrier, inc=1, device_id=((h + d) % LINE, b), device_id_type=MESH
        )
    for d in range(1, blk):
        pl.semaphore_signal(barrier, inc=1, device_id=(h, (b + d) % blk), device_id_type=MESH)
    pl.semaphore_wait(barrier, LINE - 1 + blk - 1)


def gather_kernel(blk, count, *refs):
    x_ref, shards = refs[0], refs[1 : 1 + count]
    wide, spill, fulls = refs[1 + count], refs[2 + count], refs[3 + count : 3 + 2 * count]
    local, zs, zr, cs, cr, ss, sr, us, ur, ds, dr, ns, nr, fs, fr = refs[3 + 2 * count :]
    h, b = lax.axis_index("head"), lax.axis_index("blk")
    chips = blk // CORES
    chip, core = b // CORES, b % CORES
    sibling = chip * CORES + 1 - core
    rows = x_ref.shape[0] // PIECES

    def piece(ref, p):
        return ref.at[pl.ds(p * rows, rows)]

    def place(hh, j):
        slot = 2 + j - hh
        return wide.at[slot] if 0 <= slot < 5 else spill

    def own(a):
        return pltpu.make_async_copy(shards[a], fulls[a].at[h, b], local.at[a])

    def along(a, d):
        return remote(
            shards[a], fulls[a].at[h, b], zs.at[a, d - 1], zr.at[a, d - 1], (h + d) % LINE, b
        )

    def along_arrives(a, d):
        src = (h - d + LINE) % LINE
        return remote(
            shards[a], fulls[a].at[src, b], zs.at[a, d - 1], zr.at[a, d - 1], (h + d) % LINE, b
        )

    def over(a, e):
        part = fulls[a].at[:, b]
        there = ((chip + e) % chips) * CORES + core
        return remote(part, part, cs.at[a, e - 1], cr.at[a, e - 1], h, there)

    def over_arrives(a, e):
        there = ((chip - e + chips) % chips) * CORES + core
        part = fulls[a].at[:, there]
        return remote(part, part, cs.at[a, e - 1], cr.at[a, e - 1], h, there)

    def across(a, e):
        part = fulls[a].at[:, ((chip - e + chips) % chips) * CORES + core]
        return remote(part, part, ss.at[a, e], sr.at[a, e], h, sibling)

    def across_arrives(a, e):
        part = fulls[a].at[:, ((chip - e + chips) % chips) * CORES + 1 - core]
        return remote(part, part, ss.at[a, e], sr.at[a, e], h, sibling)

    def spread(a):
        for d in range(1, LINE):
            along_arrives(a, d).wait_recv()
        own(a).wait()
        for e in range(1, chips):
            over(a, e).start()
        across(a, 0).start()

    def hand_over(a):
        for e in range(1, chips):
            over_arrives(a, e).wait_recv()
            across(a, e).start()

    def up(hh, j, p):
        source = x_ref if j == hh else place(hh, j)
        return remote(
            piece(source, p), piece(place(hh + 1, j), p), us.at[j, p], ur.at[j, p], (h + 1) % LINE, b
        )

    def up_arrives(hh, j, p):
        target = piece(place(hh, j), p)
        return remote(target, target, us.at[j, p], ur.at[j, p], (h + 1) % LINE, b)

    def down(hh, j, p):
        source = x_ref if j == hh else place(hh, j)
        return remote(
            piece(source, p), piece(place(hh - 1, j), p), ds.at[j, p], dr.at[j, p], (h + 3) % LINE, b
        )

    def down_arrives(hh, j, p):
        target = piece(place(hh, j), p)
        return remote(target, target, ds.at[j, p], dr.at[j, p], (h + 3) % LINE, b)

    def sides(hh, j):
        near, far = (3, 2) if hh < 2 else (0, 1)
        if j == near:
            return [(NEAR_SLOT[hh], ns, nr)]
        if j == far and FAR_SLOT[hh] is not None:
            return [(FAR_SLOT[hh], fs, fr)]
        return []

    def side(hh, j, p, slot, send, recv):
        target = (b + 1) % blk if hh < 2 else (b + blk - 1) % blk
        return remote(
            piece(place(hh, j), p), piece(wide.at[slot], p), send.at[p], recv.at[p], h, target
        )

    def sends_side(hh):
        return b < blk - 1 if hh < 2 else b > 0

    def gets_side(hh):
        return b > 0 if hh < 2 else b < blk - 1

    def side_slots(hh):
        found = [(NEAR_SLOT[hh], ns, nr)]
        if FAR_SLOT[hh] is not None:
            found.append((FAR_SLOT[hh], fs, fr))
        return found

    def fill(n, slot):
        return pltpu.make_async_copy(x_ref, wide.at[slot], local.at[count + 1 + n])

    def own_rows():
        return pltpu.make_async_copy(x_ref, wide.at[2], local.at[count])

    def begin(hh):
        for p in range(PIECES):
            if hh < LINE - 1:
                up(hh, hh, p).start()
            if hh > 0:
                down(hh, hh, p).start()

        @pl.when(jnp.logical_not(gets_side(hh)))
        def _():
            for n, (slot, _, _) in enumerate(side_slots(hh)):
                fill(n, slot).start()

    def pass_on(distance, hh):
        for p in range(PIECES):
            for j, arrives, onward, ends in (
                (hh - distance, up_arrives, up, hh == LINE - 1),
                (hh + distance, down_arrives, down, hh == 0),
            ):
                if not 0 <= j < LINE:
                    continue
                arrives(hh, j, p).wait_recv()
                if not ends:
                    onward(hh, j, p).start()
                for slot, send, recv in sides(hh, j):

                    @pl.when(sends_side(hh))
                    def _(slot=slot, send=send, recv=recv):
                        side(hh, j, p, slot, send, recv).start()

    def finish(hh):
        for p in range(PIECES):
            for j in range(LINE):
                if j <= hh < LINE - 1:
                    up(hh, j, p).wait_send()
                if j >= hh > 0:
                    down(hh, j, p).wait_send()

        @pl.when(sends_side(hh))
        def _():
            for j in range(LINE):
                for slot, send, recv in sides(hh, j):
                    for p in range(PIECES):
                        side(hh, j, p, slot, send, recv).wait_send()

        @pl.when(gets_side(hh))
        def _():
            for slot, send, recv in side_slots(hh):
                for p in range(PIECES):
                    target = piece(wide.at[slot], p)
                    remote(target, target, send.at[p], recv.at[p], h, (b + 1) % blk).wait_recv()

        @pl.when(jnp.logical_not(gets_side(hh)))
        def _():
            for n, (slot, _, _) in enumerate(side_slots(hh)):
                fill(n, slot).wait()

    own_rows().start()
    for a in range(count):
        own(a).start()
    greet_plane_and_line(h, b, blk)
    for a in range(count):
        for d in range(1, LINE):
            along(a, d).start()
    at_each_head(h, begin)
    for a in range(count):
        spread(a)
    at_each_head(h, partial(pass_on, 1))
    for a in range(count - 2):
        hand_over(a)
    at_each_head(h, partial(pass_on, 2))
    hand_over(count - 2)
    at_each_head(h, partial(pass_on, 3))
    hand_over(count - 1)
    for a in range(count):
        for d in range(1, LINE):
            along(a, d).wait_send()
        for e in range(1, chips):
            over(a, e).wait_send()
        for e in range(chips):
            across(a, e).wait_send()
            across_arrives(a, e).wait_recv()
    own_rows().wait()
    at_each_head(h, finish)


def gather(tokens, shards, blk):
    rows, width = tokens.shape
    count, chips = len(shards), blk // CORES
    anywhere = pl.BlockSpec(memory_space=pl.ANY)
    dma = pltpu.SemaphoreType.DMA
    outs = pl.pallas_call(
        partial(gather_kernel, blk, count),
        out_shape=[
            jax.ShapeDtypeStruct((5, rows, width), tokens.dtype),
            jax.ShapeDtypeStruct((rows, width), tokens.dtype),
        ]
        + [jax.ShapeDtypeStruct((LINE, blk) + s.shape, s.dtype) for s in shards],
        in_specs=[anywhere] * (1 + count),
        out_specs=[anywhere] * (2 + count),
        scratch_shapes=[dma((count + 3,))]
        + [dma((count, LINE - 1))] * 2
        + [dma((count, chips - 1))] * 2
        + [dma((count, chips))] * 2
        + [dma((LINE, PIECES))] * 4
        + [dma((PIECES,))] * 4,
        compiler_params=pltpu.CompilerParams(collective_id=0, has_side_effects=True),
        name="gather",
    )(tokens, *shards)
    return outs[0], outs[2:]


def pair_kernel(blk, *refs):
    chips = blk // CORES
    grads, outs, rest = refs[:2], refs[2 : 2 + chips], refs[2 + chips :]
    held, arrived, (load, send, recv) = rest[:2], rest[2:4], rest[4:]
    h, b = lax.axis_index("head"), lax.axis_index("blk")
    chip, core = b // CORES, b % CORES
    sibling = chip * CORES + 1 - core

    def part(a, there):
        if a == 0:
            return grads[a].at[:, there, :, pl.ds(3 * 768, 768)]
        return grads[a].at[:, there]

    def mine(a, e):
        there = ((chip + e) % chips) * CORES + core
        return pltpu.make_async_copy(part(a, there), held[a].at[e], load.at[a, e])

    def across(a, e):
        there = ((chip + e) % chips) * CORES + 1 - core
        return remote(
            part(a, there), arrived[a].at[e], send.at[a, e], recv.at[a, e], h, sibling
        )

    order = [e % chips for e in range(1, chips + 1)]
    for e in order:
        for a in range(2):
            mine(a, e).start()
    barrier = pltpu.get_barrier_semaphore()
    pl.semaphore_signal(barrier, inc=1, device_id=(h, sibling), device_id_type=MESH)
    pl.semaphore_wait(barrier, 1)
    for e in order:
        for a in range(2):
            across(a, e).start()
    for e in order:
        for a in range(2):
            mine(a, e).wait()
            across(a, e).wait_recv()

        def one(n, carry, e=e):
            inner, outer = (
                held[a][e, n].astype(f32) + arrived[a][e, n].astype(f32) for a in range(2)
            )
            spare = jnp.zeros((8, 768), f32)
            outs[e][n, 0:32] = jnp.concatenate([inner, spare], axis=0).astype(bf16)
            outs[e][n, 32:128] = outer.astype(bf16)
            return carry

        lax.fori_loop(0, LINE, one, 0)
    for e in order:
        for a in range(2):
            across(a, e).wait_send()


def pair_sums(grads, blk):
    chips = blk // CORES
    shard = [(24, 768), (96, 768)]
    dma = pltpu.SemaphoreType.DMA
    inside = pl.BlockSpec(memory_space=pltpu.VMEM)
    return pl.pallas_call(
        partial(pair_kernel, blk),
        out_shape=[jax.ShapeDtypeStruct((LINE, 128, 768), bf16)] * chips,
        in_specs=[pl.BlockSpec(memory_space=pl.ANY)] * 2,
        out_specs=[inside] * chips,
        scratch_shapes=[pltpu.VMEM((chips, LINE) + s, bf16) for s in shard] * 2
        + [dma((2, chips))] * 3,
        compiler_params=pltpu.CompilerParams(
            collective_id=2, has_side_effects=True, vmem_limit_bytes=56 << 20
        ),
        name="pair_sums",
    )(*grads)


def over_plane(sums, blk, head):
    chips = blk // CORES
    received = [sums[0]]
    for e in range(1, chips):
        pairs = [
            (
                h * blk + k * CORES + c,
                h * blk + ((k + e) % chips) * CORES + c,
            )
            for h in range(head)
            for k in range(chips)
            for c in range(CORES)
        ]
        received.append(lax.ppermute(sums[e], ("head", "blk"), pairs))
    return received


def reduce_kernel(blk, count, *refs):
    small_ref, wide_ref, query_ref, key_ref, value_ref = refs[:5]
    weights, first_ref = refs[5:8], refs[8]
    chips = blk // CORES
    early, raw = refs[9 : 9 + chips], refs[9 + chips : 11 + chips]
    rest = refs[11 + chips :]
    sum_ref, outs, early_outs = rest[0], rest[1 : 1 + count], rest[1 + count : 4 + count]
    early_sum, early_in, es, er = rest[4 + count : 8 + count]
    totals, (wide_in, key_in, value_in, fed) = rest[8 + count : 11 + count], rest[11 + count : 15 + count]
    rest = rest[15 + count :]
    weight_in, early_here, loaded = rest[:3], rest[3 : 3 + chips], rest[3 + chips]
    rest = rest[4 + chips :]
    extra = count
    held, from_core, rest = rest[: count + 1], rest[count + 1 : 2 * count + 1], rest[2 * count + 1 :]
    from_chip, from_line, rest = rest[: count + 1], rest[count + 1 : 2 * count + 2], rest[2 * count + 2 :]
    raw_own, raw_in, (rl, rs, rr), rest = rest[:2], rest[2:4], rest[4:7], rest[7:]
    frame, arrived, aside = rest[:3]
    load, ss, sr, cs, cr, zs, zr, us, ur, ds, dr, ns, nr, fs, fr = rest[3:]
    grads = (small_ref,) + tuple(totals)
    h, b = lax.axis_index("head"), lax.axis_index("blk")
    chip, core = b // CORES, b % CORES
    sibling = chip * CORES + 1 - core
    chunk_rows = sum_ref.shape[0]
    rows = chunk_rows // PIECES_BACK

    feed_rows = wide_in.shape[1]
    halves = chunk_rows // feed_rows
    slots = 1 + 2 * REACH

    def slot_at(n):
        slot = REACH
        for hh in range(LINE):
            for k in range(slots):
                slot = jnp.where((h == hh) & (n == k), WORK_ORDER[hh][k], slot)
        return slot

    def feed(slot, half):
        some = pl.ds(slot * chunk_rows + half * feed_rows, feed_rows)
        return [
            pltpu.make_async_copy(source.at[some], target.at[half], fed.at[n, half])
            for n, (source, target) in enumerate(
                ((wide_ref, wide_in), (key_ref, key_in), (value_ref, value_in))
            )
        ]

    def feed_queries(half):
        some = pl.ds(half * feed_rows, feed_rows)
        wide_some = pl.ds(REACH * chunk_rows + half * feed_rows, feed_rows)
        return [
            pltpu.make_async_copy(wide_ref.at[wide_some], wide_in.at[half], fed.at[0, half]),
            pltpu.make_async_copy(query_ref.at[some], key_in.at[half], fed.at[1, half]),
        ]

    def start(copies):
        for copy in copies:
            copy.start()

    def wait(copies):
        for copy in copies:
            copy.wait()

    def standing():
        pairs = list(zip(weights, weight_in)) + list(zip(early, early_here)) + [(first_ref, sum_ref)]
        return [
            pltpu.make_async_copy(source, target, loaded.at[n])
            for n, (source, target) in enumerate(pairs)
        ]

    def add_product(total, left, right, fresh):
        half = left.shape[1] // 2
        for n in range(2):
            lines = LINE // 2
            part = mm_tn(left[:, n * half : (n + 1) * half], right)
            part = part.reshape((lines,) + total.shape[1:])
            here = pl.ds(n * lines, lines)
            total[here] = part if fresh else total[here] + part

    def work(n, carry):
        slot = slot_at(n)
        for half in range(halves):
            if half + 1 < halves:
                start(feed(slot, half + 1))
            else:

                @pl.when(n + 1 < slots)
                def _():
                    start(feed(slot_at(n + 1), 0))

            wait(feed(slot, half))
            for t in range(feed_rows // ROWS):
                s = pl.ds(t * ROWS, ROWS)
                grad = mm_nt(key_in[half, s], weight_in[1][...]) + mm_nt(
                    value_in[half, s], weight_in[2][...]
                )
                frame[slot, pl.ds(half * feed_rows + t * ROWS, ROWS)] = grad.astype(bf16)
            add_product(totals[1], wide_in[half], key_in[half], False)
            add_product(totals[2], wide_in[half], value_in[half], False)
        for hh in range(LINE):
            for k in range(slots):
                pl.when((h == hh) & (n == k))(partial(send_off, hh, WORK_ORDER[hh][k]))
        return carry

    def query_work():
        start(feed_queries(0))
        for half in range(halves):
            if half + 1 < halves:
                start(feed_queries(half + 1))
            wait(feed_queries(half))
            for t in range(feed_rows // ROWS):
                s = pl.ds(t * ROWS, ROWS)
                here = pl.ds(half * feed_rows + t * ROWS, ROWS)
                sum_ref[here] += mm_nt(key_in[half, s], weight_in[0][...])
            add_product(totals[0], wide_in[half], key_in[half], half == 0)

    def mine(a, k):
        return pltpu.make_async_copy(grads[a].at[:, k * CORES + core], held[a].at[k], load.at[a, k])

    def raw_part(n, there):
        return raw[n].at[:, there, :, pl.ds(0, raw_own[n].shape[3])]

    def mine_raw(n, k):
        there = k * CORES + core
        return pltpu.make_async_copy(raw_part(n, there), raw_own[n].at[k], rl.at[n, k])

    def across_raw(n, k):
        there = k * CORES + 1 - core
        return remote(raw_part(n, there), raw_in[n].at[k], rs.at[n, k], rr.at[n, k], h, sibling)

    def pack_raw(k):
        for n in range(2):
            mine_raw(n, k).wait()
            across_raw(n, k).wait_recv()

        def one(m, carry):
            attn, inner = (
                raw_own[n][k, m].astype(f32) + raw_in[n][k, m].astype(f32) for n in range(2)
            )
            parts = [attn] + [inner[:, c * 768 : (c + 1) * 768] for c in range(3)]
            for c in range(2):
                both = jnp.concatenate(parts[2 * c : 2 * c + 2], axis=0)
                held[extra][k, m, 48 * c : 48 * (c + 1)] = both.astype(bf16)
            return carry

        lax.fori_loop(0, LINE, one, 0)

    def across(a, k):
        return remote(
            grads[a].at[:, k * CORES + 1 - core],
            from_core[a].at[k],
            ss.at[a, k],
            sr.at[a, k],
            h,
            sibling,
        )

    def over(a, e):
        k = (chip + e) % chips
        return remote(
            held[a].at[k],
            from_chip[a].at[e - 1],
            cs.at[a, e - 1],
            cr.at[a, e - 1],
            h,
            k * CORES + core,
        )

    def along(a, d):
        there = (h + d) % LINE
        return remote(
            held[a].at[chip, there],
            from_line[a].at[d - 1],
            zs.at[a, d - 1],
            zr.at[a, d - 1],
            there,
            b,
        )

    def add_cores(a, k):
        def one(n, carry):
            own = held[a][k, n] if a == 0 else grads[a][n, k * CORES + core]
            held[a][k, n] = (own + from_core[a][k, n]).astype(held[a].dtype)
            return carry

        lax.fori_loop(0, LINE, one, 0)

    def to_chips(a):
        for k in range(chips):
            if a == 0:
                mine(a, k).wait()
            across(a, k).wait_recv()
        for e in range(1, chips):
            add_cores(a, (chip + e) % chips)
            over(a, e).start()
        add_cores(a, chip)

    def to_line(a):
        for e in range(1, chips):
            over(a, e).wait_recv()

        def one(n, carry):
            total = held[a][chip, n].astype(f32)
            for e in range(1, chips):
                total = total + from_chip[a][e - 1, n].astype(f32)
            held[a][chip, n] = total.astype(held[a].dtype)
            return carry

        lax.fori_loop(0, LINE, one, 0)
        for d in range(1, LINE):
            along(a, d).start()

    def to_owner(a):
        for d in range(1, LINE):
            along(a, d).wait_recv()
        total = held[a][chip, h].astype(f32)
        for d in range(1, LINE):
            total = total + from_line[a][d - 1].astype(f32)
        outs[a][...] = total

    def early_along(d):
        there = (h + d) % LINE
        return remote(
            early_sum.at[there], early_in.at[d - 1], es.at[d - 1], er.at[d - 1], there, b
        )

    def early_to_line():
        def one(n, carry):
            total = early_here[0][n].astype(f32)
            for ref in early_here[1:]:
                total = total + ref[n].astype(f32)
            early_sum[n] = total.astype(bf16)
            return carry

        lax.fori_loop(0, LINE, one, 0)
        for d in range(1, LINE):
            early_along(d).start()

    def early_to_owner():
        for d in range(1, LINE):
            early_along(d).wait_recv()
        total = early_sum[h].astype(f32)
        for d in range(1, LINE):
            total = total + early_in[d - 1].astype(f32)
        attn_ref, inner_ref, outer_ref = early_outs
        inner_ref[:, 3 * 768 :] = total[:24]
        outer_ref[...] = total[32:]
        for d in range(1, LINE):
            along(extra, d).wait_recv()
        total = held[extra][chip, h].astype(f32)
        for d in range(1, LINE):
            total = total + from_line[extra][d - 1].astype(f32)
        attn_ref[...] = total[:24]
        for n in range(3):
            inner_ref[:, n * 768 : (n + 1) * 768] = total[24 * (n + 1) : 24 * (n + 2)]

    def part(p):
        return pl.ds(p * rows, rows)

    def piece(ref, p):
        return ref.at[part(p)]

    def add_rows(target, j, source, n, p):
        def one(step, carry):
            some = pl.ds(p * rows + step * 64, 64)
            target[j, some] = (
                target[j, some].astype(f32) + source[n, some].astype(f32)
            ).astype(target.dtype)
            return carry

        lax.fori_loop(0, rows // 64, one, 0)

    def slot_of(hh, j):
        slot = 2 + j - hh
        return slot if 0 <= slot < slots else slots

    def arrival(hh, j, upward):
        return arrived.at[LINE if j == hh and not upward else j]

    def up(hh, j, p):
        return remote(
            piece(frame.at[slot_of(hh, j)], p),
            piece(arrival(hh + 1, j, True), p),
            us.at[j, p],
            ur.at[j, p],
            (h + 1) % LINE,
            b,
        )

    def up_arrives(hh, j, p):
        here = piece(arrival(hh, j, True), p)
        return remote(here, here, us.at[j, p], ur.at[j, p], (h + 1) % LINE, b)

    def down(hh, j, p):
        return remote(
            piece(frame.at[slot_of(hh, j)], p),
            piece(arrival(hh - 1, j, False), p),
            ds.at[j, p],
            dr.at[j, p],
            (h + 3) % LINE,
            b,
        )

    def down_arrives(hh, j, p):
        here = piece(arrival(hh, j, False), p)
        return remote(here, here, ds.at[j, p], dr.at[j, p], (h + 3) % LINE, b)

    def side_parts(hh):
        near, far = (3, 2) if hh < 2 else (0, 1)
        found = [(NEAR_SLOT[hh], near, 0, ns, nr)]
        if FAR_SLOT[hh] is not None:
            found.append((FAR_SLOT[hh], far, 1, fs, fr))
        return found

    def side(hh, slot, n, send, recv, p):
        target = (b + blk - 1) % blk if hh < 2 else (b + 1) % blk
        return remote(
            piece(frame.at[slot], p), piece(aside.at[n], p), send.at[p], recv.at[p], h, target
        )

    def sends_side(hh):
        return b > 0 if hh < 2 else b < blk - 1

    def gets_side(hh):
        return b < blk - 1 if hh < 2 else b > 0

    def send_off(hh, slot):
        @pl.when(sends_side(hh))
        def _():
            for p in range(PIECES_BACK):
                for side_slot, _, n, send, recv in side_parts(hh):
                    if side_slot == slot:
                        side(hh, slot, n, send, recv, p).start()

        for p in range(PIECES_BACK):
            if hh == 0 and slot == slot_of(0, 1):
                up(hh, 1, p).start()
            if hh == LINE - 1 and slot == slot_of(LINE - 1, 2):
                down(hh, 2, p).start()

    def take_sides(hh):
        for p in range(PIECES_BACK):
            for _, j, n, send, recv in side_parts(hh):

                @pl.when(gets_side(hh))
                def _(j=j, n=n, send=send, recv=recv):
                    here = piece(aside.at[n], p)
                    remote(here, here, send.at[p], recv.at[p], h, (b + 1) % blk).wait_recv()
                    add_rows(frame, slot_of(hh, j), aside, n, p)

                if hh == 0:
                    up(hh, j, p).start()
                if hh == LINE - 1:
                    down(hh, j, p).start()

    def pass_on(hh):
        moves = []
        if hh == 1:
            moves = [(3, True), (2, True), (0, False)]
        if hh == 2:
            moves = [(0, False), (1, False), (3, True)]
        for p in range(PIECES_BACK):
            for j, upward in moves:
                (up_arrives if upward else down_arrives)(hh, j, p).wait_recv()
                add_rows(frame, slot_of(hh, j), arrived, j, p)
                (up if upward else down)(hh, j, p).start()

    def finish(hh):
        for p in range(PIECES_BACK):
            sources = []
            if hh > 0:
                up_arrives(hh, hh, p).wait_recv()
                sources.append(hh)
            if hh < LINE - 1:
                down_arrives(hh, hh, p).wait_recv()
                sources.append(LINE)

            def one(step, carry, p=p, sources=tuple(sources)):
                some = pl.ds(p * rows + step * 64, 64)
                total = sum_ref[some] + frame[REACH, some].astype(f32)
                for n in sources:
                    total = total + arrived[n, some].astype(f32)
                sum_ref[some] = total
                return carry

            lax.fori_loop(0, rows // 64, one, 0)
        for p in range(PIECES_BACK):
            for j in range(LINE):
                if j > hh:
                    up(hh, j, p).wait_send()
                if j < hh:
                    down(hh, j, p).wait_send()

        @pl.when(sends_side(hh))
        def _():
            for p in range(PIECES_BACK):
                for slot, _, n, send, recv in side_parts(hh):
                    side(hh, slot, n, send, recv, p).wait_send()

    start(feed(slot_at(0), 0))
    start(standing())
    for k in range(chips):
        mine(0, k).start()
        for n in range(2):
            mine_raw(n, k).start()
    frame[slots] = jnp.zeros(frame.shape[1:], frame.dtype)
    for n in (1, 2):
        totals[n][...] = jnp.zeros_like(totals[n])
    greet_plane_and_line(h, b, blk)
    for k in range(chips):
        for n in range(2):
            across_raw(n, k).start()
    ready = standing()
    wait(ready[3:-1])
    early_to_line()
    wait(ready[:3] + ready[-1:])
    lax.fori_loop(0, slots, work, 0)
    query_work()
    for e in range(1, chips):
        pack_raw((chip + e) % chips)
        over(extra, e).start()
    pack_raw(chip)
    for a in range(count):
        for k in range(chips):
            across(a, k).start()
    at_each_head(h, take_sides)
    for a in range(count):
        to_chips(a)
    at_each_head(h, pass_on)
    for a in range(count + 1):
        to_line(a)
    at_each_head(h, finish)
    early_to_owner()
    for d in range(1, LINE):
        early_along(d).wait_send()
    for a in range(count):
        to_owner(a)
    for a in range(count):
        for k in range(chips):
            across(a, k).wait_send()
    for a in range(count + 1):
        for e in range(1, chips):
            over(a, e).wait_send()
        for d in range(1, LINE):
            along(a, d).wait_send()
    for k in range(chips):
        for n in range(2):
            across_raw(n, k).wait_send()


def reduce_to_owners(small, wide, projected, weights, first, early, raw, blk):
    rows, width = first.shape
    count, chips = 4, blk // CORES
    anywhere = pl.BlockSpec(memory_space=pl.ANY)
    inside = pl.BlockSpec(memory_space=pltpu.VMEM)
    dma = pltpu.SemaphoreType.DMA
    square = (width // (LINE * blk), width)
    shard = [small.shape[2:]] + [square] * 3
    kinds = [f32] + [bf16] * 4
    travels = shard + [(96, 768)]
    early_shapes = ((24, 768), (24, 3072), (96, 768))
    outs = pl.pallas_call(
        partial(reduce_kernel, blk, count),
        out_shape=[jax.ShapeDtypeStruct((rows, width), f32)]
        + [jax.ShapeDtypeStruct(s, f32) for s in shard]
        + [jax.ShapeDtypeStruct(s, f32) for s in early_shapes],
        in_specs=[anywhere] * (11 + chips),
        out_specs=[inside] * (4 + count),
        scratch_shapes=[
            pltpu.VMEM(early[0].shape, bf16),
            pltpu.VMEM((LINE - 1,) + early[0].shape[1:], bf16),
            dma((LINE - 1,)),
            dma((LINE - 1,)),
        ]
        + [pltpu.VMEM((LINE, blk) + square, f32)] * 3
        + [pltpu.VMEM((2, rows // 2, width), bf16)] * 3
        + [dma((3, 2))]
        + [pltpu.VMEM((width, width), bf16)] * 3
        + [pltpu.VMEM(early[0].shape, bf16)] * chips
        + [dma((4 + chips,))]
        + [pltpu.VMEM((chips, LINE) + s, t) for s, t in zip(travels, kinds)]
        + [pltpu.VMEM((chips, LINE) + s, f32) for s in shard]
        + [pltpu.VMEM((chips - 1, LINE) + s, t) for s, t in zip(travels, kinds)]
        + [pltpu.VMEM((LINE - 1,) + s, t) for s, t in zip(travels, kinds)]
        + [pltpu.VMEM((chips, LINE, 24, size), bf16) for size in (768, 3 * 768)] * 2
        + [dma((2, chips))] * 3
        + [
            pltpu.VMEM((2 + 2 * REACH, rows, width), bf16),
            pltpu.VMEM((LINE + 1, rows, width), bf16),
            pltpu.VMEM((2, rows, width), bf16),
        ]
        + [dma((count + 1, chips))] * 3
        + [dma((count + 1, chips - 1))] * 2
        + [dma((count + 1, LINE - 1))] * 2
        + [dma((LINE, PIECES_BACK))] * 4
        + [dma((PIECES_BACK,))] * 4,
        compiler_params=pltpu.CompilerParams(
            collective_id=1, has_side_effects=True, vmem_limit_bytes=62 << 20
        ),
        name="reduce_to_owners",
    )(small, wide, *projected, *weights, first, *early, *raw)
    return outs[0], outs[1:-3], outs[-3:]


def whole(shard):
    return lax.all_gather(shard, ("head", "blk"), axis=0, tiled=True)


def shared_out(grad):
    return lax.psum_scatter(grad.astype(bf16), ("head", "blk"), scatter_dimension=0, tiled=True).astype(f32)


def padded_to(flat, size):
    return jnp.pad(flat, [(0, 0)] * (flat.ndim - 1) + [(0, size - flat.shape[-1])])


def per_device(blk, head, tokens, *rest):
    weights, vectors, (out_grad, segment_ids, random_blocks) = rest[:6], rest[6:15], rest[15:]
    rows = tokens.shape[0]
    by_kernel = head == LINE and blk == LINE * CORES
    short = [vectors[n] for n in (2, 3, 4, 6, 7, 8, 0, 1)]
    if by_kernel:
        packed = jnp.concatenate(
            [
                padded_to(jnp.stack(short), 128),
                padded_to(vectors[5][None], 128),
                jnp.zeros((7, 128), bf16),
            ]
        )
        wide, fulls = gather(tokens, [packed] + list(weights), blk)
        wide = wide.reshape(-1, tokens.shape[1])
        w_query, w_key, w_value, w_attn, w_inner, w_outer = [
            w.reshape(-1, w.shape[-1]) for w in fulls[1:]
        ]
        table = fulls[0].reshape(head * blk, 16, 128)
    else:
        wide = widen(tokens, blk, head)
        w_query, w_key, w_value, w_attn, w_inner, w_outer = [whole(w) for w in weights]
        packed = jnp.concatenate(
            [padded_to(jnp.stack(short), 128), padded_to(vectors[5][None], 128)]
        )
        table = whole(packed[None])
    short_rows = jnp.transpose(table[:, :8, : short[0].shape[0]], (1, 0, 2)).astype(f32)
    short_rows = short_rows.reshape(8, -1)
    bias_inner = table[:, 8, : vectors[5].shape[0]].astype(f32).reshape(-1, 1, PIECE)

    rows_of, docs = tile_plan(segment_ids, random_blocks, rows)
    keys, values, queries = project(wide, w_key, w_value, w_query, short_rows, rows)
    attended, probs = attend(rows_of, queries, keys, values, docs)

    result, grad_first_sum, grad_attended, grad_w_attn, grad_w_inner, grad_w_outer, sums_d, sums_ff = (
        middle(
            attended,
            tokens,
            out_grad,
            w_attn,
            w_inner,
            w_outer,
            short_rows,
            bias_inner,
        )
    )

    early_grads = [grad_w_attn, grad_w_inner, grad_w_outer]
    if by_kernel:
        raw = [g.reshape(head, blk, -1, g.shape[-1]) for g in early_grads]
        early = over_plane(pair_sums(raw[1:], blk), blk, head)
    grad_scaled, grad_keyed, grad_valued, sums_qv = attend_back(
        rows_of, queries, grad_attended, keys, values, probs
    )
    sums = jnp.concatenate([sums_d[:6], sums_qv[6:]])
    sums = jnp.transpose(sums.reshape(8, head * blk, -1), (1, 0, 2))
    packed = jnp.concatenate(
        [
            padded_to(sums, 128),
            padded_to(sums_ff.reshape(head * blk, 1, -1), 128),
            jnp.zeros((head * blk, 7, 128), f32),
        ],
        axis=1,
    )
    if by_kernel:
        grad_tokens, late, early_sum = reduce_to_owners(
            packed.reshape(head, blk, 16, 128),
            wide,
            (grad_scaled, grad_keyed, grad_valued),
            (w_query, w_key, w_value),
            grad_first_sum,
            early,
            raw[:2],
            blk,
        )
        matrix_grads = tuple(late[1:]) + tuple(early_sum)
        packed = late[0]
    else:
        grad_wide = (mm_nt(grad_keyed, w_key) + mm_nt(grad_valued, w_value)).astype(bf16)
        grad_tokens = (
            grad_first_sum
            + mm_nt(grad_scaled, w_query)
            + narrow(grad_wide, rows, blk, head).astype(f32)
        )
        late_grads = [mm_tn(tokens, grad_scaled), mm_tn(wide, grad_keyed), mm_tn(wide, grad_valued)]
        matrix_grads = tuple(shared_out(g) for g in late_grads + early_grads)
        packed = lax.psum_scatter(packed, ("head", "blk"), scatter_dimension=0, tiled=True)[0]
    order = (6, 7, 0, 1, 2, 8, 3, 4, 5)
    vector_grads = tuple(packed[n, : v.shape[0]] for n, v in zip(order, vectors))
    return (result, grad_tokens) + matrix_grads + vector_grads


def solution(mesh):
    row = P(("blk", "head"), None)
    matrix = P(("head", "blk"), None)
    vector = P(("head", "blk"))
    return jax.shard_map(
        partial(per_device, mesh.shape["blk"], mesh.shape["head"]),
        mesh=mesh,
        in_specs=(row,) + (matrix,) * 6 + (vector,) * 9 + (row, P(), P()),
        out_specs=(row, row) + (matrix,) * 6 + (vector,) * 9,
        check_vma=False,
    )
```

```python
from functools import partial

import jax
import jax.numpy as jnp
from jax import lax
from jax.experimental import pallas as pl
from jax.experimental.pallas import tpu as pltpu
from jax.sharding import PartitionSpec as P

HEAD_DIM = 64
BLOCK = 64
RANDOM = 3
TILES = 5 + RANDOM
REACH = 2
GROUP = 4
FORWARD_BLOCKS = 8
BACKWARD_BLOCKS = 8
ROWS = 256
PIECE = 768

epsilon = 1e-06
masked_value = -1e30
query_scale = 0.125
gelu_scale = 0.7978845608028654
gelu_cubic = 0.044715
far_away = -(1 << 24)
repeated = 1 << 20
f32, bf16 = jnp.float32, jnp.bfloat16


def mm(a, b):
    return jnp.dot(a, b, preferred_element_type=f32)


def mm_nt(a, b):
    return lax.dot_general(a, b, (((1,), (1,)), ((), ())), preferred_element_type=f32)


def mm_tn(a, b):
    return lax.dot_general(a, b, (((0,), (0,)), ((), ())), preferred_element_type=f32)


def head_mask(rows, cols, first):
    lanes = lax.broadcasted_iota(jnp.int32, (rows, cols), 1)
    return (lanes >= first) & (lanes < first + HEAD_DIM)


def stacked_by_head(tile):
    rows, cols = tile.shape
    return jnp.concatenate(
        [
            jnp.where(head_mask(rows, cols, h * HEAD_DIM), tile, jnp.zeros_like(tile))
            for h in range(cols // HEAD_DIM)
        ],
        axis=0,
    )


def own_head_columns(stacked):
    cols = stacked.shape[1]
    total = None
    for h in range(cols // HEAD_DIM):
        part = stacked[h * BLOCK : (h + 1) * BLOCK]
        part = jnp.where(head_mask(BLOCK, cols, h * HEAD_DIM), part, 0.0)
        total = part if total is None else total + part
    return total


def block_rows(row):
    return pl.ds(pl.multiple_of(row * BLOCK, BLOCK), BLOCK)


def gathered(table_ref, fixed_row, random_row):
    tiles = [table_ref[block_rows(fixed_row(t)), :] for t in range(5)]
    low = head_mask(BLOCK, 2 * HEAD_DIM, 0)
    for t in range(RANDOM):
        halves = []
        for pair in range(GROUP // 2):
            cols = pl.ds(pair * 2 * HEAD_DIM, 2 * HEAD_DIM)
            a = table_ref[block_rows(random_row(2 * pair, t)), cols]
            b = table_ref[block_rows(random_row(2 * pair + 1, t)), cols]
            halves.append(jnp.where(low, a, b))
        tiles.append(jnp.concatenate(halves, axis=1))
    return jnp.concatenate(tiles, axis=0)


def row_readers(rows_ref, blocks, i):
    group = pl.program_id(0)

    def fixed_code(t):
        return rows_ref[(group * GROUP * blocks + i) * TILES + t]

    def random_code(h, t):
        return rows_ref[((group * GROUP + h) * blocks + i) * TILES + 5 + t]

    def fixed_row(t):
        return fixed_code(t) % repeated

    def random_row(h, t):
        return random_code(h, t) % repeated

    return (fixed_row, random_row), (fixed_code, random_code)


def first_place(code):
    return jnp.where(code >= repeated, far_away, code * BLOCK)


def attend_kernel(blocks, rows_ref, q_ref, k_ref, v_ref, doc_ref, out_ref, p_ref):
    head_of = lax.broadcasted_iota(jnp.int32, (1, GROUP * BLOCK), 1) // BLOCK
    within = lax.broadcasted_iota(jnp.int32, (BLOCK, GROUP * BLOCK), 0)
    for u in range(FORWARD_BLOCKS):
        here = pl.ds(u * BLOCK, BLOCK)
        readers, (fixed_code, random_code) = row_readers(
            rows_ref, blocks, pl.program_id(1) * FORWARD_BLOCKS + u
        )
        keys = gathered(k_ref, *readers)
        values = gathered(v_ref, *readers)
        scores = mm_nt(keys, stacked_by_head(q_ref[here, :]))
        lo = doc_ref[u, 0:1, :]
        hi = doc_ref[u, 1:2, :]
        masked = []
        for t in range(TILES):
            if t < 5:
                base = first_place(fixed_code(t))
            else:
                base = first_place(random_code(0, t - 5))
                for n in range(1, GROUP):
                    base = jnp.where(head_of == n, first_place(random_code(n, t - 5)), base)
            place = within + base
            allowed = (place >= lo) & (place < hi)
            masked.append(jnp.where(allowed, scores[t * BLOCK : (t + 1) * BLOCK], masked_value))
        scores = jnp.concatenate(masked, axis=0)
        raised = jnp.exp(scores - jnp.max(scores, axis=0, keepdims=True))
        probs = (raised * (1.0 / jnp.sum(raised, axis=0, keepdims=True))).astype(bf16)
        p_ref[0, u] = probs
        out_ref[here, :] = own_head_columns(mm_tn(probs, values)).astype(bf16)


def attend_back_kernel(
    blocks,
    rows_ref,
    q_ref,
    g_ref,
    k_ref,
    v_ref,
    p_ref,
    dq_ref,
    dk_ref,
    dv_ref,
    sums_ref,
    dk_sum,
    dv_sum,
):
    step = pl.program_id(1)

    @pl.when(step == 0)
    def _():
        sums_ref[...] = jnp.zeros_like(sums_ref)
        dk_sum[...] = jnp.zeros_like(dk_sum)
        dv_sum[...] = jnp.zeros_like(dv_sum)

    found = []
    for u in range(BACKWARD_BLOCKS):
        here = pl.ds(u * BLOCK, BLOCK)
        readers, _ = row_readers(rows_ref, blocks, step * BACKWARD_BLOCKS + u)
        keys = gathered(k_ref, *readers)
        values = gathered(v_ref, *readers)
        queries = stacked_by_head(q_ref[here, :])
        grads = stacked_by_head(g_ref[here, :])
        probs = p_ref[0, u]
        grad_probs = mm_nt(values, grads)
        wide = probs.astype(f32)
        balance = jnp.sum(wide * grad_probs, axis=0, keepdims=True)
        grad_scores = (wide * (grad_probs - balance)).astype(bf16)
        dq_ref[here, :] = (query_scale * own_head_columns(mm_tn(grad_scores, keys))).astype(bf16)
        found.append((readers, mm(grad_scores, queries), mm(probs, grads)))
    for (fixed_row, random_row), grad_keys, grad_values in found:
        for total, part in ((dk_sum, grad_keys), (dv_sum, grad_values)):
            for t in range(5):
                total[block_rows(fixed_row(t)), :] += part[t * BLOCK : (t + 1) * BLOCK]
            for t in range(RANDOM):
                rows = part[(5 + t) * BLOCK : (6 + t) * BLOCK]
                for h in range(GROUP):
                    first = (h // 2) * 2 * HEAD_DIM
                    mine = head_mask(BLOCK, 2 * HEAD_DIM, (h % 2) * HEAD_DIM)
                    total[block_rows(random_row(h, t)), pl.ds(first, 2 * HEAD_DIM)] += jnp.where(
                        mine, rows[:, first : first + 2 * HEAD_DIM], 0.0
                    )

    sums_ref[6:7, :] += jnp.sum(dq_ref[...].astype(f32), axis=0, keepdims=True)

    @pl.when(step == blocks // BACKWARD_BLOCKS - 1)
    def _():
        dk_ref[...] = dk_sum[...].astype(bf16)
        dv_ref[...] = dv_sum[...].astype(bf16)
        sums_ref[7:8, :] = jnp.sum(dv_ref[...].astype(f32), axis=0, keepdims=True)


def attend(rows, queries, keys, values, docs):
    tokens, width = queries.shape
    ext = keys.shape[0]
    blocks, cols, some = tokens // BLOCK, GROUP * HEAD_DIM, FORWARD_BLOCKS
    groups = width // cols
    tile = pl.BlockSpec((some * BLOCK, cols), lambda g, i, r: (i, g))
    table = pl.BlockSpec((ext, cols), lambda g, i, r: (0, g))
    return pl.pallas_call(
        partial(attend_kernel, blocks),
        grid_spec=pltpu.PrefetchScalarGridSpec(
            num_scalar_prefetch=1,
            grid=(groups, blocks // some),
            in_specs=[
                tile,
                table,
                table,
                pl.BlockSpec((some, 8, cols), lambda g, i, r: (i, 0, 0)),
            ],
            out_specs=[
                tile,
                pl.BlockSpec((1, some, TILES * BLOCK, cols), lambda g, i, r: (g, i, 0, 0)),
            ],
        ),
        out_shape=[
            jax.ShapeDtypeStruct((tokens, width), bf16),
            jax.ShapeDtypeStruct((groups, blocks, TILES * BLOCK, cols), bf16),
        ],
        compiler_params=pltpu.CompilerParams(vmem_limit_bytes=60 << 20),
        name="attend",
    )(rows, queries, keys, values, docs)


def attend_back(rows, queries, grads, keys, values, probs):
    tokens, width = queries.shape
    ext = keys.shape[0]
    blocks, cols, some = tokens // BLOCK, GROUP * HEAD_DIM, BACKWARD_BLOCKS
    groups = width // cols
    tile = pl.BlockSpec((some * BLOCK, cols), lambda g, i, r: (i, g))
    table = pl.BlockSpec((ext, cols), lambda g, i, r: (0, g))
    return pl.pallas_call(
        partial(attend_back_kernel, blocks),
        grid_spec=pltpu.PrefetchScalarGridSpec(
            num_scalar_prefetch=1,
            grid=(groups, blocks // some),
            in_specs=[
                tile,
                tile,
                table,
                table,
                pl.BlockSpec((1, some, TILES * BLOCK, cols), lambda g, i, r: (g, i, 0, 0)),
            ],
            out_specs=[tile, table, table, pl.BlockSpec((8, cols), lambda g, i, r: (0, g))],
            scratch_shapes=[pltpu.VMEM((ext, cols), f32), pltpu.VMEM((ext, cols), f32)],
        ),
        out_shape=[
            jax.ShapeDtypeStruct((tokens, width), bf16),
            jax.ShapeDtypeStruct((ext, width), bf16),
            jax.ShapeDtypeStruct((ext, width), bf16),
            jax.ShapeDtypeStruct((8, width), f32),
        ],
        compiler_params=pltpu.CompilerParams(vmem_limit_bytes=56 << 20),
        cost_estimate=pl.CostEstimate(
            flops=10 * groups * blocks * TILES * BLOCK * cols * cols,
            bytes_accessed=100 << 20,
            transcendentals=0,
        ),
        name="attend_back",
    )(rows, queries, grads, keys, values, probs)


def normalized(values):
    centred = values - jnp.mean(values, axis=-1, keepdims=True)
    root = lax.rsqrt(jnp.mean(centred * centred, axis=-1, keepdims=True) + epsilon)
    return centred * root, root


def norm_back(grad, normal, root, gain):
    scaled = grad * gain
    along = jnp.mean(scaled * normal, axis=-1, keepdims=True)
    return root * (scaled - jnp.mean(scaled, axis=-1, keepdims=True) - normal * along)


def gelu_and_slope(u):
    square = u * u
    bend = jnp.tanh(gelu_scale * (u + gelu_cubic * (square * u)))
    half = 0.5 * (1.0 + bend)
    slope = half + (0.5 * gelu_scale) * u * (1.0 - bend * bend) * (
        1.0 + (3.0 * gelu_cubic) * square
    )
    return u * half, slope


def middle_kernel(
    att_ref,
    x_ref,
    og_ref,
    wa_ref,
    wi_ref,
    wo_ref,
    vec_ref,
    bi_ref,
    res_ref,
    sum_ref,
    ga_ref,
    dwa_ref,
    dwi_ref,
    dwo_ref,
    dvec_ref,
    dbi_ref,
    normal,
    root,
    low,
    act,
    slope,
    inner,
):
    step, half = pl.program_id(0), pl.num_programs(0) // 2
    tokens, width = x_ref.shape
    slices = [pl.ds(t * ROWS, ROWS) for t in range(tokens // ROWS)]
    bias_attn, gain_one, offset_one, bias_outer, gain_two, offset_two = (
        vec_ref[n : n + 1, :] for n in range(6)
    )

    def row_sum(total, values):
        part = jnp.sum(values, axis=0, keepdims=True)
        return part if total is None else total + part

    @pl.when(step == 0)
    def _():
        for s in slices:
            values = x_ref[s, :].astype(f32) + mm(att_ref[s, :], wa_ref[...]) + bias_attn
            flat, scale = normalized(values)
            normal[s, :] = flat
            root[s, :] = jnp.broadcast_to(scale, (ROWS, 128))
            first = flat * gain_one + offset_one
            low[s, :] = first.astype(bf16)
            sum_ref[s, :] = first + bias_outer

    @pl.when(step < half)
    def _():
        for s in slices:
            active, bend = gelu_and_slope(mm(low[s, :], wi_ref[...]) + bi_ref[0])
            active = active.astype(bf16)
            act[step, s, :] = active
            slope[step, s, :] = bend.astype(bf16)
            sum_ref[s, :] += mm(active, wo_ref[...])

    @pl.when(step == half)
    def _():
        outer_sum, gain_sum, offset_sum = None, None, None
        for s in slices:
            flat, scale = normalized(sum_ref[s, :])
            res_ref[s, :] = (flat * gain_two + offset_two).astype(bf16)
            grad = og_ref[s, :].astype(f32)
            gain_sum = row_sum(gain_sum, grad * flat)
            offset_sum = row_sum(offset_sum, grad)
            second = norm_back(grad, flat, scale, gain_two)
            sum_ref[s, :] = second
            second = second.astype(bf16)
            ga_ref[s, :] = second
            outer_sum = row_sum(outer_sum, second.astype(f32))
        dvec_ref[3:4, :] = outer_sum
        dvec_ref[4:5, :] = gain_sum
        dvec_ref[5:6, :] = offset_sum
        dvec_ref[6:8, :] = jnp.zeros((2, width), f32)

    @pl.when(step >= half)
    def _():
        now = step - half
        total = None
        for s in slices:
            grad = mm_nt(ga_ref[s, :], wo_ref[...]) * slope[now, s, :].astype(f32)
            grad = grad.astype(bf16)
            inner[s, :] = grad
            total = row_sum(total, grad.astype(f32))
            sum_ref[s, :] += mm_nt(grad, wi_ref[...])
        dbi_ref[0] = total
        for n in range(width // 256):
            some = pl.ds(n * 256, 256)
            dwi_ref[some, :] = mm_tn(low[:, some], inner[...]).astype(bf16)
        for n in range(PIECE // 256):
            some = pl.ds(n * 256, 256)
            dwo_ref[some, :] = mm_tn(act[now, :, some], ga_ref[...]).astype(bf16)

    @pl.when(step == 2 * half - 1)
    def _():
        attn_sum, gain_sum, offset_sum = None, None, None
        for s in slices:
            grad, flat = sum_ref[s, :], normal[s, :]
            gain_sum = row_sum(gain_sum, grad * flat)
            offset_sum = row_sum(offset_sum, grad)
            grad = norm_back(grad, flat, root[s, 0:1], gain_one)
            sum_ref[s, :] = grad
            grad = grad.astype(bf16)
            inner[s, :width] = grad
            attn_sum = row_sum(attn_sum, grad.astype(f32))
            ga_ref[s, :] = mm_nt(grad, wa_ref[...]).astype(bf16)
        dvec_ref[0:1, :] = attn_sum
        dvec_ref[1:2, :] = gain_sum
        dvec_ref[2:3, :] = offset_sum
        for n in range(width // 256):
            some = pl.ds(n * 256, 256)
            dwa_ref[some, :] = mm_tn(att_ref[:, some], inner[:, :width]).astype(bf16)


def middle(attended, tokens, out_grad, w_attn, w_inner, w_outer, vectors, bias_inner):
    rows, width = tokens.shape
    steps = w_inner.shape[1] // PIECE
    one = pl.Buffered(1)
    still = pl.BlockSpec((rows, width), lambda i: (0, 0), pipeline_mode=one)
    square = pl.BlockSpec((width, width), lambda i: (0, 0), pipeline_mode=one)
    few = pl.BlockSpec((8, width), lambda i: (0, 0))
    later = lambda i: jnp.maximum(i - steps, 0)
    return pl.pallas_call(
        middle_kernel,
        grid=(2 * steps,),
        in_specs=[
            still,
            still,
            still,
            square,
            pl.BlockSpec((width, PIECE), lambda i: (0, i % steps)),
            pl.BlockSpec((PIECE, width), lambda i: (i % steps, 0)),
            few,
            pl.BlockSpec((1, 1, PIECE), lambda i: (i % steps, 0, 0)),
        ],
        out_specs=[
            still,
            still,
            still,
            square,
            pl.BlockSpec((width, PIECE), lambda i: (0, later(i))),
            pl.BlockSpec((PIECE, width), lambda i: (later(i), 0)),
            few,
            pl.BlockSpec((1, 1, PIECE), lambda i: (later(i), 0, 0)),
        ],
        out_shape=[
            jax.ShapeDtypeStruct((rows, width), bf16),
            jax.ShapeDtypeStruct((rows, width), f32),
            jax.ShapeDtypeStruct((rows, width), bf16),
            jax.ShapeDtypeStruct(w_attn.shape, bf16),
            jax.ShapeDtypeStruct(w_inner.shape, bf16),
            jax.ShapeDtypeStruct(w_outer.shape, bf16),
            jax.ShapeDtypeStruct((8, width), f32),
            jax.ShapeDtypeStruct((steps, 1, PIECE), f32),
        ],
        scratch_shapes=[
            pltpu.VMEM((rows, width), f32),
            pltpu.VMEM((rows, 128), f32),
            pltpu.VMEM((rows, width), bf16),
            pltpu.VMEM((steps, rows, PIECE), bf16),
            pltpu.VMEM((steps, rows, PIECE), bf16),
            pltpu.VMEM((rows, PIECE), bf16),
        ],
        compiler_params=pltpu.CompilerParams(vmem_limit_bytes=60 << 20),
        name="middle",
    )(attended, tokens, out_grad, w_attn, w_inner, w_outer, vectors, bias_inner)


def project_kernel(wide_ref, wk_ref, wv_ref, wq_ref, vec_ref, k_ref, v_ref, q_ref):
    rows = wide_ref.shape[0]
    slices = [pl.ds(t * ROWS, ROWS) for t in range(rows // ROWS)]
    for s in slices:
        k_ref[s, :] = mm(wide_ref[s, :], wk_ref[...]).astype(bf16)
        v_ref[s, :] = (mm(wide_ref[s, :], wv_ref[...]) + vec_ref[7:8, :]).astype(bf16)

    @pl.when(pl.program_id(0) == REACH)
    def _():
        for s in slices:
            queries = mm(wide_ref[s, :], wq_ref[...]) + vec_ref[6:7, :]
            q_ref[s, :] = (query_scale * queries).astype(bf16)


def project(wide, w_key, w_value, w_query, vectors, rows):
    width = wide.shape[1]
    one = pl.Buffered(1)
    tile = pl.BlockSpec((rows, width), lambda i: (i, 0))
    still = pl.BlockSpec((rows, width), lambda i: (0, 0), pipeline_mode=one)
    square = pl.BlockSpec((width, width), lambda i: (0, 0), pipeline_mode=one)
    table = jax.ShapeDtypeStruct(wide.shape, bf16)
    return pl.pallas_call(
        project_kernel,
        grid=(1 + 2 * REACH,),
        in_specs=[tile, square, square, square, pl.BlockSpec((8, width), lambda i: (0, 0))],
        out_specs=[tile, tile, still],
        out_shape=[table, table, jax.ShapeDtypeStruct((rows, width), bf16)],
        compiler_params=pltpu.CompilerParams(vmem_limit_bytes=60 << 20),
        name="project",
    )(wide, w_key, w_value, w_query, vectors)


def tile_plan(segment_ids, random_blocks, tokens):
    heads, total_blocks, _ = random_blocks.shape
    blocks = tokens // BLOCK
    chunk = lax.axis_index("blk") * lax.axis_size("head") + lax.axis_index("head")
    margin = REACH * tokens
    padded = jnp.concatenate(
        [
            jnp.full((margin,), -1, jnp.int32),
            segment_ids,
            jnp.full((margin,), jnp.iinfo(jnp.int32).max, jnp.int32),
        ]
    )
    near = lax.dynamic_slice_in_dim(padded, chunk * tokens, tokens + 2 * margin)
    own = near[margin : margin + tokens]
    before, after = near[: margin + tokens], near[margin:]
    begins = jnp.sum((before[None, :] < own[:, None]).astype(jnp.int32), axis=1)
    ends = margin + jnp.sum((after[None, :] <= own[:, None]).astype(jnp.int32), axis=1)
    docs = jnp.stack([begins, ends]).reshape(2, blocks, BLOCK)
    docs = jnp.tile(jnp.transpose(docs, (1, 0, 2)), (1, 4, GROUP))
    first = begins[::BLOCK] // BLOCK
    here = REACH * blocks + jnp.arange(blocks, dtype=jnp.int32)
    fixed = jnp.stack([here - 1, here, here + 1, first, first + 1], axis=-1)
    picked = lax.dynamic_slice_in_dim(random_blocks, chunk * blocks, blocks, axis=1)
    picked = picked - (chunk - REACH) * blocks
    rows = jnp.concatenate(
        [jnp.broadcast_to(fixed[None], (heads, blocks, 5)), picked], axis=-1
    )
    earlier = jnp.arange(TILES)[None, :] < jnp.arange(TILES)[:, None]
    repeat = jnp.any((rows[..., :, None] == rows[..., None, :]) & earlier, axis=-1)
    rows = jnp.clip(rows, 0, (1 + 2 * REACH) * blocks - 1)
    return (rows + jnp.where(repeat, repeated, 0)).reshape(-1), docs


def side_pairs(blk, head, far):
    pairs = []
    for b in range(blk):
        for h in range(head):
            down = h < head // 2
            if far and h not in (0, head - 1):
                continue
            source = b - 1 if down else b + 1
            if 0 <= source < blk:
                pairs.append((h * blk + source, h * blk + b))
    return pairs


def widen(tokens_rows, blk, head):
    rows = tokens_rows.shape[0]
    h = lax.axis_index("head")
    line = lax.all_gather(tokens_rows, "head", axis=0, tiled=True)
    low = h < head // 2
    near = lax.dynamic_slice_in_dim(line, jnp.where(low, head - 1, 0) * rows, rows)
    far = lax.dynamic_slice_in_dim(line, jnp.where(low, head - 2, 1) * rows, rows)
    near = lax.ppermute(near, ("head", "blk"), side_pairs(blk, head, False))
    far = lax.ppermute(far, ("head", "blk"), side_pairs(blk, head, True))
    whole = jnp.concatenate([far, near, line, near, far], axis=0)
    return lax.dynamic_slice_in_dim(whole, h * rows, (1 + 2 * REACH) * rows)


def narrow(wide_rows, rows, blk, head):
    h = lax.axis_index("head")
    low = h < head // 2
    frame = jnp.zeros(((head + 2 * REACH) * rows, wide_rows.shape[1]), wide_rows.dtype)
    frame = lax.dynamic_update_slice_in_dim(frame, wide_rows, h * rows, 0)
    near = lax.dynamic_slice_in_dim(frame, jnp.where(low, 1, head + REACH) * rows, rows)
    far = lax.dynamic_slice_in_dim(frame, jnp.where(low, 0, head + REACH + 1) * rows, rows)
    back = [(t, s) for s, t in side_pairs(blk, head, False)]
    near = lax.ppermute(near, ("head", "blk"), back)
    back = [(t, s) for s, t in side_pairs(blk, head, True)]
    far = lax.ppermute(far, ("head", "blk"), back)
    line = frame[REACH * rows : (REACH + head) * rows].reshape(head, rows, -1)
    place = jnp.arange(head, dtype=jnp.int32)[:, None, None]
    line = line + jnp.where(place == jnp.where(low, head - 1, 0), near[None], 0)
    line = line + jnp.where(place == jnp.where(low, head - 2, 1), far[None], 0)
    return lax.psum_scatter(line.reshape(head * rows, -1), "head", scatter_dimension=0, tiled=True)


LINE = 4
CORES = 2
PIECES = 4
PIECES_BACK = 8
MESH = pl.DeviceIdType.MESH
NEAR_SLOT = (1, 0, 4, 3)
FAR_SLOT = (0, None, None, 4)
WORK_ORDER = ((3, 1, 0, 4, 2), (0, 4, 3, 1, 2), (4, 0, 1, 3, 2), (1, 3, 4, 0, 2))


def remote(source, target, send, recv, head, blk):
    return pltpu.make_async_remote_copy(
        src_ref=source,
        dst_ref=target,
        send_sem=send,
        recv_sem=recv,
        device_id=(head, blk),
        device_id_type=MESH,
    )


def at_each_head(h, body):
    for hh in range(LINE):
        pl.when(h == hh)(partial(body, hh))


def greet_plane_and_line(h, b, blk):
    barrier = pltpu.get_barrier_semaphore()
    for d in range(1, LINE):
        pl.semaphore_signal(
            barrier, inc=1, device_id=((h + d) % LINE, b), device_id_type=MESH
        )
    for d in range(1, blk):
        pl.semaphore_signal(barrier, inc=1, device_id=(h, (b + d) % blk), device_id_type=MESH)
    pl.semaphore_wait(barrier, LINE - 1 + blk - 1)


def gather_kernel(blk, count, *refs):
    x_ref, shards = refs[0], refs[1 : 1 + count]
    wide, spill, fulls = refs[1 + count], refs[2 + count], refs[3 + count : 3 + 2 * count]
    local, zs, zr, cs, cr, ss, sr, us, ur, ds, dr, ns, nr, fs, fr = refs[3 + 2 * count :]
    h, b = lax.axis_index("head"), lax.axis_index("blk")
    chips = blk // CORES
    chip, core = b // CORES, b % CORES
    sibling = chip * CORES + 1 - core
    rows = x_ref.shape[0] // PIECES

    def piece(ref, p):
        return ref.at[pl.ds(p * rows, rows)]

    def place(hh, j):
        slot = 2 + j - hh
        return wide.at[slot] if 0 <= slot < 5 else spill

    def own(a):
        return pltpu.make_async_copy(shards[a], fulls[a].at[h, b], local.at[a])

    def along(a, d):
        return remote(
            shards[a], fulls[a].at[h, b], zs.at[a, d - 1], zr.at[a, d - 1], (h + d) % LINE, b
        )

    def along_arrives(a, d):
        src = (h - d + LINE) % LINE
        return remote(
            shards[a], fulls[a].at[src, b], zs.at[a, d - 1], zr.at[a, d - 1], (h + d) % LINE, b
        )

    def over(a, e):
        part = fulls[a].at[:, b]
        there = ((chip + e) % chips) * CORES + core
        return remote(part, part, cs.at[a, e - 1], cr.at[a, e - 1], h, there)

    def over_arrives(a, e):
        there = ((chip - e + chips) % chips) * CORES + core
        part = fulls[a].at[:, there]
        return remote(part, part, cs.at[a, e - 1], cr.at[a, e - 1], h, there)

    def across(a, e):
        part = fulls[a].at[:, ((chip - e + chips) % chips) * CORES + core]
        return remote(part, part, ss.at[a, e], sr.at[a, e], h, sibling)

    def across_arrives(a, e):
        part = fulls[a].at[:, ((chip - e + chips) % chips) * CORES + 1 - core]
        return remote(part, part, ss.at[a, e], sr.at[a, e], h, sibling)

    def spread(a):
        for d in range(1, LINE):
            along_arrives(a, d).wait_recv()
        own(a).wait()
        for e in range(1, chips):
            over(a, e).start()
        across(a, 0).start()

    def hand_over(a):
        for e in range(1, chips):
            over_arrives(a, e).wait_recv()
            across(a, e).start()

    def up(hh, j, p):
        source = x_ref if j == hh else place(hh, j)
        return remote(
            piece(source, p), piece(place(hh + 1, j), p), us.at[j, p], ur.at[j, p], (h + 1) % LINE, b
        )

    def up_arrives(hh, j, p):
        target = piece(place(hh, j), p)
        return remote(target, target, us.at[j, p], ur.at[j, p], (h + 1) % LINE, b)

    def down(hh, j, p):
        source = x_ref if j == hh else place(hh, j)
        return remote(
            piece(source, p), piece(place(hh - 1, j), p), ds.at[j, p], dr.at[j, p], (h + 3) % LINE, b
        )

    def down_arrives(hh, j, p):
        target = piece(place(hh, j), p)
        return remote(target, target, ds.at[j, p], dr.at[j, p], (h + 3) % LINE, b)

    def sides(hh, j):
        near, far = (3, 2) if hh < 2 else (0, 1)
        if j == near:
            return [(NEAR_SLOT[hh], ns, nr)]
        if j == far and FAR_SLOT[hh] is not None:
            return [(FAR_SLOT[hh], fs, fr)]
        return []

    def side(hh, j, p, slot, send, recv):
        target = (b + 1) % blk if hh < 2 else (b + blk - 1) % blk
        return remote(
            piece(place(hh, j), p), piece(wide.at[slot], p), send.at[p], recv.at[p], h, target
        )

    def sends_side(hh):
        return b < blk - 1 if hh < 2 else b > 0

    def gets_side(hh):
        return b > 0 if hh < 2 else b < blk - 1

    def side_slots(hh):
        found = [(NEAR_SLOT[hh], ns, nr)]
        if FAR_SLOT[hh] is not None:
            found.append((FAR_SLOT[hh], fs, fr))
        return found

    def fill(n, slot):
        return pltpu.make_async_copy(x_ref, wide.at[slot], local.at[count + 1 + n])

    def own_rows():
        return pltpu.make_async_copy(x_ref, wide.at[2], local.at[count])

    def begin(hh):
        for p in range(PIECES):
            if hh < LINE - 1:
                up(hh, hh, p).start()
            if hh > 0:
                down(hh, hh, p).start()

        @pl.when(jnp.logical_not(gets_side(hh)))
        def _():
            for n, (slot, _, _) in enumerate(side_slots(hh)):
                fill(n, slot).start()

    def pass_on(distance, hh):
        for p in range(PIECES):
            for j, arrives, onward, ends in (
                (hh - distance, up_arrives, up, hh == LINE - 1),
                (hh + distance, down_arrives, down, hh == 0),
            ):
                if not 0 <= j < LINE:
                    continue
                arrives(hh, j, p).wait_recv()
                if not ends:
                    onward(hh, j, p).start()
                for slot, send, recv in sides(hh, j):

                    @pl.when(sends_side(hh))
                    def _(slot=slot, send=send, recv=recv):
                        side(hh, j, p, slot, send, recv).start()

    def finish(hh):
        for p in range(PIECES):
            for j in range(LINE):
                if j <= hh < LINE - 1:
                    up(hh, j, p).wait_send()
                if j >= hh > 0:
                    down(hh, j, p).wait_send()

        @pl.when(sends_side(hh))
        def _():
            for j in range(LINE):
                for slot, send, recv in sides(hh, j):
                    for p in range(PIECES):
                        side(hh, j, p, slot, send, recv).wait_send()

        @pl.when(gets_side(hh))
        def _():
            for slot, send, recv in side_slots(hh):
                for p in range(PIECES):
                    target = piece(wide.at[slot], p)
                    remote(target, target, send.at[p], recv.at[p], h, (b + 1) % blk).wait_recv()

        @pl.when(jnp.logical_not(gets_side(hh)))
        def _():
            for n, (slot, _, _) in enumerate(side_slots(hh)):
                fill(n, slot).wait()

    own_rows().start()
    for a in range(count):
        own(a).start()
    greet_plane_and_line(h, b, blk)
    for a in range(count):
        for d in range(1, LINE):
            along(a, d).start()
    at_each_head(h, begin)
    for a in range(count):
        spread(a)
    at_each_head(h, partial(pass_on, 1))
    for a in range(count - 2):
        hand_over(a)
    at_each_head(h, partial(pass_on, 2))
    hand_over(count - 2)
    at_each_head(h, partial(pass_on, 3))
    hand_over(count - 1)
    for a in range(count):
        for d in range(1, LINE):
            along(a, d).wait_send()
        for e in range(1, chips):
            over(a, e).wait_send()
        for e in range(chips):
            across(a, e).wait_send()
            across_arrives(a, e).wait_recv()
    own_rows().wait()
    at_each_head(h, finish)


def gather(tokens, shards, blk):
    rows, width = tokens.shape
    count, chips = len(shards), blk // CORES
    anywhere = pl.BlockSpec(memory_space=pl.ANY)
    dma = pltpu.SemaphoreType.DMA
    outs = pl.pallas_call(
        partial(gather_kernel, blk, count),
        out_shape=[
            jax.ShapeDtypeStruct((5, rows, width), tokens.dtype),
            jax.ShapeDtypeStruct((rows, width), tokens.dtype),
        ]
        + [jax.ShapeDtypeStruct((LINE, blk) + s.shape, s.dtype) for s in shards],
        in_specs=[anywhere] * (1 + count),
        out_specs=[anywhere] * (2 + count),
        scratch_shapes=[dma((count + 3,))]
        + [dma((count, LINE - 1))] * 2
        + [dma((count, chips - 1))] * 2
        + [dma((count, chips))] * 2
        + [dma((LINE, PIECES))] * 4
        + [dma((PIECES,))] * 4,
        compiler_params=pltpu.CompilerParams(collective_id=0, has_side_effects=True),
        name="gather",
    )(tokens, *shards)
    return outs[0], outs[2:]


def pair_kernel(blk, *refs):
    chips = blk // CORES
    grads, outs, rest = refs[:2], refs[2 : 2 + chips], refs[2 + chips :]
    held, arrived, (load, send, recv) = rest[:2], rest[2:4], rest[4:]
    h, b = lax.axis_index("head"), lax.axis_index("blk")
    chip, core = b // CORES, b % CORES
    sibling = chip * CORES + 1 - core

    def part(a, there):
        if a == 0:
            return grads[a].at[:, there, :, pl.ds(3 * 768, 768)]
        return grads[a].at[:, there]

    def mine(a, e):
        there = ((chip + e) % chips) * CORES + core
        return pltpu.make_async_copy(part(a, there), held[a].at[e], load.at[a, e])

    def across(a, e):
        there = ((chip + e) % chips) * CORES + 1 - core
        return remote(
            part(a, there), arrived[a].at[e], send.at[a, e], recv.at[a, e], h, sibling
        )

    order = [e % chips for e in range(1, chips + 1)]
    for e in order:
        for a in range(2):
            mine(a, e).start()
    barrier = pltpu.get_barrier_semaphore()
    pl.semaphore_signal(barrier, inc=1, device_id=(h, sibling), device_id_type=MESH)
    pl.semaphore_wait(barrier, 1)
    for e in order:
        for a in range(2):
            across(a, e).start()
    for e in order:
        for a in range(2):
            mine(a, e).wait()
            across(a, e).wait_recv()

        def one(n, carry, e=e):
            inner, outer = (
                held[a][e, n].astype(f32) + arrived[a][e, n].astype(f32) for a in range(2)
            )
            spare = jnp.zeros((8, 768), f32)
            outs[e][n, 0:32] = jnp.concatenate([inner, spare], axis=0).astype(bf16)
            outs[e][n, 32:128] = outer.astype(bf16)
            return carry

        lax.fori_loop(0, LINE, one, 0)
    for e in order:
        for a in range(2):
            across(a, e).wait_send()


def pair_sums(grads, blk):
    chips = blk // CORES
    shard = [(24, 768), (96, 768)]
    dma = pltpu.SemaphoreType.DMA
    inside = pl.BlockSpec(memory_space=pltpu.VMEM)
    return pl.pallas_call(
        partial(pair_kernel, blk),
        out_shape=[jax.ShapeDtypeStruct((LINE, 128, 768), bf16)] * chips,
        in_specs=[pl.BlockSpec(memory_space=pl.ANY)] * 2,
        out_specs=[inside] * chips,
        scratch_shapes=[pltpu.VMEM((chips, LINE) + s, bf16) for s in shard] * 2
        + [dma((2, chips))] * 3,
        compiler_params=pltpu.CompilerParams(
            collective_id=2, has_side_effects=True, vmem_limit_bytes=56 << 20
        ),
        name="pair_sums",
    )(*grads)


def over_plane(sums, blk, head):
    chips = blk // CORES
    received = [sums[0]]
    for e in range(1, chips):
        pairs = [
            (
                h * blk + k * CORES + c,
                h * blk + ((k + e) % chips) * CORES + c,
            )
            for h in range(head)
            for k in range(chips)
            for c in range(CORES)
        ]
        received.append(lax.ppermute(sums[e], ("head", "blk"), pairs))
    return received


def reduce_kernel(blk, count, *refs):
    small_ref, wide_ref, query_ref, key_ref, value_ref = refs[:5]
    weights, first_ref = refs[5:8], refs[8]
    chips = blk // CORES
    early, raw = refs[9 : 9 + chips], refs[9 + chips : 11 + chips]
    rest = refs[11 + chips :]
    sum_ref, outs, early_outs = rest[0], rest[1 : 1 + count], rest[1 + count : 4 + count]
    early_sum, early_in, es, er = rest[4 + count : 8 + count]
    totals, (wide_in, key_in, value_in, fed) = rest[8 + count : 11 + count], rest[11 + count : 15 + count]
    rest = rest[15 + count :]
    weight_in, early_here, loaded = rest[:3], rest[3 : 3 + chips], rest[3 + chips]
    rest = rest[4 + chips :]
    extra = count
    held, from_core, rest = rest[: count + 1], rest[count + 1 : 2 * count + 1], rest[2 * count + 1 :]
    from_chip, from_line, rest = rest[: count + 1], rest[count + 1 : 2 * count + 2], rest[2 * count + 2 :]
    raw_own, raw_in, (rl, rs, rr), rest = rest[:2], rest[2:4], rest[4:7], rest[7:]
    frame, arrived, aside = rest[:3]
    load, ss, sr, cs, cr, zs, zr, us, ur, ds, dr, ns, nr, fs, fr = rest[3:]
    grads = (small_ref,) + tuple(totals)
    h, b = lax.axis_index("head"), lax.axis_index("blk")
    chip, core = b // CORES, b % CORES
    sibling = chip * CORES + 1 - core
    chunk_rows = sum_ref.shape[0]
    rows = chunk_rows // PIECES_BACK

    feed_rows = wide_in.shape[1]
    halves = chunk_rows // feed_rows
    slots = 1 + 2 * REACH

    def slot_at(n):
        slot = REACH
        for hh in range(LINE):
            for k in range(slots):
                slot = jnp.where((h == hh) & (n == k), WORK_ORDER[hh][k], slot)
        return slot

    def feed(slot, half):
        some = pl.ds(slot * chunk_rows + half * feed_rows, feed_rows)
        return [
            pltpu.make_async_copy(source.at[some], target.at[half], fed.at[n, half])
            for n, (source, target) in enumerate(
                ((wide_ref, wide_in), (key_ref, key_in), (value_ref, value_in))
            )
        ]

    def feed_queries(half):
        some = pl.ds(half * feed_rows, feed_rows)
        wide_some = pl.ds(REACH * chunk_rows + half * feed_rows, feed_rows)
        return [
            pltpu.make_async_copy(wide_ref.at[wide_some], wide_in.at[half], fed.at[0, half]),
            pltpu.make_async_copy(query_ref.at[some], key_in.at[half], fed.at[1, half]),
        ]

    def start(copies):
        for copy in copies:
            copy.start()

    def wait(copies):
        for copy in copies:
            copy.wait()

    def standing():
        pairs = list(zip(weights, weight_in)) + list(zip(early, early_here)) + [(first_ref, sum_ref)]
        return [
            pltpu.make_async_copy(source, target, loaded.at[n])
            for n, (source, target) in enumerate(pairs)
        ]

    def add_product(total, left, right, fresh):
        half = left.shape[1] // 2
        for n in range(2):
            lines = LINE // 2
            part = mm_tn(left[:, n * half : (n + 1) * half], right)
            part = part.reshape((lines,) + total.shape[1:])
            here = pl.ds(n * lines, lines)
            total[here] = part if fresh else total[here] + part

    def work(n, carry):
        slot = slot_at(n)
        for half in range(halves):
            if half + 1 < halves:
                start(feed(slot, half + 1))
            else:

                @pl.when(n + 1 < slots)
                def _():
                    start(feed(slot_at(n + 1), 0))

            wait(feed(slot, half))
            for t in range(feed_rows // ROWS):
                s = pl.ds(t * ROWS, ROWS)
                grad = mm_nt(key_in[half, s], weight_in[1][...]) + mm_nt(
                    value_in[half, s], weight_in[2][...]
                )
                frame[slot, pl.ds(half * feed_rows + t * ROWS, ROWS)] = grad.astype(bf16)
            add_product(totals[1], wide_in[half], key_in[half], False)
            add_product(totals[2], wide_in[half], value_in[half], False)
        for hh in range(LINE):
            for k in range(slots):
                pl.when((h == hh) & (n == k))(partial(send_off, hh, WORK_ORDER[hh][k]))
        return carry

    def query_work():
        start(feed_queries(0))
        for half in range(halves):
            if half + 1 < halves:
                start(feed_queries(half + 1))
            wait(feed_queries(half))
            for t in range(feed_rows // ROWS):
                s = pl.ds(t * ROWS, ROWS)
                here = pl.ds(half * feed_rows + t * ROWS, ROWS)
                sum_ref[here] += mm_nt(key_in[half, s], weight_in[0][...])
            add_product(totals[0], wide_in[half], key_in[half], half == 0)

    def mine(a, k):
        return pltpu.make_async_copy(grads[a].at[:, k * CORES + core], held[a].at[k], load.at[a, k])

    def raw_part(n, there):
        return raw[n].at[:, there, :, pl.ds(0, raw_own[n].shape[3])]

    def mine_raw(n, k):
        there = k * CORES + core
        return pltpu.make_async_copy(raw_part(n, there), raw_own[n].at[k], rl.at[n, k])

    def across_raw(n, k):
        there = k * CORES + 1 - core
        return remote(raw_part(n, there), raw_in[n].at[k], rs.at[n, k], rr.at[n, k], h, sibling)

    def pack_raw(k):
        for n in range(2):
            mine_raw(n, k).wait()
            across_raw(n, k).wait_recv()

        def one(m, carry):
            attn, inner = (
                raw_own[n][k, m].astype(f32) + raw_in[n][k, m].astype(f32) for n in range(2)
            )
            parts = [attn] + [inner[:, c * 768 : (c + 1) * 768] for c in range(3)]
            for c in range(2):
                both = jnp.concatenate(parts[2 * c : 2 * c + 2], axis=0)
                held[extra][k, m, 48 * c : 48 * (c + 1)] = both.astype(bf16)
            return carry

        lax.fori_loop(0, LINE, one, 0)

    def across(a, k):
        return remote(
            grads[a].at[:, k * CORES + 1 - core],
            from_core[a].at[k],
            ss.at[a, k],
            sr.at[a, k],
            h,
            sibling,
        )

    def over(a, e):
        k = (chip + e) % chips
        return remote(
            held[a].at[k],
            from_chip[a].at[e - 1],
            cs.at[a, e - 1],
            cr.at[a, e - 1],
            h,
            k * CORES + core,
        )

    def along(a, d):
        there = (h + d) % LINE
        return remote(
            held[a].at[chip, there],
            from_line[a].at[d - 1],
            zs.at[a, d - 1],
            zr.at[a, d - 1],
            there,
            b,
        )

    def add_cores(a, k):
        def one(n, carry):
            own = held[a][k, n] if a == 0 else grads[a][n, k * CORES + core]
            held[a][k, n] = (own + from_core[a][k, n]).astype(held[a].dtype)
            return carry

        lax.fori_loop(0, LINE, one, 0)

    def to_chips(a):
        for k in range(chips):
            if a == 0:
                mine(a, k).wait()
            across(a, k).wait_recv()
        for e in range(1, chips):
            add_cores(a, (chip + e) % chips)
            over(a, e).start()
        add_cores(a, chip)

    def to_line(a):
        for e in range(1, chips):
            over(a, e).wait_recv()

        def one(n, carry):
            total = held[a][chip, n].astype(f32)
            for e in range(1, chips):
                total = total + from_chip[a][e - 1, n].astype(f32)
            held[a][chip, n] = total.astype(held[a].dtype)
            return carry

        lax.fori_loop(0, LINE, one, 0)
        for d in range(1, LINE):
            along(a, d).start()

    def to_owner(a):
        for d in range(1, LINE):
            along(a, d).wait_recv()
        total = held[a][chip, h].astype(f32)
        for d in range(1, LINE):
            total = total + from_line[a][d - 1].astype(f32)
        outs[a][...] = total

    def early_along(d):
        there = (h + d) % LINE
        return remote(
            early_sum.at[there], early_in.at[d - 1], es.at[d - 1], er.at[d - 1], there, b
        )

    def early_to_line():
        def one(n, carry):
            total = early_here[0][n].astype(f32)
            for ref in early_here[1:]:
                total = total + ref[n].astype(f32)
            early_sum[n] = total.astype(bf16)
            return carry

        lax.fori_loop(0, LINE, one, 0)
        for d in range(1, LINE):
            early_along(d).start()

    def early_to_owner():
        for d in range(1, LINE):
            early_along(d).wait_recv()
        total = early_sum[h].astype(f32)
        for d in range(1, LINE):
            total = total + early_in[d - 1].astype(f32)
        attn_ref, inner_ref, outer_ref = early_outs
        inner_ref[:, 3 * 768 :] = total[:24]
        outer_ref[...] = total[32:]
        for d in range(1, LINE):
            along(extra, d).wait_recv()
        total = held[extra][chip, h].astype(f32)
        for d in range(1, LINE):
            total = total + from_line[extra][d - 1].astype(f32)
        attn_ref[...] = total[:24]
        for n in range(3):
            inner_ref[:, n * 768 : (n + 1) * 768] = total[24 * (n + 1) : 24 * (n + 2)]

    def part(p):
        return pl.ds(p * rows, rows)

    def piece(ref, p):
        return ref.at[part(p)]

    def add_rows(target, j, source, n, p):
        def one(step, carry):
            some = pl.ds(p * rows + step * 64, 64)
            target[j, some] = (
                target[j, some].astype(f32) + source[n, some].astype(f32)
            ).astype(target.dtype)
            return carry

        lax.fori_loop(0, rows // 64, one, 0)

    def slot_of(hh, j):
        slot = 2 + j - hh
        return slot if 0 <= slot < slots else slots

    def arrival(hh, j, upward):
        return arrived.at[LINE if j == hh and not upward else j]

    def up(hh, j, p):
        return remote(
            piece(frame.at[slot_of(hh, j)], p),
            piece(arrival(hh + 1, j, True), p),
            us.at[j, p],
            ur.at[j, p],
            (h + 1) % LINE,
            b,
        )

    def up_arrives(hh, j, p):
        here = piece(arrival(hh, j, True), p)
        return remote(here, here, us.at[j, p], ur.at[j, p], (h + 1) % LINE, b)

    def down(hh, j, p):
        return remote(
            piece(frame.at[slot_of(hh, j)], p),
            piece(arrival(hh - 1, j, False), p),
            ds.at[j, p],
            dr.at[j, p],
            (h + 3) % LINE,
            b,
        )

    def down_arrives(hh, j, p):
        here = piece(arrival(hh, j, False), p)
        return remote(here, here, ds.at[j, p], dr.at[j, p], (h + 3) % LINE, b)

    def side_parts(hh):
        near, far = (3, 2) if hh < 2 else (0, 1)
        found = [(NEAR_SLOT[hh], near, 0, ns, nr)]
        if FAR_SLOT[hh] is not None:
            found.append((FAR_SLOT[hh], far, 1, fs, fr))
        return found

    def side(hh, slot, n, send, recv, p):
        target = (b + blk - 1) % blk if hh < 2 else (b + 1) % blk
        return remote(
            piece(frame.at[slot], p), piece(aside.at[n], p), send.at[p], recv.at[p], h, target
        )

    def sends_side(hh):
        return b > 0 if hh < 2 else b < blk - 1

    def gets_side(hh):
        return b < blk - 1 if hh < 2 else b > 0

    def send_off(hh, slot):
        @pl.when(sends_side(hh))
        def _():
            for p in range(PIECES_BACK):
                for side_slot, _, n, send, recv in side_parts(hh):
                    if side_slot == slot:
                        side(hh, slot, n, send, recv, p).start()

        for p in range(PIECES_BACK):
            if hh == 0 and slot == slot_of(0, 1):
                up(hh, 1, p).start()
            if hh == LINE - 1 and slot == slot_of(LINE - 1, 2):
                down(hh, 2, p).start()

    def take_sides(hh):
        for p in range(PIECES_BACK):
            for _, j, n, send, recv in side_parts(hh):

                @pl.when(gets_side(hh))
                def _(j=j, n=n, send=send, recv=recv):
                    here = piece(aside.at[n], p)
                    remote(here, here, send.at[p], recv.at[p], h, (b + 1) % blk).wait_recv()
                    add_rows(frame, slot_of(hh, j), aside, n, p)

                if hh == 0:
                    up(hh, j, p).start()
                if hh == LINE - 1:
                    down(hh, j, p).start()

    def pass_on(hh):
        moves = []
        if hh == 1:
            moves = [(3, True), (2, True), (0, False)]
        if hh == 2:
            moves = [(0, False), (1, False), (3, True)]
        for p in range(PIECES_BACK):
            for j, upward in moves:
                (up_arrives if upward else down_arrives)(hh, j, p).wait_recv()
                add_rows(frame, slot_of(hh, j), arrived, j, p)
                (up if upward else down)(hh, j, p).start()

    def finish(hh):
        for p in range(PIECES_BACK):
            sources = []
            if hh > 0:
                up_arrives(hh, hh, p).wait_recv()
                sources.append(hh)
            if hh < LINE - 1:
                down_arrives(hh, hh, p).wait_recv()
                sources.append(LINE)

            def one(step, carry, p=p, sources=tuple(sources)):
                some = pl.ds(p * rows + step * 64, 64)
                total = sum_ref[some] + frame[REACH, some].astype(f32)
                for n in sources:
                    total = total + arrived[n, some].astype(f32)
                sum_ref[some] = total
                return carry

            lax.fori_loop(0, rows // 64, one, 0)
        for p in range(PIECES_BACK):
            for j in range(LINE):
                if j > hh:
                    up(hh, j, p).wait_send()
                if j < hh:
                    down(hh, j, p).wait_send()

        @pl.when(sends_side(hh))
        def _():
            for p in range(PIECES_BACK):
                for slot, _, n, send, recv in side_parts(hh):
                    side(hh, slot, n, send, recv, p).wait_send()

    start(feed(slot_at(0), 0))
    start(standing())
    for k in range(chips):
        mine(0, k).start()
        for n in range(2):
            mine_raw(n, k).start()
    frame[slots] = jnp.zeros(frame.shape[1:], frame.dtype)
    for n in (1, 2):
        totals[n][...] = jnp.zeros_like(totals[n])
    greet_plane_and_line(h, b, blk)
    for k in range(chips):
        for n in range(2):
            across_raw(n, k).start()
    ready = standing()
    wait(ready[3:-1])
    early_to_line()
    wait(ready[:3] + ready[-1:])
    lax.fori_loop(0, slots, work, 0)
    for a in (0, 2, 3):
        for k in range(chips):
            across(a, k).start()
    for e in range(1, chips):
        pack_raw((chip + e) % chips)
        over(extra, e).start()
    pack_raw(chip)
    query_work()
    for k in range(chips):
        across(1, k).start()
    at_each_head(h, take_sides)
    for a in range(count):
        to_chips(a)
    at_each_head(h, pass_on)
    for a in range(count + 1):
        to_line(a)
    at_each_head(h, finish)
    early_to_owner()
    for d in range(1, LINE):
        early_along(d).wait_send()
    for a in range(count):
        to_owner(a)
    for a in range(count):
        for k in range(chips):
            across(a, k).wait_send()
    for a in range(count + 1):
        for e in range(1, chips):
            over(a, e).wait_send()
        for d in range(1, LINE):
            along(a, d).wait_send()
    for k in range(chips):
        for n in range(2):
            across_raw(n, k).wait_send()


def reduce_to_owners(small, wide, projected, weights, first, early, raw, blk):
    rows, width = first.shape
    count, chips = 4, blk // CORES
    anywhere = pl.BlockSpec(memory_space=pl.ANY)
    inside = pl.BlockSpec(memory_space=pltpu.VMEM)
    dma = pltpu.SemaphoreType.DMA
    square = (width // (LINE * blk), width)
    shard = [small.shape[2:]] + [square] * 3
    kinds = [f32] + [bf16] * 4
    travels = shard + [(96, 768)]
    early_shapes = ((24, 768), (24, 3072), (96, 768))
    outs = pl.pallas_call(
        partial(reduce_kernel, blk, count),
        out_shape=[jax.ShapeDtypeStruct((rows, width), f32)]
        + [jax.ShapeDtypeStruct(s, f32) for s in shard]
        + [jax.ShapeDtypeStruct(s, f32) for s in early_shapes],
        in_specs=[anywhere] * (11 + chips),
        out_specs=[inside] * (4 + count),
        scratch_shapes=[
            pltpu.VMEM(early[0].shape, bf16),
            pltpu.VMEM((LINE - 1,) + early[0].shape[1:], bf16),
            dma((LINE - 1,)),
            dma((LINE - 1,)),
        ]
        + [pltpu.VMEM((LINE, blk) + square, f32)] * 3
        + [pltpu.VMEM((2, rows // 2, width), bf16)] * 3
        + [dma((3, 2))]
        + [pltpu.VMEM((width, width), bf16)] * 3
        + [pltpu.VMEM(early[0].shape, bf16)] * chips
        + [dma((4 + chips,))]
        + [pltpu.VMEM((chips, LINE) + s, t) for s, t in zip(travels, kinds)]
        + [pltpu.VMEM((chips, LINE) + s, f32) for s in shard]
        + [pltpu.VMEM((chips - 1, LINE) + s, t) for s, t in zip(travels, kinds)]
        + [pltpu.VMEM((LINE - 1,) + s, t) for s, t in zip(travels, kinds)]
        + [pltpu.VMEM((chips, LINE, 24, size), bf16) for size in (768, 3 * 768)] * 2
        + [dma((2, chips))] * 3
        + [
            pltpu.VMEM((2 + 2 * REACH, rows, width), bf16),
            pltpu.VMEM((LINE + 1, rows, width), bf16),
            pltpu.VMEM((2, rows, width), bf16),
        ]
        + [dma((count + 1, chips))] * 3
        + [dma((count + 1, chips - 1))] * 2
        + [dma((count + 1, LINE - 1))] * 2
        + [dma((LINE, PIECES_BACK))] * 4
        + [dma((PIECES_BACK,))] * 4,
        compiler_params=pltpu.CompilerParams(
            collective_id=1, has_side_effects=True, vmem_limit_bytes=62 << 20
        ),
        name="reduce_to_owners",
    )(small, wide, *projected, *weights, first, *early, *raw)
    return outs[0], outs[1:-3], outs[-3:]


def whole(shard):
    return lax.all_gather(shard, ("head", "blk"), axis=0, tiled=True)


def shared_out(grad):
    return lax.psum_scatter(grad.astype(bf16), ("head", "blk"), scatter_dimension=0, tiled=True).astype(f32)


def padded_to(flat, size):
    return jnp.pad(flat, [(0, 0)] * (flat.ndim - 1) + [(0, size - flat.shape[-1])])


def per_device(blk, head, tokens, *rest):
    weights, vectors, (out_grad, segment_ids, random_blocks) = rest[:6], rest[6:15], rest[15:]
    rows = tokens.shape[0]
    by_kernel = head == LINE and blk == LINE * CORES
    short = [vectors[n] for n in (2, 3, 4, 6, 7, 8, 0, 1)]
    if by_kernel:
        packed = jnp.concatenate(
            [
                padded_to(jnp.stack(short), 128),
                padded_to(vectors[5][None], 128),
                jnp.zeros((7, 128), bf16),
            ]
        )
        wide, fulls = gather(tokens, [packed] + list(weights), blk)
        wide = wide.reshape(-1, tokens.shape[1])
        w_query, w_key, w_value, w_attn, w_inner, w_outer = [
            w.reshape(-1, w.shape[-1]) for w in fulls[1:]
        ]
        table = fulls[0].reshape(head * blk, 16, 128)
    else:
        wide = widen(tokens, blk, head)
        w_query, w_key, w_value, w_attn, w_inner, w_outer = [whole(w) for w in weights]
        packed = jnp.concatenate(
            [padded_to(jnp.stack(short), 128), padded_to(vectors[5][None], 128)]
        )
        table = whole(packed[None])
    short_rows = jnp.transpose(table[:, :8, : short[0].shape[0]], (1, 0, 2)).astype(f32)
    short_rows = short_rows.reshape(8, -1)
    bias_inner = table[:, 8, : vectors[5].shape[0]].astype(f32).reshape(-1, 1, PIECE)

    rows_of, docs = tile_plan(segment_ids, random_blocks, rows)
    keys, values, queries = project(wide, w_key, w_value, w_query, short_rows, rows)
    attended, probs = attend(rows_of, queries, keys, values, docs)

    result, grad_first_sum, grad_attended, grad_w_attn, grad_w_inner, grad_w_outer, sums_d, sums_ff = (
        middle(
            attended,
            tokens,
            out_grad,
            w_attn,
            w_inner,
            w_outer,
            short_rows,
            bias_inner,
        )
    )

    early_grads = [grad_w_attn, grad_w_inner, grad_w_outer]
    if by_kernel:
        raw = [g.reshape(head, blk, -1, g.shape[-1]) for g in early_grads]
        early = over_plane(pair_sums(raw[1:], blk), blk, head)
    grad_scaled, grad_keyed, grad_valued, sums_qv = attend_back(
        rows_of, queries, grad_attended, keys, values, probs
    )
    sums = jnp.concatenate([sums_d[:6], sums_qv[6:]])
    sums = jnp.transpose(sums.reshape(8, head * blk, -1), (1, 0, 2))
    packed = jnp.concatenate(
        [
            padded_to(sums, 128),
            padded_to(sums_ff.reshape(head * blk, 1, -1), 128),
            jnp.zeros((head * blk, 7, 128), f32),
        ],
        axis=1,
    )
    if by_kernel:
        grad_tokens, late, early_sum = reduce_to_owners(
            packed.reshape(head, blk, 16, 128),
            wide,
            (grad_scaled, grad_keyed, grad_valued),
            (w_query, w_key, w_value),
            grad_first_sum,
            early,
            raw[:2],
            blk,
        )
        matrix_grads = tuple(late[1:]) + tuple(early_sum)
        packed = late[0]
    else:
        grad_wide = (mm_nt(grad_keyed, w_key) + mm_nt(grad_valued, w_value)).astype(bf16)
        grad_tokens = (
            grad_first_sum
            + mm_nt(grad_scaled, w_query)
            + narrow(grad_wide, rows, blk, head).astype(f32)
        )
        late_grads = [mm_tn(tokens, grad_scaled), mm_tn(wide, grad_keyed), mm_tn(wide, grad_valued)]
        matrix_grads = tuple(shared_out(g) for g in late_grads + early_grads)
        packed = lax.psum_scatter(packed, ("head", "blk"), scatter_dimension=0, tiled=True)[0]
    order = (6, 7, 0, 1, 2, 8, 3, 4, 5)
    vector_grads = tuple(packed[n, : v.shape[0]] for n, v in zip(order, vectors))
    return (result, grad_tokens) + matrix_grads + vector_grads


def solution(mesh):
    row = P(("blk", "head"), None)
    matrix = P(("head", "blk"), None)
    vector = P(("head", "blk"))
    return jax.shard_map(
        partial(per_device, mesh.shape["blk"], mesh.shape["head"]),
        mesh=mesh,
        in_specs=(row,) + (matrix,) * 6 + (vector,) * 9 + (row, P(), P()),
        out_specs=(row, row) + (matrix,) * 6 + (vector,) * 9,
        check_vma=False,
    )
```
